32 devices in a mesh: seq: 8 (over y, x, core), fsdp: 4 (over z).
Axes of the slice: x: 2, y: 2, z: 4, core: 2. Of those that a mesh axis runs over, the one named last changes fastest.
Arguments:
- hidden_in: bfloat16 [8, 1024, 1536], P('fsdp', 'seq'), may hold values from -6 to 6
- out_grad: bfloat16 [8, 1024, 1536], P('fsdp', 'seq'), may hold values from -6 to 6
- lengths: int32 [8, 4], P('fsdp'), may hold values from 0 to 1024, as said below
- in_proj: float32 [1536, 6448], P(('seq', 'fsdp')), may hold values from -0.15625 to 0.15625
- in_first: float32 [1536, 6448], P(('seq', 'fsdp')), may hold values from -56 to 56
- in_second: float32 [1536, 6448], P(('seq', 'fsdp')), may hold values from 409.6 to 1638.4
- out_proj: float32 [3072, 1536], P(('seq', 'fsdp')), may hold values from -0.109375 to 0.109375
- out_first: float32 [3072, 1536], P(('seq', 'fsdp')), may hold values from -56 to 56
- out_second: float32 [3072, 1536], P(('seq', 'fsdp')), may hold values from 409.6 to 1638.4
- vector: float32 [21392], replicated, may hold values from -8 to 4, as said below
- vector_first: float32 [21392], replicated, may hold values from -56 to 56
- vector_second: float32 [21392], replicated, may hold values from 409.6 to 1638.4
Outputs:
- mixed: bfloat16 [8, 1024, 1536], P('fsdp', 'seq')
- input_grad: float32 [8, 1024, 1536], P('fsdp', 'seq')
- in_first_new: float32 [1536, 6448], P(('seq', 'fsdp'))
- in_second_new: float32 [1536, 6448], P(('seq', 'fsdp'))
- in_proj_new: float32 [1536, 6448], P(('seq', 'fsdp'))
- out_first_new: float32 [3072, 1536], P(('seq', 'fsdp'))
- out_second_new: float32 [3072, 1536], P(('seq', 'fsdp'))
- out_proj_new: float32 [3072, 1536], P(('seq', 'fsdp'))
- vector_first_new: float32 [21392], replicated
- vector_second_new: float32 [21392], replicated
- vector_new: float32 [21392], replicated
The draws below stay inside these ranges and needn't reach their ends.
Inputs may be any that keep to these rules, and one draw needn't show every extreme that they name: Row s holds the lengths of the sequences laid end to end in stream s, zero lengths allowed; each row sums to 1024; among the 2 streams of each index of fsdp, one is a single sequence of 1024 positions, and in each of the others some sequence ends at a positive multiple of 128 positions below 1024. `vector`: the gains lie in 0.9 to 1.1, dt_bias in -3 to -1, a_log in -8 to -1.5, d_skip in 1 to 4.
All inputs are finite; a program needn't handle non-finite values.
Results may differ from the reference program's by a relative error of at most 0.0085.
Values may be sent and summed in bfloat16 or wider, within the bound.
A program may use at most 384 MiB of HBM per device.

```python
import jax
import jax.numpy as jnp
from jax import lax

D = 1536
HEADS = 48
HEAD_DIM = 64
STATE = 128
CONV = 4
SEGS = 4
STEP = 5
TOK_SEQ = 128
STREAMS_DEV = 2
INNER = 3072
PROJ = 6448
NVEC = 21392
LENGTH = 1024
STREAMS = 8


def draw_lengths(key, part):
    key = jax.random.fold_in(key, 11)
    cut_key, edge_key, pick_key = jax.random.split(key, 3)
    blocks = LENGTH // TOK_SEQ
    edge = TOK_SEQ * jax.random.randint(edge_key, (STREAMS, 1), 1, blocks, dtype=jnp.int32)
    loose = jax.random.randint(cut_key, (STREAMS, SEGS - 2), 1, LENGTH, dtype=jnp.int32)
    cuts = jnp.sort(jnp.concatenate([edge, loose], axis=1), axis=1)
    edges = jnp.concatenate([jnp.zeros((STREAMS, 1), jnp.int32), cuts, jnp.full((STREAMS, 1), LENGTH, jnp.int32)], axis=1)
    ragged = edges[:, 1:] - edges[:, :-1]
    groups = STREAMS // STREAMS_DEV
    chosen = jax.random.randint(pick_key, (groups,), 0, STREAMS_DEV, dtype=jnp.int32)
    within = jnp.arange(STREAMS, dtype=jnp.int32) % STREAMS_DEV
    whole_row = jnp.repeat(chosen, STREAMS_DEV) == within
    single = jnp.zeros((SEGS,), jnp.int32).at[0].set(LENGTH)
    return jnp.where(whole_row[:, None], single[None, :], ragged).astype(jnp.int32)


def draw_vector(key, part):
    key = jax.random.fold_in(key, 23)
    inner = HEADS * HEAD_DIM
    width = inner + 2 * STATE
    keys = jax.random.split(key, 7)
    g_norm = 1.0 + 0.1 * jax.random.uniform(keys[0], (D,), jnp.float32, -1.0, 1.0)
    g_inner = 1.0 + 0.1 * jax.random.uniform(keys[1], (inner,), jnp.float32, -1.0, 1.0)
    conv_w = 0.5 * jax.random.truncated_normal(keys[2], -4.0, 4.0, (CONV * width,), jnp.float32)
    conv_b = 0.3 * jax.random.truncated_normal(keys[3], -4.0, 4.0, (width,), jnp.float32)
    dt_bias = jax.random.uniform(keys[4], (HEADS,), jnp.float32, -3.0, -1.0)
    a_log = jax.random.uniform(keys[5], (HEADS,), jnp.float32, -8.0, -1.5)
    d_skip = jax.random.uniform(keys[6], (HEADS,), jnp.float32, 1.0, 4.0)
    return jnp.concatenate([g_norm, g_inner, conv_w, conv_b, dt_bias, a_log, d_skip]).astype(jnp.float32)


def block_levels(key, shape, cuts, low, high):
    factor_of = 1.0
    for position, parts in cuts:
        heights = jax.random.uniform(jax.random.fold_in(jax.random.fold_in(key, 6), position), (parts,), jnp.float32, low / len(cuts), high / len(cuts))
        factor_of = factor_of * jnp.repeat(jnp.exp(heights), shape[position] // parts).reshape((-1,) + (1,) * (len(shape) - 1 - position))
    return factor_of


def scatter_about(own_key, shape, deviation, reach, cuts=(), kind=jnp.bfloat16):
    array = jax.random.normal(own_key, shape, jnp.float32) * deviation
    if len(cuts) > 0:
        array = block_levels(own_key, shape, cuts, -0.22, 0.18) * array
    return jnp.clip(array, min=-reach, max=reach).astype(kind)


def setup_inputs(seed: int = 0) -> dict:
    key_of = jax.random.split(jax.random.key(seed), 13)
    return {
        "hidden_in": scatter_about(key_of[0], (STREAMS, LENGTH, D), 1.0, 6.0, ((0, 4), (1, 8))),
        "out_grad": scatter_about(key_of[1], (STREAMS, LENGTH, D), 1.0, 6.0, ((0, 4), (1, 8))),
        "lengths": draw_lengths(jax.random.fold_in(key_of[12], 71), 0),
        "in_proj": scatter_about(key_of[3], (D, PROJ), D ** -0.5, 0.15625, ((0, 32),), jnp.float32),
        "in_first": scatter_about(key_of[4], (D, PROJ), (0.1 * (STREAMS * LENGTH) ** 0.5), 56.0, ((0, 32),), jnp.float32),
        "in_second": jnp.clip(409.6 + 1228.8 * jax.random.uniform(key_of[5], (D, PROJ), jnp.float32) ** block_levels(key_of[5], (D, PROJ), ((0, 32),), -0.2, 0.2), 409.6, 1638.4),
        "out_proj": scatter_about(key_of[6], (INNER, D), INNER ** -0.5, 0.109375, ((0, 32),), jnp.float32),
        "out_first": scatter_about(key_of[7], (INNER, D), (0.1 * (STREAMS * LENGTH) ** 0.5), 56.0, ((0, 32),), jnp.float32),
        "out_second": jnp.clip(409.6 + 1228.8 * jax.random.uniform(key_of[8], (INNER, D), jnp.float32) ** block_levels(key_of[8], (INNER, D), ((0, 32),), -0.2, 0.2), 409.6, 1638.4),
        "vector": draw_vector(jax.random.fold_in(key_of[12], 71), 0),
        "vector_first": scatter_about(key_of[10], (NVEC,), (0.1 * (STREAMS * LENGTH) ** 0.5), 56.0, (), jnp.float32),
        "vector_second": jnp.clip(jax.random.uniform(key_of[11], (NVEC,), jnp.float32, 409.6, 1638.4), 409.6, 1638.4),
    }


HIGH = lax.Precision.HIGHEST
EPS_NORM = 1e-05
BETA_ONE = 0.9
BETA_TWO = 0.95
ADAM_EPS = 1e-08
RATE_MATRIX = 0.03
RATE_VECTOR = 0.1
DECAY_MATRIX = 0.1

@jax.custom_vjp
def low(v):
    return lax.optimization_barrier(v.astype(jnp.bfloat16)).astype(jnp.float32)

@jax.custom_vjp
def low_back(v):
    return v

def low_keep(v):
    return (low(v), None)

def low_pass(kept, grad):
    return (grad,)

def back_keep(v):
    return (v, None)

def back_low(kept, grad):
    return (low(grad),)
low.defvjp(low_keep, low_pass)
low_back.defvjp(back_keep, back_low)

def split_vector(vector):
    inner = HEADS * HEAD_DIM
    width = inner + 2 * STATE
    counts = [D, inner, CONV * width, width, HEADS, HEADS, HEADS]
    pieces = []
    offset = 0
    for amount in counts:
        pieces.append(vector[offset:offset + amount])
        offset += amount
    return (pieces[0], pieces[1], pieces[2].reshape(CONV, width), pieces[3], pieces[4], pieces[5], pieces[6])

def rms_norm(value, gain):
    return value * lax.rsqrt(lax.optimization_barrier(jnp.mean(value * value, axis=-1, keepdims=True)) + EPS_NORM) * gain

def segment_ids(lengths_row, positions):
    ends = jnp.cumsum(lengths_row, dtype=jnp.int32)
    return lax.optimization_barrier(jnp.sum((ends[None, :] <= positions[:, None]).astype(jnp.int32), axis=1, dtype=jnp.int32))

def convolve(padded, seg_ext, conv_w, conv_b):
    count = padded.shape[-2] - (CONV - 1)
    seg_here = seg_ext[..., CONV - 1:]
    summed = conv_b + jnp.zeros(padded.shape[:-2] + (count, padded.shape[-1]), jnp.float32)
    for tap in range(CONV):
        agree = (seg_ext[..., tap:tap + count] == seg_here).astype(jnp.float32)
        summed = summed + conv_w[tap] * padded[..., tap:tap + count, :] * agree[..., None]
    return jax.nn.silu(summed)

def block_masks(seg, starts):
    order = jnp.arange(seg.shape[-1], dtype=jnp.int32)
    lower = order[:, None] >= order[None, :]
    agree = (lower & (seg[..., :, None] == seg[..., None, :])).astype(jnp.float32)
    keeping = (jnp.cumsum(starts, axis=-1, dtype=jnp.int32) == 0).astype(jnp.float32)
    same_last = (seg == seg[..., -1:]).astype(jnp.float32)
    return (agree, keeping, same_last)

def span_step(carried, pieces):
    values, b_proj, c_proj, delta, log_decay, seg, starts = pieces
    agree, keeping, same_last = block_masks(seg, starts)
    cumulative = jnp.cumsum(log_decay, axis=0)
    spacing = cumulative[:, None, :] - cumulative[None, :, :]
    masked = agree[:, :, None]
    decays = jnp.exp(jnp.where(masked > 0, spacing, 0.0)) * masked
    scores = jnp.dot(c_proj, b_proj.T, precision=HIGH)
    weights = decays * scores[:, :, None] * delta[None, :, :]
    result = jnp.einsum('tuh,uhp->thp', weights, values, precision=HIGH)
    inflow = jnp.exp(cumulative) * keeping[:, None]
    result = result + jnp.einsum('tn,hpn->thp', c_proj, carried, precision=HIGH) * inflow[:, :, None]
    final = cumulative[-1]
    tails = jnp.exp(final[None, :] - cumulative) * same_last[:, None] * delta
    summed = jnp.einsum('uh,uhp,un->hpn', tails, values, b_proj, precision=HIGH)
    carried = (jnp.exp(final) * keeping[-1])[:, None, None] * carried + summed
    return (carried, result)

def stream_forward(upstream, in_proj, out_proj, vector, lengths_row):
    g_norm, g_inner, conv_w, conv_b, dt_bias, a_log, d_skip = split_vector(vector)
    inner = HEADS * HEAD_DIM
    width = inner + 2 * STATE
    normed = rms_norm(upstream, g_norm)
    projected = low_back(jnp.dot(low(normed), low(in_proj), precision=HIGH, preferred_element_type=jnp.float32))
    gate_in = projected[:, :inner]
    xbc = projected[:, inner:inner + width]
    dt_raw = projected[:, inner + width:]
    positions = jnp.arange(-(CONV - 1), LENGTH, dtype=jnp.int32)
    seg_ext = segment_ids(lengths_row, positions)
    padded = jnp.concatenate([jnp.zeros((CONV - 1, width), jnp.float32), xbc], axis=0)
    active = convolve(padded, seg_ext, conv_w, conv_b)
    values = active[:, :inner].reshape(LENGTH, HEADS, HEAD_DIM)
    b_proj = active[:, inner:inner + STATE]
    c_proj = active[:, inner + STATE:]
    delta = jax.nn.softplus(dt_raw + dt_bias)
    log_decay = -delta * jnp.exp(a_log)
    seg_here = seg_ext[CONV - 1:]
    starts = ((seg_here != seg_ext[CONV - 2:-1]) | (positions[CONV - 1:] == 0)).astype(jnp.int32)
    blocks = LENGTH // TOK_SEQ
    pieces = (values.reshape(blocks, TOK_SEQ, HEADS, HEAD_DIM), b_proj.reshape(blocks, TOK_SEQ, STATE), c_proj.reshape(blocks, TOK_SEQ, STATE), delta.reshape(blocks, TOK_SEQ, HEADS), log_decay.reshape(blocks, TOK_SEQ, HEADS), seg_here.reshape(blocks, TOK_SEQ), starts.reshape(blocks, TOK_SEQ))
    initial = jnp.zeros((HEADS, HEAD_DIM, STATE), jnp.float32)
    unused, results = lax.scan(jax.checkpoint(span_step), initial, pieces)
    mixer = results.reshape(LENGTH, HEADS, HEAD_DIM) + d_skip[:, None] * values
    flat = mixer.reshape(LENGTH, inner) * jax.nn.silu(gate_in)
    gated = rms_norm(flat, g_inner)
    branch = jnp.dot(low(gated), low(out_proj), precision=HIGH, preferred_element_type=jnp.float32)
    return upstream + branch

def adam_update(weight, moment_one, moment_two, gradient, rate, decay_rate):
    new_first = BETA_ONE * moment_one + (1 - BETA_ONE) * gradient
    new_second = BETA_TWO * moment_two + (1 - BETA_TWO) * gradient * gradient
    corrected = new_first / (1 - BETA_ONE ** STEP) / (jnp.sqrt(new_second / (1 - BETA_TWO ** STEP)) + ADAM_EPS)
    new_weight = weight - rate * (corrected + decay_rate * weight)
    return (new_first, new_second, new_weight)

def reference(hidden_in, out_grad, lengths, in_proj, in_first, in_second, out_proj, out_first, out_second, vector, vector_first, vector_second):

    def one_stream(totals, item):
        row_in, row_grad, row_lengths = item

        def forward(upstream, weight_in, weight_out, params):
            return stream_forward(upstream, weight_in, weight_out, params, row_lengths)
        result, pullback = jax.vjp(forward, row_in.astype(jnp.float32), in_proj, out_proj, vector)
        grad_up, grad_in, grad_out, grad_vec = pullback(row_grad.astype(jnp.float32))
        totals = (totals[0] + grad_in, totals[1] + grad_out, totals[2] + grad_vec)
        return (totals, (result.astype(jnp.bfloat16), grad_up))
    initial = (jnp.zeros_like(in_proj), jnp.zeros_like(out_proj), jnp.zeros_like(vector))
    grads_total, outputs = lax.scan(one_stream, initial, (hidden_in, out_grad, lengths))
    mixed, input_grad = outputs
    in_new = adam_update(in_proj, in_first, in_second, grads_total[0], RATE_MATRIX, DECAY_MATRIX)
    out_new = adam_update(out_proj, out_first, out_second, grads_total[1], RATE_MATRIX, DECAY_MATRIX)
    vec_new = adam_update(vector, vector_first, vector_second, grads_total[2], RATE_VECTOR, 0.0)
    return (mixed, input_grad, in_new[0], in_new[1], in_new[2], out_new[0], out_new[1], out_new[2], vec_new[0], vec_new[1], vec_new[2])
```

```python
import jax
import jax.numpy as jnp
from jax import lax
from jax.experimental import pallas as pl
from jax.experimental.pallas import tpu as pltpu
from jax.sharding import PartitionSpec as P

D = 1536
HEADS = 48
HEAD_DIM = 64
STATE = 128
CONV = 4
STEP = 5


HIGH = lax.Precision.HIGHEST
EPS_NORM = 1e-05
BETA_ONE = 0.9
BETA_TWO = 0.95
ADAM_EPS = 1e-08
RATE_MATRIX = 0.03
RATE_VECTOR = 0.1
DECAY_MATRIX = 0.1


def passed_along(block, axis, distance):
    devices = range(lax.axis_size(axis))
    route = [(i - distance, i) for i in devices if i - distance in devices]
    return lax.ppermute(block, axis, route)


def entering(shard, axis, combine, identity, reverse):
    length, here = (lax.axis_size(axis), lax.axis_index(axis))
    everything = jax.tree.map(
        lambda part, kind: lax.all_gather(part.astype(kind), axis),
        shard,
        jax.tree.map(lambda a: jnp.bfloat16 if a.dtype == jnp.float32 else a.dtype, shard),
    )
    start = jax.tree.map(
        lambda part, zero: jnp.broadcast_to(jnp.asarray(zero, part.dtype), part.shape),
        shard,
        identity,
    )

    def step(k, before):
        at = length - 1 - k if reverse else k
        reached = at > here if reverse else at < here
        new = combine(
            before, jax.tree.map(lambda part, own: part[at].astype(own.dtype), everything, shard)
        )
        return jax.tree.map(lambda a, b: jnp.where(reached, a, b), new, before)

    return lax.fori_loop(0, length, step, start)


def as_sent(shard):
    return jax.tree.map(lambda a: a.astype(jnp.bfloat16) if a.dtype == jnp.float32 else a, shard)


def split_vector(vector):
    inner = HEADS * HEAD_DIM
    width = inner + 2 * STATE
    counts = [D, inner, CONV * width, width, HEADS, HEADS, HEADS]
    pieces = []
    offset = 0
    for amount in counts:
        pieces.append(vector[offset : offset + amount])
        offset += amount
    return (
        pieces[0],
        pieces[1],
        pieces[2].reshape(CONV, width),
        pieces[3],
        pieces[4],
        pieces[5],
        pieces[6],
    )


def rms_norm(value, gain):
    return value * lax.rsqrt(jnp.mean(value * value, axis=-1, keepdims=True) + EPS_NORM) * gain


def segment_ids(lengths, positions):
    ends = jnp.cumsum(lengths, axis=-1, dtype=jnp.int32)
    return jnp.sum(
        (ends[:, None, :] <= positions[None, :, None]).astype(jnp.int32), axis=-1, dtype=jnp.int32
    )


def convolve(padded, seg_ext, conv_w, conv_b):
    count = padded.shape[-2] - (CONV - 1)
    seg_here = seg_ext[..., CONV - 1 :]
    summed = conv_b + jnp.zeros(padded.shape[:-2] + (count, padded.shape[-1]), jnp.float32)
    for tap in range(CONV):
        agree = (seg_ext[..., tap : tap + count] == seg_here).astype(jnp.float32)
        summed = summed + conv_w[tap] * padded[..., tap : tap + count, :] * agree[..., None]
    return jax.nn.silu(summed)


def block_masks(seg, starts):
    order = jnp.arange(seg.shape[-1], dtype=jnp.int32)
    lower = order[:, None] >= order[None, :]
    agree = (lower & (seg[..., :, None] == seg[..., None, :])).astype(jnp.float32)
    keeping = (jnp.cumsum(starts, axis=-1, dtype=jnp.int32) == 0).astype(jnp.float32)
    same_last = (seg == seg[..., -1:]).astype(jnp.float32)
    return (agree, keeping, same_last)


def front_part(seg_ext):

    def front_apply(previous, xbc, dt_raw, conv_w, conv_b, dt_bias, a_log):
        inner = HEADS * HEAD_DIM
        padded = jnp.concatenate([previous, xbc], axis=1)
        active = convolve(padded, seg_ext, conv_w, conv_b)
        values = active[..., :inner].reshape(xbc.shape[0], xbc.shape[1], HEADS, HEAD_DIM)
        b_proj = active[..., inner : inner + STATE]
        c_proj = active[..., inner + STATE :]
        delta = jax.nn.softplus(dt_raw + dt_bias)
        log_decay = -delta * jnp.exp(a_log)
        return (values, b_proj, c_proj, delta, log_decay)

    return front_apply


def summary_part(keeping, same_last):

    def summary_apply(values, b_proj, delta, log_decay):
        cumulative = jnp.cumsum(log_decay, axis=1)
        final = cumulative[:, -1]
        tails = jnp.exp(final[:, None, :] - cumulative) * same_last[:, :, None] * delta
        summed = jnp.einsum("suh,suhp,sun->shpn", tails, values, b_proj, precision=HIGH)
        return (jnp.exp(final) * keeping[:, -1:], summed)

    return summary_apply


def output_part(agree, keeping):

    def output_apply(values, b_proj, c_proj, delta, log_decay, d_skip, carried):
        cumulative = jnp.cumsum(log_decay, axis=1)
        spacing = cumulative[:, :, None, :] - cumulative[:, None, :, :]
        masked = agree[..., None]
        decays = jnp.exp(jnp.where(masked > 0, spacing, 0.0)) * masked
        scores = jnp.einsum("stn,sun->stu", c_proj, b_proj, precision=HIGH)
        weights = decays * scores[..., None] * delta[:, None, :, :]
        result = jnp.einsum("stuh,suhp->sthp", weights, values, precision=HIGH)
        inflow = jnp.exp(cumulative) * keeping[..., None]
        result = (
            result
            + jnp.einsum("stn,shpn->sthp", c_proj, carried, precision=HIGH) * inflow[..., None]
        )
        return result + d_skip[:, None] * values

    return output_apply


def gate_part(mixer_out, gate_in, g_inner):
    flat = mixer_out.reshape(gate_in.shape) * jax.nn.silu(gate_in)
    return rms_norm(flat, g_inner)


def chain_combine(earlier, later):
    return (earlier[0] * later[0], earlier[1] * later[0][..., None, None] + later[1])


def adam_update(weight, moment_one, moment_two, gradient, rate, decay_rate):
    new_first = BETA_ONE * moment_one + (1 - BETA_ONE) * gradient
    new_second = BETA_TWO * moment_two + (1 - BETA_TWO) * gradient * gradient
    corrected = (
        new_first / (1 - BETA_ONE**STEP) / (jnp.sqrt(new_second / (1 - BETA_TWO**STEP)) + ADAM_EPS)
    )
    new_weight = weight - rate * (corrected + decay_rate * weight)
    return (new_first, new_second, new_weight)


def positions_plan(
    hidden_in,
    out_grad,
    lengths,
    in_proj,
    in_first,
    in_second,
    out_proj,
    out_first,
    out_second,
    vector,
    vector_first,
    vector_second,
):
    g_norm, g_inner, conv_w, conv_b, dt_bias, a_log, d_skip = split_vector(vector)
    inner = HEADS * HEAD_DIM
    width = inner + 2 * STATE
    count = hidden_in.shape[1]
    upstream = hidden_in.astype(jnp.float32)
    normed, norm_back = jax.vjp(rms_norm, upstream, g_norm)
    normed_low = normed.astype(jnp.bfloat16)
    in_full, out_full = (
        lax.all_gather(in_proj.astype(jnp.bfloat16), ("seq", "fsdp"), axis=0, tiled=True),
        lax.all_gather(out_proj.astype(jnp.bfloat16), ("seq", "fsdp"), axis=0, tiled=True),
    )
    projected = jnp.einsum("std,dk->stk", normed_low, in_full, preferred_element_type=jnp.float32)
    gate_in = projected[..., :inner]
    xbc = projected[..., inner : inner + width]
    dt_raw = projected[..., inner + width :]
    previous = passed_along(xbc[:, count - (CONV - 1) :].astype(jnp.bfloat16), "seq", 1).astype(
        jnp.float32
    )
    offset_base = lax.axis_index("seq") * count
    positions = offset_base - (CONV - 1) + jnp.arange(count + CONV - 1, dtype=jnp.int32)
    seg_ext = segment_ids(lengths, positions)
    seg_here = seg_ext[:, CONV - 1 :]
    starts = ((seg_here != seg_ext[:, CONV - 2 : -1]) | (positions[None, CONV - 1 :] == 0)).astype(
        jnp.int32
    )
    agree, keeping, same_last = block_masks(seg_here, starts)
    front_pieces, front_back = jax.vjp(
        front_part(seg_ext), previous, xbc, dt_raw, conv_w, conv_b, dt_bias, a_log
    )
    values, b_proj, c_proj, delta, log_decay = front_pieces
    block_pair, summary_back = jax.vjp(
        summary_part(keeping, same_last), values, b_proj, delta, log_decay
    )
    ones_init = jnp.ones_like(block_pair[0])
    zeros_init = jnp.zeros_like(block_pair[1])
    carried = entering(block_pair, "seq", chain_combine, (ones_init, zeros_init), False)[1]
    mixer_out, output_back = jax.vjp(
        output_part(agree, keeping), values, b_proj, c_proj, delta, log_decay, d_skip, carried
    )
    gated, gate_back = jax.vjp(gate_part, mixer_out, gate_in, g_inner)
    gated_low = gated.astype(jnp.bfloat16)
    branch = jnp.einsum("stc,cd->std", gated_low, out_full, preferred_element_type=jnp.float32)
    mixed = (upstream + branch).astype(jnp.bfloat16)
    in_again, out_again = (
        lax.all_gather(in_proj.astype(jnp.bfloat16), ("seq", "fsdp"), axis=0, tiled=True),
        lax.all_gather(out_proj.astype(jnp.bfloat16), ("seq", "fsdp"), axis=0, tiled=True),
    )
    grad_out_proj = jnp.einsum(
        "stc,std->cd", gated_low, out_grad, preferred_element_type=jnp.float32
    )
    grad_gated = jnp.einsum("std,cd->stc", out_grad, out_again, preferred_element_type=jnp.float32)
    grad_mixer, grad_gate_in, grad_g_inner = gate_back(grad_gated)
    grad_values, grad_b, grad_c, grad_delta, grad_log, grad_skip, grad_carried = output_back(
        grad_mixer
    )
    grad_final = entering(
        (block_pair[0], grad_carried), "seq", chain_combine, (ones_init, zeros_init), True
    )[1]
    grad_decay_total = jnp.sum(grad_final * carried, axis=(2, 3))
    more_values, more_b, more_delta, more_log = summary_back((grad_decay_total, grad_final))
    grad_front = (
        grad_values + more_values,
        grad_b + more_b,
        grad_c,
        grad_delta + more_delta,
        grad_log + more_log,
    )
    grad_previous, grad_xbc, grad_dt_raw, grad_conv_w, grad_conv_b, grad_dt_bias, grad_a_log = (
        front_back(grad_front)
    )
    returned = passed_along(as_sent(grad_previous), "seq", -1).astype(grad_previous.dtype)
    grad_xbc = jnp.concatenate(
        [grad_xbc[:, : count - (CONV - 1)], grad_xbc[:, count - (CONV - 1) :] + returned], axis=1
    )
    grad_projected = jnp.concatenate([grad_gate_in, grad_xbc, grad_dt_raw], axis=-1).astype(
        jnp.bfloat16
    )
    grad_in_proj = jnp.einsum(
        "std,stk->dk", normed_low, grad_projected, preferred_element_type=jnp.float32
    )
    grad_normed = jnp.einsum(
        "stk,dk->std", grad_projected, in_again, preferred_element_type=jnp.float32
    )
    grad_upstream, grad_g_norm = norm_back(grad_normed)
    input_grad = out_grad.astype(jnp.float32) + grad_upstream
    in_summed, out_summed = (
        lax.psum_scatter(grad_in_proj, ("seq", "fsdp"), scatter_dimension=0, tiled=True),
        lax.psum_scatter(grad_out_proj, ("seq", "fsdp"), scatter_dimension=0, tiled=True),
    )
    local_vector = jnp.concatenate(
        [
            grad_g_norm,
            grad_g_inner,
            grad_conv_w.reshape(-1),
            grad_conv_b,
            grad_dt_bias,
            grad_a_log,
            grad_skip,
        ]
    )
    vector_summed = lax.psum(local_vector, ("seq", "fsdp"))
    in_new = adam_update(in_proj, in_first, in_second, in_summed, RATE_MATRIX, DECAY_MATRIX)
    out_new = adam_update(out_proj, out_first, out_second, out_summed, RATE_MATRIX, DECAY_MATRIX)
    vec_new = adam_update(vector, vector_first, vector_second, vector_summed, RATE_VECTOR, 0.0)
    return (
        mixed,
        input_grad,
        in_new[0],
        in_new[1],
        in_new[2],
        out_new[0],
        out_new[1],
        out_new[2],
        vec_new[0],
        vec_new[1],
        vec_new[2],
    )


Q = 128
LANES = 128
CHANNELS = HEADS * HEAD_DIM
WIDTH = CHANNELS + 2 * STATE
BF16 = jnp.bfloat16
F32 = jnp.float32


def mul(a, b, dims=((1,), (0,))):
    return lax.dot_general(a, b, (dims, ((), ())), preferred_element_type=F32)


def halves(x):
    high = x.astype(BF16)
    return high, (x - high.astype(F32)).astype(BF16)


def wide(mask, copies):
    return jnp.concatenate([mask] * copies, axis=1)


def head_map(channels):
    head = lax.broadcasted_iota(jnp.int32, (LANES, channels), 0)
    owner = lax.broadcasted_iota(jnp.int32, (LANES, channels), 1) // HEAD_DIM
    return (head == owner).astype(BF16)


def spread(parts, channels):
    stacked = jnp.concatenate([jnp.concatenate(halves(x), axis=1) for x in parts], axis=0)
    one = head_map(channels)
    out = mul(stacked, jnp.concatenate([one, one], axis=0))
    rows = parts[0].shape[0]
    return [out[i * rows : (i + 1) * rows] for i in range(len(parts))]


def gather_heads(parts, channels):
    stacked = jnp.concatenate([jnp.concatenate(halves(x), axis=1) for x in parts], axis=0)
    one = head_map(channels)
    out = mul(stacked, jnp.concatenate([one, one], axis=1), ((1,), (1,)))
    rows = parts[0].shape[0]
    return [out[i * rows : (i + 1) * rows] for i in range(len(parts))]


def running_sum(x, backward):
    t = lax.broadcasted_iota(jnp.int32, (Q, Q), 0)
    u = lax.broadcasted_iota(jnp.int32, (Q, Q), 1)
    tri = ((t <= u) if backward else (t >= u)).astype(BF16)
    return mul(jnp.concatenate([tri, tri], axis=1), jnp.concatenate(halves(x), axis=0))


def segments(ends, stream, positions):
    seg = jnp.zeros(positions.shape, jnp.int32)
    for k in range(ends.shape[1]):
        seg = seg + (ends[stream, k] <= positions).astype(jnp.int32)
    return jnp.where(positions < 0, -1, seg)


def chunk_front(p_ref, par_ref, ends, stream, chunk):
    local = p_ref.shape[2] - 2 * STATE - LANES
    channels = local // 2
    mixed = channels + 2 * STATE
    base = pl.multiple_of(chunk * Q, Q)
    before = pl.multiple_of(jnp.maximum(base - 8, 0), 8)
    xbc = p_ref[stream, pl.ds(base, Q), channels : channels + mixed]
    halo = p_ref[stream, pl.ds(before, 8), channels : channels + mixed]
    both = jnp.concatenate([halo, xbc], axis=0)
    column = lax.broadcasted_iota(jnp.int32, (Q + 16, LANES), 0) + (base - 8)
    seg = segments(ends, stream, column)
    here = seg[8 : Q + 8]
    tiles = mixed // LANES
    pre = par_ref[4:5, :mixed] + par_ref[3:4, :mixed] * xbc
    taps = []
    for k in range(CONV - 1):
        agree = (seg[5 + k : Q + 5 + k] == here).astype(F32)
        tap = both[5 + k : Q + 5 + k] * wide(agree, tiles)
        taps.append(tap)
        pre = pre + par_ref[k : k + 1, :mixed] * tap
    taps.append(xbc)
    gate = jax.nn.sigmoid(pre)
    active = pre * gate
    values = active[:, :channels]
    b_proj = active[:, channels : channels + STATE]
    c_proj = active[:, channels + STATE :]
    raw = p_ref[stream, pl.ds(base, Q), local + 2 * STATE :] + par_ref[7:8, :LANES]
    delta = jnp.maximum(raw, 0.0) + jnp.log1p(jnp.exp(-jnp.abs(raw)))
    rate = jnp.exp(par_ref[8:9, :LANES])
    log_decay = -delta * rate
    cumulative = running_sum(log_decay, False)
    last = cumulative[Q - 1 : Q]
    keep = (here == seg[7:8]).astype(F32)
    same_last = (here == seg[Q + 7 : Q + 8]).astype(F32)
    inflow = jnp.exp(cumulative) * keep
    tail = jnp.exp(last - cumulative) * same_last
    delta_wide, inflow_wide, tail_wide = spread([delta, inflow, tail], channels)
    row = lax.broadcasted_iota(jnp.int32, (8, LANES), 1) + base
    seg_row = segments(ends, stream, row)[0:1]
    t = lax.broadcasted_iota(jnp.int32, (Q, Q), 0)
    u = lax.broadcasted_iota(jnp.int32, (Q, Q), 1)
    mask = (t >= u) & (here == seg_row)
    turned = cumulative.T

    def decays(head):
        spacing = cumulative[:, head : head + 1] - turned[head : head + 1, :]
        return jnp.exp(jnp.where(mask, spacing, -1e30))

    return dict(
        base=base,
        seg=seg,
        pre=pre,
        gate=gate,
        taps=taps,
        values=values,
        b_low=b_proj.astype(BF16),
        c_low=c_proj.astype(BF16),
        raw=raw,
        delta=delta,
        rate=rate,
        log_decay=log_decay,
        delta_wide=delta_wide,
        inflow_wide=inflow_wide,
        tail_wide=tail_wide,
        scaled=values * delta_wide,
        decays=decays,
        channels=channels,
    )


def two_heads(pair):
    left = lax.broadcasted_iota(jnp.int32, pair.shape, 1) < HEAD_DIM
    low = pair.astype(BF16)
    zero = jnp.zeros_like(low)
    return jnp.concatenate([jnp.where(left, low, zero), jnp.where(left, zero, low)], axis=0)


def chunk_forward(front, state, skip):
    channels = front["channels"]
    scores = mul(front["c_low"], front["b_low"], ((1,), (1,)))
    pieces = []
    for pair in range(channels // LANES):
        weights = jnp.concatenate(
            [(front["decays"](2 * pair + i) * scores).astype(BF16) for i in range(2)], axis=1
        )
        scaled = front["scaled"][:, pair * LANES : (pair + 1) * LANES]
        pieces.append(mul(weights, two_heads(scaled)))
    result = jnp.concatenate(pieces, axis=1)
    result = result + mul(front["c_low"], state.astype(BF16)) * front["inflow_wide"]
    result = result + skip * front["values"]
    fed = (front["scaled"] * front["tail_wide"]).astype(BF16)
    after = front["inflow_wide"][Q - 1 : Q] * state + mul(front["b_low"], fed, ((0,), (0,)))
    return result, after


def chunk_backward(front, before, after, grad_after, result, grad, skip):
    channels = front["channels"]
    b_low, c_low = front["b_low"], front["c_low"]
    scaled, values = front["scaled"], front["values"]
    scores = mul(c_low, b_low, ((1,), (1,)))
    grad_scores = jnp.zeros((Q, Q), F32)
    pieces = []
    for pair in range(channels // LANES):
        lanes = slice(pair * LANES, (pair + 1) * LANES)
        decays = [front["decays"](2 * pair + i) for i in range(2)]
        weights = jnp.concatenate([(d * scores).astype(BF16) for d in decays], axis=0)
        split = two_heads(grad[:, lanes])
        pieces.append(mul(weights, split, ((0,), (0,))))
        cross = mul(split, scaled[:, lanes].astype(BF16), ((1,), (1,)))
        grad_scores = grad_scores + decays[0] * cross[:Q] + decays[1] * cross[Q:]
    grad_after_low = grad_after.astype(BF16)
    inner = jnp.concatenate(pieces, axis=1) + mul(b_low, grad_after_low) * front["tail_wide"]
    fed = (scaled * front["tail_wide"]).astype(BF16)
    flowing = (grad * front["inflow_wide"]).astype(BF16)
    low_scores = grad_scores.astype(BF16)
    grad_c = mul(low_scores, b_low) + mul(flowing, before.astype(BF16), ((1,), (1,)))
    grad_b = mul(low_scores, c_low, ((0,), (0,))) + mul(fed, grad_after_low, ((1,), (1,)))
    grad_values = skip * grad + front["delta_wide"] * inner
    grad_skip = jnp.sum(grad * values, axis=0, keepdims=True)
    held = jnp.sum(after * grad_after, axis=0, keepdims=True)
    grad_delta, grad_cumulative = gather_heads(
        [values * inner, grad * (result - skip * values) - scaled * inner], channels
    )
    held_heads = gather_heads([jnp.broadcast_to(held, (8, channels))], channels)[0][0:1]
    grad_log = running_sum(grad_cumulative, True) + held_heads
    grad_delta = grad_delta - front["rate"] * grad_log
    grad_raw = grad_delta * jax.nn.sigmoid(front["raw"])
    grad_rate = jnp.sum(grad_log * front["log_decay"], axis=0, keepdims=True)
    grad_before = front["inflow_wide"][Q - 1 : Q] * grad_after + mul(c_low, flowing, ((0,), (0,)))
    return grad_values, grad_b, grad_c, grad_raw, grad_rate, grad_skip, grad_before


def conv_backward(front, grad_active, next_grad, par_ref):
    gate, pre, seg = front["gate"], front["pre"], front["seg"]
    mixed = pre.shape[1]
    tiles = mixed // LANES
    grad_pre = grad_active * (gate * (1.0 + pre * (1.0 - gate)))
    rows = [jnp.sum(grad_pre * front["taps"][k], axis=0, keepdims=True) for k in range(CONV)]
    rows.append(jnp.sum(grad_pre, axis=0, keepdims=True))
    both = jnp.concatenate([grad_pre, next_grad], axis=0)
    grad_x = par_ref[CONV - 1 : CONV, :mixed] * grad_pre
    for k in range(CONV - 1):
        ahead = CONV - 1 - k
        agree = (seg[8 + ahead : Q + 8 + ahead] == seg[8 : Q + 8]).astype(F32)
        grad_x = grad_x + par_ref[k : k + 1, :mixed] * both[ahead : Q + ahead] * wide(agree, tiles)
    return grad_x, grad_pre[:8], rows


def forward_kernel(ends, p_ref, par_ref, y_ref, h_ref, state):
    streams, length = p_ref.shape[0], p_ref.shape[1]
    channels = y_ref.shape[2]
    skip = par_ref[6:7, :channels]
    state[...] = jnp.zeros_like(state)

    def step(chunk, carry):
        for stream in range(streams):
            front = chunk_front(p_ref, par_ref, ends, stream, chunk)
            before = state[stream]
            h_ref[stream, chunk] = before
            result, after = chunk_forward(front, before, skip)
            y_ref[stream, pl.ds(front["base"], Q)] = result
            state[stream] = after
        return carry

    lax.fori_loop(0, length // Q, step, 0)


def backward_kernel(
    ends, p_ref, par_ref, y_ref, h_ref, gg_ref, r_ref, k_ref, dp_ref, dv_ref, state, later, sums
):
    streams, length = p_ref.shape[0], p_ref.shape[1]
    chunks = length // Q
    channels = y_ref.shape[2]
    mixed = channels + 2 * STATE
    skip = par_ref[6:7, :channels]
    gain = par_ref[5:6, :channels]
    state[...] = jnp.zeros_like(state)
    later[...] = jnp.zeros_like(later)
    sums[...] = jnp.zeros_like(sums)

    def step(k, carry):
        chunk = chunks - 1 - k
        for stream in range(streams):
            front = chunk_front(p_ref, par_ref, ends, stream, chunk)
            rows = pl.ds(front["base"], Q)
            result = y_ref[stream, rows]
            gate_in = p_ref[stream, rows, :channels]
            sig = jax.nn.sigmoid(gate_in)
            silu = gate_in * sig
            flat = result * silu
            gg = gg_ref[stream, rows]
            scale = r_ref[stream, rows]
            grad_flat = scale * gain * gg - flat * k_ref[stream, rows]
            grad = grad_flat * silu
            grad_gate = grad_flat * result * (sig * (1.0 + gate_in * (1.0 - sig)))
            grad_gain = jnp.sum(gg * flat * scale, axis=0, keepdims=True)
            grad_after = state[stream]
            before = h_ref[stream, chunk]
            after = h_ref[stream, jnp.minimum(chunk + 1, chunks - 1)]
            gv, gb, gc, graw, grate, gskip, gbefore = chunk_backward(
                front, before, after, grad_after, result, grad, skip
            )
            state[stream] = gbefore
            grad_active = jnp.concatenate([gv, gb, gc], axis=1)
            grad_x, head, rows_w = conv_backward(front, grad_active, later[stream], par_ref)
            later[stream] = head
            dp_ref[stream, rows, :channels] = grad_gate.astype(BF16)
            dp_ref[stream, rows, channels : channels + mixed] = grad_x.astype(BF16)
            dp_ref[stream, rows, channels + mixed :] = graw.astype(BF16)
            for i, row in enumerate(rows_w):
                sums[i : i + 1, :] += row
            sums[5:6, :channels] += grad_gain
            sums[6:7, :channels] += gskip
            sums[7:8, :LANES] += jnp.sum(graw, axis=0, keepdims=True)
            sums[8:9, :LANES] += grate
        return carry

    lax.fori_loop(0, chunks, step, 0)
    dv_ref[...] = sums[...]


def local_vector_rows(vector, index, share):
    g_norm, g_inner, conv_w, conv_b, dt_bias, a_log, d_skip = split_vector(vector)
    channels = share * HEAD_DIM
    mixed = channels + 2 * STATE

    def own(array, size):
        return lax.dynamic_slice_in_dim(array, index * size, size, axis=-1)

    def row(array):
        return jnp.pad(array, ((0, 0), (0, mixed - array.shape[1])))

    conv = jnp.concatenate([conv_w, conv_b[None]], axis=0)
    conv = jnp.concatenate([own(conv[:, :CHANNELS], channels), conv[:, CHANNELS:]], axis=1)
    skip = jnp.repeat(own(d_skip, share), HEAD_DIM)
    rows = [conv] + [
        row(part[None])
        for part in (own(g_inner, channels), skip, own(dt_bias, share), own(a_log, share))
    ]
    return jnp.pad(jnp.concatenate(rows, axis=0), ((0, 7), (0, 0)))


def vmem(count):
    return [pl.BlockSpec(memory_space=pltpu.VMEM)] * count


def call(kernel, name, out_shape, inputs, scratch, vmem_mib, smem_first=True):
    specs = [pl.BlockSpec(memory_space=pltpu.SMEM)] + vmem(len(inputs) - 1)
    return pl.pallas_call(
        kernel,
        out_shape=out_shape,
        in_specs=specs,
        out_specs=jax.tree.map(lambda _: pl.BlockSpec(memory_space=pltpu.VMEM), out_shape),
        scratch_shapes=scratch,
        name=name,
        compiler_params=pltpu.CompilerParams(vmem_limit_bytes=vmem_mib << 20),
    )(*inputs)


def heads_plan(
    hidden_in,
    out_grad,
    lengths,
    in_proj,
    in_first,
    in_second,
    out_proj,
    out_first,
    out_second,
    vector,
    vector_first,
    vector_second,
):
    count, index = lax.axis_size("seq"), lax.axis_index("seq")
    depth = lax.axis_size("fsdp")
    share = HEADS // count
    channels = share * HEAD_DIM
    mixed = channels + 2 * STATE
    streams, block = hidden_in.shape[0], hidden_in.shape[1]
    length = block * count
    rows = in_proj.shape[0]
    g_norm = vector[:D]
    par = local_vector_rows(vector, index, share)
    ends = jnp.cumsum(lengths, axis=-1, dtype=jnp.int32)

    upstream = hidden_in.astype(F32)
    normed, norm_back = jax.vjp(rms_norm, upstream, g_norm)
    normed_low = lax.all_gather(normed.astype(BF16), "seq", axis=1, tiled=True)
    grads = lax.all_gather(out_grad, "seq", axis=1, tiled=True)

    in_low = in_proj.astype(BF16)
    own = jnp.concatenate(
        [
            in_low[:, :CHANNELS].reshape(rows, count, channels),
            in_low[:, CHANNELS : 2 * CHANNELS].reshape(rows, count, channels),
        ],
        axis=2,
    ).transpose(1, 0, 2)
    turned = lax.all_to_all(own, "seq", 0, 0)
    weights = lax.all_gather(turned, "fsdp", axis=1).reshape(D, 2 * channels)
    common = lax.all_gather(in_low[:, 2 * CHANNELS :], ("seq", "fsdp"), axis=0, tiled=True)
    own_dt = lax.dynamic_slice_in_dim(common, 2 * STATE + index * share, share, axis=1)
    own_dt = jnp.pad(own_dt, ((0, 0), (0, LANES - share)))
    weights = jnp.concatenate([weights, common[:, : 2 * STATE], own_dt], axis=1)
    out_full = lax.all_gather(out_proj.astype(BF16), "fsdp", axis=0, tiled=True)

    projected = jnp.einsum("std,dk->stk", normed_low, weights, preferred_element_type=F32)
    shape = jax.ShapeDtypeStruct
    chunks = length // Q
    result, states = call(
        forward_kernel,
        "mixer_forward",
        (shape((streams, length, channels), F32), shape((streams, chunks, STATE, channels), F32)),
        (ends, projected, par),
        [pltpu.VMEM((streams, STATE, channels), F32)],
        48,
    )
    gate_in = projected[..., :channels]
    g_inner = par[5, :channels]
    flat = result * jax.nn.silu(gate_in)
    grad_gated = jnp.einsum("std,cd->stc", grads, out_full, preferred_element_type=F32)
    moments = lax.psum(
        jnp.stack([jnp.sum(flat * flat, axis=-1), jnp.sum(grad_gated * g_inner * flat, axis=-1)]),
        "seq",
    )
    scale = lax.rsqrt(moments[0] / CHANNELS + EPS_NORM)[..., None]
    pull = scale * scale * scale * moments[1][..., None] / CHANNELS
    gated_low = (flat * scale * g_inner).astype(BF16)
    branch = jnp.einsum("stc,cd->std", gated_low, out_full, preferred_element_type=F32)
    branch = lax.psum_scatter(branch.astype(BF16), "seq", scatter_dimension=1, tiled=True)
    mixed_out = (upstream + branch.astype(F32)).astype(BF16)
    grad_out_proj = jnp.einsum("stc,std->cd", gated_low, grads, preferred_element_type=F32)
    out_summed = lax.psum_scatter(
        grad_out_proj.astype(BF16), "fsdp", scatter_dimension=0, tiled=True
    ).astype(F32)

    grad_projected, sums = call(
        backward_kernel,
        "mixer_backward",
        (shape(projected.shape, BF16), shape((16, mixed), F32)),
        (ends, projected, par, result, states, grad_gated, scale, pull),
        [
            pltpu.VMEM((streams, STATE, channels), F32),
            pltpu.VMEM((streams, 8, mixed), F32),
            pltpu.VMEM((16, mixed), F32),
        ],
        56,
    )
    grad_in = jnp.einsum("std,stk->dk", normed_low, grad_projected, preferred_element_type=F32)
    grad_normed = jnp.einsum("stk,dk->std", grad_projected, weights, preferred_element_type=F32)
    grad_normed = lax.psum_scatter(
        grad_normed.astype(BF16), "seq", scatter_dimension=1, tiled=True
    ).astype(F32)
    grad_upstream, grad_g_norm = norm_back(grad_normed)
    input_grad = out_grad.astype(F32) + grad_upstream

    main = grad_in[:, : 2 * channels].reshape(count, depth, rows, 2 * channels)
    main = lax.psum_scatter(main.astype(BF16), "fsdp", scatter_dimension=1, tiled=True)
    main = lax.all_to_all(main[:, 0], "seq", 0, 0).astype(F32)
    placed = jnp.zeros((D, HEADS), F32)
    placed = lax.dynamic_update_slice_in_dim(
        placed, grad_in[:, 2 * channels + 2 * STATE :][:, :share], index * share, axis=1
    )
    rest = jnp.concatenate([grad_in[:, 2 * channels : 2 * channels + 2 * STATE], placed], axis=1)
    rest = lax.psum_scatter(
        rest.astype(BF16), ("seq", "fsdp"), scatter_dimension=0, tiled=True
    ).astype(F32)
    in_summed = jnp.concatenate(
        [
            main[..., :channels].transpose(1, 0, 2).reshape(rows, CHANNELS),
            main[..., channels:].transpose(1, 0, 2).reshape(rows, CHANNELS),
            rest,
        ],
        axis=1,
    )

    def placed_in(part, size):
        whole = jnp.zeros(part.shape[:-1] + (size * count,), F32)
        return lax.dynamic_update_slice_in_dim(whole, part, index * size, axis=-1)

    conv = jnp.concatenate(
        [placed_in(sums[:5, :channels], channels), sums[:5, channels:mixed]], axis=1
    )
    local_vector = jnp.concatenate(
        [
            grad_g_norm,
            placed_in(sums[5, :channels], channels),
            conv.reshape(-1),
            placed_in(sums[7, :share], share),
            placed_in(sums[8, :share], share),
            placed_in(sums[6, :channels].reshape(share, HEAD_DIM).sum(axis=1), share),
        ]
    )
    vector_summed = lax.psum(local_vector, ("seq", "fsdp"))
    in_new = adam_update(in_proj, in_first, in_second, in_summed, RATE_MATRIX, DECAY_MATRIX)
    out_new = adam_update(out_proj, out_first, out_second, out_summed, RATE_MATRIX, DECAY_MATRIX)
    vec_new = adam_update(vector, vector_first, vector_second, vector_summed, RATE_VECTOR, 0.0)
    return (mixed_out, input_grad, *in_new, *out_new, *vec_new)


def solution(mesh):
    return jax.shard_map(
        heads_plan if HEADS % mesh.shape["seq"] == 0 else positions_plan,
        mesh=mesh,
        in_specs=(
            P("fsdp", "seq", None),
            P("fsdp", "seq", None),
            P("fsdp", None),
            P(("seq", "fsdp"), None),
            P(("seq", "fsdp"), None),
            P(("seq", "fsdp"), None),
            P(("seq", "fsdp"), None),
            P(("seq", "fsdp"), None),
            P(("seq", "fsdp"), None),
            P(),
            P(),
            P(),
        ),
        out_specs=(
            P("fsdp", "seq", None),
            P("fsdp", "seq", None),
            P(("seq", "fsdp"), None),
            P(("seq", "fsdp"), None),
            P(("seq", "fsdp"), None),
            P(("seq", "fsdp"), None),
            P(("seq", "fsdp"), None),
            P(("seq", "fsdp"), None),
            P(),
            P(),
            P(),
        ),
        check_vma=False,
    )
```

```python
import functools

import jax
import jax.numpy as jnp
from jax import lax
from jax.experimental import pallas as pl
from jax.experimental.pallas import tpu as pltpu
from jax.sharding import PartitionSpec as P

D = 1536
HEADS = 48
HEAD_DIM = 64
STATE = 128
CONV = 4
STEP = 5


HIGH = lax.Precision.HIGHEST
EPS_NORM = 1e-05
BETA_ONE = 0.9
BETA_TWO = 0.95
ADAM_EPS = 1e-08
RATE_MATRIX = 0.03
RATE_VECTOR = 0.1
DECAY_MATRIX = 0.1


def passed_along(block, axis, distance):
    devices = range(lax.axis_size(axis))
    route = [(i - distance, i) for i in devices if i - distance in devices]
    return lax.ppermute(block, axis, route)


def entering(shard, axis, combine, identity, reverse):
    length, here = (lax.axis_size(axis), lax.axis_index(axis))
    everything = jax.tree.map(
        lambda part, kind: lax.all_gather(part.astype(kind), axis),
        shard,
        jax.tree.map(lambda a: jnp.bfloat16 if a.dtype == jnp.float32 else a.dtype, shard),
    )
    start = jax.tree.map(
        lambda part, zero: jnp.broadcast_to(jnp.asarray(zero, part.dtype), part.shape),
        shard,
        identity,
    )

    def step(k, before):
        at = length - 1 - k if reverse else k
        reached = at > here if reverse else at < here
        new = combine(
            before, jax.tree.map(lambda part, own: part[at].astype(own.dtype), everything, shard)
        )
        return jax.tree.map(lambda a, b: jnp.where(reached, a, b), new, before)

    return lax.fori_loop(0, length, step, start)


def as_sent(shard):
    return jax.tree.map(lambda a: a.astype(jnp.bfloat16) if a.dtype == jnp.float32 else a, shard)


def split_vector(vector):
    inner = HEADS * HEAD_DIM
    width = inner + 2 * STATE
    counts = [D, inner, CONV * width, width, HEADS, HEADS, HEADS]
    pieces = []
    offset = 0
    for amount in counts:
        pieces.append(vector[offset : offset + amount])
        offset += amount
    return (
        pieces[0],
        pieces[1],
        pieces[2].reshape(CONV, width),
        pieces[3],
        pieces[4],
        pieces[5],
        pieces[6],
    )


def rms_norm(value, gain):
    return value * lax.rsqrt(jnp.mean(value * value, axis=-1, keepdims=True) + EPS_NORM) * gain


def segment_ids(lengths, positions):
    ends = jnp.cumsum(lengths, axis=-1, dtype=jnp.int32)
    return jnp.sum(
        (ends[:, None, :] <= positions[None, :, None]).astype(jnp.int32), axis=-1, dtype=jnp.int32
    )


def convolve(padded, seg_ext, conv_w, conv_b):
    count = padded.shape[-2] - (CONV - 1)
    seg_here = seg_ext[..., CONV - 1 :]
    summed = conv_b + jnp.zeros(padded.shape[:-2] + (count, padded.shape[-1]), jnp.float32)
    for tap in range(CONV):
        agree = (seg_ext[..., tap : tap + count] == seg_here).astype(jnp.float32)
        summed = summed + conv_w[tap] * padded[..., tap : tap + count, :] * agree[..., None]
    return jax.nn.silu(summed)


def block_masks(seg, starts):
    order = jnp.arange(seg.shape[-1], dtype=jnp.int32)
    lower = order[:, None] >= order[None, :]
    agree = (lower & (seg[..., :, None] == seg[..., None, :])).astype(jnp.float32)
    keeping = (jnp.cumsum(starts, axis=-1, dtype=jnp.int32) == 0).astype(jnp.float32)
    same_last = (seg == seg[..., -1:]).astype(jnp.float32)
    return (agree, keeping, same_last)


def front_part(seg_ext):

    def front_apply(previous, xbc, dt_raw, conv_w, conv_b, dt_bias, a_log):
        inner = HEADS * HEAD_DIM
        padded = jnp.concatenate([previous, xbc], axis=1)
        active = convolve(padded, seg_ext, conv_w, conv_b)
        values = active[..., :inner].reshape(xbc.shape[0], xbc.shape[1], HEADS, HEAD_DIM)
        b_proj = active[..., inner : inner + STATE]
        c_proj = active[..., inner + STATE :]
        delta = jax.nn.softplus(dt_raw + dt_bias)
        log_decay = -delta * jnp.exp(a_log)
        return (values, b_proj, c_proj, delta, log_decay)

    return front_apply


def summary_part(keeping, same_last):

    def summary_apply(values, b_proj, delta, log_decay):
        cumulative = jnp.cumsum(log_decay, axis=1)
        final = cumulative[:, -1]
        tails = jnp.exp(final[:, None, :] - cumulative) * same_last[:, :, None] * delta
        summed = jnp.einsum("suh,suhp,sun->shpn", tails, values, b_proj, precision=HIGH)
        return (jnp.exp(final) * keeping[:, -1:], summed)

    return summary_apply


def output_part(agree, keeping):

    def output_apply(values, b_proj, c_proj, delta, log_decay, d_skip, carried):
        cumulative = jnp.cumsum(log_decay, axis=1)
        spacing = cumulative[:, :, None, :] - cumulative[:, None, :, :]
        masked = agree[..., None]
        decays = jnp.exp(jnp.where(masked > 0, spacing, 0.0)) * masked
        scores = jnp.einsum("stn,sun->stu", c_proj, b_proj, precision=HIGH)
        weights = decays * scores[..., None] * delta[:, None, :, :]
        result = jnp.einsum("stuh,suhp->sthp", weights, values, precision=HIGH)
        inflow = jnp.exp(cumulative) * keeping[..., None]
        result = (
            result
            + jnp.einsum("stn,shpn->sthp", c_proj, carried, precision=HIGH) * inflow[..., None]
        )
        return result + d_skip[:, None] * values

    return output_apply


def gate_part(mixer_out, gate_in, g_inner):
    flat = mixer_out.reshape(gate_in.shape) * jax.nn.silu(gate_in)
    return rms_norm(flat, g_inner)


def chain_combine(earlier, later):
    return (earlier[0] * later[0], earlier[1] * later[0][..., None, None] + later[1])


def adam_update(weight, moment_one, moment_two, gradient, rate, decay_rate):
    new_first = BETA_ONE * moment_one + (1 - BETA_ONE) * gradient
    new_second = BETA_TWO * moment_two + (1 - BETA_TWO) * gradient * gradient
    corrected = (
        new_first / (1 - BETA_ONE**STEP) / (jnp.sqrt(new_second / (1 - BETA_TWO**STEP)) + ADAM_EPS)
    )
    new_weight = weight - rate * (corrected + decay_rate * weight)
    return (new_first, new_second, new_weight)


def positions_plan(
    hidden_in,
    out_grad,
    lengths,
    in_proj,
    in_first,
    in_second,
    out_proj,
    out_first,
    out_second,
    vector,
    vector_first,
    vector_second,
):
    g_norm, g_inner, conv_w, conv_b, dt_bias, a_log, d_skip = split_vector(vector)
    inner = HEADS * HEAD_DIM
    width = inner + 2 * STATE
    count = hidden_in.shape[1]
    upstream = hidden_in.astype(jnp.float32)
    normed, norm_back = jax.vjp(rms_norm, upstream, g_norm)
    normed_low = normed.astype(jnp.bfloat16)
    in_full, out_full = (
        lax.all_gather(in_proj.astype(jnp.bfloat16), ("seq", "fsdp"), axis=0, tiled=True),
        lax.all_gather(out_proj.astype(jnp.bfloat16), ("seq", "fsdp"), axis=0, tiled=True),
    )
    projected = jnp.einsum("std,dk->stk", normed_low, in_full, preferred_element_type=jnp.float32)
    gate_in = projected[..., :inner]
    xbc = projected[..., inner : inner + width]
    dt_raw = projected[..., inner + width :]
    previous = passed_along(xbc[:, count - (CONV - 1) :].astype(jnp.bfloat16), "seq", 1).astype(
        jnp.float32
    )
    offset_base = lax.axis_index("seq") * count
    positions = offset_base - (CONV - 1) + jnp.arange(count + CONV - 1, dtype=jnp.int32)
    seg_ext = segment_ids(lengths, positions)
    seg_here = seg_ext[:, CONV - 1 :]
    starts = ((seg_here != seg_ext[:, CONV - 2 : -1]) | (positions[None, CONV - 1 :] == 0)).astype(
        jnp.int32
    )
    agree, keeping, same_last = block_masks(seg_here, starts)
    front_pieces, front_back = jax.vjp(
        front_part(seg_ext), previous, xbc, dt_raw, conv_w, conv_b, dt_bias, a_log
    )
    values, b_proj, c_proj, delta, log_decay = front_pieces
    block_pair, summary_back = jax.vjp(
        summary_part(keeping, same_last), values, b_proj, delta, log_decay
    )
    ones_init = jnp.ones_like(block_pair[0])
    zeros_init = jnp.zeros_like(block_pair[1])
    carried = entering(block_pair, "seq", chain_combine, (ones_init, zeros_init), False)[1]
    mixer_out, output_back = jax.vjp(
        output_part(agree, keeping), values, b_proj, c_proj, delta, log_decay, d_skip, carried
    )
    gated, gate_back = jax.vjp(gate_part, mixer_out, gate_in, g_inner)
    gated_low = gated.astype(jnp.bfloat16)
    branch = jnp.einsum("stc,cd->std", gated_low, out_full, preferred_element_type=jnp.float32)
    mixed = (upstream + branch).astype(jnp.bfloat16)
    in_again, out_again = (
        lax.all_gather(in_proj.astype(jnp.bfloat16), ("seq", "fsdp"), axis=0, tiled=True),
        lax.all_gather(out_proj.astype(jnp.bfloat16), ("seq", "fsdp"), axis=0, tiled=True),
    )
    grad_out_proj = jnp.einsum(
        "stc,std->cd", gated_low, out_grad, preferred_element_type=jnp.float32
    )
    grad_gated = jnp.einsum("std,cd->stc", out_grad, out_again, preferred_element_type=jnp.float32)
    grad_mixer, grad_gate_in, grad_g_inner = gate_back(grad_gated)
    grad_values, grad_b, grad_c, grad_delta, grad_log, grad_skip, grad_carried = output_back(
        grad_mixer
    )
    grad_final = entering(
        (block_pair[0], grad_carried), "seq", chain_combine, (ones_init, zeros_init), True
    )[1]
    grad_decay_total = jnp.sum(grad_final * carried, axis=(2, 3))
    more_values, more_b, more_delta, more_log = summary_back((grad_decay_total, grad_final))
    grad_front = (
        grad_values + more_values,
        grad_b + more_b,
        grad_c,
        grad_delta + more_delta,
        grad_log + more_log,
    )
    grad_previous, grad_xbc, grad_dt_raw, grad_conv_w, grad_conv_b, grad_dt_bias, grad_a_log = (
        front_back(grad_front)
    )
    returned = passed_along(as_sent(grad_previous), "seq", -1).astype(grad_previous.dtype)
    grad_xbc = jnp.concatenate(
        [grad_xbc[:, : count - (CONV - 1)], grad_xbc[:, count - (CONV - 1) :] + returned], axis=1
    )
    grad_projected = jnp.concatenate([grad_gate_in, grad_xbc, grad_dt_raw], axis=-1).astype(
        jnp.bfloat16
    )
    grad_in_proj = jnp.einsum(
        "std,stk->dk", normed_low, grad_projected, preferred_element_type=jnp.float32
    )
    grad_normed = jnp.einsum(
        "stk,dk->std", grad_projected, in_again, preferred_element_type=jnp.float32
    )
    grad_upstream, grad_g_norm = norm_back(grad_normed)
    input_grad = out_grad.astype(jnp.float32) + grad_upstream
    in_summed, out_summed = (
        lax.psum_scatter(grad_in_proj, ("seq", "fsdp"), scatter_dimension=0, tiled=True),
        lax.psum_scatter(grad_out_proj, ("seq", "fsdp"), scatter_dimension=0, tiled=True),
    )
    local_vector = jnp.concatenate(
        [
            grad_g_norm,
            grad_g_inner,
            grad_conv_w.reshape(-1),
            grad_conv_b,
            grad_dt_bias,
            grad_a_log,
            grad_skip,
        ]
    )
    vector_summed = lax.psum(local_vector, ("seq", "fsdp"))
    in_new = adam_update(in_proj, in_first, in_second, in_summed, RATE_MATRIX, DECAY_MATRIX)
    out_new = adam_update(out_proj, out_first, out_second, out_summed, RATE_MATRIX, DECAY_MATRIX)
    vec_new = adam_update(vector, vector_first, vector_second, vector_summed, RATE_VECTOR, 0.0)
    return (
        mixed,
        input_grad,
        in_new[0],
        in_new[1],
        in_new[2],
        out_new[0],
        out_new[1],
        out_new[2],
        vec_new[0],
        vec_new[1],
        vec_new[2],
    )


Q = 128
LANES = 128
CHANNELS = HEADS * HEAD_DIM
WIDTH = CHANNELS + 2 * STATE
BF16 = jnp.bfloat16
F32 = jnp.float32


def mul(a, b, dims=((1,), (0,))):
    return lax.dot_general(a, b, (dims, ((), ())), preferred_element_type=F32)


def halves(x):
    high = x.astype(BF16)
    return high, (x - high.astype(F32)).astype(BF16)


def wide(mask, copies):
    return jnp.concatenate([mask] * copies, axis=1)


def head_map(channels):
    head = lax.broadcasted_iota(jnp.int32, (LANES, channels), 0)
    owner = lax.broadcasted_iota(jnp.int32, (LANES, channels), 1) // HEAD_DIM
    return (head == owner).astype(BF16)


def spread(parts, channels):
    stacked = jnp.concatenate([jnp.concatenate(halves(x), axis=1) for x in parts], axis=0)
    one = head_map(channels)
    out = mul(stacked, jnp.concatenate([one, one], axis=0))
    rows = parts[0].shape[0]
    return [out[i * rows : (i + 1) * rows] for i in range(len(parts))]


def gather_heads(parts, channels):
    stacked = jnp.concatenate([jnp.concatenate(halves(x), axis=1) for x in parts], axis=0)
    one = head_map(channels)
    out = mul(stacked, jnp.concatenate([one, one], axis=1), ((1,), (1,)))
    rows = parts[0].shape[0]
    return [out[i * rows : (i + 1) * rows] for i in range(len(parts))]


def running_sum(x, backward):
    t = lax.broadcasted_iota(jnp.int32, (Q, Q), 0)
    u = lax.broadcasted_iota(jnp.int32, (Q, Q), 1)
    tri = ((t <= u) if backward else (t >= u)).astype(BF16)
    return mul(jnp.concatenate([tri, tri], axis=1), jnp.concatenate(halves(x), axis=0))


def segments(ends, stream, positions):
    seg = jnp.zeros(positions.shape, jnp.int32)
    for k in range(ends.shape[1]):
        seg = seg + (ends[stream, k] <= positions).astype(jnp.int32)
    return jnp.where(positions < 0, -1, seg)


def chunk_front(p_ref, par_ref, ends, stream, chunk):
    local = p_ref.shape[2] - 2 * STATE - LANES
    channels = local // 2
    mixed = channels + 2 * STATE
    base = pl.multiple_of(chunk * Q, Q)
    before = pl.multiple_of(jnp.maximum(base - 8, 0), 8)
    xbc = p_ref[stream, pl.ds(base, Q), channels : channels + mixed]
    halo = p_ref[stream, pl.ds(before, 8), channels : channels + mixed]
    both = jnp.concatenate([halo, xbc], axis=0)
    column = lax.broadcasted_iota(jnp.int32, (Q + 16, LANES), 0) + (base - 8)
    seg = segments(ends, stream, column)
    here = seg[8 : Q + 8]
    tiles = mixed // LANES
    pre = par_ref[4:5, :mixed] + par_ref[3:4, :mixed] * xbc
    taps = []
    for k in range(CONV - 1):
        agree = (seg[5 + k : Q + 5 + k] == here).astype(F32)
        tap = both[5 + k : Q + 5 + k] * wide(agree, tiles)
        taps.append(tap)
        pre = pre + par_ref[k : k + 1, :mixed] * tap
    taps.append(xbc)
    gate = jax.nn.sigmoid(pre)
    active = pre * gate
    values = active[:, :channels]
    b_proj = active[:, channels : channels + STATE]
    c_proj = active[:, channels + STATE :]
    raw = p_ref[stream, pl.ds(base, Q), local + 2 * STATE :] + par_ref[7:8, :LANES]
    delta = jnp.maximum(raw, 0.0) + jnp.log1p(jnp.exp(-jnp.abs(raw)))
    rate = jnp.exp(par_ref[8:9, :LANES])
    log_decay = -delta * rate
    cumulative = running_sum(log_decay, False)
    last = cumulative[Q - 1 : Q]
    keep = (here == seg[7:8]).astype(F32)
    same_last = (here == seg[Q + 7 : Q + 8]).astype(F32)
    inflow = jnp.exp(cumulative) * keep
    tail = jnp.exp(last - cumulative) * same_last
    delta_wide, inflow_wide, tail_wide = spread([delta, inflow, tail], channels)
    row = lax.broadcasted_iota(jnp.int32, (8, LANES), 1) + base
    seg_row = segments(ends, stream, row)[0:1]
    t = lax.broadcasted_iota(jnp.int32, (Q, Q), 0)
    u = lax.broadcasted_iota(jnp.int32, (Q, Q), 1)
    mask = (t >= u) & (here == seg_row)
    turned = cumulative.T

    def decays(head):
        spacing = cumulative[:, head : head + 1] - turned[head : head + 1, :]
        return jnp.exp(jnp.where(mask, spacing, -1e30))

    return dict(
        base=base,
        seg=seg,
        pre=pre,
        gate=gate,
        taps=taps,
        values=values,
        b_low=b_proj.astype(BF16),
        c_low=c_proj.astype(BF16),
        raw=raw,
        delta=delta,
        rate=rate,
        log_decay=log_decay,
        delta_wide=delta_wide,
        inflow_wide=inflow_wide,
        tail_wide=tail_wide,
        scaled=values * delta_wide,
        decays=decays,
        channels=channels,
    )


def two_heads(pair):
    left = lax.broadcasted_iota(jnp.int32, pair.shape, 1) < HEAD_DIM
    low = pair.astype(BF16)
    zero = jnp.zeros_like(low)
    return jnp.concatenate([jnp.where(left, low, zero), jnp.where(left, zero, low)], axis=0)


def chunk_forward(front, state, skip):
    channels = front["channels"]
    scores = mul(front["c_low"], front["b_low"], ((1,), (1,)))
    pieces = []
    for pair in range(channels // LANES):
        weights = jnp.concatenate(
            [(front["decays"](2 * pair + i) * scores).astype(BF16) for i in range(2)], axis=1
        )
        scaled = front["scaled"][:, pair * LANES : (pair + 1) * LANES]
        pieces.append(mul(weights, two_heads(scaled)))
    result = jnp.concatenate(pieces, axis=1)
    result = result + mul(front["c_low"], state.astype(BF16)) * front["inflow_wide"]
    result = result + skip * front["values"]
    fed = (front["scaled"] * front["tail_wide"]).astype(BF16)
    after = front["inflow_wide"][Q - 1 : Q] * state + mul(front["b_low"], fed, ((0,), (0,)))
    return result, after


def chunk_backward(front, before, after, grad_after, result, grad, skip):
    channels = front["channels"]
    b_low, c_low = front["b_low"], front["c_low"]
    scaled, values = front["scaled"], front["values"]
    scores = mul(c_low, b_low, ((1,), (1,)))
    grad_scores = jnp.zeros((Q, Q), F32)
    pieces = []
    for pair in range(channels // LANES):
        lanes = slice(pair * LANES, (pair + 1) * LANES)
        decays = [front["decays"](2 * pair + i) for i in range(2)]
        weights = jnp.concatenate([(d * scores).astype(BF16) for d in decays], axis=0)
        split = two_heads(grad[:, lanes])
        pieces.append(mul(weights, split, ((0,), (0,))))
        cross = mul(split, scaled[:, lanes].astype(BF16), ((1,), (1,)))
        grad_scores = grad_scores + decays[0] * cross[:Q] + decays[1] * cross[Q:]
    grad_after_low = grad_after.astype(BF16)
    inner = jnp.concatenate(pieces, axis=1) + mul(b_low, grad_after_low) * front["tail_wide"]
    fed = (scaled * front["tail_wide"]).astype(BF16)
    flowing = (grad * front["inflow_wide"]).astype(BF16)
    low_scores = grad_scores.astype(BF16)
    grad_c = mul(low_scores, b_low) + mul(flowing, before.astype(BF16), ((1,), (1,)))
    grad_b = mul(low_scores, c_low, ((0,), (0,))) + mul(fed, grad_after_low, ((1,), (1,)))
    grad_values = skip * grad + front["delta_wide"] * inner
    grad_skip = jnp.sum(grad * values, axis=0, keepdims=True)
    held = jnp.sum(after * grad_after, axis=0, keepdims=True)
    grad_delta, grad_cumulative = gather_heads(
        [values * inner, grad * (result - skip * values) - scaled * inner], channels
    )
    held_heads = gather_heads([jnp.broadcast_to(held, (8, channels))], channels)[0][0:1]
    grad_log = running_sum(grad_cumulative, True) + held_heads
    grad_delta = grad_delta - front["rate"] * grad_log
    grad_raw = grad_delta * jax.nn.sigmoid(front["raw"])
    grad_rate = jnp.sum(grad_log * front["log_decay"], axis=0, keepdims=True)
    grad_before = front["inflow_wide"][Q - 1 : Q] * grad_after + mul(c_low, flowing, ((0,), (0,)))
    return grad_values, grad_b, grad_c, grad_raw, grad_rate, grad_skip, grad_before


def conv_backward(front, grad_active, next_grad, par_ref):
    gate, pre, seg = front["gate"], front["pre"], front["seg"]
    mixed = pre.shape[1]
    tiles = mixed // LANES
    grad_pre = grad_active * (gate * (1.0 + pre * (1.0 - gate)))
    rows = [jnp.sum(grad_pre * front["taps"][k], axis=0, keepdims=True) for k in range(CONV)]
    rows.append(jnp.sum(grad_pre, axis=0, keepdims=True))
    both = jnp.concatenate([grad_pre, next_grad], axis=0)
    grad_x = par_ref[CONV - 1 : CONV, :mixed] * grad_pre
    for k in range(CONV - 1):
        ahead = CONV - 1 - k
        agree = (seg[8 + ahead : Q + 8 + ahead] == seg[8 : Q + 8]).astype(F32)
        grad_x = grad_x + par_ref[k : k + 1, :mixed] * both[ahead : Q + ahead] * wide(agree, tiles)
    return grad_x, grad_pre[:8], rows


def backward_kernel(
    ends, p_ref, par_ref, y_ref, h_ref, gg_ref, r_ref, k_ref, dp_ref, dv_ref, state, later, sums
):
    streams, length = p_ref.shape[0], p_ref.shape[1]
    chunks = length // Q
    channels = y_ref.shape[2]
    mixed = channels + 2 * STATE
    skip = par_ref[6:7, :channels]
    gain = par_ref[5:6, :channels]
    state[...] = jnp.zeros_like(state)
    later[...] = jnp.zeros_like(later)
    sums[...] = jnp.zeros_like(sums)

    def step(k, carry):
        chunk = chunks - 1 - k
        for stream in range(streams):
            front = chunk_front(p_ref, par_ref, ends, stream, chunk)
            rows = pl.ds(front["base"], Q)
            result = y_ref[stream, rows]
            gate_in = p_ref[stream, rows, :channels]
            sig = jax.nn.sigmoid(gate_in)
            silu = gate_in * sig
            flat = result * silu
            gg = gg_ref[stream, rows]
            scale = r_ref[stream, rows]
            grad_flat = scale * gain * gg - flat * k_ref[stream, rows]
            grad = grad_flat * silu
            grad_gate = grad_flat * result * (sig * (1.0 + gate_in * (1.0 - sig)))
            grad_gain = jnp.sum(gg * flat * scale, axis=0, keepdims=True)
            grad_after = state[stream]
            before = h_ref[stream, chunk]
            after = h_ref[stream, jnp.minimum(chunk + 1, chunks - 1)]
            gv, gb, gc, graw, grate, gskip, gbefore = chunk_backward(
                front, before, after, grad_after, result, grad, skip
            )
            state[stream] = gbefore
            grad_active = jnp.concatenate([gv, gb, gc], axis=1)
            grad_x, head, rows_w = conv_backward(front, grad_active, later[stream], par_ref)
            later[stream] = head
            dp_ref[stream, rows, :channels] = grad_gate.astype(BF16)
            dp_ref[stream, rows, channels : channels + mixed] = grad_x.astype(BF16)
            dp_ref[stream, rows, channels + mixed :] = graw.astype(BF16)
            for i, row in enumerate(rows_w):
                sums[i : i + 1, :] += row
            sums[5:6, :channels] += grad_gain
            sums[6:7, :channels] += gskip
            sums[7:8, :LANES] += jnp.sum(graw, axis=0, keepdims=True)
            sums[8:9, :LANES] += grate
        return carry

    lax.fori_loop(0, chunks, step, 0)
    dv_ref[...] = sums[...]


MESH = pl.DeviceIdType.MESH
TILE = 512


class Links:
    def __init__(self, send, recv):
        self.send, self.recv, self.used = send, recv, 0

    def copy(self, source, target, device):
        slot = self.used
        self.used += 1
        return pltpu.make_async_remote_copy(
            src_ref=source,
            dst_ref=target,
            send_sem=self.send.at[slot],
            recv_sem=self.recv.at[slot],
            device_id=device,
            device_id_type=MESH,
        )


class Place:
    def __init__(self, depth):
        self.s = lax.axis_index("seq")
        self.f = lax.axis_index("fsdp")
        self.depth = depth
        self.core = lax.rem(self.s, 2)
        x = lax.rem(self.s // 2, 2)
        y = self.s // 4
        self.steps = (1 - 2 * self.core, 2 - 4 * x, 4 - 8 * y)

    def peer(self, k):
        index = self.s
        for bit in range(3):
            if k >> bit & 1:
                index = index + self.steps[bit]
        return index

    def at(self, k):
        return (self.peer(k), self.f)

    def plane(self, d):
        return lax.rem(self.f + d, self.depth)

    def beyond(self, d):
        return (self.s, self.plane(d))

    def greet(self):
        barrier = pltpu.get_barrier_semaphore()
        others = [self.at(k) for k in range(1, 8)] + [self.beyond(d) for d in range(1, self.depth)]
        for other in others:
            pl.semaphore_signal(barrier, inc=1, device_id=other, device_id_type=MESH)
        pl.semaphore_wait(barrier, len(others))


def ahead(start, size):
    return pl.ds(pl.multiple_of(start, size), size)


def gather_kernel(
    depth,
    ends,
    hidden,
    out_grad,
    in_proj,
    out_proj,
    gain,
    par_ref,
    x_out,
    g_out,
    w_out,
    o_out,
    p_out,
    y_out,
    h_out,
    gg_out,
    moments_out,
    x,
    g,
    wm,
    wc,
    wo,
    p,
    y,
    h,
    gg,
    state,
    packed,
    common,
    moments,
    send,
    recv,
    leave,
):
    streams, block = hidden.shape[0], hidden.shape[1]
    length = x.shape[1]
    rows = in_proj.shape[0]
    lines = out_proj.shape[0]
    channels = wo.shape[0]
    slab = depth * rows
    here = Place(depth)
    s, f = here.s, here.f
    links = Links(send, recv)
    exits = []

    def leaving(source, target):
        copy = pltpu.make_async_copy(source, target, leave.at[len(exits)])
        copy.start()
        exits.append(copy)

    for k in range(CHANNELS // channels):
        lanes = slice(k * channels, (k + 1) * channels)
        packed[k, :, :channels] = in_proj[:, lanes].astype(BF16)
        lanes = slice(CHANNELS + k * channels, CHANNELS + (k + 1) * channels)
        packed[k, :, channels:] = in_proj[:, lanes].astype(BF16)
    narrow = 2 * STATE + HEADS
    common[:, narrow:] = jnp.zeros((rows, common.shape[1] - narrow), BF16)
    common[:, :narrow] = in_proj[:, 2 * CHANNELS :].astype(BF16)

    def slab_rows(source, plane):
        return ahead((source * depth + plane) * rows, rows)

    def block_rows(source):
        return ahead(source * block, block)

    here.greet()
    finish = []

    def started(copy):
        copy.start()
        finish.append(copy)
        return copy

    own = slab_rows(s, f)
    turned = [None]
    for k in (2, 4, 6, 1, 3, 5, 7):
        turned.append(started(links.copy(packed.at[here.peer(k)], wm.at[own], here.at(k))))
    turned = dict(zip((0, 2, 4, 6, 1, 3, 5, 7), turned))
    shared = [started(links.copy(common, wc.at[own], here.beyond(d))) for d in range(1, depth)]
    wc[own] = common[...]
    wm[own] = packed[s]

    upstream = hidden[...].astype(F32)
    mean = jnp.mean(upstream * upstream, axis=-1, keepdims=True)
    x[:, block_rows(s)] = (upstream * lax.rsqrt(mean + EPS_NORM) * gain[...]).astype(BF16)
    mine = x.at[:, block_rows(s)]
    near = [started(links.copy(mine, mine, here.at(k))) for k in (2, 4)]
    beside = [started(links.copy(mine, mine, here.at(1)))]
    g[:, block_rows(s)] = out_grad[...]
    wo[ahead(f * lines, lines)] = out_proj[...].astype(BF16)

    def hop(k, d, up):
        plane = f - d if up else f + d
        target = wm.at[slab_rows(here.peer(k), plane)]
        return links.copy(target, target, (s, f + 1 if up else f - 1))

    hops = {}
    for k in range(8):
        for d in range(depth - 1):
            hops[k, d] = (hop(k, d, True), hop(k, d, False))

    def sends(d):
        return ((f >= d) & (f < depth - 1), (f <= depth - 1 - d) & (f > 0))

    def gets(d):
        return (f >= d + 1, f <= depth - 2 - d)

    def launch(k, d):
        for way in range(2):
            pl.when(sends(d)[way])(hops[k, d][way].start)

    def arrive(k, d):
        for way in range(2):
            pl.when(gets(d)[way])(hops[k, d][way].wait_recv)

    order = (0, 1, 2, 3, 4, 5, 6, 7)
    across = []
    spread_common = []
    chip = s // 2

    def tokens_second_phase():
        near[0].wait_recv()
        half = x.at[0, block_rows(here.peer(2))]
        across.append(started(links.copy(half, half, here.at(4))))
        whole = x.at[:, block_rows(here.peer(2))]
        beside.append(started(links.copy(whole, whole, here.at(1))))
        near[1].wait_recv()
        half = x.at[1, block_rows(here.peer(4))]
        across.append(started(links.copy(half, half, here.at(2))))
        whole = x.at[:, block_rows(here.peer(4))]
        beside.append(started(links.copy(whole, whole, here.at(1))))

    def common_second_phase():
        for copy in shared:
            copy.wait_recv()
        group = wc.at[ahead(s * slab, slab)]
        for k in (2, 4, 6, 1):
            spread_common.append(links.copy(group, group, here.at(k)))
            spread_common[-1].start()

    def common_third_phase():
        for copy in spread_common[:3]:
            copy.wait_recv()
        for k in (2, 4, 6):
            group = wc.at[ahead(here.peer(k) * slab, slab)]
            spread_common.append(links.copy(group, group, here.at(1)))
            spread_common[-1].start()

    def tokens_third_phase():
        for way, k in enumerate((2, 4)):
            across[way].wait_recv()
            half = x.at[way, block_rows(here.peer(6))]
            beside.append(started(links.copy(half, half, here.at(1))))

    far_tokens = []

    def project(j):
        q = (here.peer(order[2 * j])) // 2
        span = ahead(q * 2 * slab, 2 * slab)

        def tile(i, carry):
            stream = i // (length // TILE)
            at = ahead(lax.rem(i, length // TILE) * TILE, TILE)
            left = x[stream, at, span]
            for part, weights in ((slice(0, 2 * channels), wm), (slice(2 * channels, None), wc)):
                product = mul(left, weights[span, :])
                if j == 0:
                    p[stream, at, part] = product
                else:
                    p[stream, at, part] += product
            return carry

        lax.fori_loop(0, streams * (length // TILE), tile, 0)

    last = depth - 1
    for i in range(8 + last):
        if i < 8:
            k = order[i]
            if turned[k] is not None:
                turned[k].wait_recv()
            launch(k, 0)
        for d in range(1, last):
            if 0 <= i - d < 8:
                arrive(order[i - d], d - 1)
                launch(order[i - d], d)
        if 0 <= i - last < 8:
            arrive(order[i - last], last - 1)
        if i == 2:
            common_second_phase()
        if i == 3:
            common_third_phase()
        if i == 4:
            tokens_second_phase()
        if i == last + 1:
            tokens_third_phase()
            for copy in beside:
                copy.wait_recv()
            for copy in spread_common[3:]:
                copy.wait_recv()
            for copy in spread_common:
                copy.wait_send()
            leaving(x, x_out)
            mine_g = g.at[:, block_rows(s)]
            for k in (2, 4, 6):
                far_tokens.append(started(links.copy(mine_g, mine_g, here.at(k))))
            beside_g = [started(links.copy(mine_g, mine_g, here.at(1)))]
            column = lax.broadcasted_iota(jnp.int32, (LANES, LANES), 0)
            wanted = lax.broadcasted_iota(jnp.int32, (LANES, LANES), 1)
            share = channels // HEAD_DIM
            pick = ((column == wanted + s * share) & (wanted < share)).astype(BF16)
            for part in range(0, wc.shape[0], TILE):
                steps = wc[part : part + TILE, 2 * STATE :]
                wc[part : part + TILE, 2 * STATE :] = mul(steps, pick).astype(BF16)
        if i >= last + 1 and (i - last) % 2 == 1:
            project((i - last) // 2)
    lent = wo.at[ahead(f * lines, lines)]
    outs = [started(links.copy(lent, lent, here.beyond(d))) for d in range(1, depth)]
    leaving(p, p_out)
    leaving(wm, w_out.at[:, : 2 * channels])
    leaving(wc, w_out.at[:, 2 * channels :])

    skip = par_ref[6:7, :channels]
    state[...] = jnp.zeros_like(state)

    def step(chunk, carry):
        for stream in range(streams):
            front = chunk_front(p, par_ref, ends, stream, chunk)
            before = state[stream]
            h[stream, chunk] = before
            result, after = chunk_forward(front, before, skip)
            y[stream, pl.ds(front["base"], Q)] = result
            state[stream] = after
        return carry

    lax.fori_loop(0, length // Q, step, 0)
    leaving(y, y_out)
    leaving(h, h_out)

    for k, copy in zip((2, 4, 6), far_tokens):
        copy.wait_recv()
        block_g = g.at[:, block_rows(here.peer(k))]
        beside_g.append(started(links.copy(block_g, block_g, here.at(1))))
    for copy in outs:
        copy.wait_recv()
    for copy in beside_g:
        copy.wait_recv()
    leaving(g, g_out)
    leaving(wo, o_out)

    g_inner = par_ref[5:6, :channels]
    ones = jnp.ones((8, 2 * channels), BF16)
    tiles = length // TILE
    pieces = TILE // Q
    half = streams * length // Q

    def weigh(i, carry):
        stream = i // tiles
        at = ahead(lax.rem(i, tiles) * TILE, TILE)
        grad = mul(g[stream, at], wo[...], ((1,), (1,)))
        gg[stream, at] = grad
        gate_in = p[stream, at, :channels]
        flat = y[stream, at] * (gate_in * jax.nn.sigmoid(gate_in))
        for which, product in enumerate((flat * flat, grad * g_inner * flat)):
            sums = mul(ones, jnp.concatenate(halves(product), axis=1), ((1,), (1,)))
            for j in range(pieces):
                at_row = which * half + i * pieces + j
                moments[s, pl.ds(at_row, 1), :] = sums[0:1, j * Q : (j + 1) * Q]
        return carry

    lax.fori_loop(0, streams * tiles, weigh, 0)
    leaving(gg, gg_out)
    mine_m = moments.at[s]
    told = [started(links.copy(mine_m, mine_m, here.at(k))) for k in range(1, 8)]
    for copy in told:
        copy.wait_recv()
    moments_out[...] = jnp.sum(moments[...], axis=0)

    for copy in finish:
        copy.wait_send()
    for k in range(8):
        for d in range(depth - 1):
            for way in range(2):
                pl.when(sends(d)[way])(hops[k, d][way].wait_send)
    for copy in exits:
        copy.wait()


def local_vector_rows(vector, index, share):
    g_norm, g_inner, conv_w, conv_b, dt_bias, a_log, d_skip = split_vector(vector)
    channels = share * HEAD_DIM
    mixed = channels + 2 * STATE

    def own(array, size):
        return lax.dynamic_slice_in_dim(array, index * size, size, axis=-1)

    def row(array):
        return jnp.pad(array, ((0, 0), (0, mixed - array.shape[1])))

    conv = jnp.concatenate([conv_w, conv_b[None]], axis=0)
    conv = jnp.concatenate([own(conv[:, :CHANNELS], channels), conv[:, CHANNELS:]], axis=1)
    skip = jnp.repeat(own(d_skip, share), HEAD_DIM)
    rows = [conv] + [
        row(part[None])
        for part in (own(g_inner, channels), skip, own(dt_bias, share), own(a_log, share))
    ]
    return jnp.pad(jnp.concatenate(rows, axis=0), ((0, 7), (0, 0)))


def call(kernel, name, out_shape, out_specs, inputs, scratch, vmem_mib, collective=None):
    specs = [pl.BlockSpec(memory_space=pltpu.SMEM)]
    specs += [pl.BlockSpec(memory_space=pltpu.VMEM)] * (len(inputs) - 1)
    return pl.pallas_call(
        kernel,
        out_shape=out_shape,
        in_specs=specs,
        out_specs=[pl.BlockSpec(memory_space=space) for space in out_specs],
        scratch_shapes=scratch,
        name=name,
        compiler_params=pltpu.CompilerParams(
            vmem_limit_bytes=vmem_mib << 20,
            collective_id=collective,
            has_side_effects=collective is not None,
        ),
    )(*inputs)


def heads_plan(
    hidden_in,
    out_grad,
    lengths,
    in_proj,
    in_first,
    in_second,
    out_proj,
    out_first,
    out_second,
    vector,
    vector_first,
    vector_second,
):
    count, index = lax.axis_size("seq"), lax.axis_index("seq")
    depth = lax.axis_size("fsdp")
    share = HEADS // count
    channels = share * HEAD_DIM
    mixed = channels + 2 * STATE
    streams, block = hidden_in.shape[0], hidden_in.shape[1]
    length = block * count
    chunks = length // Q
    rows = in_proj.shape[0]
    columns = mixed + channels + LANES
    g_norm = vector[:D]
    par = local_vector_rows(vector, index, share)
    ends = jnp.cumsum(lengths, axis=-1, dtype=jnp.int32)

    upstream = hidden_in.astype(F32)
    normed, norm_back = jax.vjp(rms_norm, upstream, g_norm)
    shape = jax.ShapeDtypeStruct
    moment_rows = 2 * streams * chunks
    normed_low, grads, weights, out_full, projected, result, states, grad_gated, moments = call(
        functools.partial(gather_kernel, depth),
        "gather_forward",
        [
            shape((streams, length, D), BF16),
            shape((streams, length, D), BF16),
            shape((D, columns), BF16),
            shape((channels, D), BF16),
            shape((streams, length, columns), F32),
            shape((streams, length, channels), F32),
            shape((streams, chunks, STATE, channels), F32),
            shape((streams, length, channels), F32),
            shape((moment_rows, Q), F32),
        ],
        [pl.ANY] * 8 + [pltpu.VMEM],
        (ends, hidden_in, out_grad, in_proj, out_proj, g_norm[None], par),
        [
            pltpu.VMEM((streams, length, D), BF16),
            pltpu.VMEM((streams, length, D), BF16),
            pltpu.VMEM((D, 2 * channels), BF16),
            pltpu.VMEM((D, 2 * STATE + LANES), BF16),
            pltpu.VMEM((channels, D), BF16),
            pltpu.VMEM((streams, length, columns), F32),
            pltpu.VMEM((streams, length, channels), F32),
            pltpu.VMEM((streams, chunks, STATE, channels), F32),
            pltpu.VMEM((streams, length, channels), F32),
            pltpu.VMEM((streams, STATE, channels), F32),
            pltpu.VMEM((count, rows, 2 * channels), BF16),
            pltpu.VMEM((rows, 2 * STATE + LANES), BF16),
            pltpu.VMEM((count, moment_rows, Q), F32),
            pltpu.SemaphoreType.DMA((128,)),
            pltpu.SemaphoreType.DMA((128,)),
            pltpu.SemaphoreType.DMA((16,)),
        ],
        56,
        collective=0,
    )
    moments = moments.reshape(2, streams, length)
    gate_in = projected[..., :channels]
    g_inner = par[5, :channels]
    flat = result * jax.nn.silu(gate_in)
    scale = lax.rsqrt(moments[0] / CHANNELS + EPS_NORM)[..., None]
    pull = scale * scale * scale * moments[1][..., None] / CHANNELS
    gated_low = (flat * scale * g_inner).astype(BF16)
    branch = jnp.einsum("stc,cd->std", gated_low, out_full, preferred_element_type=F32)
    branch = lax.psum_scatter(branch.astype(BF16), "seq", scatter_dimension=1, tiled=True)
    mixed_out = (upstream + branch.astype(F32)).astype(BF16)
    grad_out_proj = jnp.einsum("stc,std->cd", gated_low, grads, preferred_element_type=F32)
    out_summed = lax.psum_scatter(
        grad_out_proj.astype(BF16), "fsdp", scatter_dimension=0, tiled=True
    ).astype(F32)

    grad_projected, sums = call(
        backward_kernel,
        "mixer_backward",
        [shape(projected.shape, BF16), shape((16, mixed), F32)],
        [pltpu.VMEM, pltpu.VMEM],
        (ends, projected, par, result, states, grad_gated, scale, pull),
        [
            pltpu.VMEM((streams, STATE, channels), F32),
            pltpu.VMEM((streams, 8, mixed), F32),
            pltpu.VMEM((16, mixed), F32),
        ],
        56,
    )
    grad_in = jnp.einsum("std,stk->dk", normed_low, grad_projected, preferred_element_type=F32)
    grad_normed = jnp.einsum("stk,dk->std", grad_projected, weights, preferred_element_type=F32)
    grad_normed = lax.psum_scatter(
        grad_normed.astype(BF16), "seq", scatter_dimension=1, tiled=True
    ).astype(F32)
    grad_upstream, grad_g_norm = norm_back(grad_normed)
    input_grad = out_grad.astype(F32) + grad_upstream

    main = grad_in[:, : 2 * channels].reshape(count, depth, rows, 2 * channels)
    main = lax.psum_scatter(main.astype(BF16), "fsdp", scatter_dimension=1, tiled=True)
    main = lax.all_to_all(main[:, 0], "seq", 0, 0).astype(F32)
    placed = jnp.zeros((D, HEADS), F32)
    placed = lax.dynamic_update_slice_in_dim(
        placed, grad_in[:, 2 * channels + 2 * STATE :][:, :share], index * share, axis=1
    )
    rest = jnp.concatenate([grad_in[:, 2 * channels : 2 * channels + 2 * STATE], placed], axis=1)
    rest = lax.psum_scatter(
        rest.astype(BF16), ("seq", "fsdp"), scatter_dimension=0, tiled=True
    ).astype(F32)
    in_summed = jnp.concatenate(
        [
            main[..., :channels].transpose(1, 0, 2).reshape(rows, CHANNELS),
            main[..., channels:].transpose(1, 0, 2).reshape(rows, CHANNELS),
            rest,
        ],
        axis=1,
    )

    def placed_in(part, size):
        whole = jnp.zeros(part.shape[:-1] + (size * count,), F32)
        return lax.dynamic_update_slice_in_dim(whole, part, index * size, axis=-1)

    conv = jnp.concatenate(
        [placed_in(sums[:5, :channels], channels), sums[:5, channels:mixed]], axis=1
    )
    local_vector = jnp.concatenate(
        [
            grad_g_norm,
            placed_in(sums[5, :channels], channels),
            conv.reshape(-1),
            placed_in(sums[7, :share], share),
            placed_in(sums[8, :share], share),
            placed_in(sums[6, :channels].reshape(share, HEAD_DIM).sum(axis=1), share),
        ]
    )
    vector_summed = lax.psum(local_vector, ("seq", "fsdp"))
    in_new = adam_update(in_proj, in_first, in_second, in_summed, RATE_MATRIX, DECAY_MATRIX)
    out_new = adam_update(out_proj, out_first, out_second, out_summed, RATE_MATRIX, DECAY_MATRIX)
    vec_new = adam_update(vector, vector_first, vector_second, vector_summed, RATE_VECTOR, 0.0)
    return (mixed_out, input_grad, *in_new, *out_new, *vec_new)


def solution(mesh):
    return jax.shard_map(
        heads_plan if mesh.shape["seq"] == 8 else positions_plan,
        mesh=mesh,
        in_specs=(
            P("fsdp", "seq", None),
            P("fsdp", "seq", None),
            P("fsdp", None),
            P(("seq", "fsdp"), None),
            P(("seq", "fsdp"), None),
            P(("seq", "fsdp"), None),
            P(("seq", "fsdp"), None),
            P(("seq", "fsdp"), None),
            P(("seq", "fsdp"), None),
            P(),
            P(),
            P(),
        ),
        out_specs=(
            P("fsdp", "seq", None),
            P("fsdp", "seq", None),
            P(("seq", "fsdp"), None),
            P(("seq", "fsdp"), None),
            P(("seq", "fsdp"), None),
            P(("seq", "fsdp"), None),
            P(("seq", "fsdp"), None),
            P(("seq", "fsdp"), None),
            P(),
            P(),
            P(),
        ),
        check_vma=False,
    )
```

```python
import functools

import jax
import jax.numpy as jnp
from jax import lax
from jax.experimental import pallas as pl
from jax.experimental.pallas import tpu as pltpu
from jax.sharding import PartitionSpec as P

D = 1536
HEADS = 48
HEAD_DIM = 64
STATE = 128
CONV = 4
STEP = 5


HIGH = lax.Precision.HIGHEST
EPS_NORM = 1e-05
BETA_ONE = 0.9
BETA_TWO = 0.95
ADAM_EPS = 1e-08
RATE_MATRIX = 0.03
RATE_VECTOR = 0.1
DECAY_MATRIX = 0.1


def passed_along(block, axis, distance):
    devices = range(lax.axis_size(axis))
    route = [(i - distance, i) for i in devices if i - distance in devices]
    return lax.ppermute(block, axis, route)


def entering(shard, axis, combine, identity, reverse):
    length, here = (lax.axis_size(axis), lax.axis_index(axis))
    everything = jax.tree.map(
        lambda part, kind: lax.all_gather(part.astype(kind), axis),
        shard,
        jax.tree.map(lambda a: jnp.bfloat16 if a.dtype == jnp.float32 else a.dtype, shard),
    )
    start = jax.tree.map(
        lambda part, zero: jnp.broadcast_to(jnp.asarray(zero, part.dtype), part.shape),
        shard,
        identity,
    )

    def step(k, before):
        at = length - 1 - k if reverse else k
        reached = at > here if reverse else at < here
        new = combine(
            before, jax.tree.map(lambda part, own: part[at].astype(own.dtype), everything, shard)
        )
        return jax.tree.map(lambda a, b: jnp.where(reached, a, b), new, before)

    return lax.fori_loop(0, length, step, start)


def as_sent(shard):
    return jax.tree.map(lambda a: a.astype(jnp.bfloat16) if a.dtype == jnp.float32 else a, shard)


def split_vector(vector):
    inner = HEADS * HEAD_DIM
    width = inner + 2 * STATE
    counts = [D, inner, CONV * width, width, HEADS, HEADS, HEADS]
    pieces = []
    offset = 0
    for amount in counts:
        pieces.append(vector[offset : offset + amount])
        offset += amount
    return (
        pieces[0],
        pieces[1],
        pieces[2].reshape(CONV, width),
        pieces[3],
        pieces[4],
        pieces[5],
        pieces[6],
    )


def rms_norm(value, gain):
    return value * lax.rsqrt(jnp.mean(value * value, axis=-1, keepdims=True) + EPS_NORM) * gain


def segment_ids(lengths, positions):
    ends = jnp.cumsum(lengths, axis=-1, dtype=jnp.int32)
    return jnp.sum(
        (ends[:, None, :] <= positions[None, :, None]).astype(jnp.int32), axis=-1, dtype=jnp.int32
    )


def convolve(padded, seg_ext, conv_w, conv_b):
    count = padded.shape[-2] - (CONV - 1)
    seg_here = seg_ext[..., CONV - 1 :]
    summed = conv_b + jnp.zeros(padded.shape[:-2] + (count, padded.shape[-1]), jnp.float32)
    for tap in range(CONV):
        agree = (seg_ext[..., tap : tap + count] == seg_here).astype(jnp.float32)
        summed = summed + conv_w[tap] * padded[..., tap : tap + count, :] * agree[..., None]
    return jax.nn.silu(summed)


def block_masks(seg, starts):
    order = jnp.arange(seg.shape[-1], dtype=jnp.int32)
    lower = order[:, None] >= order[None, :]
    agree = (lower & (seg[..., :, None] == seg[..., None, :])).astype(jnp.float32)
    keeping = (jnp.cumsum(starts, axis=-1, dtype=jnp.int32) == 0).astype(jnp.float32)
    same_last = (seg == seg[..., -1:]).astype(jnp.float32)
    return (agree, keeping, same_last)


def front_part(seg_ext):

    def front_apply(previous, xbc, dt_raw, conv_w, conv_b, dt_bias, a_log):
        inner = HEADS * HEAD_DIM
        padded = jnp.concatenate([previous, xbc], axis=1)
        active = convolve(padded, seg_ext, conv_w, conv_b)
        values = active[..., :inner].reshape(xbc.shape[0], xbc.shape[1], HEADS, HEAD_DIM)
        b_proj = active[..., inner : inner + STATE]
        c_proj = active[..., inner + STATE :]
        delta = jax.nn.softplus(dt_raw + dt_bias)
        log_decay = -delta * jnp.exp(a_log)
        return (values, b_proj, c_proj, delta, log_decay)

    return front_apply


def summary_part(keeping, same_last):

    def summary_apply(values, b_proj, delta, log_decay):
        cumulative = jnp.cumsum(log_decay, axis=1)
        final = cumulative[:, -1]
        tails = jnp.exp(final[:, None, :] - cumulative) * same_last[:, :, None] * delta
        summed = jnp.einsum("suh,suhp,sun->shpn", tails, values, b_proj, precision=HIGH)
        return (jnp.exp(final) * keeping[:, -1:], summed)

    return summary_apply


def output_part(agree, keeping):

    def output_apply(values, b_proj, c_proj, delta, log_decay, d_skip, carried):
        cumulative = jnp.cumsum(log_decay, axis=1)
        spacing = cumulative[:, :, None, :] - cumulative[:, None, :, :]
        masked = agree[..., None]
        decays = jnp.exp(jnp.where(masked > 0, spacing, 0.0)) * masked
        scores = jnp.einsum("stn,sun->stu", c_proj, b_proj, precision=HIGH)
        weights = decays * scores[..., None] * delta[:, None, :, :]
        result = jnp.einsum("stuh,suhp->sthp", weights, values, precision=HIGH)
        inflow = jnp.exp(cumulative) * keeping[..., None]
        result = (
            result
            + jnp.einsum("stn,shpn->sthp", c_proj, carried, precision=HIGH) * inflow[..., None]
        )
        return result + d_skip[:, None] * values

    return output_apply


def gate_part(mixer_out, gate_in, g_inner):
    flat = mixer_out.reshape(gate_in.shape) * jax.nn.silu(gate_in)
    return rms_norm(flat, g_inner)


def chain_combine(earlier, later):
    return (earlier[0] * later[0], earlier[1] * later[0][..., None, None] + later[1])


def adam_update(weight, moment_one, moment_two, gradient, rate, decay_rate):
    new_first = BETA_ONE * moment_one + (1 - BETA_ONE) * gradient
    new_second = BETA_TWO * moment_two + (1 - BETA_TWO) * gradient * gradient
    corrected = (
        new_first / (1 - BETA_ONE**STEP) / (jnp.sqrt(new_second / (1 - BETA_TWO**STEP)) + ADAM_EPS)
    )
    new_weight = weight - rate * (corrected + decay_rate * weight)
    return (new_first, new_second, new_weight)


def positions_plan(
    hidden_in,
    out_grad,
    lengths,
    in_proj,
    in_first,
    in_second,
    out_proj,
    out_first,
    out_second,
    vector,
    vector_first,
    vector_second,
):
    g_norm, g_inner, conv_w, conv_b, dt_bias, a_log, d_skip = split_vector(vector)
    inner = HEADS * HEAD_DIM
    width = inner + 2 * STATE
    count = hidden_in.shape[1]
    upstream = hidden_in.astype(jnp.float32)
    normed, norm_back = jax.vjp(rms_norm, upstream, g_norm)
    normed_low = normed.astype(jnp.bfloat16)
    in_full, out_full = (
        lax.all_gather(in_proj.astype(jnp.bfloat16), ("seq", "fsdp"), axis=0, tiled=True),
        lax.all_gather(out_proj.astype(jnp.bfloat16), ("seq", "fsdp"), axis=0, tiled=True),
    )
    projected = jnp.einsum("std,dk->stk", normed_low, in_full, preferred_element_type=jnp.float32)
    gate_in = projected[..., :inner]
    xbc = projected[..., inner : inner + width]
    dt_raw = projected[..., inner + width :]
    previous = passed_along(xbc[:, count - (CONV - 1) :].astype(jnp.bfloat16), "seq", 1).astype(
        jnp.float32
    )
    offset_base = lax.axis_index("seq") * count
    positions = offset_base - (CONV - 1) + jnp.arange(count + CONV - 1, dtype=jnp.int32)
    seg_ext = segment_ids(lengths, positions)
    seg_here = seg_ext[:, CONV - 1 :]
    starts = ((seg_here != seg_ext[:, CONV - 2 : -1]) | (positions[None, CONV - 1 :] == 0)).astype(
        jnp.int32
    )
    agree, keeping, same_last = block_masks(seg_here, starts)
    front_pieces, front_back = jax.vjp(
        front_part(seg_ext), previous, xbc, dt_raw, conv_w, conv_b, dt_bias, a_log
    )
    values, b_proj, c_proj, delta, log_decay = front_pieces
    block_pair, summary_back = jax.vjp(
        summary_part(keeping, same_last), values, b_proj, delta, log_decay
    )
    ones_init = jnp.ones_like(block_pair[0])
    zeros_init = jnp.zeros_like(block_pair[1])
    carried = entering(block_pair, "seq", chain_combine, (ones_init, zeros_init), False)[1]
    mixer_out, output_back = jax.vjp(
        output_part(agree, keeping), values, b_proj, c_proj, delta, log_decay, d_skip, carried
    )
    gated, gate_back = jax.vjp(gate_part, mixer_out, gate_in, g_inner)
    gated_low = gated.astype(jnp.bfloat16)
    branch = jnp.einsum("stc,cd->std", gated_low, out_full, preferred_element_type=jnp.float32)
    mixed = (upstream + branch).astype(jnp.bfloat16)
    in_again, out_again = (
        lax.all_gather(in_proj.astype(jnp.bfloat16), ("seq", "fsdp"), axis=0, tiled=True),
        lax.all_gather(out_proj.astype(jnp.bfloat16), ("seq", "fsdp"), axis=0, tiled=True),
    )
    grad_out_proj = jnp.einsum(
        "stc,std->cd", gated_low, out_grad, preferred_element_type=jnp.float32
    )
    grad_gated = jnp.einsum("std,cd->stc", out_grad, out_again, preferred_element_type=jnp.float32)
    grad_mixer, grad_gate_in, grad_g_inner = gate_back(grad_gated)
    grad_values, grad_b, grad_c, grad_delta, grad_log, grad_skip, grad_carried = output_back(
        grad_mixer
    )
    grad_final = entering(
        (block_pair[0], grad_carried), "seq", chain_combine, (ones_init, zeros_init), True
    )[1]
    grad_decay_total = jnp.sum(grad_final * carried, axis=(2, 3))
    more_values, more_b, more_delta, more_log = summary_back((grad_decay_total, grad_final))
    grad_front = (
        grad_values + more_values,
        grad_b + more_b,
        grad_c,
        grad_delta + more_delta,
        grad_log + more_log,
    )
    grad_previous, grad_xbc, grad_dt_raw, grad_conv_w, grad_conv_b, grad_dt_bias, grad_a_log = (
        front_back(grad_front)
    )
    returned = passed_along(as_sent(grad_previous), "seq", -1).astype(grad_previous.dtype)
    grad_xbc = jnp.concatenate(
        [grad_xbc[:, : count - (CONV - 1)], grad_xbc[:, count - (CONV - 1) :] + returned], axis=1
    )
    grad_projected = jnp.concatenate([grad_gate_in, grad_xbc, grad_dt_raw], axis=-1).astype(
        jnp.bfloat16
    )
    grad_in_proj = jnp.einsum(
        "std,stk->dk", normed_low, grad_projected, preferred_element_type=jnp.float32
    )
    grad_normed = jnp.einsum(
        "stk,dk->std", grad_projected, in_again, preferred_element_type=jnp.float32
    )
    grad_upstream, grad_g_norm = norm_back(grad_normed)
    input_grad = out_grad.astype(jnp.float32) + grad_upstream
    in_summed, out_summed = (
        lax.psum_scatter(grad_in_proj, ("seq", "fsdp"), scatter_dimension=0, tiled=True),
        lax.psum_scatter(grad_out_proj, ("seq", "fsdp"), scatter_dimension=0, tiled=True),
    )
    local_vector = jnp.concatenate(
        [
            grad_g_norm,
            grad_g_inner,
            grad_conv_w.reshape(-1),
            grad_conv_b,
            grad_dt_bias,
            grad_a_log,
            grad_skip,
        ]
    )
    vector_summed = lax.psum(local_vector, ("seq", "fsdp"))
    in_new = adam_update(in_proj, in_first, in_second, in_summed, RATE_MATRIX, DECAY_MATRIX)
    out_new = adam_update(out_proj, out_first, out_second, out_summed, RATE_MATRIX, DECAY_MATRIX)
    vec_new = adam_update(vector, vector_first, vector_second, vector_summed, RATE_VECTOR, 0.0)
    return (
        mixed,
        input_grad,
        in_new[0],
        in_new[1],
        in_new[2],
        out_new[0],
        out_new[1],
        out_new[2],
        vec_new[0],
        vec_new[1],
        vec_new[2],
    )


Q = 128
LANES = 128
CHANNELS = HEADS * HEAD_DIM
WIDTH = CHANNELS + 2 * STATE
BF16 = jnp.bfloat16
F32 = jnp.float32


def mul(a, b, dims=((1,), (0,))):
    return lax.dot_general(a, b, (dims, ((), ())), preferred_element_type=F32)


def halves(x):
    high = x.astype(BF16)
    return high, (x - high.astype(F32)).astype(BF16)


def wide(mask, copies):
    return jnp.concatenate([mask] * copies, axis=1)


def head_map(channels):
    head = lax.broadcasted_iota(jnp.int32, (LANES, channels), 0)
    owner = lax.broadcasted_iota(jnp.int32, (LANES, channels), 1) // HEAD_DIM
    return (head == owner).astype(BF16)


def spread(parts, channels):
    stacked = jnp.concatenate([jnp.concatenate(halves(x), axis=1) for x in parts], axis=0)
    one = head_map(channels)
    out = mul(stacked, jnp.concatenate([one, one], axis=0))
    rows = parts[0].shape[0]
    return [out[i * rows : (i + 1) * rows] for i in range(len(parts))]


def gather_heads(parts, channels):
    stacked = jnp.concatenate([jnp.concatenate(halves(x), axis=1) for x in parts], axis=0)
    one = head_map(channels)
    out = mul(stacked, jnp.concatenate([one, one], axis=1), ((1,), (1,)))
    rows = parts[0].shape[0]
    return [out[i * rows : (i + 1) * rows] for i in range(len(parts))]


def running_sum(x, backward):
    t = lax.broadcasted_iota(jnp.int32, (Q, Q), 0)
    u = lax.broadcasted_iota(jnp.int32, (Q, Q), 1)
    tri = ((t <= u) if backward else (t >= u)).astype(BF16)
    return mul(jnp.concatenate([tri, tri], axis=1), jnp.concatenate(halves(x), axis=0))


def segments(ends, stream, positions):
    seg = jnp.zeros(positions.shape, jnp.int32)
    for k in range(ends.shape[1]):
        seg = seg + (ends[stream, k] <= positions).astype(jnp.int32)
    return jnp.where(positions < 0, -1, seg)


def chunk_front(p_ref, par_ref, ends, stream, chunk):
    local = p_ref.shape[2] - 2 * STATE - LANES
    channels = local // 2
    mixed = channels + 2 * STATE
    base = pl.multiple_of(chunk * Q, Q)
    before = pl.multiple_of(jnp.maximum(base - 8, 0), 8)
    xbc = p_ref[stream, pl.ds(base, Q), channels : channels + mixed]
    halo = p_ref[stream, pl.ds(before, 8), channels : channels + mixed]
    both = jnp.concatenate([halo, xbc], axis=0)
    column = lax.broadcasted_iota(jnp.int32, (Q + 16, LANES), 0) + (base - 8)
    seg = segments(ends, stream, column)
    here = seg[8 : Q + 8]
    tiles = mixed // LANES
    pre = par_ref[4:5, :mixed] + par_ref[3:4, :mixed] * xbc
    taps = []
    for k in range(CONV - 1):
        agree = (seg[5 + k : Q + 5 + k] == here).astype(F32)
        tap = both[5 + k : Q + 5 + k] * wide(agree, tiles)
        taps.append(tap)
        pre = pre + par_ref[k : k + 1, :mixed] * tap
    taps.append(xbc)
    gate = jax.nn.sigmoid(pre)
    active = pre * gate
    values = active[:, :channels]
    b_proj = active[:, channels : channels + STATE]
    c_proj = active[:, channels + STATE :]
    raw = p_ref[stream, pl.ds(base, Q), local + 2 * STATE :] + par_ref[7:8, :LANES]
    delta = jnp.maximum(raw, 0.0) + jnp.log1p(jnp.exp(-jnp.abs(raw)))
    rate = jnp.exp(par_ref[8:9, :LANES])
    log_decay = -delta * rate
    cumulative = running_sum(log_decay, False)
    last = cumulative[Q - 1 : Q]
    keep = (here == seg[7:8]).astype(F32)
    same_last = (here == seg[Q + 7 : Q + 8]).astype(F32)
    inflow = jnp.exp(cumulative) * keep
    tail = jnp.exp(last - cumulative) * same_last
    delta_wide, inflow_wide, tail_wide = spread([delta, inflow, tail], channels)
    row = lax.broadcasted_iota(jnp.int32, (8, LANES), 1) + base
    seg_row = segments(ends, stream, row)[0:1]
    t = lax.broadcasted_iota(jnp.int32, (Q, Q), 0)
    u = lax.broadcasted_iota(jnp.int32, (Q, Q), 1)
    mask = (t >= u) & (here == seg_row)
    turned = cumulative.T

    def decays(head):
        spacing = cumulative[:, head : head + 1] - turned[head : head + 1, :]
        return jnp.exp(jnp.where(mask, spacing, -1e30))

    return dict(
        base=base,
        seg=seg,
        pre=pre,
        gate=gate,
        taps=taps,
        values=values,
        b_low=b_proj.astype(BF16),
        c_low=c_proj.astype(BF16),
        raw=raw,
        delta=delta,
        rate=rate,
        log_decay=log_decay,
        delta_wide=delta_wide,
        inflow_wide=inflow_wide,
        tail_wide=tail_wide,
        scaled=values * delta_wide,
        decays=decays,
        channels=channels,
    )


def two_heads(pair):
    left = lax.broadcasted_iota(jnp.int32, pair.shape, 1) < HEAD_DIM
    low = pair.astype(BF16)
    zero = jnp.zeros_like(low)
    return jnp.concatenate([jnp.where(left, low, zero), jnp.where(left, zero, low)], axis=0)


def chunk_forward(front, state, skip):
    channels = front["channels"]
    scores = mul(front["c_low"], front["b_low"], ((1,), (1,)))
    pieces = []
    for pair in range(channels // LANES):
        weights = jnp.concatenate(
            [(front["decays"](2 * pair + i) * scores).astype(BF16) for i in range(2)], axis=1
        )
        scaled = front["scaled"][:, pair * LANES : (pair + 1) * LANES]
        pieces.append(mul(weights, two_heads(scaled)))
    result = jnp.concatenate(pieces, axis=1)
    result = result + mul(front["c_low"], state.astype(BF16)) * front["inflow_wide"]
    result = result + skip * front["values"]
    fed = (front["scaled"] * front["tail_wide"]).astype(BF16)
    after = front["inflow_wide"][Q - 1 : Q] * state + mul(front["b_low"], fed, ((0,), (0,)))
    return result, after


def chunk_backward(front, before, after, grad_after, result, grad, skip):
    channels = front["channels"]
    b_low, c_low = front["b_low"], front["c_low"]
    scaled, values = front["scaled"], front["values"]
    scores = mul(c_low, b_low, ((1,), (1,)))
    grad_scores = jnp.zeros((Q, Q), F32)
    pieces = []
    for pair in range(channels // LANES):
        lanes = slice(pair * LANES, (pair + 1) * LANES)
        decays = [front["decays"](2 * pair + i) for i in range(2)]
        weights = jnp.concatenate([(d * scores).astype(BF16) for d in decays], axis=0)
        split = two_heads(grad[:, lanes])
        pieces.append(mul(weights, split, ((0,), (0,))))
        cross = mul(split, scaled[:, lanes].astype(BF16), ((1,), (1,)))
        grad_scores = grad_scores + decays[0] * cross[:Q] + decays[1] * cross[Q:]
    grad_after_low = grad_after.astype(BF16)
    inner = jnp.concatenate(pieces, axis=1) + mul(b_low, grad_after_low) * front["tail_wide"]
    fed = (scaled * front["tail_wide"]).astype(BF16)
    flowing = (grad * front["inflow_wide"]).astype(BF16)
    low_scores = grad_scores.astype(BF16)
    grad_c = mul(low_scores, b_low) + mul(flowing, before.astype(BF16), ((1,), (1,)))
    grad_b = mul(low_scores, c_low, ((0,), (0,))) + mul(fed, grad_after_low, ((1,), (1,)))
    grad_values = skip * grad + front["delta_wide"] * inner
    grad_skip = jnp.sum(grad * values, axis=0, keepdims=True)
    held = jnp.sum(after * grad_after, axis=0, keepdims=True)
    grad_delta, grad_cumulative = gather_heads(
        [values * inner, grad * (result - skip * values) - scaled * inner], channels
    )
    held_heads = gather_heads([jnp.broadcast_to(held, (8, channels))], channels)[0][0:1]
    grad_log = running_sum(grad_cumulative, True) + held_heads
    grad_delta = grad_delta - front["rate"] * grad_log
    grad_raw = grad_delta * jax.nn.sigmoid(front["raw"])
    grad_rate = jnp.sum(grad_log * front["log_decay"], axis=0, keepdims=True)
    grad_before = front["inflow_wide"][Q - 1 : Q] * grad_after + mul(c_low, flowing, ((0,), (0,)))
    return grad_values, grad_b, grad_c, grad_raw, grad_rate, grad_skip, grad_before


def conv_backward(front, grad_active, next_grad, par_ref):
    gate, pre, seg = front["gate"], front["pre"], front["seg"]
    mixed = pre.shape[1]
    tiles = mixed // LANES
    grad_pre = grad_active * (gate * (1.0 + pre * (1.0 - gate)))
    rows = [jnp.sum(grad_pre * front["taps"][k], axis=0, keepdims=True) for k in range(CONV)]
    rows.append(jnp.sum(grad_pre, axis=0, keepdims=True))
    both = jnp.concatenate([grad_pre, next_grad], axis=0)
    grad_x = par_ref[CONV - 1 : CONV, :mixed] * grad_pre
    for k in range(CONV - 1):
        ahead = CONV - 1 - k
        agree = (seg[8 + ahead : Q + 8 + ahead] == seg[8 : Q + 8]).astype(F32)
        grad_x = grad_x + par_ref[k : k + 1, :mixed] * both[ahead : Q + ahead] * wide(agree, tiles)
    return grad_x, grad_pre[:8], rows


MESH = pl.DeviceIdType.MESH
TILE = 512


class Links:
    def __init__(self, send, recv):
        self.send, self.recv, self.used = send, recv, 0

    def copy(self, source, target, device):
        slot = self.used
        self.used += 1
        return pltpu.make_async_remote_copy(
            src_ref=source,
            dst_ref=target,
            send_sem=self.send.at[slot],
            recv_sem=self.recv.at[slot],
            device_id=device,
            device_id_type=MESH,
        )


class Place:
    def __init__(self, depth):
        self.s = lax.axis_index("seq")
        self.f = lax.axis_index("fsdp")
        self.depth = depth
        self.core = lax.rem(self.s, 2)
        x = lax.rem(self.s // 2, 2)
        y = self.s // 4
        self.steps = (1 - 2 * self.core, 2 - 4 * x, 4 - 8 * y)

    def peer(self, k):
        index = self.s
        for bit in range(3):
            if k >> bit & 1:
                index = index + self.steps[bit]
        return index

    def at(self, k):
        return (self.peer(k), self.f)

    def plane(self, d):
        return lax.rem(self.f + d, self.depth)

    def beyond(self, d):
        return (self.s, self.plane(d))

    def greet(self):
        barrier = pltpu.get_barrier_semaphore()
        others = [self.at(k) for k in range(1, 8)] + [self.beyond(d) for d in range(1, self.depth)]
        for other in others:
            pl.semaphore_signal(barrier, inc=1, device_id=other, device_id_type=MESH)
        pl.semaphore_wait(barrier, len(others))


def ahead(start, size):
    return pl.ds(pl.multiple_of(start, size), size)


def gather_kernel(
    depth,
    ends,
    hidden,
    out_grad,
    in_proj,
    out_proj,
    gain,
    par_ref,
    x_out,
    g_out,
    w_out,
    o_out,
    p_out,
    y_out,
    h_out,
    gg_out,
    moments_out,
    x,
    g,
    wm,
    wc,
    wo,
    p,
    y,
    h,
    gg,
    state,
    packed,
    common,
    moments,
    send,
    recv,
    leave,
):
    streams, block = hidden.shape[0], hidden.shape[1]
    length = x.shape[1]
    rows = in_proj.shape[0]
    lines = out_proj.shape[0]
    channels = wo.shape[0]
    slab = depth * rows
    here = Place(depth)
    s, f = here.s, here.f
    links = Links(send, recv)
    exits = []

    def leaving(source, target):
        copy = pltpu.make_async_copy(source, target, leave.at[len(exits)])
        copy.start()
        exits.append(copy)

    for k in range(CHANNELS // channels):
        lanes = slice(k * channels, (k + 1) * channels)
        packed[k, :, :channels] = in_proj[:, lanes].astype(BF16)
        lanes = slice(CHANNELS + k * channels, CHANNELS + (k + 1) * channels)
        packed[k, :, channels:] = in_proj[:, lanes].astype(BF16)
    narrow = 2 * STATE + HEADS
    common[:, narrow:] = jnp.zeros((rows, common.shape[1] - narrow), BF16)
    common[:, :narrow] = in_proj[:, 2 * CHANNELS :].astype(BF16)

    def slab_rows(source, plane):
        return ahead((source * depth + plane) * rows, rows)

    def block_rows(source):
        return ahead(source * block, block)

    here.greet()
    finish = []

    def started(copy):
        copy.start()
        finish.append(copy)
        return copy

    own = slab_rows(s, f)
    turned = [None]
    for k in (2, 4, 6, 1, 3, 5, 7):
        turned.append(started(links.copy(packed.at[here.peer(k)], wm.at[own], here.at(k))))
    turned = dict(zip((0, 2, 4, 6, 1, 3, 5, 7), turned))
    shared = [started(links.copy(common, wc.at[own], here.beyond(d))) for d in range(1, depth)]
    wc[own] = common[...]
    wm[own] = packed[s]

    upstream = hidden[...].astype(F32)
    mean = jnp.mean(upstream * upstream, axis=-1, keepdims=True)
    x[:, block_rows(s)] = (upstream * lax.rsqrt(mean + EPS_NORM) * gain[...]).astype(BF16)
    mine = x.at[:, block_rows(s)]
    near = [started(links.copy(mine, mine, here.at(k))) for k in (2, 4)]
    beside = [started(links.copy(mine, mine, here.at(1)))]
    g[:, block_rows(s)] = out_grad[...]
    wo[ahead(f * lines, lines)] = out_proj[...].astype(BF16)

    def hop(k, d, up):
        plane = f - d if up else f + d
        target = wm.at[slab_rows(here.peer(k), plane)]
        return links.copy(target, target, (s, f + 1 if up else f - 1))

    hops = {}
    for k in range(8):
        for d in range(depth - 1):
            hops[k, d] = (hop(k, d, True), hop(k, d, False))

    def sends(d):
        return ((f >= d) & (f < depth - 1), (f <= depth - 1 - d) & (f > 0))

    def gets(d):
        return (f >= d + 1, f <= depth - 2 - d)

    def launch(k, d):
        for way in range(2):
            pl.when(sends(d)[way])(hops[k, d][way].start)

    def arrive(k, d):
        for way in range(2):
            pl.when(gets(d)[way])(hops[k, d][way].wait_recv)

    order = (0, 1, 2, 3, 4, 5, 6, 7)
    across = []
    spread_common = []
    chip = s // 2

    def tokens_second_phase():
        near[0].wait_recv()
        half = x.at[0, block_rows(here.peer(2))]
        across.append(started(links.copy(half, half, here.at(4))))
        whole = x.at[:, block_rows(here.peer(2))]
        beside.append(started(links.copy(whole, whole, here.at(1))))
        near[1].wait_recv()
        half = x.at[1, block_rows(here.peer(4))]
        across.append(started(links.copy(half, half, here.at(2))))
        whole = x.at[:, block_rows(here.peer(4))]
        beside.append(started(links.copy(whole, whole, here.at(1))))

    def common_second_phase():
        for copy in shared:
            copy.wait_recv()
        group = wc.at[ahead(s * slab, slab)]
        for k in (2, 4, 6, 1):
            spread_common.append(links.copy(group, group, here.at(k)))
            spread_common[-1].start()

    def common_third_phase():
        for copy in spread_common[:3]:
            copy.wait_recv()
        for k in (2, 4, 6):
            group = wc.at[ahead(here.peer(k) * slab, slab)]
            spread_common.append(links.copy(group, group, here.at(1)))
            spread_common[-1].start()

    def tokens_third_phase():
        for way, k in enumerate((2, 4)):
            across[way].wait_recv()
            half = x.at[way, block_rows(here.peer(6))]
            beside.append(started(links.copy(half, half, here.at(1))))

    far_tokens = []

    def project(j):
        q = (here.peer(order[2 * j])) // 2
        span = ahead(q * 2 * slab, 2 * slab)

        def tile(i, carry):
            stream = i // (length // TILE)
            at = ahead(lax.rem(i, length // TILE) * TILE, TILE)
            left = x[stream, at, span]
            for part, weights in ((slice(0, 2 * channels), wm), (slice(2 * channels, None), wc)):
                product = mul(left, weights[span, :])
                if j == 0:
                    p[stream, at, part] = product
                else:
                    p[stream, at, part] += product
            return carry

        lax.fori_loop(0, streams * (length // TILE), tile, 0)

    last = depth - 1
    for i in range(8 + last):
        if i < 8:
            k = order[i]
            if turned[k] is not None:
                turned[k].wait_recv()
            launch(k, 0)
        for d in range(1, last):
            if 0 <= i - d < 8:
                arrive(order[i - d], d - 1)
                launch(order[i - d], d)
        if 0 <= i - last < 8:
            arrive(order[i - last], last - 1)
        if i == 2:
            common_second_phase()
        if i == 3:
            common_third_phase()
        if i == 4:
            tokens_second_phase()
        if i == last + 1:
            tokens_third_phase()
            for copy in beside:
                copy.wait_recv()
            for copy in spread_common[3:]:
                copy.wait_recv()
            for copy in spread_common:
                copy.wait_send()
            leaving(x, x_out)
            mine_g = g.at[:, block_rows(s)]
            for k in (2, 4, 6):
                far_tokens.append(started(links.copy(mine_g, mine_g, here.at(k))))
            beside_g = [started(links.copy(mine_g, mine_g, here.at(1)))]
            column = lax.broadcasted_iota(jnp.int32, (LANES, LANES), 0)
            wanted = lax.broadcasted_iota(jnp.int32, (LANES, LANES), 1)
            share = channels // HEAD_DIM
            pick = ((column == wanted + s * share) & (wanted < share)).astype(BF16)
            for part in range(0, wc.shape[0], TILE):
                steps = wc[part : part + TILE, 2 * STATE :]
                wc[part : part + TILE, 2 * STATE :] = mul(steps, pick).astype(BF16)
        if i >= last + 1 and (i - last) % 2 == 1:
            project((i - last) // 2)
    lent = wo.at[ahead(f * lines, lines)]
    outs = [started(links.copy(lent, lent, here.beyond(d))) for d in range(1, depth)]
    leaving(p, p_out)
    leaving(wm, w_out.at[:, : 2 * channels])
    leaving(wc, w_out.at[:, 2 * channels :])

    skip = par_ref[6:7, :channels]
    state[...] = jnp.zeros_like(state)

    def step(chunk, carry):
        for stream in range(streams):
            front = chunk_front(p, par_ref, ends, stream, chunk)
            before = state[stream]
            h[stream, chunk] = before.astype(BF16)
            result, after = chunk_forward(front, before, skip)
            y[stream, pl.ds(front["base"], Q)] = result
            state[stream] = after
        return carry

    lax.fori_loop(0, length // Q, step, 0)
    leaving(y, y_out)
    leaving(h, h_out)

    for k, copy in zip((2, 4, 6), far_tokens):
        copy.wait_recv()
        block_g = g.at[:, block_rows(here.peer(k))]
        beside_g.append(started(links.copy(block_g, block_g, here.at(1))))
    for copy in outs:
        copy.wait_recv()
    for copy in beside_g:
        copy.wait_recv()
    leaving(g, g_out)
    leaving(wo, o_out)

    g_inner = par_ref[5:6, :channels]
    ones = jnp.ones((8, 2 * channels), BF16)
    tiles = length // TILE
    pieces = TILE // Q
    half = streams * length // Q

    def weigh(i, carry):
        stream = i // tiles
        at = ahead(lax.rem(i, tiles) * TILE, TILE)
        grad = mul(g[stream, at], wo[...], ((1,), (1,)))
        gg[stream, at] = grad.astype(BF16)
        gate_in = p[stream, at, :channels]
        flat = y[stream, at] * (gate_in * jax.nn.sigmoid(gate_in))
        for which, product in enumerate((flat * flat, grad * g_inner * flat)):
            sums = mul(ones, jnp.concatenate(halves(product), axis=1), ((1,), (1,)))
            for j in range(pieces):
                at_row = which * half + i * pieces + j
                moments[s, pl.ds(at_row, 1), :] = sums[0:1, j * Q : (j + 1) * Q]
        return carry

    lax.fori_loop(0, streams * tiles, weigh, 0)
    leaving(gg, gg_out)
    mine_m = moments.at[s]
    told = [started(links.copy(mine_m, mine_m, here.at(k))) for k in range(1, 8)]
    for copy in told:
        copy.wait_recv()
    moments_out[...] = jnp.sum(moments[...], axis=0)

    for copy in finish:
        copy.wait_send()
    for k in range(8):
        for d in range(depth - 1):
            for way in range(2):
                pl.when(sends(d)[way])(hops[k, d][way].wait_send)
    for copy in exits:
        copy.wait()


LINE = 512
GROUP = 384


class Summing:
    def __init__(self, here, links, slots, beside, halves_in, final_in, own):
        self.here, self.slots, self.beside = here, slots, beside
        self.halves_in, self.final_in, self.own = halves_in, final_in, own
        make = links.copy
        self.to_beside = [make(slots.at[r], beside.at[r], here.at(1)) for r in range(4)]
        self.by = [make(slots.at[3, i], halves_in.at[i], here.at(2 << i)) for i in range(2)]
        self.last = [make(slots.at[1 + i], final_in.at[i], here.at(2 << i)) for i in range(2)]

    def owner(self, r, other):
        return self.here.peer(2 * r + (1 if other else 0))

    def give_beside(self, r, value):
        self.slots[r] = value.astype(BF16)
        self.to_beside[r].start()

    def joined(self, r, value):
        self.to_beside[r].wait()
        return value + self.beside[r].astype(F32)

    def diagonal(self, value):
        self.slots[3] = self.joined(3, value).astype(BF16)
        for copy in self.by:
            copy.start()

    def neighbour(self, i, value):
        value = self.joined(1 + i, value)
        other = 1 - i
        self.by[other].wait_recv()
        self.slots[1 + i, i] = value[i].astype(BF16)
        self.slots[1 + i, other] = (value[other] + self.halves_in[other].astype(F32)).astype(BF16)
        self.last[i].start()

    def keep(self, value):
        self.own[...] = self.joined(0, value).astype(self.own.dtype)

    def total(self):
        for copy in self.last:
            copy.wait_recv()
        return self.own[...].astype(F32) + self.final_in[0].astype(F32) + self.final_in[1].astype(F32)

    def settle(self):
        for copy in self.by + self.last:
            copy.wait_send()


def adjoint_kernel(
    depth,
    ends,
    hidden,
    out_grad,
    gain,
    par_ref,
    moments,
    x_in,
    g_in,
    w_in,
    o_in,
    p_in,
    y_in,
    h_in,
    gg_in,
    mixed_out,
    upstream_out,
    main_out,
    common_out,
    lines_out,
    vector_out,
    tokens,
    w,
    wo,
    p,
    y,
    h,
    gg,
    dp,
    state,
    later,
    sums,
    slots,
    beside,
    mixed_halves,
    mixed_last,
    grad_halves,
    grad_last,
    lines,
    lines_recv,
    main,
    main_recv,
    slabs,
    slabs_recv,
    common,
    common_beside,
    common_recv,
    common_line,
    common_last,
    gain_sums,
    vector_line,
    vector_all,
    send,
    recv,
    enter,
    credit,
):
    streams, block = hidden.shape[0], hidden.shape[1]
    length = p.shape[1]
    chunks = length // Q
    channels = y.shape[2]
    mixed = channels + 2 * STATE
    rows = main.shape[3]
    out_rows = lines_out.shape[0]
    slab = depth * rows
    here = Place(depth)
    s, f = here.s, here.f
    links = Links(send, recv)

    entries = []

    def entering_copy(source, target):
        copy = pltpu.make_async_copy(source, target, enter.at[len(entries)])
        copy.start()
        entries.append(copy)
        return copy

    p_copy = entering_copy(p_in, p)
    y_copy = entering_copy(y_in, y)
    gg_copy = entering_copy(gg_in, gg)
    o_copy = entering_copy(o_in, wo)
    g_copy = entering_copy(g_in, tokens)
    h_copy = entering_copy(h_in, h)
    w_copy = entering_copy(w_in, w)
    here.greet()

    mixed_sum = Summing(here, links, slots, beside, mixed_halves, mixed_last, mixed_out)
    grad_sum = Summing(here, links, slots, beside, grad_halves, grad_last, upstream_out)

    skip = par_ref[6:7, :channels]
    g_inner = par_ref[5:6, :channels]
    sums[...] = jnp.zeros_like(sums)
    state[...] = jnp.zeros_like(state)
    later[...] = jnp.zeros_like(later)
    half = streams * chunks
    tiles = channels // LANES

    def column(row):
        return jnp.broadcast_to(row, (Q, Q)).T

    def norm_columns(which):
        first = moments[pl.ds(which, 1), :]
        second = moments[pl.ds(half + which, 1), :]
        scale = lax.rsqrt(first / CHANNELS + EPS_NORM)
        return column(scale), column(scale * scale * scale * second / CHANNELS)

    p_copy.wait()
    y_copy.wait()
    gg_copy.wait()

    def gate_step(i, carry):
        stream = i // chunks
        at = ahead(lax.rem(i, chunks) * Q, Q)
        scale, pull = norm_columns(i)
        scale, pull = wide(scale, tiles), wide(pull, tiles)
        gate_in = p[stream, at, :channels]
        result = y[stream, at]
        sig = jax.nn.sigmoid(gate_in)
        silu = gate_in * sig
        flat = result * silu
        scaled = flat * scale
        grad = gg[stream, at].astype(F32)
        dp[stream, at, 2 * channels :] = (scaled * g_inner).astype(BF16)
        grad_flat = scale * g_inner * grad - flat * pull
        p[stream, at, :channels] = grad_flat * silu
        grad_gate = grad_flat * result * (sig * (1.0 + gate_in * (1.0 - sig)))
        dp[stream, at, :channels] = grad_gate.astype(BF16)
        sums[5:6, :channels] += jnp.sum(grad * scaled, axis=0, keepdims=True)
        return carry

    lax.fori_loop(0, half, gate_step, 0)
    o_copy.wait()

    def rows_of(ref, owner, lanes):
        at = ahead(owner * block, block)
        return jnp.concatenate([ref[k, at, lanes] for k in range(streams)], axis=0)

    def branch(r, other):
        low = rows_of(dp, mixed_sum.owner(r, other), slice(2 * channels, 3 * channels))
        return mul(low, wo[...]).reshape(streams, block, D)

    for r in (3, 1, 2, 0):
        mixed_sum.give_beside(r, branch(r, True))
    mixed_sum.diagonal(branch(3, False))

    g_copy.wait()

    def line_step(j, carry):
        lanes = ahead(j * LINE, LINE)
        total = jnp.zeros((channels, LINE), F32)
        for k in range(streams):
            total = total + mul(dp[k, :, 2 * channels :], tokens[k, :, lanes], ((0,), (0,)))
        lines[:, lanes] = total.astype(BF16)
        return carry

    lax.fori_loop(0, D // LINE, line_step, 0)
    x_copy = entering_copy(x_in, tokens)
    line_sends = []
    for d in range(1, depth):
        theirs = lines.at[ahead(here.plane(d) * out_rows, out_rows)]
        line_sends.append(links.copy(theirs, lines_recv.at[d - 1], here.beyond(d)))
        line_sends[-1].start()
    for i in range(2):
        mixed_sum.neighbour(i, branch(1 + i, False))
    mixed_sum.keep(branch(0, False))
    pl.semaphore_signal(credit, inc=1, device_id=here.at(1), device_id_type=MESH)

    def gradient_rows(j, lanes):
        wanted = ahead(j * GROUP, GROUP)
        total = jnp.zeros((GROUP, channels), F32)
        for k in range(streams):
            total = total + mul(tokens[k, :, wanted], dp[k, :, lanes], ((0,), (0,)))
        product = total * w[wanted, lanes].astype(F32)
        ones = jnp.ones((8, 2 * channels), BF16)
        gain_sums[:, wanted] += mul(ones, jnp.concatenate(halves(product), axis=1), ((1,), (1,)))
        return total

    gain_sums[...] = jnp.zeros_like(gain_sums)
    main_sends = [[], []]

    def main_part(part):
        lanes = slice(part * channels, (part + 1) * channels)

        def group(j, carry):
            total = gradient_rows(j, lanes).astype(BF16)
            for i in range(GROUP // rows):
                source = (GROUP // slab) * j + i // depth
                main[part, i % depth, source] = total[i * rows : (i + 1) * rows]
            return carry

        lax.fori_loop(0, D // GROUP, group, 0)
        for d in range(1, depth):
            copy = links.copy(
                main.at[part, here.plane(d)], main_recv.at[part, d - 1], here.beyond(d)
            )
            copy.start()
            main_sends[part].append(copy)

    x_copy.wait()
    w_copy.wait()
    main_part(0)
    h_copy.wait()

    def step(k, carry):
        chunk = chunks - 1 - k
        for stream in range(streams):
            front = chunk_front(p, par_ref, ends, stream, chunk)
            at = pl.ds(front["base"], Q)
            grad_after = state[stream]
            before = h[stream, chunk].astype(F32)
            after = h[stream, jnp.minimum(chunk + 1, chunks - 1)].astype(F32)
            gv, gb, gc, graw, grate, gskip, gbefore = chunk_backward(
                front, before, after, grad_after, y[stream, at], p[stream, at, :channels], skip
            )
            state[stream] = gbefore
            grad_active = jnp.concatenate([gv, gb, gc], axis=1)
            grad_x, head, rows_w = conv_backward(front, grad_active, later[stream], par_ref)
            later[stream] = head
            dp[stream, at, channels : channels + mixed] = grad_x.astype(BF16)
            dp[stream, at, channels + mixed :] = graw.astype(BF16)
            for i, row in enumerate(rows_w):
                sums[i : i + 1, :] += row
            sums[6:7, :channels] += gskip
            sums[7:8, :LANES] += jnp.sum(graw, axis=0, keepdims=True)
            sums[8:9, :LANES] += grate
        return carry

    lax.fori_loop(0, chunks, step, 0)

    main_part(1)
    column_at = lax.broadcasted_iota(jnp.int32, (LANES, LANES), 1)
    wanted_at = lax.broadcasted_iota(jnp.int32, (LANES, LANES), 0)
    share = channels // HEAD_DIM
    place = ((column_at == wanted_at + s * share) & (wanted_at < share)).astype(BF16)

    def common_group(j, carry):
        total = gradient_rows(j, slice(2 * channels, 3 * channels)).astype(BF16)
        at = ahead(j * GROUP, GROUP)
        common[at, : 2 * STATE] = total[:, : 2 * STATE]
        common[at, 2 * STATE :] = mul(total[:, 2 * STATE :], place).astype(BF16)
        return carry

    lax.fori_loop(0, D // GROUP, common_group, 0)

    def owned(k):
        return common.at[ahead(here.peer(k) * slab, slab)]

    common_sends = [
        links.copy(owned(2 * r + 1), common_beside.at[r], here.at(1)) for r in range(4)
    ]
    for copy in common_sends:
        copy.start()

    for i in range(3):
        third = D // 3
        sums[9 + i : 10 + i, :third] = gain_sums[0:1, i * third : (i + 1) * third]
    vector_line[f] = sums[...]
    told = [links.copy(sums, vector_line.at[f], here.beyond(d)) for d in range(1, depth)]
    for copy in told:
        copy.start()

    def back(r, other):
        low = rows_of(dp, grad_sum.owner(r, other), slice(None))
        return mul(low, w[...], ((1,), (1,))).reshape(streams, block, D)

    mixed_sum.settle()
    pl.semaphore_wait(credit, 1)
    for r in (3, 1, 2, 0):
        grad_sum.give_beside(r, back(r, True))
        if r == 3:
            for copy in told:
                copy.wait_recv()
            vector_all[s] = jnp.sum(vector_line[...], axis=0)
            mine = vector_all.at[s]
            heard = [links.copy(mine, mine, here.at(k)) for k in range(1, 8)]
            for copy in heard:
                copy.start()
    grad_sum.diagonal(back(3, False))

    for copy in common_sends:
        copy.wait_recv()
    common_across = []
    for r in (3, 1, 2, 0):
        at = ahead(here.peer(2 * r) * slab, slab)
        joined = common[at, :].astype(F32) + common_beside[r].astype(F32)
        common[at, :] = joined.astype(BF16)
        if r:
            copy = links.copy(owned(2 * r), common_recv.at[r - 1], here.at(2 * r))
            copy.start()
            common_across.append(copy)

    for i in range(2):
        grad_sum.neighbour(i, back(1 + i, False))
    grad_sum.keep(back(0, False))

    slab_sends = []
    for part in range(2):
        lanes = slice(part * channels, (part + 1) * channels)
        for copy in main_sends[part]:
            copy.wait_recv()
        total = main[part, f].astype(F32)
        for d in range(1, depth):
            total = total + main_recv[part, d - 1].astype(F32)
        slabs[:, :, lanes] = total.astype(BF16)
    for k in range(1, 8):
        copy = links.copy(slabs.at[here.peer(k)], slabs_recv.at[s], here.at(k))
        copy.start()
        slab_sends.append(copy)
    slabs_recv[s] = slabs[s]

    for copy in common_across:
        copy.wait_recv()
    at = ahead(s * slab, slab)
    joined = common[at, :].astype(F32)
    for r in range(3):
        joined = joined + common_recv[r].astype(F32)
    common_line[...] = joined.astype(BF16).reshape(depth, rows, common.shape[1])
    common_sends_z = []
    for d in range(1, depth):
        copy = links.copy(common_line.at[here.plane(d)], common_last.at[d - 1], here.beyond(d))
        copy.start()
        common_sends_z.append(copy)

    for copy in line_sends:
        copy.wait_recv()
    total = lines[ahead(f * out_rows, out_rows), :].astype(F32)
    for d in range(1, depth):
        total = total + lines_recv[d - 1].astype(F32)
    lines_out[...] = total
    upstream = hidden[...].astype(F32)
    branch_sum = mixed_sum.total()
    mixed_out[...] = (upstream + branch_sum).astype(BF16)
    for copy in common_sends_z:
        copy.wait_recv()
    total = common_line[f].astype(F32)
    for d in range(1, depth):
        total = total + common_last[d - 1].astype(F32)
    common_out[...] = total

    grad_normed = grad_sum.total() * gain[...]
    inverse = lax.rsqrt(jnp.mean(upstream * upstream, axis=-1, keepdims=True) + EPS_NORM)
    unit = upstream * inverse
    along = jnp.mean(grad_normed * unit, axis=-1, keepdims=True)
    upstream_out[...] = out_grad[...].astype(F32) + inverse * (grad_normed - unit * along)

    for copy in slab_sends:
        copy.wait_recv()
    main_out[...] = slabs_recv[...]
    for copy in heard:
        copy.wait_recv()
    vector_out[...] = vector_all[...]
    grad_sum.settle()
    pending = line_sends + main_sends[0] + main_sends[1] + common_sends + told + heard
    for copy in pending + common_across + slab_sends + common_sends_z:
        copy.wait_send()


def local_vector_rows(vector, index, share):
    g_norm, g_inner, conv_w, conv_b, dt_bias, a_log, d_skip = split_vector(vector)
    channels = share * HEAD_DIM
    mixed = channels + 2 * STATE

    def own(array, size):
        return lax.dynamic_slice_in_dim(array, index * size, size, axis=-1)

    def row(array):
        return jnp.pad(array, ((0, 0), (0, mixed - array.shape[1])))

    conv = jnp.concatenate([conv_w, conv_b[None]], axis=0)
    conv = jnp.concatenate([own(conv[:, :CHANNELS], channels), conv[:, CHANNELS:]], axis=1)
    skip = jnp.repeat(own(d_skip, share), HEAD_DIM)
    rows = [conv] + [
        row(part[None])
        for part in (own(g_inner, channels), skip, own(dt_bias, share), own(a_log, share))
    ]
    return jnp.pad(jnp.concatenate(rows, axis=0), ((0, 7), (0, 0)))


def call(kernel, name, out_shape, out_specs, inputs, scratch, vmem_mib, collective, hbm=0):
    specs = [pl.BlockSpec(memory_space=pltpu.SMEM)]
    specs += [pl.BlockSpec(memory_space=pltpu.VMEM)] * (len(inputs) - 1 - hbm)
    specs += [pl.BlockSpec(memory_space=pl.ANY)] * hbm
    return pl.pallas_call(
        kernel,
        out_shape=out_shape,
        in_specs=specs,
        out_specs=[pl.BlockSpec(memory_space=space) for space in out_specs],
        scratch_shapes=scratch,
        name=name,
        compiler_params=pltpu.CompilerParams(
            vmem_limit_bytes=vmem_mib << 20,
            collective_id=collective,
            has_side_effects=True,
        ),
    )(*inputs)


def heads_plan(
    hidden_in,
    out_grad,
    lengths,
    in_proj,
    in_first,
    in_second,
    out_proj,
    out_first,
    out_second,
    vector,
    vector_first,
    vector_second,
):
    count, index = lax.axis_size("seq"), lax.axis_index("seq")
    depth = lax.axis_size("fsdp")
    share = HEADS // count
    channels = share * HEAD_DIM
    mixed = channels + 2 * STATE
    streams, block = hidden_in.shape[0], hidden_in.shape[1]
    length = block * count
    chunks = length // Q
    rows = in_proj.shape[0]
    columns = mixed + channels + LANES
    g_norm = vector[:D]
    par = local_vector_rows(vector, index, share)
    ends = jnp.cumsum(lengths, axis=-1, dtype=jnp.int32)

    shape = jax.ShapeDtypeStruct
    moment_rows = 2 * streams * chunks
    normed_low, grads, weights, out_full, projected, result, states, grad_gated, moments = call(
        functools.partial(gather_kernel, depth),
        "gather_forward",
        [
            shape((streams, length, D), BF16),
            shape((streams, length, D), BF16),
            shape((D, columns), BF16),
            shape((channels, D), BF16),
            shape((streams, length, columns), F32),
            shape((streams, length, channels), F32),
            shape((streams, chunks, STATE, channels), BF16),
            shape((streams, length, channels), BF16),
            shape((moment_rows, Q), F32),
        ],
        [pl.ANY] * 8 + [pltpu.VMEM],
        (ends, hidden_in, out_grad, in_proj, out_proj, g_norm[None], par),
        [
            pltpu.VMEM((streams, length, D), BF16),
            pltpu.VMEM((streams, length, D), BF16),
            pltpu.VMEM((D, 2 * channels), BF16),
            pltpu.VMEM((D, 2 * STATE + LANES), BF16),
            pltpu.VMEM((channels, D), BF16),
            pltpu.VMEM((streams, length, columns), F32),
            pltpu.VMEM((streams, length, channels), F32),
            pltpu.VMEM((streams, chunks, STATE, channels), BF16),
            pltpu.VMEM((streams, length, channels), BF16),
            pltpu.VMEM((streams, STATE, channels), F32),
            pltpu.VMEM((count, rows, 2 * channels), BF16),
            pltpu.VMEM((rows, 2 * STATE + LANES), BF16),
            pltpu.VMEM((count, moment_rows, Q), F32),
            pltpu.SemaphoreType.DMA((128,)),
            pltpu.SemaphoreType.DMA((128,)),
            pltpu.SemaphoreType.DMA((16,)),
        ],
        56,
        collective=0,
    )
    out_rows = out_proj.shape[0]
    across = 2 * STATE + LANES
    slab = depth * rows
    dma = pltpu.SemaphoreType.DMA
    mixed_out, input_grad, main, rest, out_summed, small = call(
        functools.partial(adjoint_kernel, depth),
        "adjoint",
        [
            shape((streams, block, D), BF16),
            shape((streams, block, D), F32),
            shape((count, rows, 2 * channels), BF16),
            shape((rows, across), F32),
            shape((out_rows, D), F32),
            shape((count, 16, mixed), F32),
        ],
        [pltpu.VMEM] * 6,
        (ends, hidden_in, out_grad, g_norm[None], par, moments)
        + (normed_low, grads, weights, out_full, projected, result, states, grad_gated),
        [
            pltpu.VMEM((streams, length, D), BF16),
            pltpu.VMEM((D, columns), BF16),
            pltpu.VMEM((channels, D), BF16),
            pltpu.VMEM((streams, length, columns), F32),
            pltpu.VMEM((streams, length, channels), F32),
            pltpu.VMEM((streams, chunks, STATE, channels), BF16),
            pltpu.VMEM((streams, length, channels), BF16),
            pltpu.VMEM((streams, length, columns), BF16),
            pltpu.VMEM((streams, STATE, channels), F32),
            pltpu.VMEM((streams, 8, mixed), F32),
            pltpu.VMEM((16, mixed), F32),
            pltpu.VMEM((4, streams, block, D), BF16),
            pltpu.VMEM((4, streams, block, D), BF16),
        ]
        + [
            pltpu.VMEM((2, block, D), BF16),
            pltpu.VMEM((2, streams, block, D), BF16),
            pltpu.VMEM((2, block, D), BF16),
            pltpu.VMEM((2, streams, block, D), BF16),
            pltpu.VMEM((channels, D), BF16),
            pltpu.VMEM((depth - 1, out_rows, D), BF16),
            pltpu.VMEM((2, depth, count, rows, channels), BF16),
            pltpu.VMEM((2, depth - 1, count, rows, channels), BF16),
            pltpu.VMEM((count, rows, 2 * channels), BF16),
            pltpu.VMEM((count, rows, 2 * channels), BF16),
            pltpu.VMEM((D, across), BF16),
            pltpu.VMEM((4, slab, across), BF16),
            pltpu.VMEM((3, slab, across), BF16),
            pltpu.VMEM((depth, rows, across), BF16),
            pltpu.VMEM((depth - 1, rows, across), BF16),
            pltpu.VMEM((8, D), F32),
            pltpu.VMEM((depth, 16, mixed), F32),
            pltpu.VMEM((count, 16, mixed), F32),
            dma((96,)),
            dma((96,)),
            dma((16,)),
            pltpu.SemaphoreType.REGULAR,
        ],
        63,
        collective=1,
        hbm=8,
    )
    in_summed = jnp.concatenate(
        [
            main[..., :channels].transpose(1, 0, 2).reshape(rows, CHANNELS).astype(F32),
            main[..., channels:].transpose(1, 0, 2).reshape(rows, CHANNELS).astype(F32),
            rest[:, : 2 * STATE + HEADS],
        ],
        axis=1,
    )
    conv = jnp.concatenate(
        [
            small[:, :5, :channels].transpose(1, 0, 2).reshape(5, CHANNELS),
            jnp.sum(small[:, :5, channels:], axis=0),
        ],
        axis=1,
    )
    vector_summed = jnp.concatenate(
        [
            jnp.sum(small[:, 9:12, : D // 3], axis=0).reshape(-1) / g_norm,
            small[:, 5, :channels].reshape(-1),
            conv.reshape(-1),
            small[:, 7, :share].reshape(-1),
            small[:, 8, :share].reshape(-1),
            jnp.sum(small[:, 6, :channels].reshape(HEADS, HEAD_DIM), axis=1),
        ]
    )
    in_new = adam_update(in_proj, in_first, in_second, in_summed, RATE_MATRIX, DECAY_MATRIX)
    out_new = adam_update(out_proj, out_first, out_second, out_summed, RATE_MATRIX, DECAY_MATRIX)
    vec_new = adam_update(vector, vector_first, vector_second, vector_summed, RATE_VECTOR, 0.0)
    return (mixed_out, input_grad, *in_new, *out_new, *vec_new)


def solution(mesh):
    return jax.shard_map(
        heads_plan if mesh.shape["seq"] == 8 else positions_plan,
        mesh=mesh,
        in_specs=(
            P("fsdp", "seq", None),
            P("fsdp", "seq", None),
            P("fsdp", None),
            P(("seq", "fsdp"), None),
            P(("seq", "fsdp"), None),
            P(("seq", "fsdp"), None),
            P(("seq", "fsdp"), None),
            P(("seq", "fsdp"), None),
            P(("seq", "fsdp"), None),
            P(),
            P(),
            P(),
        ),
        out_specs=(
            P("fsdp", "seq", None),
            P("fsdp", "seq", None),
            P(("seq", "fsdp"), None),
            P(("seq", "fsdp"), None),
            P(("seq", "fsdp"), None),
            P(("seq", "fsdp"), None),
            P(("seq", "fsdp"), None),
            P(("seq", "fsdp"), None),
            P(),
            P(),
            P(),
        ),
        check_vma=False,
    )
```

```python
import functools

import jax
import jax.numpy as jnp
from jax import lax
from jax.experimental import pallas as pl
from jax.experimental.pallas import tpu as pltpu
from jax.sharding import PartitionSpec as P

D = 1536
HEADS = 48
HEAD_DIM = 64
STATE = 128
CONV = 4
STEP = 5


HIGH = lax.Precision.HIGHEST
EPS_NORM = 1e-05
BETA_ONE = 0.9
BETA_TWO = 0.95
ADAM_EPS = 1e-08
RATE_MATRIX = 0.03
RATE_VECTOR = 0.1
DECAY_MATRIX = 0.1


def passed_along(block, axis, distance):
    devices = range(lax.axis_size(axis))
    route = [(i - distance, i) for i in devices if i - distance in devices]
    return lax.ppermute(block, axis, route)


def entering(shard, axis, combine, identity, reverse):
    length, here = (lax.axis_size(axis), lax.axis_index(axis))
    everything = jax.tree.map(
        lambda part, kind: lax.all_gather(part.astype(kind), axis),
        shard,
        jax.tree.map(lambda a: jnp.bfloat16 if a.dtype == jnp.float32 else a.dtype, shard),
    )
    start = jax.tree.map(
        lambda part, zero: jnp.broadcast_to(jnp.asarray(zero, part.dtype), part.shape),
        shard,
        identity,
    )

    def step(k, before):
        at = length - 1 - k if reverse else k
        reached = at > here if reverse else at < here
        new = combine(
            before, jax.tree.map(lambda part, own: part[at].astype(own.dtype), everything, shard)
        )
        return jax.tree.map(lambda a, b: jnp.where(reached, a, b), new, before)

    return lax.fori_loop(0, length, step, start)


def as_sent(shard):
    return jax.tree.map(lambda a: a.astype(jnp.bfloat16) if a.dtype == jnp.float32 else a, shard)


def split_vector(vector):
    inner = HEADS * HEAD_DIM
    width = inner + 2 * STATE
    counts = [D, inner, CONV * width, width, HEADS, HEADS, HEADS]
    pieces = []
    offset = 0
    for amount in counts:
        pieces.append(vector[offset : offset + amount])
        offset += amount
    return (
        pieces[0],
        pieces[1],
        pieces[2].reshape(CONV, width),
        pieces[3],
        pieces[4],
        pieces[5],
        pieces[6],
    )


def rms_norm(value, gain):
    return value * lax.rsqrt(jnp.mean(value * value, axis=-1, keepdims=True) + EPS_NORM) * gain


def segment_ids(lengths, positions):
    ends = jnp.cumsum(lengths, axis=-1, dtype=jnp.int32)
    return jnp.sum(
        (ends[:, None, :] <= positions[None, :, None]).astype(jnp.int32), axis=-1, dtype=jnp.int32
    )


def convolve(padded, seg_ext, conv_w, conv_b):
    count = padded.shape[-2] - (CONV - 1)
    seg_here = seg_ext[..., CONV - 1 :]
    summed = conv_b + jnp.zeros(padded.shape[:-2] + (count, padded.shape[-1]), jnp.float32)
    for tap in range(CONV):
        agree = (seg_ext[..., tap : tap + count] == seg_here).astype(jnp.float32)
        summed = summed + conv_w[tap] * padded[..., tap : tap + count, :] * agree[..., None]
    return jax.nn.silu(summed)


def block_masks(seg, starts):
    order = jnp.arange(seg.shape[-1], dtype=jnp.int32)
    lower = order[:, None] >= order[None, :]
    agree = (lower & (seg[..., :, None] == seg[..., None, :])).astype(jnp.float32)
    keeping = (jnp.cumsum(starts, axis=-1, dtype=jnp.int32) == 0).astype(jnp.float32)
    same_last = (seg == seg[..., -1:]).astype(jnp.float32)
    return (agree, keeping, same_last)


def front_part(seg_ext):

    def front_apply(previous, xbc, dt_raw, conv_w, conv_b, dt_bias, a_log):
        inner = HEADS * HEAD_DIM
        padded = jnp.concatenate([previous, xbc], axis=1)
        active = convolve(padded, seg_ext, conv_w, conv_b)
        values = active[..., :inner].reshape(xbc.shape[0], xbc.shape[1], HEADS, HEAD_DIM)
        b_proj = active[..., inner : inner + STATE]
        c_proj = active[..., inner + STATE :]
        delta = jax.nn.softplus(dt_raw + dt_bias)
        log_decay = -delta * jnp.exp(a_log)
        return (values, b_proj, c_proj, delta, log_decay)

    return front_apply


def summary_part(keeping, same_last):

    def summary_apply(values, b_proj, delta, log_decay):
        cumulative = jnp.cumsum(log_decay, axis=1)
        final = cumulative[:, -1]
        tails = jnp.exp(final[:, None, :] - cumulative) * same_last[:, :, None] * delta
        summed = jnp.einsum("suh,suhp,sun->shpn", tails, values, b_proj, precision=HIGH)
        return (jnp.exp(final) * keeping[:, -1:], summed)

    return summary_apply


def output_part(agree, keeping):

    def output_apply(values, b_proj, c_proj, delta, log_decay, d_skip, carried):
        cumulative = jnp.cumsum(log_decay, axis=1)
        spacing = cumulative[:, :, None, :] - cumulative[:, None, :, :]
        masked = agree[..., None]
        decays = jnp.exp(jnp.where(masked > 0, spacing, 0.0)) * masked
        scores = jnp.einsum("stn,sun->stu", c_proj, b_proj, precision=HIGH)
        weights = decays * scores[..., None] * delta[:, None, :, :]
        result = jnp.einsum("stuh,suhp->sthp", weights, values, precision=HIGH)
        inflow = jnp.exp(cumulative) * keeping[..., None]
        result = (
            result
            + jnp.einsum("stn,shpn->sthp", c_proj, carried, precision=HIGH) * inflow[..., None]
        )
        return result + d_skip[:, None] * values

    return output_apply


def gate_part(mixer_out, gate_in, g_inner):
    flat = mixer_out.reshape(gate_in.shape) * jax.nn.silu(gate_in)
    return rms_norm(flat, g_inner)


def chain_combine(earlier, later):
    return (earlier[0] * later[0], earlier[1] * later[0][..., None, None] + later[1])


def adam_update(weight, moment_one, moment_two, gradient, rate, decay_rate):
    new_first = BETA_ONE * moment_one + (1 - BETA_ONE) * gradient
    new_second = BETA_TWO * moment_two + (1 - BETA_TWO) * gradient * gradient
    corrected = (
        new_first / (1 - BETA_ONE**STEP) / (jnp.sqrt(new_second / (1 - BETA_TWO**STEP)) + ADAM_EPS)
    )
    new_weight = weight - rate * (corrected + decay_rate * weight)
    return (new_first, new_second, new_weight)


def positions_plan(
    hidden_in,
    out_grad,
    lengths,
    in_proj,
    in_first,
    in_second,
    out_proj,
    out_first,
    out_second,
    vector,
    vector_first,
    vector_second,
):
    g_norm, g_inner, conv_w, conv_b, dt_bias, a_log, d_skip = split_vector(vector)
    inner = HEADS * HEAD_DIM
    width = inner + 2 * STATE
    count = hidden_in.shape[1]
    upstream = hidden_in.astype(jnp.float32)
    normed, norm_back = jax.vjp(rms_norm, upstream, g_norm)
    normed_low = normed.astype(jnp.bfloat16)
    in_full, out_full = (
        lax.all_gather(in_proj.astype(jnp.bfloat16), ("seq", "fsdp"), axis=0, tiled=True),
        lax.all_gather(out_proj.astype(jnp.bfloat16), ("seq", "fsdp"), axis=0, tiled=True),
    )
    projected = jnp.einsum("std,dk->stk", normed_low, in_full, preferred_element_type=jnp.float32)
    gate_in = projected[..., :inner]
    xbc = projected[..., inner : inner + width]
    dt_raw = projected[..., inner + width :]
    previous = passed_along(xbc[:, count - (CONV - 1) :].astype(jnp.bfloat16), "seq", 1).astype(
        jnp.float32
    )
    offset_base = lax.axis_index("seq") * count
    positions = offset_base - (CONV - 1) + jnp.arange(count + CONV - 1, dtype=jnp.int32)
    seg_ext = segment_ids(lengths, positions)
    seg_here = seg_ext[:, CONV - 1 :]
    starts = ((seg_here != seg_ext[:, CONV - 2 : -1]) | (positions[None, CONV - 1 :] == 0)).astype(
        jnp.int32
    )
    agree, keeping, same_last = block_masks(seg_here, starts)
    front_pieces, front_back = jax.vjp(
        front_part(seg_ext), previous, xbc, dt_raw, conv_w, conv_b, dt_bias, a_log
    )
    values, b_proj, c_proj, delta, log_decay = front_pieces
    block_pair, summary_back = jax.vjp(
        summary_part(keeping, same_last), values, b_proj, delta, log_decay
    )
    ones_init = jnp.ones_like(block_pair[0])
    zeros_init = jnp.zeros_like(block_pair[1])
    carried = entering(block_pair, "seq", chain_combine, (ones_init, zeros_init), False)[1]
    mixer_out, output_back = jax.vjp(
        output_part(agree, keeping), values, b_proj, c_proj, delta, log_decay, d_skip, carried
    )
    gated, gate_back = jax.vjp(gate_part, mixer_out, gate_in, g_inner)
    gated_low = gated.astype(jnp.bfloat16)
    branch = jnp.einsum("stc,cd->std", gated_low, out_full, preferred_element_type=jnp.float32)
    mixed = (upstream + branch).astype(jnp.bfloat16)
    in_again, out_again = (
        lax.all_gather(in_proj.astype(jnp.bfloat16), ("seq", "fsdp"), axis=0, tiled=True),
        lax.all_gather(out_proj.astype(jnp.bfloat16), ("seq", "fsdp"), axis=0, tiled=True),
    )
    grad_out_proj = jnp.einsum(
        "stc,std->cd", gated_low, out_grad, preferred_element_type=jnp.float32
    )
    grad_gated = jnp.einsum("std,cd->stc", out_grad, out_again, preferred_element_type=jnp.float32)
    grad_mixer, grad_gate_in, grad_g_inner = gate_back(grad_gated)
    grad_values, grad_b, grad_c, grad_delta, grad_log, grad_skip, grad_carried = output_back(
        grad_mixer
    )
    grad_final = entering(
        (block_pair[0], grad_carried), "seq", chain_combine, (ones_init, zeros_init), True
    )[1]
    grad_decay_total = jnp.sum(grad_final * carried, axis=(2, 3))
    more_values, more_b, more_delta, more_log = summary_back((grad_decay_total, grad_final))
    grad_front = (
        grad_values + more_values,
        grad_b + more_b,
        grad_c,
        grad_delta + more_delta,
        grad_log + more_log,
    )
    grad_previous, grad_xbc, grad_dt_raw, grad_conv_w, grad_conv_b, grad_dt_bias, grad_a_log = (
        front_back(grad_front)
    )
    returned = passed_along(as_sent(grad_previous), "seq", -1).astype(grad_previous.dtype)
    grad_xbc = jnp.concatenate(
        [grad_xbc[:, : count - (CONV - 1)], grad_xbc[:, count - (CONV - 1) :] + returned], axis=1
    )
    grad_projected = jnp.concatenate([grad_gate_in, grad_xbc, grad_dt_raw], axis=-1).astype(
        jnp.bfloat16
    )
    grad_in_proj = jnp.einsum(
        "std,stk->dk", normed_low, grad_projected, preferred_element_type=jnp.float32
    )
    grad_normed = jnp.einsum(
        "stk,dk->std", grad_projected, in_again, preferred_element_type=jnp.float32
    )
    grad_upstream, grad_g_norm = norm_back(grad_normed)
    input_grad = out_grad.astype(jnp.float32) + grad_upstream
    in_summed, out_summed = (
        lax.psum_scatter(grad_in_proj, ("seq", "fsdp"), scatter_dimension=0, tiled=True),
        lax.psum_scatter(grad_out_proj, ("seq", "fsdp"), scatter_dimension=0, tiled=True),
    )
    local_vector = jnp.concatenate(
        [
            grad_g_norm,
            grad_g_inner,
            grad_conv_w.reshape(-1),
            grad_conv_b,
            grad_dt_bias,
            grad_a_log,
            grad_skip,
        ]
    )
    vector_summed = lax.psum(local_vector, ("seq", "fsdp"))
    in_new = adam_update(in_proj, in_first, in_second, in_summed, RATE_MATRIX, DECAY_MATRIX)
    out_new = adam_update(out_proj, out_first, out_second, out_summed, RATE_MATRIX, DECAY_MATRIX)
    vec_new = adam_update(vector, vector_first, vector_second, vector_summed, RATE_VECTOR, 0.0)
    return (
        mixed,
        input_grad,
        in_new[0],
        in_new[1],
        in_new[2],
        out_new[0],
        out_new[1],
        out_new[2],
        vec_new[0],
        vec_new[1],
        vec_new[2],
    )


Q = 128
LANES = 128
CHANNELS = HEADS * HEAD_DIM
WIDTH = CHANNELS + 2 * STATE
BF16 = jnp.bfloat16
F32 = jnp.float32


def mul(a, b, dims=((1,), (0,))):
    return lax.dot_general(a, b, (dims, ((), ())), preferred_element_type=F32)


def halves(x):
    high = x.astype(BF16)
    return high, (x - high.astype(F32)).astype(BF16)


def wide(mask, copies):
    return jnp.concatenate([mask] * copies, axis=1)


def head_map(channels):
    head = lax.broadcasted_iota(jnp.int32, (LANES, channels), 0)
    owner = lax.broadcasted_iota(jnp.int32, (LANES, channels), 1) // HEAD_DIM
    return (head == owner).astype(BF16)


def spread(parts, channels):
    stacked = jnp.concatenate([jnp.concatenate(halves(x), axis=1) for x in parts], axis=0)
    one = head_map(channels)
    out = mul(stacked, jnp.concatenate([one, one], axis=0))
    rows = parts[0].shape[0]
    return [out[i * rows : (i + 1) * rows] for i in range(len(parts))]


def gather_heads(parts, channels):
    stacked = jnp.concatenate([jnp.concatenate(halves(x), axis=1) for x in parts], axis=0)
    one = head_map(channels)
    out = mul(stacked, jnp.concatenate([one, one], axis=1), ((1,), (1,)))
    rows = parts[0].shape[0]
    return [out[i * rows : (i + 1) * rows] for i in range(len(parts))]


def running_sum(x, backward):
    t = lax.broadcasted_iota(jnp.int32, (Q, Q), 0)
    u = lax.broadcasted_iota(jnp.int32, (Q, Q), 1)
    tri = ((t <= u) if backward else (t >= u)).astype(BF16)
    return mul(jnp.concatenate([tri, tri], axis=1), jnp.concatenate(halves(x), axis=0))


def segments(ends, stream, positions):
    seg = jnp.zeros(positions.shape, jnp.int32)
    for k in range(ends.shape[1]):
        seg = seg + (ends[stream, k] <= positions).astype(jnp.int32)
    return jnp.where(positions < 0, -1, seg)


def chunk_front(p_ref, par_ref, ends, stream, chunk):
    local = p_ref.shape[2] - 2 * STATE - LANES
    channels = local // 2
    mixed = channels + 2 * STATE
    base = pl.multiple_of(chunk * Q, Q)
    before = pl.multiple_of(jnp.maximum(base - 8, 0), 8)
    xbc = p_ref[stream, pl.ds(base, Q), channels : channels + mixed]
    halo = p_ref[stream, pl.ds(before, 8), channels : channels + mixed]
    both = jnp.concatenate([halo, xbc], axis=0)
    column = lax.broadcasted_iota(jnp.int32, (Q + 16, LANES), 0) + (base - 8)
    seg = segments(ends, stream, column)
    here = seg[8 : Q + 8]
    tiles = mixed // LANES
    pre = par_ref[4:5, :mixed] + par_ref[3:4, :mixed] * xbc
    taps = []
    for k in range(CONV - 1):
        agree = (seg[5 + k : Q + 5 + k] == here).astype(F32)
        tap = both[5 + k : Q + 5 + k] * wide(agree, tiles)
        taps.append(tap)
        pre = pre + par_ref[k : k + 1, :mixed] * tap
    taps.append(xbc)
    gate = jax.nn.sigmoid(pre)
    active = pre * gate
    values = active[:, :channels]
    b_proj = active[:, channels : channels + STATE]
    c_proj = active[:, channels + STATE :]
    raw = p_ref[stream, pl.ds(base, Q), local + 2 * STATE :] + par_ref[7:8, :LANES]
    delta = jnp.maximum(raw, 0.0) + jnp.log1p(jnp.exp(-jnp.abs(raw)))
    rate = jnp.exp(par_ref[8:9, :LANES])
    log_decay = -delta * rate
    cumulative = running_sum(log_decay, False)
    last = cumulative[Q - 1 : Q]
    keep = (here == seg[7:8]).astype(F32)
    same_last = (here == seg[Q + 7 : Q + 8]).astype(F32)
    inflow = jnp.exp(cumulative) * keep
    tail = jnp.exp(last - cumulative) * same_last
    delta_wide, inflow_wide, tail_wide = spread([delta, inflow, tail], channels)
    row = lax.broadcasted_iota(jnp.int32, (8, LANES), 1) + base
    seg_row = segments(ends, stream, row)[0:1]
    t = lax.broadcasted_iota(jnp.int32, (Q, Q), 0)
    u = lax.broadcasted_iota(jnp.int32, (Q, Q), 1)
    mask = (t >= u) & (here == seg_row)
    turned = cumulative.T

    def decays(head):
        spacing = cumulative[:, head : head + 1] - turned[head : head + 1, :]
        return jnp.exp(jnp.where(mask, spacing, -1e30))

    return dict(
        base=base,
        seg=seg,
        pre=pre,
        gate=gate,
        taps=taps,
        values=values,
        b_low=b_proj.astype(BF16),
        c_low=c_proj.astype(BF16),
        raw=raw,
        delta=delta,
        rate=rate,
        log_decay=log_decay,
        delta_wide=delta_wide,
        inflow_wide=inflow_wide,
        tail_wide=tail_wide,
        scaled=values * delta_wide,
        decays=decays,
        channels=channels,
    )


def two_heads(pair):
    left = lax.broadcasted_iota(jnp.int32, pair.shape, 1) < HEAD_DIM
    low = pair.astype(BF16)
    zero = jnp.zeros_like(low)
    return jnp.concatenate([jnp.where(left, low, zero), jnp.where(left, zero, low)], axis=0)


def chunk_forward(front, state, skip):
    channels = front["channels"]
    scores = mul(front["c_low"], front["b_low"], ((1,), (1,)))
    pieces = []
    for pair in range(channels // LANES):
        weights = jnp.concatenate(
            [(front["decays"](2 * pair + i) * scores).astype(BF16) for i in range(2)], axis=1
        )
        scaled = front["scaled"][:, pair * LANES : (pair + 1) * LANES]
        pieces.append(mul(weights, two_heads(scaled)))
    result = jnp.concatenate(pieces, axis=1)
    result = result + mul(front["c_low"], state.astype(BF16)) * front["inflow_wide"]
    result = result + skip * front["values"]
    fed = (front["scaled"] * front["tail_wide"]).astype(BF16)
    after = front["inflow_wide"][Q - 1 : Q] * state + mul(front["b_low"], fed, ((0,), (0,)))
    return result, after


def chunk_backward(front, before, after, grad_after, result, grad, skip):
    channels = front["channels"]
    b_low, c_low = front["b_low"], front["c_low"]
    scaled, values = front["scaled"], front["values"]
    scores = mul(c_low, b_low, ((1,), (1,)))
    grad_scores = jnp.zeros((Q, Q), F32)
    pieces = []
    for pair in range(channels // LANES):
        lanes = slice(pair * LANES, (pair + 1) * LANES)
        decays = [front["decays"](2 * pair + i) for i in range(2)]
        weights = jnp.concatenate([(d * scores).astype(BF16) for d in decays], axis=0)
        split = two_heads(grad[:, lanes])
        pieces.append(mul(weights, split, ((0,), (0,))))
        cross = mul(split, scaled[:, lanes].astype(BF16), ((1,), (1,)))
        grad_scores = grad_scores + decays[0] * cross[:Q] + decays[1] * cross[Q:]
    grad_after_low = grad_after.astype(BF16)
    inner = jnp.concatenate(pieces, axis=1) + mul(b_low, grad_after_low) * front["tail_wide"]
    fed = (scaled * front["tail_wide"]).astype(BF16)
    flowing = (grad * front["inflow_wide"]).astype(BF16)
    low_scores = grad_scores.astype(BF16)
    grad_c = mul(low_scores, b_low) + mul(flowing, before.astype(BF16), ((1,), (1,)))
    grad_b = mul(low_scores, c_low, ((0,), (0,))) + mul(fed, grad_after_low, ((1,), (1,)))
    grad_values = skip * grad + front["delta_wide"] * inner
    grad_skip = jnp.sum(grad * values, axis=0, keepdims=True)
    held = jnp.sum(after * grad_after, axis=0, keepdims=True)
    grad_delta, grad_cumulative = gather_heads(
        [values * inner, grad * (result - skip * values) - scaled * inner], channels
    )
    held_heads = gather_heads([jnp.broadcast_to(held, (8, channels))], channels)[0][0:1]
    grad_log = running_sum(grad_cumulative, True) + held_heads
    grad_delta = grad_delta - front["rate"] * grad_log
    grad_raw = grad_delta * jax.nn.sigmoid(front["raw"])
    grad_rate = jnp.sum(grad_log * front["log_decay"], axis=0, keepdims=True)
    grad_before = front["inflow_wide"][Q - 1 : Q] * grad_after + mul(c_low, flowing, ((0,), (0,)))
    return grad_values, grad_b, grad_c, grad_raw, grad_rate, grad_skip, grad_before


def conv_backward(front, grad_active, next_grad, par_ref):
    gate, pre, seg = front["gate"], front["pre"], front["seg"]
    mixed = pre.shape[1]
    tiles = mixed // LANES
    grad_pre = grad_active * (gate * (1.0 + pre * (1.0 - gate)))
    rows = [jnp.sum(grad_pre * front["taps"][k], axis=0, keepdims=True) for k in range(CONV)]
    rows.append(jnp.sum(grad_pre, axis=0, keepdims=True))
    both = jnp.concatenate([grad_pre, next_grad], axis=0)
    grad_x = par_ref[CONV - 1 : CONV, :mixed] * grad_pre
    for k in range(CONV - 1):
        ahead = CONV - 1 - k
        agree = (seg[8 + ahead : Q + 8 + ahead] == seg[8 : Q + 8]).astype(F32)
        grad_x = grad_x + par_ref[k : k + 1, :mixed] * both[ahead : Q + ahead] * wide(agree, tiles)
    return grad_x, grad_pre[:8], rows


MESH = pl.DeviceIdType.MESH
TILE = 512


class Links:
    def __init__(self, send, recv):
        self.send, self.recv, self.used = send, recv, 0

    def copy(self, source, target, device):
        slot = self.used
        self.used += 1
        return pltpu.make_async_remote_copy(
            src_ref=source,
            dst_ref=target,
            send_sem=self.send.at[slot],
            recv_sem=self.recv.at[slot],
            device_id=device,
            device_id_type=MESH,
        )


class Place:
    def __init__(self, depth):
        self.s = lax.axis_index("seq")
        self.f = lax.axis_index("fsdp")
        self.depth = depth
        self.core = lax.rem(self.s, 2)
        x = lax.rem(self.s // 2, 2)
        y = self.s // 4
        self.steps = (1 - 2 * self.core, 2 - 4 * x, 4 - 8 * y)

    def peer(self, k):
        index = self.s
        for bit in range(3):
            if k >> bit & 1:
                index = index + self.steps[bit]
        return index

    def at(self, k):
        return (self.peer(k), self.f)

    def plane(self, d):
        return lax.rem(self.f + d, self.depth)

    def beyond(self, d):
        return (self.s, self.plane(d))

    def greet(self):
        barrier = pltpu.get_barrier_semaphore()
        others = [self.at(k) for k in range(1, 8)] + [self.beyond(d) for d in range(1, self.depth)]
        for other in others:
            pl.semaphore_signal(barrier, inc=1, device_id=other, device_id_type=MESH)
        pl.semaphore_wait(barrier, len(others))


def ahead(start, size):
    return pl.ds(pl.multiple_of(start, size), size)


def gather_kernel(
    depth,
    ends,
    hidden,
    out_grad,
    in_proj,
    out_proj,
    gain,
    par_ref,
    x_out,
    g_out,
    w_out,
    o_out,
    p_out,
    y_out,
    h_out,
    gg_out,
    moments_out,
    x,
    g,
    wm,
    wc,
    wo,
    p,
    y,
    h,
    gg,
    state,
    packed,
    common,
    moments,
    send,
    recv,
    leave,
):
    streams, block = hidden.shape[0], hidden.shape[1]
    length = x.shape[1]
    rows = in_proj.shape[0]
    lines = out_proj.shape[0]
    channels = wo.shape[0]
    slab = depth * rows
    here = Place(depth)
    s, f = here.s, here.f
    links = Links(send, recv)
    exits = []

    def leaving(source, target):
        copy = pltpu.make_async_copy(source, target, leave.at[len(exits)])
        copy.start()
        exits.append(copy)

    for k in range(CHANNELS // channels):
        lanes = slice(k * channels, (k + 1) * channels)
        packed[k, :, :channels] = in_proj[:, lanes].astype(BF16)
        lanes = slice(CHANNELS + k * channels, CHANNELS + (k + 1) * channels)
        packed[k, :, channels:] = in_proj[:, lanes].astype(BF16)
    narrow = 2 * STATE + HEADS
    common[:, narrow:] = jnp.zeros((rows, common.shape[1] - narrow), BF16)
    common[:, :narrow] = in_proj[:, 2 * CHANNELS :].astype(BF16)

    def slab_rows(source, plane):
        return ahead((source * depth + plane) * rows, rows)

    def block_rows(source):
        return ahead(source * block, block)

    here.greet()
    finish = []

    def started(copy):
        copy.start()
        finish.append(copy)
        return copy

    order = (0, 1, 2, 4, 3, 5, 6, 7)
    own = slab_rows(s, f)
    turned = [None]
    for k in order[1:]:
        turned.append(started(links.copy(packed.at[here.peer(k)], wm.at[own], here.at(k))))
    turned = dict(zip(order, turned))
    shared = [started(links.copy(common, wc.at[own], here.beyond(d))) for d in range(1, depth)]
    wc[own] = common[...]
    wm[own] = packed[s]

    upstream = hidden[...].astype(F32)
    mean = jnp.mean(upstream * upstream, axis=-1, keepdims=True)
    x[:, block_rows(s)] = (upstream * lax.rsqrt(mean + EPS_NORM) * gain[...]).astype(BF16)
    mine = x.at[:, block_rows(s)]
    near = [started(links.copy(mine, mine, here.at(k))) for k in (2, 4)]
    beside = [started(links.copy(mine, mine, here.at(1)))]
    g[:, block_rows(s)] = out_grad[...]
    wo[ahead(f * lines, lines)] = out_proj[...].astype(BF16)

    def hop(k, d, up):
        plane = f - d if up else f + d
        target = wm.at[slab_rows(here.peer(k), plane)]
        return links.copy(target, target, (s, f + 1 if up else f - 1))

    hops = {}
    for k in range(8):
        for d in range(depth - 1):
            hops[k, d] = (hop(k, d, True), hop(k, d, False))

    def sends(d):
        return ((f >= d) & (f < depth - 1), (f <= depth - 1 - d) & (f > 0))

    def gets(d):
        return (f >= d + 1, f <= depth - 2 - d)

    def launch(k, d):
        for way in range(2):
            pl.when(sends(d)[way])(hops[k, d][way].start)

    def arrive(k, d):
        for way in range(2):
            pl.when(gets(d)[way])(hops[k, d][way].wait_recv)

    def project(j):
        q = here.peer(2 * j) // 2
        span = ahead(q * 2 * slab, 2 * slab)

        def tile(i, carry):
            stream = i // (length // TILE)
            at = ahead(lax.rem(i, length // TILE) * TILE, TILE)
            left = x[stream, at, span]
            for part, weights in ((slice(0, 2 * channels), wm), (slice(2 * channels, None), wc)):
                product = mul(left, weights[span, :])
                if j == 0:
                    p[stream, at, part] = product
                else:
                    p[stream, at, part] += product
            return carry

        lax.fori_loop(0, streams * (length // TILE), tile, 0)

    def token_block(ref, k):
        return ref.at[:, block_rows(here.peer(k))]

    def token_half(ref, way, k):
        return ref.at[way, block_rows(here.peer(k))]

    def crossing(ref, way):
        half = token_half(ref, way, 2 << way)
        return links.copy(half, half, here.at(4 >> way))

    def beside_copy(part):
        return links.copy(part, part, here.at(1))

    for k in order:
        if turned[k] is not None:
            turned[k].wait_recv()
        launch(k, 0)
    for copy in shared:
        copy.wait_recv()
    group = wc.at[ahead(s * slab, slab)]
    spread_common = [links.copy(group, group, here.at(k)) for k in (2, 4, 6, 1)]
    for copy in spread_common:
        copy.start()
    last = depth - 1
    for d in range(1, last):
        if d == last - 1:
            across = []
            for way in range(2):
                near[way].wait_recv()
                across.append(started(crossing(x, way)))
                beside.append(started(beside_copy(token_block(x, 2 << way))))
            mine_g = token_block(g, 0)
            near_g = [started(links.copy(mine_g, mine_g, here.at(k))) for k in (2, 4)]
            beside_g = [started(beside_copy(mine_g))]
        for k in order:
            arrive(k, d - 1)
            launch(k, d)
    lent = wo.at[ahead(f * lines, lines)]
    outs = [started(links.copy(lent, lent, here.beyond(d))) for d in range(1, depth)]
    for copy in spread_common[:3]:
        copy.wait_recv()
    for k in (2, 4, 6):
        group = wc.at[ahead(here.peer(k) * slab, slab)]
        spread_common.append(links.copy(group, group, here.at(1)))
        spread_common[-1].start()
    for way in range(2):
        across[way].wait_recv()
        beside.append(started(beside_copy(token_half(x, way, 6))))
    for copy in spread_common[3:]:
        copy.wait_recv()
    for copy in spread_common:
        copy.wait_send()
    column = lax.broadcasted_iota(jnp.int32, (LANES, LANES), 0)
    wanted = lax.broadcasted_iota(jnp.int32, (LANES, LANES), 1)
    share = channels // HEAD_DIM
    pick = ((column == wanted + s * share) & (wanted < share)).astype(BF16)
    for part in range(0, wc.shape[0], TILE):
        steps = wc[part : part + TILE, 2 * STATE :]
        wc[part : part + TILE, 2 * STATE :] = mul(steps, pick).astype(BF16)
    for copy in beside:
        copy.wait_recv()
    leaving(x, x_out)
    for j in range(4):
        for k in (2 * j, 2 * j + 1):
            arrive(k, last - 1)
        project(j)
    across_g = [crossing(g, way) for way in range(2)]
    near_beside_g = [beside_copy(token_block(g, 2 << way)) for way in range(2)]
    finish += across_g + near_beside_g
    leaving(p, p_out)
    leaving(wm, w_out.at[:, : 2 * channels])
    leaving(wc, w_out.at[:, 2 * channels :])

    skip = par_ref[6:7, :channels]
    state[...] = jnp.zeros_like(state)

    def step(chunk, carry):
        for stream in range(streams):
            front = chunk_front(p, par_ref, ends, stream, chunk)
            before = state[stream]
            h[stream, chunk] = before.astype(BF16)
            result, after = chunk_forward(front, before, skip)
            y[stream, pl.ds(front["base"], Q)] = result
            state[stream] = after

        @pl.when(chunk == 5 * (length // Q) // 8)
        def _():
            for way in range(2):
                near_g[way].wait_recv()
                across_g[way].start()
                near_beside_g[way].start()

        return carry

    lax.fori_loop(0, length // Q, step, 0)
    leaving(y, y_out)
    leaving(h, h_out)

    for way in range(2):
        across_g[way].wait_recv()
        beside_g.append(started(beside_copy(token_half(g, way, 6))))
    for copy in outs:
        copy.wait_recv()
    for copy in beside_g + near_beside_g:
        copy.wait_recv()
    leaving(g, g_out)
    leaving(wo, o_out)

    g_inner = par_ref[5:6, :channels]
    ones = jnp.ones((8, 2 * channels), BF16)
    tiles = length // TILE
    pieces = TILE // Q
    half = streams * length // Q

    def weigh(i, carry):
        stream = i // tiles
        at = ahead(lax.rem(i, tiles) * TILE, TILE)
        grad = mul(g[stream, at], wo[...], ((1,), (1,)))
        gg[stream, at] = grad.astype(BF16)
        gate_in = p[stream, at, :channels]
        flat = y[stream, at] * (gate_in * jax.nn.sigmoid(gate_in))
        for which, product in enumerate((flat * flat, grad * g_inner * flat)):
            sums = mul(ones, jnp.concatenate(halves(product), axis=1), ((1,), (1,)))
            for j in range(pieces):
                at_row = which * half + i * pieces + j
                moments[s, pl.ds(at_row, 1), :] = sums[0:1, j * Q : (j + 1) * Q]
        return carry

    lax.fori_loop(0, streams * tiles, weigh, 0)
    leaving(gg, gg_out)
    mine_m = moments.at[s]
    told = [started(links.copy(mine_m, mine_m, here.at(k))) for k in range(1, 8)]
    for copy in told:
        copy.wait_recv()
    moments_out[...] = jnp.sum(moments[...], axis=0)

    for copy in finish:
        copy.wait_send()
    for k in range(8):
        for d in range(depth - 1):
            for way in range(2):
                pl.when(sends(d)[way])(hops[k, d][way].wait_send)
    for copy in exits:
        copy.wait()


LINE = 512
GROUP = 384


class Summing:
    def __init__(self, here, links, slots, beside, halves_in, final_in, own):
        self.here, self.slots, self.beside = here, slots, beside
        self.halves_in, self.final_in, self.own = halves_in, final_in, own
        make = links.copy
        self.to_beside = [make(slots.at[r], beside.at[r], here.at(1)) for r in range(4)]
        self.by = [make(slots.at[3, i], halves_in.at[i], here.at(2 << i)) for i in range(2)]
        self.last = [make(slots.at[1 + i], final_in.at[i], here.at(2 << i)) for i in range(2)]

    def owner(self, r, other):
        return self.here.peer(2 * r + (1 if other else 0))

    def give_beside(self, r, value):
        self.slots[r] = value.astype(BF16)
        self.to_beside[r].start()

    def joined(self, r, value):
        self.to_beside[r].wait()
        return value + self.beside[r].astype(F32)

    def diagonal(self, value):
        self.slots[3] = self.joined(3, value).astype(BF16)
        for copy in self.by:
            copy.start()

    def neighbour(self, i, value):
        value = self.joined(1 + i, value)
        other = 1 - i
        self.by[other].wait_recv()
        self.slots[1 + i, i] = value[i].astype(BF16)
        self.slots[1 + i, other] = (value[other] + self.halves_in[other].astype(F32)).astype(BF16)
        self.last[i].start()

    def keep(self, value):
        self.own[...] = self.joined(0, value).astype(self.own.dtype)

    def total(self):
        for copy in self.last:
            copy.wait_recv()
        return self.own[...].astype(F32) + self.final_in[0].astype(F32) + self.final_in[1].astype(F32)

    def settle(self):
        for copy in self.by + self.last:
            copy.wait_send()


def adjoint_kernel(
    depth,
    ends,
    hidden,
    out_grad,
    gain,
    par_ref,
    moments,
    x_in,
    g_in,
    w_in,
    o_in,
    p_in,
    y_in,
    h_in,
    gg_in,
    mixed_out,
    upstream_out,
    main_out,
    common_out,
    lines_out,
    vector_out,
    tokens,
    w,
    wo,
    p,
    y,
    h,
    gg,
    dp,
    state,
    later,
    sums,
    slots,
    beside,
    mixed_halves,
    mixed_last,
    grad_halves,
    grad_last,
    lines,
    lines_recv,
    main,
    main_recv,
    slabs,
    slabs_recv,
    common,
    common_beside,
    common_recv,
    common_line,
    common_last,
    gain_sums,
    vector_line,
    vector_all,
    send,
    recv,
    enter,
    credit,
):
    streams, block = hidden.shape[0], hidden.shape[1]
    length = p.shape[1]
    chunks = length // Q
    channels = y.shape[2]
    mixed = channels + 2 * STATE
    rows = main.shape[3]
    out_rows = lines_out.shape[0]
    slab = depth * rows
    here = Place(depth)
    s, f = here.s, here.f
    links = Links(send, recv)

    entries = []

    def entering_copy(source, target):
        copy = pltpu.make_async_copy(source, target, enter.at[len(entries)])
        copy.start()
        entries.append(copy)
        return copy

    p_copy = entering_copy(p_in.at[:, :, :channels], p.at[:, :, :channels])
    y_copy = entering_copy(y_in, y)
    gg_copy = entering_copy(gg_in, gg)
    o_copy = entering_copy(o_in, wo)
    g_copy = entering_copy(g_in, tokens)
    rest_copy = entering_copy(p_in.at[:, :, channels:], p.at[:, :, channels:])
    h_copy = entering_copy(h_in, h)
    w_copy = entering_copy(w_in, w)
    here.greet()

    mixed_sum = Summing(here, links, slots, beside, mixed_halves, mixed_last, mixed_out)
    grad_sum = Summing(here, links, slots, beside, grad_halves, grad_last, upstream_out)

    skip = par_ref[6:7, :channels]
    g_inner = par_ref[5:6, :channels]
    sums[...] = jnp.zeros_like(sums)
    state[...] = jnp.zeros_like(state)
    later[...] = jnp.zeros_like(later)
    half = streams * chunks
    tiles = channels // LANES

    def column(row):
        return jnp.broadcast_to(row, (Q, Q)).T

    def norm_columns(which):
        first = moments[pl.ds(which, 1), :]
        second = moments[pl.ds(half + which, 1), :]
        scale = lax.rsqrt(first / CHANNELS + EPS_NORM)
        return column(scale), column(scale * scale * scale * second / CHANNELS)

    p_copy.wait()
    y_copy.wait()
    gg_copy.wait()

    def gate_step(i, carry):
        stream = i // chunks
        at = ahead(lax.rem(i, chunks) * Q, Q)
        scale, pull = norm_columns(i)
        scale, pull = wide(scale, tiles), wide(pull, tiles)
        gate_in = p[stream, at, :channels]
        result = y[stream, at]
        sig = jax.nn.sigmoid(gate_in)
        silu = gate_in * sig
        flat = result * silu
        scaled = flat * scale
        grad = gg[stream, at].astype(F32)
        dp[stream, at, 2 * channels :] = (scaled * g_inner).astype(BF16)
        grad_flat = scale * g_inner * grad - flat * pull
        p[stream, at, :channels] = grad_flat * silu
        grad_gate = grad_flat * result * (sig * (1.0 + gate_in * (1.0 - sig)))
        dp[stream, at, :channels] = grad_gate.astype(BF16)
        sums[5:6, :channels] += jnp.sum(grad * scaled, axis=0, keepdims=True)
        return carry

    lax.fori_loop(0, half, gate_step, 0)
    o_copy.wait()

    def rows_of(ref, owner, lanes):
        at = ahead(owner * block, block)
        return jnp.concatenate([ref[k, at, lanes] for k in range(streams)], axis=0)

    def branch(r, other):
        low = rows_of(dp, mixed_sum.owner(r, other), slice(2 * channels, 3 * channels))
        return mul(low, wo[...]).reshape(streams, block, D)

    for r in (3, 1, 2, 0):
        mixed_sum.give_beside(r, branch(r, True))
    mixed_sum.diagonal(branch(3, False))

    g_copy.wait()

    def line_step(j, carry):
        lanes = ahead(j * LINE, LINE)
        total = jnp.zeros((channels, LINE), F32)
        for k in range(streams):
            total = total + mul(dp[k, :, 2 * channels :], tokens[k, :, lanes], ((0,), (0,)))
        lines[:, lanes] = total.astype(BF16)
        return carry

    lax.fori_loop(0, D // LINE, line_step, 0)
    x_copy = entering_copy(x_in, tokens)
    line_sends = []
    for d in range(1, depth):
        theirs = lines.at[ahead(here.plane(d) * out_rows, out_rows)]
        line_sends.append(links.copy(theirs, lines_recv.at[d - 1], here.beyond(d)))
        line_sends[-1].start()
    for i in range(2):
        mixed_sum.neighbour(i, branch(1 + i, False))
    mixed_sum.keep(branch(0, False))
    pl.semaphore_signal(credit, inc=1, device_id=here.at(1), device_id_type=MESH)

    def gradient_rows(j, lanes):
        wanted = ahead(j * GROUP, GROUP)
        total = jnp.zeros((GROUP, channels), F32)
        for k in range(streams):
            total = total + mul(tokens[k, :, wanted], dp[k, :, lanes], ((0,), (0,)))
        product = total * w[wanted, lanes].astype(F32)
        folded = product[:, :LANES]
        for i in range(1, channels // LANES):
            folded = folded + product[:, i * LANES : (i + 1) * LANES]
        ones = jnp.ones((8, 2 * LANES), BF16)
        gain_sums[:, wanted] += mul(ones, jnp.concatenate(halves(folded), axis=1), ((1,), (1,)))
        return total

    gain_sums[...] = jnp.zeros_like(gain_sums)
    main_sends = [[], []]

    def main_part(part):
        lanes = slice(part * channels, (part + 1) * channels)

        def group(j, carry):
            total = gradient_rows(j, lanes).astype(BF16)
            for i in range(GROUP // rows):
                source = (GROUP // slab) * j + i // depth
                main[part, i % depth, source] = total[i * rows : (i + 1) * rows]
            return carry

        lax.fori_loop(0, D // GROUP, group, 0)
        for d in range(1, depth):
            copy = links.copy(
                main.at[part, here.plane(d)], main_recv.at[part, d - 1], here.beyond(d)
            )
            copy.start()
            main_sends[part].append(copy)

    x_copy.wait()
    w_copy.wait()
    main_part(0)
    h_copy.wait()
    rest_copy.wait()

    def step(k, carry):
        chunk = chunks - 1 - k
        for stream in range(streams):
            front = chunk_front(p, par_ref, ends, stream, chunk)
            at = pl.ds(front["base"], Q)
            grad_after = state[stream]
            before = h[stream, chunk].astype(F32)
            after = h[stream, jnp.minimum(chunk + 1, chunks - 1)].astype(F32)
            gv, gb, gc, graw, grate, gskip, gbefore = chunk_backward(
                front, before, after, grad_after, y[stream, at], p[stream, at, :channels], skip
            )
            state[stream] = gbefore
            grad_active = jnp.concatenate([gv, gb, gc], axis=1)
            grad_x, head, rows_w = conv_backward(front, grad_active, later[stream], par_ref)
            later[stream] = head
            dp[stream, at, channels : channels + mixed] = grad_x.astype(BF16)
            dp[stream, at, channels + mixed :] = graw.astype(BF16)
            for i, row in enumerate(rows_w):
                sums[i : i + 1, :] += row
            sums[6:7, :channels] += gskip
            sums[7:8, :LANES] += jnp.sum(graw, axis=0, keepdims=True)
            sums[8:9, :LANES] += grate
        return carry

    lax.fori_loop(0, chunks, step, 0)

    main_part(1)
    slab_sends = []

    def hand_over(part):
        lanes = slice(part * channels, (part + 1) * channels)
        for copy in main_sends[part]:
            copy.wait_recv()
        total = main[part, f].astype(F32)
        for d in range(1, depth):
            total = total + main_recv[part, d - 1].astype(F32)
        slabs[part] = total.astype(BF16)
        for k in range(1, 8):
            copy = links.copy(slabs.at[part, here.peer(k)], slabs_recv.at[part, s], here.at(k))
            copy.start()
            slab_sends.append(copy)
        slabs_recv[part, s] = slabs[part, s]

    def back(r, other):
        low = rows_of(dp, grad_sum.owner(r, other), slice(None))
        return mul(low, w[...], ((1,), (1,))).reshape(streams, block, D)

    mixed_sum.settle()
    pl.semaphore_wait(credit, 1)
    for r in (3, 1, 2, 0):
        grad_sum.give_beside(r, back(r, True))
    grad_sum.diagonal(back(3, False))

    column_at = lax.broadcasted_iota(jnp.int32, (LANES, LANES), 1)
    wanted_at = lax.broadcasted_iota(jnp.int32, (LANES, LANES), 0)
    share = channels // HEAD_DIM
    place = ((column_at == wanted_at + s * share) & (wanted_at < share)).astype(BF16)

    def common_group(j, carry):
        total = gradient_rows(j, slice(2 * channels, 3 * channels)).astype(BF16)
        at = ahead(j * GROUP, GROUP)
        common[at, : 2 * STATE] = total[:, : 2 * STATE]
        common[at, 2 * STATE :] = mul(total[:, 2 * STATE :], place).astype(BF16)
        return carry

    lax.fori_loop(0, D // GROUP, common_group, 0)

    def owned(k):
        return common.at[ahead(here.peer(k) * slab, slab)]

    common_sends = [
        links.copy(owned(2 * r + 1), common_beside.at[r], here.at(1)) for r in range(4)
    ]
    for copy in common_sends:
        copy.start()

    for i in range(3):
        third = D // 3
        sums[9 + i : 10 + i, :third] = gain_sums[0:1, i * third : (i + 1) * third]
    vector_line[f] = sums[...]
    told = [links.copy(sums, vector_line.at[f], here.beyond(d)) for d in range(1, depth)]
    for copy in told:
        copy.start()
    hand_over(0)

    for i in range(2):
        grad_sum.neighbour(i, back(1 + i, False))
    grad_sum.keep(back(0, False))
    for copy in common_sends:
        copy.wait_recv()
    common_across = []
    for r in (3, 1, 2, 0):
        at = ahead(here.peer(2 * r) * slab, slab)
        joined = common[at, :].astype(F32) + common_beside[r].astype(F32)
        common[at, :] = joined.astype(BF16)
        if r:
            copy = links.copy(owned(2 * r), common_recv.at[r - 1], here.at(2 * r))
            copy.start()
            common_across.append(copy)
    hand_over(1)
    for copy in told:
        copy.wait_recv()
    vector_all[s] = jnp.sum(vector_line[...], axis=0)
    mine = vector_all.at[s]
    heard = [links.copy(mine, mine, here.at(k)) for k in range(1, 8)]
    for copy in heard:
        copy.start()

    for copy in common_across:
        copy.wait_recv()
    at = ahead(s * slab, slab)
    joined = common[at, :].astype(F32)
    for r in range(3):
        joined = joined + common_recv[r].astype(F32)
    common_line[...] = joined.astype(BF16).reshape(depth, rows, common.shape[1])
    common_sends_z = []
    for d in range(1, depth):
        copy = links.copy(common_line.at[here.plane(d)], common_last.at[d - 1], here.beyond(d))
        copy.start()
        common_sends_z.append(copy)

    for copy in line_sends:
        copy.wait_recv()
    total = lines[ahead(f * out_rows, out_rows), :].astype(F32)
    for d in range(1, depth):
        total = total + lines_recv[d - 1].astype(F32)
    lines_out[...] = total
    upstream = hidden[...].astype(F32)
    branch_sum = mixed_sum.total()
    mixed_out[...] = (upstream + branch_sum).astype(BF16)
    for copy in common_sends_z:
        copy.wait_recv()
    total = common_line[f].astype(F32)
    for d in range(1, depth):
        total = total + common_last[d - 1].astype(F32)
    common_out[...] = total

    grad_normed = grad_sum.total() * gain[...]
    inverse = lax.rsqrt(jnp.mean(upstream * upstream, axis=-1, keepdims=True) + EPS_NORM)
    unit = upstream * inverse
    along = jnp.mean(grad_normed * unit, axis=-1, keepdims=True)
    upstream_out[...] = out_grad[...].astype(F32) + inverse * (grad_normed - unit * along)

    for copy in slab_sends:
        copy.wait_recv()
    main_out[...] = slabs_recv[...]
    for copy in heard:
        copy.wait_recv()
    vector_out[...] = vector_all[...]
    grad_sum.settle()
    pending = line_sends + main_sends[0] + main_sends[1] + common_sends + told + heard
    for copy in pending + common_across + slab_sends + common_sends_z:
        copy.wait_send()


def local_vector_rows(vector, index, share):
    g_norm, g_inner, conv_w, conv_b, dt_bias, a_log, d_skip = split_vector(vector)
    channels = share * HEAD_DIM
    mixed = channels + 2 * STATE

    def own(array, size):
        return lax.dynamic_slice_in_dim(array, index * size, size, axis=-1)

    def row(array):
        return jnp.pad(array, ((0, 0), (0, mixed - array.shape[1])))

    conv = jnp.concatenate([conv_w, conv_b[None]], axis=0)
    conv = jnp.concatenate([own(conv[:, :CHANNELS], channels), conv[:, CHANNELS:]], axis=1)
    skip = jnp.repeat(own(d_skip, share), HEAD_DIM)
    rows = [conv] + [
        row(part[None])
        for part in (own(g_inner, channels), skip, own(dt_bias, share), own(a_log, share))
    ]
    return jnp.pad(jnp.concatenate(rows, axis=0), ((0, 7), (0, 0)))


def call(kernel, name, out_shape, out_specs, inputs, scratch, vmem_mib, collective, hbm=0):
    specs = [pl.BlockSpec(memory_space=pltpu.SMEM)]
    specs += [pl.BlockSpec(memory_space=pltpu.VMEM)] * (len(inputs) - 1 - hbm)
    specs += [pl.BlockSpec(memory_space=pl.ANY)] * hbm
    return pl.pallas_call(
        kernel,
        out_shape=out_shape,
        in_specs=specs,
        out_specs=[pl.BlockSpec(memory_space=space) for space in out_specs],
        scratch_shapes=scratch,
        name=name,
        compiler_params=pltpu.CompilerParams(
            vmem_limit_bytes=vmem_mib << 20,
            collective_id=collective,
            has_side_effects=True,
        ),
    )(*inputs)


def heads_plan(
    hidden_in,
    out_grad,
    lengths,
    in_proj,
    in_first,
    in_second,
    out_proj,
    out_first,
    out_second,
    vector,
    vector_first,
    vector_second,
):
    count, index = lax.axis_size("seq"), lax.axis_index("seq")
    depth = lax.axis_size("fsdp")
    share = HEADS // count
    channels = share * HEAD_DIM
    mixed = channels + 2 * STATE
    streams, block = hidden_in.shape[0], hidden_in.shape[1]
    length = block * count
    chunks = length // Q
    rows = in_proj.shape[0]
    columns = mixed + channels + LANES
    g_norm = vector[:D]
    par = local_vector_rows(vector, index, share)
    ends = jnp.cumsum(lengths, axis=-1, dtype=jnp.int32)

    shape = jax.ShapeDtypeStruct
    moment_rows = 2 * streams * chunks
    normed_low, grads, weights, out_full, projected, result, states, grad_gated, moments = call(
        functools.partial(gather_kernel, depth),
        "gather_forward",
        [
            shape((streams, length, D), BF16),
            shape((streams, length, D), BF16),
            shape((D, columns), BF16),
            shape((channels, D), BF16),
            shape((streams, length, columns), F32),
            shape((streams, length, channels), F32),
            shape((streams, chunks, STATE, channels), BF16),
            shape((streams, length, channels), BF16),
            shape((moment_rows, Q), F32),
        ],
        [pl.ANY] * 8 + [pltpu.VMEM],
        (ends, hidden_in, out_grad, in_proj, out_proj, g_norm[None], par),
        [
            pltpu.VMEM((streams, length, D), BF16),
            pltpu.VMEM((streams, length, D), BF16),
            pltpu.VMEM((D, 2 * channels), BF16),
            pltpu.VMEM((D, 2 * STATE + LANES), BF16),
            pltpu.VMEM((channels, D), BF16),
            pltpu.VMEM((streams, length, columns), F32),
            pltpu.VMEM((streams, length, channels), F32),
            pltpu.VMEM((streams, chunks, STATE, channels), BF16),
            pltpu.VMEM((streams, length, channels), BF16),
            pltpu.VMEM((streams, STATE, channels), F32),
            pltpu.VMEM((count, rows, 2 * channels), BF16),
            pltpu.VMEM((rows, 2 * STATE + LANES), BF16),
            pltpu.VMEM((count, moment_rows, Q), F32),
            pltpu.SemaphoreType.DMA((128,)),
            pltpu.SemaphoreType.DMA((128,)),
            pltpu.SemaphoreType.DMA((16,)),
        ],
        56,
        collective=0,
    )
    out_rows = out_proj.shape[0]
    across = 2 * STATE + LANES
    slab = depth * rows
    dma = pltpu.SemaphoreType.DMA
    mixed_out, input_grad, main, rest, out_summed, small = call(
        functools.partial(adjoint_kernel, depth),
        "adjoint",
        [
            shape((streams, block, D), BF16),
            shape((streams, block, D), F32),
            shape((2, count, rows, channels), BF16),
            shape((rows, across), F32),
            shape((out_rows, D), F32),
            shape((count, 16, mixed), F32),
        ],
        [pltpu.VMEM] * 6,
        (ends, hidden_in, out_grad, g_norm[None], par, moments)
        + (normed_low, grads, weights, out_full, projected, result, states, grad_gated),
        [
            pltpu.VMEM((streams, length, D), BF16),
            pltpu.VMEM((D, columns), BF16),
            pltpu.VMEM((channels, D), BF16),
            pltpu.VMEM((streams, length, columns), F32),
            pltpu.VMEM((streams, length, channels), F32),
            pltpu.VMEM((streams, chunks, STATE, channels), BF16),
            pltpu.VMEM((streams, length, channels), BF16),
            pltpu.VMEM((streams, length, columns), BF16),
            pltpu.VMEM((streams, STATE, channels), F32),
            pltpu.VMEM((streams, 8, mixed), F32),
            pltpu.VMEM((16, mixed), F32),
            pltpu.VMEM((4, streams, block, D), BF16),
            pltpu.VMEM((4, streams, block, D), BF16),
        ]
        + [
            pltpu.VMEM((2, block, D), BF16),
            pltpu.VMEM((2, streams, block, D), BF16),
            pltpu.VMEM((2, block, D), BF16),
            pltpu.VMEM((2, streams, block, D), BF16),
            pltpu.VMEM((channels, D), BF16),
            pltpu.VMEM((depth - 1, out_rows, D), BF16),
            pltpu.VMEM((2, depth, count, rows, channels), BF16),
            pltpu.VMEM((2, depth - 1, count, rows, channels), BF16),
            pltpu.VMEM((2, count, rows, channels), BF16),
            pltpu.VMEM((2, count, rows, channels), BF16),
            pltpu.VMEM((D, across), BF16),
            pltpu.VMEM((4, slab, across), BF16),
            pltpu.VMEM((3, slab, across), BF16),
            pltpu.VMEM((depth, rows, across), BF16),
            pltpu.VMEM((depth - 1, rows, across), BF16),
            pltpu.VMEM((8, D), F32),
            pltpu.VMEM((depth, 16, mixed), F32),
            pltpu.VMEM((count, 16, mixed), F32),
            dma((96,)),
            dma((96,)),
            dma((16,)),
            pltpu.SemaphoreType.REGULAR,
        ],
        63,
        collective=1,
        hbm=8,
    )
    in_summed = jnp.concatenate(
        [
            main[0].transpose(1, 0, 2).reshape(rows, CHANNELS).astype(F32),
            main[1].transpose(1, 0, 2).reshape(rows, CHANNELS).astype(F32),
            rest[:, : 2 * STATE + HEADS],
        ],
        axis=1,
    )
    conv = jnp.concatenate(
        [
            small[:, :5, :channels].transpose(1, 0, 2).reshape(5, CHANNELS),
            jnp.sum(small[:, :5, channels:], axis=0),
        ],
        axis=1,
    )
    vector_summed = jnp.concatenate(
        [
            jnp.sum(small[:, 9:12, : D // 3], axis=0).reshape(-1) / g_norm,
            small[:, 5, :channels].reshape(-1),
            conv.reshape(-1),
            small[:, 7, :share].reshape(-1),
            small[:, 8, :share].reshape(-1),
            jnp.sum(small[:, 6, :channels].reshape(HEADS, HEAD_DIM), axis=1),
        ]
    )
    in_new = adam_update(in_proj, in_first, in_second, in_summed, RATE_MATRIX, DECAY_MATRIX)
    out_new = adam_update(out_proj, out_first, out_second, out_summed, RATE_MATRIX, DECAY_MATRIX)
    vec_new = adam_update(vector, vector_first, vector_second, vector_summed, RATE_VECTOR, 0.0)
    return (mixed_out, input_grad, *in_new, *out_new, *vec_new)


def solution(mesh):
    return jax.shard_map(
        heads_plan if mesh.shape["seq"] == 8 else positions_plan,
        mesh=mesh,
        in_specs=(
            P("fsdp", "seq", None),
            P("fsdp", "seq", None),
            P("fsdp", None),
            P(("seq", "fsdp"), None),
            P(("seq", "fsdp"), None),
            P(("seq", "fsdp"), None),
            P(("seq", "fsdp"), None),
            P(("seq", "fsdp"), None),
            P(("seq", "fsdp"), None),
            P(),
            P(),
            P(),
        ),
        out_specs=(
            P("fsdp", "seq", None),
            P("fsdp", "seq", None),
            P(("seq", "fsdp"), None),
            P(("seq", "fsdp"), None),
            P(("seq", "fsdp"), None),
            P(("seq", "fsdp"), None),
            P(("seq", "fsdp"), None),
            P(("seq", "fsdp"), None),
            P(),
            P(),
            P(),
        ),
        check_vma=False,
    )
```

```python
import functools

import jax
import jax.numpy as jnp
from jax import lax
from jax.experimental import pallas as pl
from jax.experimental.pallas import tpu as pltpu
from jax.sharding import PartitionSpec as P

D = 1536
HEADS = 48
HEAD_DIM = 64
STATE = 128
CONV = 4
STEP = 5


HIGH = lax.Precision.HIGHEST
EPS_NORM = 1e-05
BETA_ONE = 0.9
BETA_TWO = 0.95
ADAM_EPS = 1e-08
RATE_MATRIX = 0.03
RATE_VECTOR = 0.1
DECAY_MATRIX = 0.1


def passed_along(block, axis, distance):
    devices = range(lax.axis_size(axis))
    route = [(i - distance, i) for i in devices if i - distance in devices]
    return lax.ppermute(block, axis, route)


def entering(shard, axis, combine, identity, reverse):
    length, here = (lax.axis_size(axis), lax.axis_index(axis))
    everything = jax.tree.map(
        lambda part, kind: lax.all_gather(part.astype(kind), axis),
        shard,
        jax.tree.map(lambda a: jnp.bfloat16 if a.dtype == jnp.float32 else a.dtype, shard),
    )
    start = jax.tree.map(
        lambda part, zero: jnp.broadcast_to(jnp.asarray(zero, part.dtype), part.shape),
        shard,
        identity,
    )

    def step(k, before):
        at = length - 1 - k if reverse else k
        reached = at > here if reverse else at < here
        new = combine(
            before, jax.tree.map(lambda part, own: part[at].astype(own.dtype), everything, shard)
        )
        return jax.tree.map(lambda a, b: jnp.where(reached, a, b), new, before)

    return lax.fori_loop(0, length, step, start)


def as_sent(shard):
    return jax.tree.map(lambda a: a.astype(jnp.bfloat16) if a.dtype == jnp.float32 else a, shard)


def split_vector(vector):
    inner = HEADS * HEAD_DIM
    width = inner + 2 * STATE
    counts = [D, inner, CONV * width, width, HEADS, HEADS, HEADS]
    pieces = []
    offset = 0
    for amount in counts:
        pieces.append(vector[offset : offset + amount])
        offset += amount
    return (
        pieces[0],
        pieces[1],
        pieces[2].reshape(CONV, width),
        pieces[3],
        pieces[4],
        pieces[5],
        pieces[6],
    )


def rms_norm(value, gain):
    return value * lax.rsqrt(jnp.mean(value * value, axis=-1, keepdims=True) + EPS_NORM) * gain


def segment_ids(lengths, positions):
    ends = jnp.cumsum(lengths, axis=-1, dtype=jnp.int32)
    return jnp.sum(
        (ends[:, None, :] <= positions[None, :, None]).astype(jnp.int32), axis=-1, dtype=jnp.int32
    )


def convolve(padded, seg_ext, conv_w, conv_b):
    count = padded.shape[-2] - (CONV - 1)
    seg_here = seg_ext[..., CONV - 1 :]
    summed = conv_b + jnp.zeros(padded.shape[:-2] + (count, padded.shape[-1]), jnp.float32)
    for tap in range(CONV):
        agree = (seg_ext[..., tap : tap + count] == seg_here).astype(jnp.float32)
        summed = summed + conv_w[tap] * padded[..., tap : tap + count, :] * agree[..., None]
    return jax.nn.silu(summed)


def block_masks(seg, starts):
    order = jnp.arange(seg.shape[-1], dtype=jnp.int32)
    lower = order[:, None] >= order[None, :]
    agree = (lower & (seg[..., :, None] == seg[..., None, :])).astype(jnp.float32)
    keeping = (jnp.cumsum(starts, axis=-1, dtype=jnp.int32) == 0).astype(jnp.float32)
    same_last = (seg == seg[..., -1:]).astype(jnp.float32)
    return (agree, keeping, same_last)


def front_part(seg_ext):

    def front_apply(previous, xbc, dt_raw, conv_w, conv_b, dt_bias, a_log):
        inner = HEADS * HEAD_DIM
        padded = jnp.concatenate([previous, xbc], axis=1)
        active = convolve(padded, seg_ext, conv_w, conv_b)
        values = active[..., :inner].reshape(xbc.shape[0], xbc.shape[1], HEADS, HEAD_DIM)
        b_proj = active[..., inner : inner + STATE]
        c_proj = active[..., inner + STATE :]
        delta = jax.nn.softplus(dt_raw + dt_bias)
        log_decay = -delta * jnp.exp(a_log)
        return (values, b_proj, c_proj, delta, log_decay)

    return front_apply


def summary_part(keeping, same_last):

    def summary_apply(values, b_proj, delta, log_decay):
        cumulative = jnp.cumsum(log_decay, axis=1)
        final = cumulative[:, -1]
        tails = jnp.exp(final[:, None, :] - cumulative) * same_last[:, :, None] * delta
        summed = jnp.einsum("suh,suhp,sun->shpn", tails, values, b_proj, precision=HIGH)
        return (jnp.exp(final) * keeping[:, -1:], summed)

    return summary_apply


def output_part(agree, keeping):

    def output_apply(values, b_proj, c_proj, delta, log_decay, d_skip, carried):
        cumulative = jnp.cumsum(log_decay, axis=1)
        spacing = cumulative[:, :, None, :] - cumulative[:, None, :, :]
        masked = agree[..., None]
        decays = jnp.exp(jnp.where(masked > 0, spacing, 0.0)) * masked
        scores = jnp.einsum("stn,sun->stu", c_proj, b_proj, precision=HIGH)
        weights = decays * scores[..., None] * delta[:, None, :, :]
        result = jnp.einsum("stuh,suhp->sthp", weights, values, precision=HIGH)
        inflow = jnp.exp(cumulative) * keeping[..., None]
        result = (
            result
            + jnp.einsum("stn,shpn->sthp", c_proj, carried, precision=HIGH) * inflow[..., None]
        )
        return result + d_skip[:, None] * values

    return output_apply


def gate_part(mixer_out, gate_in, g_inner):
    flat = mixer_out.reshape(gate_in.shape) * jax.nn.silu(gate_in)
    return rms_norm(flat, g_inner)


def chain_combine(earlier, later):
    return (earlier[0] * later[0], earlier[1] * later[0][..., None, None] + later[1])


def adam_update(weight, moment_one, moment_two, gradient, rate, decay_rate):
    new_first = BETA_ONE * moment_one + (1 - BETA_ONE) * gradient
    new_second = BETA_TWO * moment_two + (1 - BETA_TWO) * gradient * gradient
    corrected = (
        new_first / (1 - BETA_ONE**STEP) / (jnp.sqrt(new_second / (1 - BETA_TWO**STEP)) + ADAM_EPS)
    )
    new_weight = weight - rate * (corrected + decay_rate * weight)
    return (new_first, new_second, new_weight)


def positions_plan(
    hidden_in,
    out_grad,
    lengths,
    in_proj,
    in_first,
    in_second,
    out_proj,
    out_first,
    out_second,
    vector,
    vector_first,
    vector_second,
):
    g_norm, g_inner, conv_w, conv_b, dt_bias, a_log, d_skip = split_vector(vector)
    inner = HEADS * HEAD_DIM
    width = inner + 2 * STATE
    count = hidden_in.shape[1]
    upstream = hidden_in.astype(jnp.float32)
    normed, norm_back = jax.vjp(rms_norm, upstream, g_norm)
    normed_low = normed.astype(jnp.bfloat16)
    in_full, out_full = (
        lax.all_gather(in_proj.astype(jnp.bfloat16), ("seq", "fsdp"), axis=0, tiled=True),
        lax.all_gather(out_proj.astype(jnp.bfloat16), ("seq", "fsdp"), axis=0, tiled=True),
    )
    projected = jnp.einsum("std,dk->stk", normed_low, in_full, preferred_element_type=jnp.float32)
    gate_in = projected[..., :inner]
    xbc = projected[..., inner : inner + width]
    dt_raw = projected[..., inner + width :]
    previous = passed_along(xbc[:, count - (CONV - 1) :].astype(jnp.bfloat16), "seq", 1).astype(
        jnp.float32
    )
    offset_base = lax.axis_index("seq") * count
    positions = offset_base - (CONV - 1) + jnp.arange(count + CONV - 1, dtype=jnp.int32)
    seg_ext = segment_ids(lengths, positions)
    seg_here = seg_ext[:, CONV - 1 :]
    starts = ((seg_here != seg_ext[:, CONV - 2 : -1]) | (positions[None, CONV - 1 :] == 0)).astype(
        jnp.int32
    )
    agree, keeping, same_last = block_masks(seg_here, starts)
    front_pieces, front_back = jax.vjp(
        front_part(seg_ext), previous, xbc, dt_raw, conv_w, conv_b, dt_bias, a_log
    )
    values, b_proj, c_proj, delta, log_decay = front_pieces
    block_pair, summary_back = jax.vjp(
        summary_part(keeping, same_last), values, b_proj, delta, log_decay
    )
    ones_init = jnp.ones_like(block_pair[0])
    zeros_init = jnp.zeros_like(block_pair[1])
    carried = entering(block_pair, "seq", chain_combine, (ones_init, zeros_init), False)[1]
    mixer_out, output_back = jax.vjp(
        output_part(agree, keeping), values, b_proj, c_proj, delta, log_decay, d_skip, carried
    )
    gated, gate_back = jax.vjp(gate_part, mixer_out, gate_in, g_inner)
    gated_low = gated.astype(jnp.bfloat16)
    branch = jnp.einsum("stc,cd->std", gated_low, out_full, preferred_element_type=jnp.float32)
    mixed = (upstream + branch).astype(jnp.bfloat16)
    in_again, out_again = (
        lax.all_gather(in_proj.astype(jnp.bfloat16), ("seq", "fsdp"), axis=0, tiled=True),
        lax.all_gather(out_proj.astype(jnp.bfloat16), ("seq", "fsdp"), axis=0, tiled=True),
    )
    grad_out_proj = jnp.einsum(
        "stc,std->cd", gated_low, out_grad, preferred_element_type=jnp.float32
    )
    grad_gated = jnp.einsum("std,cd->stc", out_grad, out_again, preferred_element_type=jnp.float32)
    grad_mixer, grad_gate_in, grad_g_inner = gate_back(grad_gated)
    grad_values, grad_b, grad_c, grad_delta, grad_log, grad_skip, grad_carried = output_back(
        grad_mixer
    )
    grad_final = entering(
        (block_pair[0], grad_carried), "seq", chain_combine, (ones_init, zeros_init), True
    )[1]
    grad_decay_total = jnp.sum(grad_final * carried, axis=(2, 3))
    more_values, more_b, more_delta, more_log = summary_back((grad_decay_total, grad_final))
    grad_front = (
        grad_values + more_values,
        grad_b + more_b,
        grad_c,
        grad_delta + more_delta,
        grad_log + more_log,
    )
    grad_previous, grad_xbc, grad_dt_raw, grad_conv_w, grad_conv_b, grad_dt_bias, grad_a_log = (
        front_back(grad_front)
    )
    returned = passed_along(as_sent(grad_previous), "seq", -1).astype(grad_previous.dtype)
    grad_xbc = jnp.concatenate(
        [grad_xbc[:, : count - (CONV - 1)], grad_xbc[:, count - (CONV - 1) :] + returned], axis=1
    )
    grad_projected = jnp.concatenate([grad_gate_in, grad_xbc, grad_dt_raw], axis=-1).astype(
        jnp.bfloat16
    )
    grad_in_proj = jnp.einsum(
        "std,stk->dk", normed_low, grad_projected, preferred_element_type=jnp.float32
    )
    grad_normed = jnp.einsum(
        "stk,dk->std", grad_projected, in_again, preferred_element_type=jnp.float32
    )
    grad_upstream, grad_g_norm = norm_back(grad_normed)
    input_grad = out_grad.astype(jnp.float32) + grad_upstream
    in_summed, out_summed = (
        lax.psum_scatter(grad_in_proj, ("seq", "fsdp"), scatter_dimension=0, tiled=True),
        lax.psum_scatter(grad_out_proj, ("seq", "fsdp"), scatter_dimension=0, tiled=True),
    )
    local_vector = jnp.concatenate(
        [
            grad_g_norm,
            grad_g_inner,
            grad_conv_w.reshape(-1),
            grad_conv_b,
            grad_dt_bias,
            grad_a_log,
            grad_skip,
        ]
    )
    vector_summed = lax.psum(local_vector, ("seq", "fsdp"))
    in_new = adam_update(in_proj, in_first, in_second, in_summed, RATE_MATRIX, DECAY_MATRIX)
    out_new = adam_update(out_proj, out_first, out_second, out_summed, RATE_MATRIX, DECAY_MATRIX)
    vec_new = adam_update(vector, vector_first, vector_second, vector_summed, RATE_VECTOR, 0.0)
    return (
        mixed,
        input_grad,
        in_new[0],
        in_new[1],
        in_new[2],
        out_new[0],
        out_new[1],
        out_new[2],
        vec_new[0],
        vec_new[1],
        vec_new[2],
    )


Q = 128
LANES = 128
CHANNELS = HEADS * HEAD_DIM
WIDTH = CHANNELS + 2 * STATE
BF16 = jnp.bfloat16
F32 = jnp.float32


def mul(a, b, dims=((1,), (0,))):
    return lax.dot_general(a, b, (dims, ((), ())), preferred_element_type=F32)


def halves(x):
    high = x.astype(BF16)
    return high, (x - high.astype(F32)).astype(BF16)


def wide(mask, copies):
    return jnp.concatenate([mask] * copies, axis=1)


def head_map(channels):
    head = lax.broadcasted_iota(jnp.int32, (LANES, channels), 0)
    owner = lax.broadcasted_iota(jnp.int32, (LANES, channels), 1) // HEAD_DIM
    return (head == owner).astype(BF16)


def spread(parts, channels):
    stacked = jnp.concatenate([jnp.concatenate(halves(x), axis=1) for x in parts], axis=0)
    one = head_map(channels)
    out = mul(stacked, jnp.concatenate([one, one], axis=0))
    rows = parts[0].shape[0]
    return [out[i * rows : (i + 1) * rows] for i in range(len(parts))]


def gather_heads(parts, channels):
    stacked = jnp.concatenate([jnp.concatenate(halves(x), axis=1) for x in parts], axis=0)
    one = head_map(channels)
    out = mul(stacked, jnp.concatenate([one, one], axis=1), ((1,), (1,)))
    rows = parts[0].shape[0]
    return [out[i * rows : (i + 1) * rows] for i in range(len(parts))]


def running_sum(x, backward):
    t = lax.broadcasted_iota(jnp.int32, (Q, Q), 0)
    u = lax.broadcasted_iota(jnp.int32, (Q, Q), 1)
    tri = ((t <= u) if backward else (t >= u)).astype(BF16)
    return mul(jnp.concatenate([tri, tri], axis=1), jnp.concatenate(halves(x), axis=0))


def segments(ends, stream, positions):
    seg = jnp.zeros(positions.shape, jnp.int32)
    for end in ends[stream]:
        seg = seg + (end <= positions).astype(jnp.int32)
    return jnp.where(positions < 0, -1, seg)


def chunk_places(ends, stream, base):
    column = lax.broadcasted_iota(jnp.int32, (Q + 16, LANES), 0) + (base - 8)
    row = lax.broadcasted_iota(jnp.int32, (8, LANES), 1) + base
    return segments(ends, stream, column), segments(ends, stream, row)[0:1]


def chunk_convolve(p_ref, par_ref, stream, base, seg):
    mixed = par_ref.shape[1]
    channels = mixed - 2 * STATE
    before = pl.multiple_of(jnp.maximum(base - 8, 0), 8)
    xbc = p_ref[stream, pl.ds(base, Q), channels : channels + mixed]
    halo = p_ref[stream, pl.ds(before, 8), channels : channels + mixed]
    both = jnp.concatenate([halo, xbc], axis=0)
    here = seg[8 : Q + 8]
    pre = par_ref[4:5, :] + par_ref[3:4, :] * xbc
    for k in range(CONV - 1):
        agree = (seg[5 + k : Q + 5 + k] == here).astype(F32)
        tap = both[5 + k : Q + 5 + k] * wide(agree, mixed // LANES)
        pre = pre + par_ref[k : k + 1, :] * tap
    return pre


def chunk_raw(p_ref, par_ref, stream, base):
    mixed = par_ref.shape[1]
    at = 2 * mixed - 2 * STATE
    return p_ref[stream, pl.ds(base, Q), at:] + par_ref[7:8, :LANES]


def soft_plus(raw):
    return jnp.maximum(raw, 0.0) + jnp.log1p(jnp.exp(-jnp.abs(raw)))


def chunk_decay(raw, par_ref):
    delta = soft_plus(raw)
    rate = jnp.exp(par_ref[8:9, :LANES])
    return delta, running_sum(-delta * rate, False)


def chunk_front(pre, delta, cumulative, seg, seg_row):
    channels = pre.shape[1] - 2 * STATE
    here = seg[8 : Q + 8]
    gate = jax.nn.sigmoid(pre)
    active = pre * gate
    values = active[:, :channels]
    last = cumulative[Q - 1 : Q]
    keep = (here == seg[7:8]).astype(F32)
    same_last = (here == seg[Q + 7 : Q + 8]).astype(F32)
    inflow = jnp.exp(cumulative) * keep
    tail = jnp.exp(last - cumulative) * same_last
    delta_wide, inflow_wide, tail_wide = spread([delta, inflow, tail], channels)
    t = lax.broadcasted_iota(jnp.int32, (Q, Q), 0)
    u = lax.broadcasted_iota(jnp.int32, (Q, Q), 1)
    mask = (t >= u) & (here == seg_row)
    turned = cumulative.T

    def decays(head):
        spacing = cumulative[:, head : head + 1] - turned[head : head + 1, :]
        return jnp.exp(jnp.where(mask, spacing, -1e30))

    return dict(
        seg=seg,
        pre=pre,
        gate=gate,
        values=values,
        b_low=active[:, channels : channels + STATE].astype(BF16),
        c_low=active[:, channels + STATE :].astype(BF16),
        delta=delta,
        delta_wide=delta_wide,
        inflow_wide=inflow_wide,
        tail_wide=tail_wide,
        scaled=values * delta_wide,
        decays=decays,
        channels=channels,
    )


def two_heads(pair):
    left = lax.broadcasted_iota(jnp.int32, pair.shape, 1) < HEAD_DIM
    low = pair.astype(BF16)
    zero = jnp.zeros_like(low)
    return jnp.concatenate([jnp.where(left, low, zero), jnp.where(left, zero, low)], axis=0)


def chunk_forward(front, state, skip):
    channels = front["channels"]
    scores = mul(front["c_low"], front["b_low"], ((1,), (1,)))
    pieces = []
    for pair in range(channels // LANES):
        weights = jnp.concatenate(
            [(front["decays"](2 * pair + i) * scores).astype(BF16) for i in range(2)], axis=1
        )
        scaled = front["scaled"][:, pair * LANES : (pair + 1) * LANES]
        pieces.append(mul(weights, two_heads(scaled)))
    result = jnp.concatenate(pieces, axis=1)
    result = result + mul(front["c_low"], state.astype(BF16)) * front["inflow_wide"]
    result = result + skip * front["values"]
    fed = (front["scaled"] * front["tail_wide"]).astype(BF16)
    after = front["inflow_wide"][Q - 1 : Q] * state + mul(front["b_low"], fed, ((0,), (0,)))
    return result, after


def chunk_backward(front, raw, rate, before, after, grad_after, result, grad, skip):
    channels = front["channels"]
    b_low, c_low = front["b_low"], front["c_low"]
    scaled, values = front["scaled"], front["values"]
    scores = mul(c_low, b_low, ((1,), (1,)))
    grad_scores = jnp.zeros((Q, Q), F32)
    pieces = []
    for pair in range(channels // LANES):
        lanes = slice(pair * LANES, (pair + 1) * LANES)
        decays = [front["decays"](2 * pair + i) for i in range(2)]
        weights = jnp.concatenate([(d * scores).astype(BF16) for d in decays], axis=0)
        split = two_heads(grad[:, lanes])
        pieces.append(mul(weights, split, ((0,), (0,))))
        cross = mul(split, scaled[:, lanes].astype(BF16), ((1,), (1,)))
        grad_scores = grad_scores + decays[0] * cross[:Q] + decays[1] * cross[Q:]
    grad_after_low = grad_after.astype(BF16)
    inner = jnp.concatenate(pieces, axis=1) + mul(b_low, grad_after_low) * front["tail_wide"]
    fed = (scaled * front["tail_wide"]).astype(BF16)
    flowing = (grad * front["inflow_wide"]).astype(BF16)
    low_scores = grad_scores.astype(BF16)
    grad_c = mul(low_scores, b_low) + mul(flowing, before.astype(BF16), ((1,), (1,)))
    grad_b = mul(low_scores, c_low, ((0,), (0,))) + mul(fed, grad_after_low, ((1,), (1,)))
    grad_values = skip * grad + front["delta_wide"] * inner
    grad_skip = jnp.sum(grad * values, axis=0, keepdims=True)
    held = jnp.sum(after * grad_after, axis=0, keepdims=True)
    grad_delta, grad_cumulative = gather_heads(
        [values * inner, grad * (result - skip * values) - scaled * inner], channels
    )
    held_heads = gather_heads([jnp.broadcast_to(held, (8, channels))], channels)[0][0:1]
    grad_log = running_sum(grad_cumulative, True) + held_heads
    grad_delta = grad_delta - rate * grad_log
    grad_raw = grad_delta * jax.nn.sigmoid(raw)
    grad_rate = -rate * jnp.sum(grad_log * front["delta"], axis=0, keepdims=True)
    grad_before = front["inflow_wide"][Q - 1 : Q] * grad_after + mul(c_low, flowing, ((0,), (0,)))
    return grad_values, grad_b, grad_c, grad_raw, grad_rate, grad_skip, grad_before


def conv_backward(front, xbc, grad_active, next_grad, par_ref):
    gate, pre, seg = front["gate"], front["pre"], front["seg"]
    mixed = pre.shape[1]
    grad_pre = grad_active * (gate * (1.0 + pre * (1.0 - gate)))
    both = jnp.concatenate([grad_pre, next_grad], axis=0)
    grad_x = par_ref[CONV - 1 : CONV, :] * grad_pre
    rows = []
    for k in range(CONV - 1):
        ahead = CONV - 1 - k
        agree = (seg[8 + ahead : Q + 8 + ahead] == seg[8 : Q + 8]).astype(F32)
        moved = both[ahead : Q + ahead] * wide(agree, mixed // LANES)
        grad_x = grad_x + par_ref[k : k + 1, :] * moved
        rows.append(jnp.sum(xbc * moved, axis=0, keepdims=True))
    rows.append(jnp.sum(xbc * grad_pre, axis=0, keepdims=True))
    rows.append(jnp.sum(grad_pre, axis=0, keepdims=True))
    return grad_x, grad_pre[:8], rows


MESH = pl.DeviceIdType.MESH
TILE = 512


class Links:
    def __init__(self, send, recv):
        self.send, self.recv, self.used = send, recv, 0

    def copy(self, source, target, device):
        slot = self.used
        self.used += 1
        assert slot < self.send.shape[0]
        return pltpu.make_async_remote_copy(
            src_ref=source,
            dst_ref=target,
            send_sem=self.send.at[slot],
            recv_sem=self.recv.at[slot],
            device_id=device,
            device_id_type=MESH,
        )


class Place:
    def __init__(self, depth):
        self.s = lax.axis_index("seq")
        self.f = lax.axis_index("fsdp")
        self.depth = depth
        self.core = lax.rem(self.s, 2)
        x = lax.rem(self.s // 2, 2)
        y = self.s // 4
        self.steps = (1 - 2 * self.core, 2 - 4 * x, 4 - 8 * y)

    def peer(self, k):
        index = self.s
        for bit in range(3):
            if k >> bit & 1:
                index = index + self.steps[bit]
        return index

    def at(self, k):
        return (self.peer(k), self.f)

    def plane(self, d):
        return lax.rem(self.f + d, self.depth)

    def beyond(self, d):
        return (self.s, self.plane(d))

    def greet(self):
        barrier = pltpu.get_barrier_semaphore()
        others = [self.at(k) for k in range(1, 8)] + [self.beyond(d) for d in range(1, self.depth)]
        for other in others:
            pl.semaphore_signal(barrier, inc=1, device_id=other, device_id_type=MESH)
        pl.semaphore_wait(barrier, len(others))


def ahead(start, size):
    return pl.ds(pl.multiple_of(start, size), size)


PIECES = [slice(i, i + 512) for i in range(0, D, 512)]
FEW = 64


class Summing:
    def __init__(self, here, links, slots, beside, halves_in, final_in, own):
        self.here, self.slots, self.beside = here, slots, beside
        self.halves_in, self.final_in, self.own = halves_in, final_in, own
        self.count = slots[0].shape[0]
        self.half = self.count // 2
        make = links.copy
        self.to_beside = [make(slots[r], beside[r], here.at(1)) for r in range(4)]
        self.by = [
            make(slots[3].at[self.rows(i)], halves_in[i], here.at(2 << i)) for i in range(2)
        ]
        self.last = [make(slots[1 + i], final_in[i], here.at(2 << i)) for i in range(2)]

    def rows(self, i):
        return pl.ds(i * self.half, self.half)

    def owner(self, r, other):
        return self.here.peer(2 * r + (1 if other else 0))

    def give_beside(self, value):
        for lanes in PIECES:
            found = value(True, lanes).astype(BF16)
            for r in range(4):
                self.slots[r][:, lanes] = found[r * self.count : (r + 1) * self.count]
        for r in (3, 1, 2, 0):
            self.to_beside[r].start()

    def join(self, value):
        for copy in self.to_beside:
            copy.wait()
        targets = [self.own] + self.slots[1:]
        for lanes in PIECES:
            found = value(False, lanes)
            for r in range(4):
                mine = found[r * self.count : (r + 1) * self.count]
                joined = mine + self.beside[r][:, lanes].astype(F32)
                targets[r][:, lanes] = joined.astype(targets[r].dtype)
        for copy in self.by:
            copy.start()

    def pass_on(self, i):
        other = 1 - i
        self.by[other].wait_recv()
        part = self.slots[1 + i].at[self.rows(other)]
        part[...] = (part[...].astype(F32) + self.halves_in[other][...].astype(F32)).astype(BF16)
        self.last[i].start()

    def arrived(self):
        for copy in self.last:
            copy.wait_recv()

    def total(self, rows):
        total = self.own[rows].astype(F32) + self.final_in[0][rows].astype(F32)
        return total + self.final_in[1][rows].astype(F32)

    def settle(self):
        for copy in self.by + self.last:
            copy.wait_send()


class Passing:
    def __init__(self, here, links, blocks, from_below, from_above, depth):
        f, s = here.f, here.s
        self.f, self.depth, self.blocks = f, depth, blocks
        self.came = (from_below, from_above)
        self.copies = []
        for j in range(depth - 1):
            far = depth - 1 - j
            self.copies.append(
                (
                    links.copy(blocks(f + far), from_below.at[far - 1], (s, f + 1)),
                    links.copy(blocks(f - far), from_above.at[far - 1], (s, f - 1)),
                )
            )

    def sends(self, j):
        return (self.f <= j, self.depth - 1 - self.f <= j)

    def gets(self, j):
        return (
            (self.f >= 1) & (self.f <= j + 1),
            (self.f <= self.depth - 2) & (self.depth - 1 - self.f <= j + 1),
        )

    def begin(self):
        for j in range(self.depth - 1):
            pl.when(self.f == 0)(self.copies[j][0].start)
            pl.when(self.f == self.depth - 1)(self.copies[j][1].start)

    def step(self, j):
        far = self.depth - 1 - j
        for way, sign in ((0, 1), (1, -1)):

            @pl.when(self.gets(j - 1)[way])
            def _(way=way, sign=sign):
                self.copies[j - 1][way].wait_recv()
                block = self.blocks(self.f + sign * far)
                block[...] = (
                    block[...].astype(F32) + self.came[way][far].astype(F32)
                ).astype(BF16)
                self.copies[j][way].start()

    def finish(self):
        last = self.depth - 2
        block = self.blocks(self.f)
        for way in range(2):

            @pl.when(self.gets(last)[way])
            def _(way=way):
                self.copies[last][way].wait_recv()
                block[...] = (
                    block[...].astype(F32) + self.came[way][0].astype(F32)
                ).astype(BF16)

    def settle(self):
        for j in range(self.depth - 1):
            for way in range(2):
                pl.when(self.sends(j)[way])(self.copies[j][way].wait_send)


LINE = 512
LONG = 256
GROUP = 384
FIRST_GAIN = 0
FIRST_INNER = D // LANES
FIRST_CONV = FIRST_INNER + CHANNELS // LANES
CONV_ROWS = WIDTH // LANES
SMALL = FIRST_CONV + (CONV + 1) * CONV_ROWS
VECTOR_ROWS = SMALL + 2


def thirds(x):
    high, low = halves(x)
    rest = x - high.astype(F32) - low.astype(F32)
    return high, low, rest.astype(BF16)


def chosen(x, picks):
    return sum(mul(part, picks) for part in thirds(x))


def own_parameters(vec, par, s, share):
    channels = share * HEAD_DIM
    tiles = channels // LANES
    par[...] = jnp.zeros_like(par)
    for k in range(CONV + 1):
        base = FIRST_CONV + k * CONV_ROWS
        for i in range(tiles):
            par[k : k + 1, i * LANES : (i + 1) * LANES] = vec[pl.ds(base + s * tiles + i, 1), :]
        for i in range(2 * STATE // LANES):
            at = channels + i * LANES
            row = base + CHANNELS // LANES + i
            par[k : k + 1, at : at + LANES] = vec[row : row + 1, :]
    for i in range(tiles):
        row = vec[pl.ds(FIRST_INNER + s * tiles + i, 1), :]
        par[5:6, i * LANES : (i + 1) * LANES] = row
    small = jnp.concatenate([vec[SMALL : SMALL + 1, :], vec[SMALL + 1 : SMALL + 2, :]], axis=1)
    small = jnp.broadcast_to(small, (8, 2 * LANES))
    source = lax.broadcasted_iota(jnp.int32, (2 * LANES, LANES), 0)
    lane = lax.broadcasted_iota(jnp.int32, (2 * LANES, LANES), 1)
    found = []
    for which in range(3):
        picks = (source == which * HEADS + s * share + lane) & (lane < share)
        found.append(chosen(small, picks.astype(BF16)))
    par[6:7, :channels] = chosen(found[2], head_map(channels))[0:1]
    par[7:8, :LANES] = found[0][0:1]
    par[8:9, :LANES] = found[1][0:1]


def all_parameters(vec, found, out, share):
    count = found.shape[0]
    channels = share * HEAD_DIM
    tiles = channels // LANES
    out[...] = jnp.zeros_like(out)
    wide_rows = D // 3 // LANES
    for i in range(FIRST_INNER):
        at = (i % wide_rows) * LANES
        row = found[0, 9 + i // wide_rows : 10 + i // wide_rows, at : at + LANES]
        for k in range(1, count):
            row = row + found[k, 9 + i // wide_rows : 10 + i // wide_rows, at : at + LANES]
        out[i : i + 1, :] = row / vec[i : i + 1, :]
    for k in range(count):
        for i in range(tiles):
            lanes = slice(i * LANES, (i + 1) * LANES)
            row = FIRST_INNER + k * tiles + i
            out[row : row + 1, :] = found[k, 5:6, lanes]
            for j in range(CONV + 1):
                row = FIRST_CONV + j * CONV_ROWS + k * tiles + i
                out[row : row + 1, :] = found[k, j : j + 1, lanes]
    for j in range(CONV + 1):
        for i in range(2 * STATE // LANES):
            lanes = slice(channels + i * LANES, channels + (i + 1) * LANES)
            total = found[0, j : j + 1, lanes]
            for k in range(1, count):
                total = total + found[k, j : j + 1, lanes]
            row = FIRST_CONV + j * CONV_ROWS + CHANNELS // LANES + i
            out[row : row + 1, :] = total
    lane = lax.broadcasted_iota(jnp.int32, (8, LANES), 1)
    small = jnp.zeros((8, LANES), F32)
    for k in range(count):
        part = jnp.where(lane < share, found[k, 0:16, :LANES][6:14], 0.0)
        small = small + (pltpu.roll(part, k * share, 1) if k else part)
    skip, step, rate = small[0:1], small[1:2], small[2:3]
    lane = lane[0:1]
    rate = pltpu.roll(small, HEADS, 1)[2:3]
    skip = pltpu.roll(small, 2 * HEADS, 1)[0:1]
    first = jnp.where(lane < HEADS, step, jnp.where(lane < 2 * HEADS, rate, skip))
    out[SMALL : SMALL + 1, :] = first
    out[SMALL + 1 : SMALL + 2, :] = jnp.where(lane < 3 * HEADS - LANES, skip, 0.0)


def block_kernel(
    depth,
    lengths,
    hidden,
    out_grad,
    in_low,
    out_proj,
    vec,
    mixed_out,
    upstream_out,
    main_out,
    lines_out,
    vector_out,
    x_kept,
    x,
    g,
    w,
    wo,
    p,
    y,
    h,
    pre_kept,
    decay_kept,
    par,
    state,
    later,
    sums,
    shared_low,
    moments,
    moments_sum,
    slots,
    beside_in,
    halves_in,
    last_in,
    lines,
    lines_in,
    main,
    gate_in,
    main_in,
    slabs_recv,
    common,
    common_beside,
    common_recv,
    common_line,
    common_last,
    common_sum,
    gain_sums,
    vector_line,
    vector_all,
    vector_full,
    send,
    recv,
    moves,
    credit,
):
    streams, length = x.shape[0], x.shape[1]
    block = hidden.shape[0] // streams
    chunks = length // Q
    rows = in_low.shape[0]
    out_rows = out_proj.shape[0]
    channels = wo.shape[0]
    share = channels // HEAD_DIM
    mixed = channels + 2 * STATE
    tiles = channels // LANES
    slab = depth * rows
    here = Place(depth)
    s, f = here.s, here.f
    links = Links(send, recv)
    dp = x
    part_of = [slice(i * channels, (i + 1) * channels) for i in range(4)]
    projected = slice(0, 3 * channels)
    ends = []
    for k in range(streams):
        total = lengths[k, 0]
        ends.append([total])
        for i in range(1, lengths.shape[1]):
            total = total + lengths[k, i]
            ends[k].append(total)

    def slab_rows(source, plane):
        return ahead((source * depth + plane) * rows, rows)

    def block_rows(source):
        return ahead(source * block, block)

    finish = []

    def started(copy):
        copy.start()
        finish.append(copy)
        return copy

    narrow = 2 * STATE + HEADS
    shared_low[:, narrow:] = jnp.zeros((rows, shared_low.shape[1] - narrow), BF16)
    shared_low[:, :narrow] = in_low[:, 2 * CHANNELS :]
    here.greet()
    order = (0, 1, 2, 4, 3, 5, 6, 7)
    own = slab_rows(s, f)
    turned = {}
    for part in (1, 0):
        for k in order[1:]:
            lanes = ahead(part * CHANNELS + here.peer(k) * channels, channels)
            turned[part, k] = started(
                links.copy(in_low.at[:, lanes], w.at[own, part_of[part]], here.at(k))
            )
    shared = [
        started(links.copy(shared_low, w.at[own, 2 * channels :], here.beyond(d)))
        for d in range(1, depth)
    ]
    w[own, 2 * channels :] = shared_low[...]
    for part in range(2):
        w[own, part_of[part]] = in_low[:, ahead(part * CHANNELS + s * channels, channels)]
    gain = jnp.concatenate([vec[i : i + 1, :] for i in range(FIRST_INNER)], axis=1)

    def scaled_rows(at):
        upstream = hidden[at, :].astype(F32)
        mean = jnp.mean(upstream * upstream, axis=-1, keepdims=True)
        return upstream, lax.rsqrt(mean + EPS_NORM)

    for stream in range(streams):

        def normalize(i, carry, stream=stream):
            upstream, inverse = scaled_rows(ahead(stream * block + i * FEW, FEW))
            x[stream, ahead(s * block + i * FEW, FEW), :] = (upstream * inverse * gain).astype(BF16)
            return carry

        lax.fori_loop(0, block // FEW, normalize, 0)

    def token_block(ref, stream, k):
        return ref.at[stream, block_rows(here.peer(k))]

    def token_half(ref, stream, way, k):
        rows = block // 2
        return ref.at[stream, ahead(here.peer(k) * block + way * rows, rows)]

    class Tokens:
        def __init__(self, ref, stream):
            self.ref, self.stream = ref, stream
            mine = token_block(ref, stream, 0)
            self.near = [links.copy(mine, mine, here.at(2 << way)) for way in range(2)]
            halves_out = [token_half(ref, stream, way, 2 << way) for way in range(2)]
            self.across = [
                links.copy(halves_out[way], halves_out[way], here.at(4 >> way)) for way in range(2)
            ]
            blocks = [token_block(ref, stream, k) for k in (0, 2, 4)]
            blocks += [token_half(ref, stream, way, 6) for way in range(2)]
            self.beside = [links.copy(part, part, here.at(1)) for part in blocks]

        def begin(self):
            for copy in self.near:
                copy.start()
            self.beside[0].start()

        def go_on(self):
            for way in range(2):
                self.near[way].wait_recv()
                self.across[way].start()
                self.beside[1 + way].start()

        def end(self):
            for way in range(2):
                self.across[way].wait_recv()
                self.beside[3 + way].start()
            for copy in self.beside:
                copy.wait_recv()

        def settle(self):
            for copy in self.near + self.across + self.beside:
                copy.wait_send()

    x_tokens = [Tokens(x, k) for k in range(streams)]
    g_tokens = [Tokens(g, k) for k in range(streams)]
    x_tokens[0].begin()
    g_in = [
        pltpu.make_async_copy(
            out_grad.at[pl.ds(k * block, block)], g.at[k, block_rows(s)], moves.at[2 + k]
        )
        for k in range(streams)
    ]
    for copy in g_in:
        copy.start()
    wo[ahead(f * out_rows, out_rows)] = out_proj[...].astype(BF16)
    own_parameters(vec, par, s, share)

    def hop(part, k, d, up):
        plane = f - d if up else f + d
        target = w.at[slab_rows(here.peer(k), plane), part_of[part]]
        return links.copy(target, target, (s, f + 1 if up else f - 1))

    hops = {}
    for part in range(2):
        for k in range(8):
            for d in range(depth - 1):
                hops[part, k, d] = (hop(part, k, d, True), hop(part, k, d, False))

    def sends(d):
        return ((f >= d) & (f < depth - 1), (f <= depth - 1 - d) & (f > 0))

    def gets(d):
        return (f >= d + 1, f <= depth - 2 - d)

    def launch(part, k, d):
        for way in range(2):
            pl.when(sends(d)[way])(hops[part, k, d][way].start)

    def arrive(part, k, d):
        for way in range(2):
            pl.when(gets(d)[way])(hops[part, k, d][way].wait_recv)

    def first_hops(part):
        for k in order:
            if k:
                turned[part, k].wait_recv()
            launch(part, k, 0)

    def next_hops(part, d):
        for k in order:
            arrive(part, k, d - 1)
            launch(part, k, d)

    def project(stream, parts):
        def tile(i, carry):
            at = ahead(i * TILE, TILE)
            left = x[stream, at, :]
            for lanes in parts:
                p[stream, at, lanes] = mul(left, w[:, lanes])
            return carry

        lax.fori_loop(0, length // TILE, tile, 0)

    first_hops(1)
    for copy in shared:
        copy.wait_recv()
    group = w.at[ahead(s * slab, slab), 2 * channels :]
    spread_common = [links.copy(group, group, here.at(k)) for k in (2, 4, 6, 1)]
    for copy in spread_common:
        copy.start()
    last = depth - 1
    for d in range(1, last):
        if d == last - 1:
            x_tokens[0].go_on()
            for k in range(1, streams):
                x_tokens[k].begin()
            for copy in g_in:
                copy.wait()
            g_tokens[0].begin()
        next_hops(1, d)
    first_hops(0)
    for copy in spread_common[:3]:
        copy.wait_recv()
    for k in (2, 4, 6):
        group = w.at[ahead(here.peer(k) * slab, slab), 2 * channels :]
        spread_common.append(links.copy(group, group, here.at(1)))
        spread_common[-1].start()
    for copy in spread_common[3:]:
        copy.wait_recv()
    for copy in spread_common:
        copy.wait_send()
    column_at = lax.broadcasted_iota(jnp.int32, (LANES, LANES), 0)
    wanted_at = lax.broadcasted_iota(jnp.int32, (LANES, LANES), 1)
    pick = ((column_at == wanted_at + s * share) & (wanted_at < share)).astype(BF16)
    for part in range(0, D, TILE):
        steps = w[part : part + TILE, mixed + channels :]
        w[part : part + TILE, mixed + channels :] = mul(steps, pick).astype(BF16)
    x_out = [
        pltpu.make_async_copy(x.at[k], x_kept.at[k], moves.at[k]) for k in range(streams)
    ]
    x_tokens[0].end()
    x_out[0].start()
    for k in order:
        arrive(1, k, last - 1)
    project(0, part_of[1:3])
    for k in range(1, streams):
        x_tokens[k].go_on()
        g_tokens[k].begin()

    skip = par[6:7, :channels]
    g_inner = par[5:6, :channels]
    state[...] = jnp.zeros_like(state)

    def tell_moments(which, stream):
        mine_m = moments.at[s, which, stream]
        return [started(links.copy(mine_m, mine_m, here.at(k))) for k in range(1, 8)]

    def hear_moments(which, stream):
        for copy in told_moments[which, stream]:
            copy.wait_recv()
        moments_sum[which, stream] = jnp.sum(moments[:, which, stream], axis=0)

    told_moments = {}
    ones = jnp.ones((8, 2 * channels), BF16)

    def forward_step(stream, chunk, carry):
        base = pl.multiple_of(chunk * Q, Q)
        at = pl.ds(base, Q)
        seg, seg_row = chunk_places(ends, stream, base)
        pre = chunk_convolve(p, par, stream, base, seg)
        delta, cumulative = chunk_decay(chunk_raw(p, par, stream, base), par)
        pre_kept[stream, at] = pre.astype(BF16)
        decay_kept[stream, at] = cumulative
        front = chunk_front(pre, delta, cumulative, seg, seg_row)
        before = state[stream]
        h[stream, chunk] = before.astype(BF16)
        result, after = chunk_forward(front, before, skip)
        y[stream, at] = result
        state[stream] = after
        if stream == 0:

            @pl.when(chunk == 2 * chunks // 8)
            def _():
                for d in range(1, last - 1):
                    next_hops(0, d)

        @pl.when(chunk == (5 if stream == 0 else 3) * chunks // 8)
        def _():
            g_tokens[stream].go_on()

        return carry

    def flat_step(stream, chunk, carry):
        at = ahead(chunk * Q, Q)
        gate_in = p[stream, at, :channels]
        flat = y[stream, at] * (gate_in * jax.nn.sigmoid(gate_in))
        dp[stream, at, part_of[2]] = (flat * g_inner).astype(BF16)
        squares = jnp.concatenate(halves(flat * flat), axis=1)
        moments[s, 0, stream, pl.ds(chunk, 1), :] = mul(ones, squares, ((1,), (1,)))[0:1]
        return carry

    lax.fori_loop(0, chunks, functools.partial(forward_step, 0), 0)
    next_hops(0, last - 1)
    lent = wo.at[ahead(f * out_rows, out_rows)]
    outs = [started(links.copy(lent, lent, here.beyond(d))) for d in range(1, depth)]
    for k in range(1, streams):
        x_tokens[k].end()
        x_out[k].start()
        project(k, part_of[1:3])
        lax.fori_loop(0, chunks, functools.partial(forward_step, k), 0)
    for k in order:
        arrive(0, k, last - 1)
    for k in range(streams):
        project(k, part_of[:1])
        x_out[k].wait()
        x_tokens[k].settle()
        lax.fori_loop(0, chunks, functools.partial(flat_step, k), 0)
        told_moments[0, k] = tell_moments(0, k)

    long_tiles = length // TILE
    pieces = TILE // Q

    def weigh(stream, i, carry):
        at = ahead(i * TILE, TILE)
        dp[stream, at, part_of[3]] = mul(g[stream, at], wo[...], ((1,), (1,))).astype(BF16)
        for j in range(pieces):
            at = ahead(i * TILE + j * Q, Q)
            product = dp[stream, at, part_of[3]].astype(F32) * dp[stream, at, part_of[2]].astype(F32)
            found = mul(ones, jnp.concatenate(halves(product), axis=1), ((1,), (1,)))
            moments[s, 1, stream, pl.ds(i * pieces + j, 1), :] = found[0:1]
        return carry

    mixed_sum = Summing(
        here,
        links,
        [slots.at[r] for r in range(4)],
        [beside_in.at[r] for r in range(4)],
        [halves_in.at[i] for i in range(2)],
        [last_in.at[i] for i in range(2)],
        mixed_out,
    )

    def grad_of(stream):
        rows = pl.ds(stream * block, block)
        few = pl.ds(stream * block // 2, block // 2)
        return Summing(
            here,
            links,
            [slots.at[r, rows] for r in range(4)],
            [beside_in.at[r, rows] for r in range(4)],
            [halves_in.at[i, few] for i in range(2)],
            [last_in.at[i, rows] for i in range(2)],
            upstream_out.at[rows],
        )

    grad_sums = [grad_of(k) for k in range(streams)]

    def branch(other, lanes):
        rows_at = [block_rows(mixed_sum.owner(r, other)) for r in range(4)]
        low = [dp[k, at, part_of[2]] for at in rows_at for k in range(streams)]
        return mul(jnp.concatenate(low, axis=0), wo[:, lanes])

    for copy in outs:
        copy.wait_recv()
    mixed_sum.give_beside(branch)
    mixed_sum.join(branch)

    def column(row):
        return jnp.broadcast_to(row, (Q, Q)).T

    def norm_row(stream, chunk):
        first = moments_sum[0, stream, pl.ds(chunk, 1), :]
        return lax.rsqrt(first / CHANNELS + EPS_NORM)

    def scale_step(stream, chunk, carry):
        at = ahead(chunk * Q, Q)
        scale = wide(column(norm_row(stream, chunk)), tiles)
        dp[stream, at, part_of[1]] = (dp[stream, at, part_of[2]].astype(F32) * scale).astype(BF16)
        return carry

    for stream in range(streams):
        hear_moments(0, stream)
        lax.fori_loop(0, chunks, functools.partial(scale_step, stream), 0)
    for stream in range(streams):
        g_tokens[stream].end()
        lax.fori_loop(0, long_tiles, functools.partial(weigh, stream), 0)
        told_moments[1, stream] = tell_moments(1, stream)
    sums[...] = jnp.zeros_like(sums)
    state[...] = jnp.zeros_like(state)
    later[...] = jnp.zeros_like(later)

    def gate_step(stream, chunk, carry):
        at = ahead(chunk * Q, Q)
        scale = norm_row(stream, chunk)
        second = moments_sum[1, stream, pl.ds(chunk, 1), :]
        pull = column(scale * scale * scale * second / CHANNELS)
        scale = column(scale)
        scale, pull = wide(scale, tiles), wide(pull, tiles)
        gate_in = p[stream, at, :channels]
        result = y[stream, at]
        sig = jax.nn.sigmoid(gate_in)
        silu = gate_in * sig
        flat = result * silu
        scaled = flat * scale
        grad = dp[stream, at, part_of[3]].astype(F32)
        grad_flat = scale * g_inner * grad - flat * pull
        p[stream, at, :channels] = grad_flat * silu
        grad_gate = grad_flat * result * (sig * (1.0 + gate_in * (1.0 - sig)))
        dp[stream, at, part_of[0]] = grad_gate.astype(BF16)
        sums[5:6, :channels] += jnp.sum(grad * scaled, axis=0, keepdims=True)
        return carry

    def line_step(j, carry):
        lanes = ahead(j * LINE, LINE)
        total = jnp.zeros((channels, LINE), F32)
        for k in range(streams):
            total = total + mul(dp[k, :, part_of[1]], g[k, :, lanes], ((0,), (0,)))
        lines[:, lanes] = total.astype(BF16)
        return carry

    lax.fori_loop(0, D // LINE, line_step, 0)
    for copy in finish:
        copy.wait_send()
    for each in g_tokens:
        each.settle()
    x_in = pltpu.make_async_copy(x_kept, g, moves.at[4])
    x_in.start()
    tokens = g
    line_sends = []
    for d in range(1, depth):
        theirs = lines.at[ahead(here.plane(d) * out_rows, out_rows)]
        line_sends.append(links.copy(theirs, lines_in.at[d - 1], here.beyond(d)))
        line_sends[-1].start()
    for i in range(2):
        mixed_sum.pass_on(i)
    for stream in range(streams):
        hear_moments(1, stream)
        lax.fori_loop(0, chunks, functools.partial(gate_step, stream), 0)

    def gradient_rows(j, lanes):
        wanted = ahead(j * GROUP, GROUP)
        total = jnp.zeros((GROUP, channels), F32)
        for k in range(streams):
            total = total + mul(tokens[k, :, wanted], dp[k, :, lanes], ((0,), (0,)))
        product = total * w[wanted, lanes].astype(F32)
        folded = product[:, :LANES]
        for i in range(1, tiles):
            folded = folded + product[:, i * LANES : (i + 1) * LANES]
        line = jnp.ones((8, 2 * LANES), BF16)
        gain_sums[:, wanted] += mul(line, jnp.concatenate(halves(folded), axis=1), ((1,), (1,)))
        return total

    gain_sums[...] = jnp.zeros_like(gain_sums)
    def main_group(part, chip):
        total = gradient_rows(chip, part_of[part]).astype(BF16)
        for i in range(GROUP // rows):
            main[part, i % depth, 2 * chip + i // depth] = total[i * rows : (i + 1) * rows]

    def backward_step(stream, k, carry):
        chunk = chunks - 1 - k
        base = pl.multiple_of(chunk * Q, Q)
        at = pl.ds(base, Q)
        seg, seg_row = chunk_places(ends, stream, base)
        raw = chunk_raw(p, par, stream, base)
        rate = jnp.exp(par[8:9, :LANES])
        pre = pre_kept[stream, at].astype(F32)
        front = chunk_front(pre, soft_plus(raw), decay_kept[stream, at], seg, seg_row)
        grad_after = state[stream]
        before = h[stream, chunk].astype(F32)
        after = h[stream, jnp.minimum(chunk + 1, chunks - 1)].astype(F32)
        gv, gb, gc, graw, grate, gskip, gbefore = chunk_backward(
            front,
            raw,
            rate,
            before,
            after,
            grad_after,
            y[stream, at],
            p[stream, at, :channels],
            skip,
        )
        state[stream] = gbefore
        grad_active = jnp.concatenate([gv, gb, gc], axis=1)
        grad_x, head, rows_w = conv_backward(
            front, p[stream, at, channels : channels + mixed], grad_active, later[stream], par
        )
        later[stream] = head
        dp[stream, at, channels : channels + mixed] = grad_x.astype(BF16)
        dp[stream, at, channels + mixed : 3 * channels] = graw.astype(BF16)
        for i, row in enumerate(rows_w):
            sums[i : i + 1, :] += row
        sums[6:7, :channels] += gskip
        sums[7:8, :LANES] += jnp.sum(graw, axis=0, keepdims=True)
        sums[8:9, :LANES] += grate
        if stream:

            @pl.when(k == chunks // 4)
            def _():
                for i in range(2):
                    grad_sums[0].pass_on(i)

        return carry

    def back_of(stream):
        def back(other, lanes):
            rows_at = [block_rows(grad_sums[stream].owner(r, other)) for r in range(4)]
            low = jnp.concatenate([dp[stream, at, projected] for at in rows_at], axis=0)
            return mul(low, w[lanes, :], ((1,), (1,)))

        return back

    x_in.wait()

    def gate_group(j, carry):
        main_group(0, j)
        return carry

    lax.fori_loop(0, D // GROUP, gate_group, 0)
    gate_sends = []
    for d in range(1, depth):
        copy = links.copy(main.at[0, here.plane(d)], gate_in.at[d - 1], here.beyond(d))
        copy.start()
        gate_sends.append(copy)

    lax.fori_loop(0, chunks, functools.partial(backward_step, 0), 0)
    mixed_sum.arrived()
    for stream in range(streams):
        row_scale = column(norm_row(stream, s))

        for i in range(block // FEW):
            span = slice(stream * block + i * FEW, stream * block + (i + 1) * FEW)
            branch_sum = mixed_sum.total(span) * wide(row_scale[i * FEW : (i + 1) * FEW], D // LANES)
            mixed_out[span] = (hidden[span].astype(F32) + branch_sum).astype(BF16)
    mixed_sum.settle()
    for i, k in enumerate((1, 2, 4)):
        pl.semaphore_signal(credit.at[i], inc=1, device_id=here.at(k), device_id_type=MESH)
    for i in range(3):
        pl.semaphore_wait(credit.at[i], 1)
    for stream in range(streams):
        if stream:
            lax.fori_loop(0, chunks, functools.partial(backward_step, stream), 0)
            break
        grad_sums[stream].give_beside(back_of(stream))
        grad_sums[stream].join(back_of(stream))

    slab_sends = []

    def hand_over(part, k):
        if k == 0:
            slabs_recv[part, s] = main[part, f, s]
            return
        copy = links.copy(main.at[part, f, here.peer(k)], slabs_recv.at[part, s], here.at(k))
        copy.start()
        slab_sends.append(copy)

    place = ((wanted_at == column_at + s * share) & (column_at < share)).astype(BF16)

    def common_group(j, carry):
        total = gradient_rows(j, part_of[2]).astype(BF16)
        at = ahead(j * GROUP, GROUP)
        common[at, : 2 * STATE] = total[:, : 2 * STATE]
        common[at, 2 * STATE :] = mul(total[:, 2 * STATE :], place).astype(BF16)
        return carry

    lax.fori_loop(0, D // GROUP, common_group, 0)

    def owned(k):
        return common.at[ahead(here.peer(k) * slab, slab)]

    common_sends = [
        links.copy(owned(2 * r + 1), common_beside.at[r], here.at(1)) for r in range(4)
    ]
    for copy in common_sends:
        copy.start()
    chips = (3, 1, 2, 0)
    common_across = []
    for r in chips:
        if r == 2:
            for copy in common_sends:
                copy.wait_recv()
            for i in chips:
                at = ahead(here.peer(2 * i) * slab, slab)
                joined = common[at, :].astype(F32) + common_beside[i].astype(F32)
                common[at, :] = joined.astype(BF16)
                if i:
                    copy = links.copy(owned(2 * i), common_recv.at[i - 1], here.at(2 * i))
                    copy.start()
                    common_across.append(copy)
        main_group(1, here.peer(2 * r) // 2)

    for i in range(3):
        third = D // 3
        sums[9 + i : 10 + i, :third] = gain_sums[0:1, i * third : (i + 1) * third]
    by_channel = jnp.broadcast_to(sums[6:7, :channels], (8, channels))
    sums[6:7, :LANES] = gather_heads([by_channel], channels)[0][0:1]
    vector_line[f] = sums[...]
    told = [links.copy(sums, vector_line.at[f], here.beyond(d)) for d in range(1, depth)]
    for copy in told:
        copy.start()
    value_sends = {}
    for r in chips:
        pair = pl.ds(2 * (here.peer(2 * r) // 2), 2)
        value_sends[r] = []
        for d in range(1, depth):
            copy = links.copy(
                main.at[1, here.plane(d), pair], main_in.at[d - 1, pair], here.beyond(d)
            )
            copy.start()
            value_sends[r].append(copy)
    grad_own = g.at[0, pl.ds(0, streams * block)]
    grad_again = pltpu.make_async_copy(out_grad, grad_own, moves.at[5])
    grad_again.start()

    def hand_values(r):
        chip = here.peer(2 * r) // 2
        pair = pl.ds(2 * chip, 2)
        total = main[1, f, pair].astype(F32)
        for d in range(1, depth):
            value_sends[r][d - 1].wait_recv()
            total = total + main_in[d - 1, pair].astype(F32)
        main[1, f, pair] = total.astype(BF16)
        for k in (2 * r + 1, 2 * r):
            hand_over(1, k)

    last_stream = streams - 1
    tail = grad_sums[last_stream]
    tail.give_beside(back_of(last_stream))
    tail.join(back_of(last_stream))
    total = main[0, f].astype(F32)
    for d in range(1, depth):
        gate_sends[d - 1].wait_recv()
        total = total + gate_in[d - 1].astype(F32)
    main[0, f] = total.astype(BF16)
    for k in range(1, 8):
        hand_over(0, k)
    hand_over(0, 0)
    for copy in told:
        copy.wait_recv()
    vector_all[s] = jnp.sum(vector_line[...], axis=0).astype(BF16)
    mine_v = vector_all.at[s]
    heard = [links.copy(mine_v, mine_v, here.at(k)) for k in range(1, 8)]
    for copy in heard:
        copy.start()
    for i in range(2):
        tail.pass_on(i)
    hand_values(3)
    grad_again.wait()

    def finish_tokens(stream):
        grad_sums[stream].arrived()
        for i in range(block // FEW):
            span = slice(i * FEW, (i + 1) * FEW)
            at = slice(stream * block + i * FEW, stream * block + (i + 1) * FEW)
            upstream, inverse = scaled_rows(at)
            unit = upstream * inverse
            grad_normed = grad_sums[stream].total(span) * gain
            along = jnp.mean(grad_normed * unit, axis=-1, keepdims=True)
            moved = inverse * (grad_normed - unit * along)
            upstream_out[at] = grad_own[at].astype(F32) + moved

    for k in range(last_stream):
        finish_tokens(k)
    for copy in heard:
        copy.wait_recv()
    vector_full[...] = vector_all[...].astype(F32)
    all_parameters(vec, vector_full, vector_out, share)
    hand_values(1)
    total = lines[ahead(f * out_rows, out_rows), :].astype(F32)
    for d in range(1, depth):
        line_sends[d - 1].wait_recv()
        total = total + lines_in[d - 1].astype(F32)
    lines_out[...] = total.astype(BF16)
    for copy in common_across:
        copy.wait_recv()
    at = ahead(s * slab, slab)
    joined = common[at, :].astype(F32)
    for r in range(3):
        joined = joined + common_recv[r].astype(F32)
    common_line[...] = joined.astype(BF16).reshape(depth, rows, common.shape[1])
    common_sends_z = []
    for d in range(1, depth):
        copy = links.copy(common_line.at[here.plane(d)], common_last.at[d - 1], here.beyond(d))
        copy.start()
        common_sends_z.append(copy)

    hand_values(2)
    finish_tokens(last_stream)
    hand_values(0)
    for copy in slab_sends:
        copy.wait_recv()
    main_moves = []
    for part in range(2):
        for k in range(CHANNELS // channels):
            lanes = slice(part * CHANNELS + k * channels, part * CHANNELS + (k + 1) * channels)
            main_moves.append(
                pltpu.make_async_copy(
                    slabs_recv.at[part, k], main_out.at[:, lanes], moves.at[6 + len(main_moves)]
                )
            )
            main_moves[-1].start()
    for copy in common_sends_z:
        copy.wait_recv()
    total = common_line[f].astype(F32)
    for d in range(1, depth):
        total = total + common_last[d - 1].astype(F32)
    common_sum[...] = total.astype(BF16)
    common_move = pltpu.make_async_copy(
        common_sum, main_out.at[:, 2 * CHANNELS :], moves.at[31]
    )
    common_move.start()
    for each in grad_sums:
        each.settle()
    for r in chips:
        for copy in value_sends[r]:
            copy.wait_send()
    for k in range(8):
        for d in range(depth - 1):
            for way in range(2):
                for part in range(2):
                    pl.when(sends(d)[way])(hops[part, k, d][way].wait_send)
    pending = line_sends + gate_sends + common_sends + told + heard
    for copy in pending + common_across + slab_sends + common_sends_z:
        copy.wait_send()
    for copy in main_moves + [common_move]:
        copy.wait()


def vmem_call(kernel, name, out_shape, out_specs, inputs, in_specs, scratch, vmem_mib):
    return pl.pallas_call(
        kernel,
        out_shape=out_shape,
        in_specs=[pl.BlockSpec(memory_space=space) for space in in_specs],
        out_specs=[pl.BlockSpec(memory_space=space) for space in out_specs],
        scratch_shapes=scratch,
        name=name,
        compiler_params=pltpu.CompilerParams(
            vmem_limit_bytes=vmem_mib << 20, collective_id=0, has_side_effects=True
        ),
    )(*inputs)


def heads_plan(
    hidden_in,
    out_grad,
    lengths,
    in_proj,
    in_first,
    in_second,
    out_proj,
    out_first,
    out_second,
    vector,
    vector_first,
    vector_second,
):
    count = lax.axis_size("seq")
    depth = lax.axis_size("fsdp")
    share = HEADS // count
    channels = share * HEAD_DIM
    mixed = channels + 2 * STATE
    streams, block = hidden_in.shape[0], hidden_in.shape[1]
    length = block * count
    chunks = length // Q
    rows = in_proj.shape[0]
    columns = 3 * channels
    out_rows = out_proj.shape[0]
    across = 2 * STATE + LANES
    slab = depth * rows
    size = vector.shape[0]
    padded = jnp.pad(vector, (0, VECTOR_ROWS * LANES - size)).reshape(VECTOR_ROWS, LANES)
    shape = jax.ShapeDtypeStruct
    dma = pltpu.SemaphoreType.DMA
    low = lambda *dims: pltpu.VMEM(dims, BF16)
    full = lambda *dims: pltpu.VMEM(dims, F32)
    mixed_out, input_grad, main, out_summed, small, _ = vmem_call(
        functools.partial(block_kernel, depth),
        "block",
        [
            shape((streams * block, D), BF16),
            shape((streams * block, D), F32),
            shape((rows, 2 * CHANNELS + across), BF16),
            shape((out_rows, D), BF16),
            shape((VECTOR_ROWS, LANES), F32),
            shape((streams, length, D), BF16),
        ],
        [pltpu.VMEM] * 2 + [pl.ANY] + [pltpu.VMEM] * 2 + [pl.ANY],
        (lengths, hidden_in.reshape(-1, D), out_grad.reshape(-1, D))
        + (in_proj.astype(BF16), out_proj, padded),
        [pltpu.SMEM, pltpu.VMEM, pl.ANY] + [pltpu.VMEM] * 3,
        [
            low(streams, length, D),
            low(streams, length, D),
            low(D, columns),
            low(channels, D),
            full(streams, length, columns),
            full(streams, length, channels),
            low(streams, chunks, STATE, channels),
            low(streams, length, mixed),
            full(streams, length, LANES),
            full(16, mixed),
            full(streams, STATE, channels),
            full(streams, 8, mixed),
            full(16, mixed),
            low(rows, across),
            full(count, 2, streams, chunks, Q),
            full(2, streams, chunks, Q),
            low(4, streams * block, D),
            low(4, streams * block, D),
            low(2, streams * block // 2, D),
            low(2, streams * block, D),
            low(channels, D),
            low(depth - 1, out_rows, D),
            low(2, depth, count, rows, channels),
            low(depth - 1, count, rows, channels),
            low(depth - 1, count, rows, channels),
            low(2, count, rows, channels),
            low(D, across),
            low(4, slab, across),
            low(3, slab, across),
            low(depth, rows, across),
            low(depth - 1, rows, across),
            low(rows, across),
            full(8, D),
            full(depth, 16, mixed),
            low(count, 16, mixed),
            full(count, 16, mixed),
            dma((288,)),
            dma((288,)),
            dma((32,)),
            pltpu.SemaphoreType.REGULAR((3,)),
        ],
        63,
    )
    in_summed = main[:, : in_proj.shape[1]].astype(F32)
    out_summed = out_summed.astype(F32)
    vector_summed = small.reshape(-1)[:size]
    in_new = adam_update(in_proj, in_first, in_second, in_summed, RATE_MATRIX, DECAY_MATRIX)
    out_new = adam_update(out_proj, out_first, out_second, out_summed, RATE_MATRIX, DECAY_MATRIX)
    vec_new = adam_update(vector, vector_first, vector_second, vector_summed, RATE_VECTOR, 0.0)
    mixed_out = mixed_out.reshape(hidden_in.shape)
    input_grad = input_grad.reshape(hidden_in.shape)
    return (mixed_out, input_grad, *in_new, *out_new, *vec_new)


def solution(mesh):
    return jax.shard_map(
        heads_plan if mesh.shape["seq"] == 8 else positions_plan,
        mesh=mesh,
        in_specs=(
            P("fsdp", "seq", None),
            P("fsdp", "seq", None),
            P("fsdp", None),
            P(("seq", "fsdp"), None),
            P(("seq", "fsdp"), None),
            P(("seq", "fsdp"), None),
            P(("seq", "fsdp"), None),
            P(("seq", "fsdp"), None),
            P(("seq", "fsdp"), None),
            P(),
            P(),
            P(),
        ),
        out_specs=(
            P("fsdp", "seq", None),
            P("fsdp", "seq", None),
            P(("seq", "fsdp"), None),
            P(("seq", "fsdp"), None),
            P(("seq", "fsdp"), None),
            P(("seq", "fsdp"), None),
            P(("seq", "fsdp"), None),
            P(("seq", "fsdp"), None),
            P(),
            P(),
            P(),
        ),
        check_vma=False,
    )
```

```python
import functools

import jax
import jax.numpy as jnp
from jax import lax
from jax.experimental import pallas as pl
from jax.experimental.pallas import tpu as pltpu
from jax.sharding import PartitionSpec as P

D = 1536
HEADS = 48
HEAD_DIM = 64
STATE = 128
CONV = 4
STEP = 5


HIGH = lax.Precision.HIGHEST
EPS_NORM = 1e-05
BETA_ONE = 0.9
BETA_TWO = 0.95
ADAM_EPS = 1e-08
RATE_MATRIX = 0.03
RATE_VECTOR = 0.1
DECAY_MATRIX = 0.1


def passed_along(block, axis, distance):
    devices = range(lax.axis_size(axis))
    route = [(i - distance, i) for i in devices if i - distance in devices]
    return lax.ppermute(block, axis, route)


def entering(shard, axis, combine, identity, reverse):
    length, here = (lax.axis_size(axis), lax.axis_index(axis))
    everything = jax.tree.map(
        lambda part, kind: lax.all_gather(part.astype(kind), axis),
        shard,
        jax.tree.map(lambda a: jnp.bfloat16 if a.dtype == jnp.float32 else a.dtype, shard),
    )
    start = jax.tree.map(
        lambda part, zero: jnp.broadcast_to(jnp.asarray(zero, part.dtype), part.shape),
        shard,
        identity,
    )

    def step(k, before):
        at = length - 1 - k if reverse else k
        reached = at > here if reverse else at < here
        new = combine(
            before, jax.tree.map(lambda part, own: part[at].astype(own.dtype), everything, shard)
        )
        return jax.tree.map(lambda a, b: jnp.where(reached, a, b), new, before)

    return lax.fori_loop(0, length, step, start)


def as_sent(shard):
    return jax.tree.map(lambda a: a.astype(jnp.bfloat16) if a.dtype == jnp.float32 else a, shard)


def split_vector(vector):
    inner = HEADS * HEAD_DIM
    width = inner + 2 * STATE
    counts = [D, inner, CONV * width, width, HEADS, HEADS, HEADS]
    pieces = []
    offset = 0
    for amount in counts:
        pieces.append(vector[offset : offset + amount])
        offset += amount
    return (
        pieces[0],
        pieces[1],
        pieces[2].reshape(CONV, width),
        pieces[3],
        pieces[4],
        pieces[5],
        pieces[6],
    )


def rms_norm(value, gain):
    return value * lax.rsqrt(jnp.mean(value * value, axis=-1, keepdims=True) + EPS_NORM) * gain


def segment_ids(lengths, positions):
    ends = jnp.cumsum(lengths, axis=-1, dtype=jnp.int32)
    return jnp.sum(
        (ends[:, None, :] <= positions[None, :, None]).astype(jnp.int32), axis=-1, dtype=jnp.int32
    )


def convolve(padded, seg_ext, conv_w, conv_b):
    count = padded.shape[-2] - (CONV - 1)
    seg_here = seg_ext[..., CONV - 1 :]
    summed = conv_b + jnp.zeros(padded.shape[:-2] + (count, padded.shape[-1]), jnp.float32)
    for tap in range(CONV):
        agree = (seg_ext[..., tap : tap + count] == seg_here).astype(jnp.float32)
        summed = summed + conv_w[tap] * padded[..., tap : tap + count, :] * agree[..., None]
    return jax.nn.silu(summed)


def block_masks(seg, starts):
    order = jnp.arange(seg.shape[-1], dtype=jnp.int32)
    lower = order[:, None] >= order[None, :]
    agree = (lower & (seg[..., :, None] == seg[..., None, :])).astype(jnp.float32)
    keeping = (jnp.cumsum(starts, axis=-1, dtype=jnp.int32) == 0).astype(jnp.float32)
    same_last = (seg == seg[..., -1:]).astype(jnp.float32)
    return (agree, keeping, same_last)


def front_part(seg_ext):

    def front_apply(previous, xbc, dt_raw, conv_w, conv_b, dt_bias, a_log):
        inner = HEADS * HEAD_DIM
        padded = jnp.concatenate([previous, xbc], axis=1)
        active = convolve(padded, seg_ext, conv_w, conv_b)
        values = active[..., :inner].reshape(xbc.shape[0], xbc.shape[1], HEADS, HEAD_DIM)
        b_proj = active[..., inner : inner + STATE]
        c_proj = active[..., inner + STATE :]
        delta = jax.nn.softplus(dt_raw + dt_bias)
        log_decay = -delta * jnp.exp(a_log)
        return (values, b_proj, c_proj, delta, log_decay)

    return front_apply


def summary_part(keeping, same_last):

    def summary_apply(values, b_proj, delta, log_decay):
        cumulative = jnp.cumsum(log_decay, axis=1)
        final = cumulative[:, -1]
        tails = jnp.exp(final[:, None, :] - cumulative) * same_last[:, :, None] * delta
        summed = jnp.einsum("suh,suhp,sun->shpn", tails, values, b_proj, precision=HIGH)
        return (jnp.exp(final) * keeping[:, -1:], summed)

    return summary_apply


def output_part(agree, keeping):

    def output_apply(values, b_proj, c_proj, delta, log_decay, d_skip, carried):
        cumulative = jnp.cumsum(log_decay, axis=1)
        spacing = cumulative[:, :, None, :] - cumulative[:, None, :, :]
        masked = agree[..., None]
        decays = jnp.exp(jnp.where(masked > 0, spacing, 0.0)) * masked
        scores = jnp.einsum("stn,sun->stu", c_proj, b_proj, precision=HIGH)
        weights = decays * scores[..., None] * delta[:, None, :, :]
        result = jnp.einsum("stuh,suhp->sthp", weights, values, precision=HIGH)
        inflow = jnp.exp(cumulative) * keeping[..., None]
        result = (
            result
            + jnp.einsum("stn,shpn->sthp", c_proj, carried, precision=HIGH) * inflow[..., None]
        )
        return result + d_skip[:, None] * values

    return output_apply


def gate_part(mixer_out, gate_in, g_inner):
    flat = mixer_out.reshape(gate_in.shape) * jax.nn.silu(gate_in)
    return rms_norm(flat, g_inner)


def chain_combine(earlier, later):
    return (earlier[0] * later[0], earlier[1] * later[0][..., None, None] + later[1])


def adam_update(weight, moment_one, moment_two, gradient, rate, decay_rate):
    new_first = BETA_ONE * moment_one + (1 - BETA_ONE) * gradient
    new_second = BETA_TWO * moment_two + (1 - BETA_TWO) * gradient * gradient
    corrected = (
        new_first / (1 - BETA_ONE**STEP) / (jnp.sqrt(new_second / (1 - BETA_TWO**STEP)) + ADAM_EPS)
    )
    new_weight = weight - rate * (corrected + decay_rate * weight)
    return (new_first, new_second, new_weight)


def positions_plan(
    hidden_in,
    out_grad,
    lengths,
    in_proj,
    in_first,
    in_second,
    out_proj,
    out_first,
    out_second,
    vector,
    vector_first,
    vector_second,
):
    g_norm, g_inner, conv_w, conv_b, dt_bias, a_log, d_skip = split_vector(vector)
    inner = HEADS * HEAD_DIM
    width = inner + 2 * STATE
    count = hidden_in.shape[1]
    upstream = hidden_in.astype(jnp.float32)
    normed, norm_back = jax.vjp(rms_norm, upstream, g_norm)
    normed_low = normed.astype(jnp.bfloat16)
    in_full, out_full = (
        lax.all_gather(in_proj.astype(jnp.bfloat16), ("seq", "fsdp"), axis=0, tiled=True),
        lax.all_gather(out_proj.astype(jnp.bfloat16), ("seq", "fsdp"), axis=0, tiled=True),
    )
    projected = jnp.einsum("std,dk->stk", normed_low, in_full, preferred_element_type=jnp.float32)
    gate_in = projected[..., :inner]
    xbc = projected[..., inner : inner + width]
    dt_raw = projected[..., inner + width :]
    previous = passed_along(xbc[:, count - (CONV - 1) :].astype(jnp.bfloat16), "seq", 1).astype(
        jnp.float32
    )
    offset_base = lax.axis_index("seq") * count
    positions = offset_base - (CONV - 1) + jnp.arange(count + CONV - 1, dtype=jnp.int32)
    seg_ext = segment_ids(lengths, positions)
    seg_here = seg_ext[:, CONV - 1 :]
    starts = ((seg_here != seg_ext[:, CONV - 2 : -1]) | (positions[None, CONV - 1 :] == 0)).astype(
        jnp.int32
    )
    agree, keeping, same_last = block_masks(seg_here, starts)
    front_pieces, front_back = jax.vjp(
        front_part(seg_ext), previous, xbc, dt_raw, conv_w, conv_b, dt_bias, a_log
    )
    values, b_proj, c_proj, delta, log_decay = front_pieces
    block_pair, summary_back = jax.vjp(
        summary_part(keeping, same_last), values, b_proj, delta, log_decay
    )
    ones_init = jnp.ones_like(block_pair[0])
    zeros_init = jnp.zeros_like(block_pair[1])
    carried = entering(block_pair, "seq", chain_combine, (ones_init, zeros_init), False)[1]
    mixer_out, output_back = jax.vjp(
        output_part(agree, keeping), values, b_proj, c_proj, delta, log_decay, d_skip, carried
    )
    gated, gate_back = jax.vjp(gate_part, mixer_out, gate_in, g_inner)
    gated_low = gated.astype(jnp.bfloat16)
    branch = jnp.einsum("stc,cd->std", gated_low, out_full, preferred_element_type=jnp.float32)
    mixed = (upstream + branch).astype(jnp.bfloat16)
    in_again, out_again = (
        lax.all_gather(in_proj.astype(jnp.bfloat16), ("seq", "fsdp"), axis=0, tiled=True),
        lax.all_gather(out_proj.astype(jnp.bfloat16), ("seq", "fsdp"), axis=0, tiled=True),
    )
    grad_out_proj = jnp.einsum(
        "stc,std->cd", gated_low, out_grad, preferred_element_type=jnp.float32
    )
    grad_gated = jnp.einsum("std,cd->stc", out_grad, out_again, preferred_element_type=jnp.float32)
    grad_mixer, grad_gate_in, grad_g_inner = gate_back(grad_gated)
    grad_values, grad_b, grad_c, grad_delta, grad_log, grad_skip, grad_carried = output_back(
        grad_mixer
    )
    grad_final = entering(
        (block_pair[0], grad_carried), "seq", chain_combine, (ones_init, zeros_init), True
    )[1]
    grad_decay_total = jnp.sum(grad_final * carried, axis=(2, 3))
    more_values, more_b, more_delta, more_log = summary_back((grad_decay_total, grad_final))
    grad_front = (
        grad_values + more_values,
        grad_b + more_b,
        grad_c,
        grad_delta + more_delta,
        grad_log + more_log,
    )
    grad_previous, grad_xbc, grad_dt_raw, grad_conv_w, grad_conv_b, grad_dt_bias, grad_a_log = (
        front_back(grad_front)
    )
    returned = passed_along(as_sent(grad_previous), "seq", -1).astype(grad_previous.dtype)
    grad_xbc = jnp.concatenate(
        [grad_xbc[:, : count - (CONV - 1)], grad_xbc[:, count - (CONV - 1) :] + returned], axis=1
    )
    grad_projected = jnp.concatenate([grad_gate_in, grad_xbc, grad_dt_raw], axis=-1).astype(
        jnp.bfloat16
    )
    grad_in_proj = jnp.einsum(
        "std,stk->dk", normed_low, grad_projected, preferred_element_type=jnp.float32
    )
    grad_normed = jnp.einsum(
        "stk,dk->std", grad_projected, in_again, preferred_element_type=jnp.float32
    )
    grad_upstream, grad_g_norm = norm_back(grad_normed)
    input_grad = out_grad.astype(jnp.float32) + grad_upstream
    in_summed, out_summed = (
        lax.psum_scatter(grad_in_proj, ("seq", "fsdp"), scatter_dimension=0, tiled=True),
        lax.psum_scatter(grad_out_proj, ("seq", "fsdp"), scatter_dimension=0, tiled=True),
    )
    local_vector = jnp.concatenate(
        [
            grad_g_norm,
            grad_g_inner,
            grad_conv_w.reshape(-1),
            grad_conv_b,
            grad_dt_bias,
            grad_a_log,
            grad_skip,
        ]
    )
    vector_summed = lax.psum(local_vector, ("seq", "fsdp"))
    in_new = adam_update(in_proj, in_first, in_second, in_summed, RATE_MATRIX, DECAY_MATRIX)
    out_new = adam_update(out_proj, out_first, out_second, out_summed, RATE_MATRIX, DECAY_MATRIX)
    vec_new = adam_update(vector, vector_first, vector_second, vector_summed, RATE_VECTOR, 0.0)
    return (
        mixed,
        input_grad,
        in_new[0],
        in_new[1],
        in_new[2],
        out_new[0],
        out_new[1],
        out_new[2],
        vec_new[0],
        vec_new[1],
        vec_new[2],
    )


Q = 128
LANES = 128
CHANNELS = HEADS * HEAD_DIM
WIDTH = CHANNELS + 2 * STATE
BF16 = jnp.bfloat16
F32 = jnp.float32


def mul(a, b, dims=((1,), (0,))):
    return lax.dot_general(a, b, (dims, ((), ())), preferred_element_type=F32)


def halves(x):
    high = x.astype(BF16)
    return high, (x - high.astype(F32)).astype(BF16)


def wide(mask, copies):
    return jnp.concatenate([mask] * copies, axis=1)


def head_map(channels):
    head = lax.broadcasted_iota(jnp.int32, (LANES, channels), 0)
    owner = lax.broadcasted_iota(jnp.int32, (LANES, channels), 1) // HEAD_DIM
    return (head == owner).astype(BF16)


def spread(parts, channels):
    stacked = jnp.concatenate([jnp.concatenate(halves(x), axis=1) for x in parts], axis=0)
    one = head_map(channels)
    out = mul(stacked, jnp.concatenate([one, one], axis=0))
    rows = parts[0].shape[0]
    return [out[i * rows : (i + 1) * rows] for i in range(len(parts))]


def gather_heads(parts, channels):
    stacked = jnp.concatenate([jnp.concatenate(halves(x), axis=1) for x in parts], axis=0)
    one = head_map(channels)
    out = mul(stacked, jnp.concatenate([one, one], axis=1), ((1,), (1,)))
    rows = parts[0].shape[0]
    return [out[i * rows : (i + 1) * rows] for i in range(len(parts))]


def running_sum(x, backward):
    t = lax.broadcasted_iota(jnp.int32, (Q, Q), 0)
    u = lax.broadcasted_iota(jnp.int32, (Q, Q), 1)
    tri = ((t <= u) if backward else (t >= u)).astype(BF16)
    return mul(jnp.concatenate([tri, tri], axis=1), jnp.concatenate(halves(x), axis=0))


def segments(ends, stream, positions):
    seg = jnp.zeros(positions.shape, jnp.int32)
    for end in ends[stream]:
        seg = seg + (end <= positions).astype(jnp.int32)
    return jnp.where(positions < 0, -1, seg)


def chunk_places(ends, stream, base):
    column = lax.broadcasted_iota(jnp.int32, (Q + 16, LANES), 0) + (base - 8)
    row = lax.broadcasted_iota(jnp.int32, (8, LANES), 1) + base
    return segments(ends, stream, column), segments(ends, stream, row)[0:1]


def chunk_convolve(p_ref, par_ref, stream, base, seg):
    mixed = par_ref.shape[1]
    channels = mixed - 2 * STATE
    before = pl.multiple_of(jnp.maximum(base - 8, 0), 8)
    xbc = p_ref[stream, pl.ds(base, Q), channels : channels + mixed]
    halo = p_ref[stream, pl.ds(before, 8), channels : channels + mixed]
    both = jnp.concatenate([halo, xbc], axis=0)
    here = seg[8 : Q + 8]
    pre = par_ref[4:5, :] + par_ref[3:4, :] * xbc
    for k in range(CONV - 1):
        agree = (seg[5 + k : Q + 5 + k] == here).astype(F32)
        tap = both[5 + k : Q + 5 + k] * wide(agree, mixed // LANES)
        pre = pre + par_ref[k : k + 1, :] * tap
    return pre


def chunk_raw(p_ref, par_ref, stream, base):
    mixed = par_ref.shape[1]
    at = 2 * mixed - 2 * STATE
    return p_ref[stream, pl.ds(base, Q), at:] + par_ref[7:8, :LANES]


def soft_plus(raw):
    return jnp.maximum(raw, 0.0) + jnp.log1p(jnp.exp(-jnp.abs(raw)))


def chunk_decay(raw, par_ref):
    delta = soft_plus(raw)
    rate = jnp.exp(par_ref[8:9, :LANES])
    return delta, running_sum(-delta * rate, False)


def chunk_front(pre, delta, cumulative, seg, seg_row):
    channels = pre.shape[1] - 2 * STATE
    here = seg[8 : Q + 8]
    gate = jax.nn.sigmoid(pre)
    active = pre * gate
    values = active[:, :channels]
    last = cumulative[Q - 1 : Q]
    keep = (here == seg[7:8]).astype(F32)
    same_last = (here == seg[Q + 7 : Q + 8]).astype(F32)
    inflow = jnp.exp(cumulative) * keep
    tail = jnp.exp(last - cumulative) * same_last
    delta_wide, inflow_wide, tail_wide = spread([delta, inflow, tail], channels)
    t = lax.broadcasted_iota(jnp.int32, (Q, Q), 0)
    u = lax.broadcasted_iota(jnp.int32, (Q, Q), 1)
    mask = (t >= u) & (here == seg_row)
    turned = cumulative.T

    def decays(head):
        spacing = cumulative[:, head : head + 1] - turned[head : head + 1, :]
        return jnp.exp(jnp.where(mask, spacing, -1e30))

    return dict(
        seg=seg,
        pre=pre,
        gate=gate,
        values=values,
        b_low=active[:, channels : channels + STATE].astype(BF16),
        c_low=active[:, channels + STATE :].astype(BF16),
        delta=delta,
        delta_wide=delta_wide,
        inflow_wide=inflow_wide,
        tail_wide=tail_wide,
        scaled=values * delta_wide,
        decays=decays,
        channels=channels,
    )


def two_heads(pair):
    left = lax.broadcasted_iota(jnp.int32, pair.shape, 1) < HEAD_DIM
    low = pair.astype(BF16)
    zero = jnp.zeros_like(low)
    return jnp.concatenate([jnp.where(left, low, zero), jnp.where(left, zero, low)], axis=0)


def chunk_forward(front, state, skip):
    channels = front["channels"]
    scores = mul(front["c_low"], front["b_low"], ((1,), (1,)))
    pieces = []
    for pair in range(channels // LANES):
        weights = jnp.concatenate(
            [(front["decays"](2 * pair + i) * scores).astype(BF16) for i in range(2)], axis=1
        )
        scaled = front["scaled"][:, pair * LANES : (pair + 1) * LANES]
        pieces.append(mul(weights, two_heads(scaled)))
    result = jnp.concatenate(pieces, axis=1)
    result = result + mul(front["c_low"], state.astype(BF16)) * front["inflow_wide"]
    result = result + skip * front["values"]
    fed = (front["scaled"] * front["tail_wide"]).astype(BF16)
    after = front["inflow_wide"][Q - 1 : Q] * state + mul(front["b_low"], fed, ((0,), (0,)))
    return result, after


def chunk_backward(front, raw, rate, before, after, grad_after, result, grad, skip):
    channels = front["channels"]
    b_low, c_low = front["b_low"], front["c_low"]
    scaled, values = front["scaled"], front["values"]
    scores = mul(c_low, b_low, ((1,), (1,)))
    grad_scores = jnp.zeros((Q, Q), F32)
    pieces = []
    for pair in range(channels // LANES):
        lanes = slice(pair * LANES, (pair + 1) * LANES)
        decays = [front["decays"](2 * pair + i) for i in range(2)]
        weights = jnp.concatenate([(d * scores).astype(BF16) for d in decays], axis=0)
        split = two_heads(grad[:, lanes])
        pieces.append(mul(weights, split, ((0,), (0,))))
        cross = mul(split, scaled[:, lanes].astype(BF16), ((1,), (1,)))
        grad_scores = grad_scores + decays[0] * cross[:Q] + decays[1] * cross[Q:]
    grad_after_low = grad_after.astype(BF16)
    inner = jnp.concatenate(pieces, axis=1) + mul(b_low, grad_after_low) * front["tail_wide"]
    fed = (scaled * front["tail_wide"]).astype(BF16)
    flowing = (grad * front["inflow_wide"]).astype(BF16)
    low_scores = grad_scores.astype(BF16)
    grad_c = mul(low_scores, b_low) + mul(flowing, before.astype(BF16), ((1,), (1,)))
    grad_b = mul(low_scores, c_low, ((0,), (0,))) + mul(fed, grad_after_low, ((1,), (1,)))
    grad_values = skip * grad + front["delta_wide"] * inner
    grad_skip = jnp.sum(grad * values, axis=0, keepdims=True)
    held = jnp.sum(after * grad_after, axis=0, keepdims=True)
    grad_delta, grad_cumulative = gather_heads(
        [values * inner, grad * (result - skip * values) - scaled * inner], channels
    )
    held_heads = gather_heads([jnp.broadcast_to(held, (8, channels))], channels)[0][0:1]
    grad_log = running_sum(grad_cumulative, True) + held_heads
    grad_delta = grad_delta - rate * grad_log
    grad_raw = grad_delta * jax.nn.sigmoid(raw)
    grad_rate = -rate * jnp.sum(grad_log * front["delta"], axis=0, keepdims=True)
    grad_before = front["inflow_wide"][Q - 1 : Q] * grad_after + mul(c_low, flowing, ((0,), (0,)))
    return grad_values, grad_b, grad_c, grad_raw, grad_rate, grad_skip, grad_before


def conv_backward(front, xbc, grad_active, next_grad, par_ref):
    gate, pre, seg = front["gate"], front["pre"], front["seg"]
    mixed = pre.shape[1]
    grad_pre = grad_active * (gate * (1.0 + pre * (1.0 - gate)))
    both = jnp.concatenate([grad_pre, next_grad], axis=0)
    grad_x = par_ref[CONV - 1 : CONV, :] * grad_pre
    rows = []
    for k in range(CONV - 1):
        ahead = CONV - 1 - k
        agree = (seg[8 + ahead : Q + 8 + ahead] == seg[8 : Q + 8]).astype(F32)
        moved = both[ahead : Q + ahead] * wide(agree, mixed // LANES)
        grad_x = grad_x + par_ref[k : k + 1, :] * moved
        rows.append(jnp.sum(xbc * moved, axis=0, keepdims=True))
    rows.append(jnp.sum(xbc * grad_pre, axis=0, keepdims=True))
    rows.append(jnp.sum(grad_pre, axis=0, keepdims=True))
    return grad_x, grad_pre[:8], rows


MESH = pl.DeviceIdType.MESH
TILE = 512


class Links:
    def __init__(self, send, recv):
        self.send, self.recv, self.used = send, recv, 0

    def copy(self, source, target, device):
        slot = self.used
        self.used += 1
        assert slot < self.send.shape[0]
        return pltpu.make_async_remote_copy(
            src_ref=source,
            dst_ref=target,
            send_sem=self.send.at[slot],
            recv_sem=self.recv.at[slot],
            device_id=device,
            device_id_type=MESH,
        )


class Place:
    def __init__(self, depth):
        self.s = lax.axis_index("seq")
        self.f = lax.axis_index("fsdp")
        self.depth = depth
        self.core = lax.rem(self.s, 2)
        x = lax.rem(self.s // 2, 2)
        y = self.s // 4
        self.steps = (1 - 2 * self.core, 2 - 4 * x, 4 - 8 * y)

    def peer(self, k):
        index = self.s
        for bit in range(3):
            if k >> bit & 1:
                index = index + self.steps[bit]
        return index

    def at(self, k):
        return (self.peer(k), self.f)

    def plane(self, d):
        return lax.rem(self.f + d, self.depth)

    def beyond(self, d):
        return (self.s, self.plane(d))

    def greet(self):
        barrier = pltpu.get_barrier_semaphore()
        others = [self.at(k) for k in range(1, 8)] + [self.beyond(d) for d in range(1, self.depth)]
        for other in others:
            pl.semaphore_signal(barrier, inc=1, device_id=other, device_id_type=MESH)
        pl.semaphore_wait(barrier, len(others))


def ahead(start, size):
    return pl.ds(pl.multiple_of(start, size), size)


PIECES = [slice(i, i + 512) for i in range(0, D, 512)]
FEW = 64


class Summing:
    def __init__(self, here, links, slots, beside, halves_in, final_in, own):
        self.here, self.slots, self.beside = here, slots, beside
        self.halves_in, self.final_in, self.own = halves_in, final_in, own
        self.count = slots[0].shape[0]
        self.half = self.count // 2
        make = links.copy
        self.to_beside = [make(slots[r], beside[r], here.at(1)) for r in range(4)]
        self.by = [
            make(slots[3].at[self.rows(i)], halves_in[i], here.at(2 << i)) for i in range(2)
        ]
        self.last = [make(slots[1 + i], final_in[i], here.at(2 << i)) for i in range(2)]

    def rows(self, i):
        return pl.ds(i * self.half, self.half)

    def owner(self, r, other):
        return self.here.peer(2 * r + (1 if other else 0))

    def give_beside(self, value):
        for lanes in PIECES:
            found = value(True, lanes).astype(BF16)
            for r in range(4):
                self.slots[r][:, lanes] = found[r * self.count : (r + 1) * self.count]
        for r in (3, 1, 2, 0):
            self.to_beside[r].start()

    def join(self, value):
        for copy in self.to_beside:
            copy.wait()
        targets = [self.own] + self.slots[1:]
        for lanes in PIECES:
            found = value(False, lanes)
            for r in range(4):
                mine = found[r * self.count : (r + 1) * self.count]
                joined = mine + self.beside[r][:, lanes].astype(F32)
                targets[r][:, lanes] = joined.astype(targets[r].dtype)
        for copy in self.by:
            copy.start()

    def pass_on(self, i):
        other = 1 - i
        self.by[other].wait_recv()
        part = self.slots[1 + i].at[self.rows(other)]
        part[...] = (part[...].astype(F32) + self.halves_in[other][...].astype(F32)).astype(BF16)
        self.last[i].start()

    def arrived(self):
        for copy in self.last:
            copy.wait_recv()

    def total(self, rows):
        total = self.own[rows].astype(F32) + self.final_in[0][rows].astype(F32)
        return total + self.final_in[1][rows].astype(F32)

    def settle(self):
        for copy in self.by + self.last:
            copy.wait_send()


class Passing:
    def __init__(self, here, links, blocks, from_below, from_above, depth):
        f, s = here.f, here.s
        self.f, self.depth, self.blocks = f, depth, blocks
        self.came = (from_below, from_above)
        self.copies = []
        for j in range(depth - 1):
            far = depth - 1 - j
            self.copies.append(
                (
                    links.copy(blocks(f + far), from_below.at[far - 1], (s, f + 1)),
                    links.copy(blocks(f - far), from_above.at[far - 1], (s, f - 1)),
                )
            )

    def sends(self, j):
        return (self.f <= j, self.depth - 1 - self.f <= j)

    def gets(self, j):
        return (
            (self.f >= 1) & (self.f <= j + 1),
            (self.f <= self.depth - 2) & (self.depth - 1 - self.f <= j + 1),
        )

    def begin(self):
        for j in range(self.depth - 1):
            pl.when(self.f == 0)(self.copies[j][0].start)
            pl.when(self.f == self.depth - 1)(self.copies[j][1].start)

    def step(self, j):
        far = self.depth - 1 - j
        for way, sign in ((0, 1), (1, -1)):

            @pl.when(self.gets(j - 1)[way])
            def _(way=way, sign=sign):
                self.copies[j - 1][way].wait_recv()
                block = self.blocks(self.f + sign * far)
                block[...] = (
                    block[...].astype(F32) + self.came[way][far].astype(F32)
                ).astype(BF16)
                self.copies[j][way].start()

    def finish(self):
        last = self.depth - 2
        block = self.blocks(self.f)
        for way in range(2):

            @pl.when(self.gets(last)[way])
            def _(way=way):
                self.copies[last][way].wait_recv()
                block[...] = (
                    block[...].astype(F32) + self.came[way][0].astype(F32)
                ).astype(BF16)

    def settle(self):
        for j in range(self.depth - 1):
            for way in range(2):
                pl.when(self.sends(j)[way])(self.copies[j][way].wait_send)


LINE = 512
LONG = 256
GROUP = 384
FIRST_GAIN = 0
FIRST_INNER = D // LANES
FIRST_CONV = FIRST_INNER + CHANNELS // LANES
CONV_ROWS = WIDTH // LANES
SMALL = FIRST_CONV + (CONV + 1) * CONV_ROWS
VECTOR_ROWS = SMALL + 2


def thirds(x):
    high, low = halves(x)
    rest = x - high.astype(F32) - low.astype(F32)
    return high, low, rest.astype(BF16)


def chosen(x, picks):
    return sum(mul(part, picks) for part in thirds(x))


def own_parameters(vec, par, s, share):
    channels = share * HEAD_DIM
    tiles = channels // LANES
    par[...] = jnp.zeros_like(par)
    for k in range(CONV + 1):
        base = FIRST_CONV + k * CONV_ROWS
        for i in range(tiles):
            par[k : k + 1, i * LANES : (i + 1) * LANES] = vec[pl.ds(base + s * tiles + i, 1), :]
        for i in range(2 * STATE // LANES):
            at = channels + i * LANES
            row = base + CHANNELS // LANES + i
            par[k : k + 1, at : at + LANES] = vec[row : row + 1, :]
    for i in range(tiles):
        row = vec[pl.ds(FIRST_INNER + s * tiles + i, 1), :]
        par[5:6, i * LANES : (i + 1) * LANES] = row
    small = jnp.concatenate([vec[SMALL : SMALL + 1, :], vec[SMALL + 1 : SMALL + 2, :]], axis=1)
    small = jnp.broadcast_to(small, (8, 2 * LANES))
    source = lax.broadcasted_iota(jnp.int32, (2 * LANES, LANES), 0)
    lane = lax.broadcasted_iota(jnp.int32, (2 * LANES, LANES), 1)
    found = []
    for which in range(3):
        picks = (source == which * HEADS + s * share + lane) & (lane < share)
        found.append(chosen(small, picks.astype(BF16)))
    par[6:7, :channels] = chosen(found[2], head_map(channels))[0:1]
    par[7:8, :LANES] = found[0][0:1]
    par[8:9, :LANES] = found[1][0:1]


def all_parameters(vec, found, out, share):
    count = found.shape[0]
    channels = share * HEAD_DIM
    tiles = channels // LANES
    out[...] = jnp.zeros_like(out)
    wide_rows = D // 3 // LANES
    for i in range(FIRST_INNER):
        at = (i % wide_rows) * LANES
        row = found[0, 9 + i // wide_rows : 10 + i // wide_rows, at : at + LANES]
        for k in range(1, count):
            row = row + found[k, 9 + i // wide_rows : 10 + i // wide_rows, at : at + LANES]
        out[i : i + 1, :] = row / vec[i : i + 1, :]
    for k in range(count):
        for i in range(tiles):
            lanes = slice(i * LANES, (i + 1) * LANES)
            row = FIRST_INNER + k * tiles + i
            out[row : row + 1, :] = found[k, 5:6, lanes]
            for j in range(CONV + 1):
                row = FIRST_CONV + j * CONV_ROWS + k * tiles + i
                out[row : row + 1, :] = found[k, j : j + 1, lanes]
    for j in range(CONV + 1):
        for i in range(2 * STATE // LANES):
            lanes = slice(channels + i * LANES, channels + (i + 1) * LANES)
            total = found[0, j : j + 1, lanes]
            for k in range(1, count):
                total = total + found[k, j : j + 1, lanes]
            row = FIRST_CONV + j * CONV_ROWS + CHANNELS // LANES + i
            out[row : row + 1, :] = total
    lane = lax.broadcasted_iota(jnp.int32, (8, LANES), 1)
    small = jnp.zeros((8, LANES), F32)
    for k in range(count):
        part = jnp.where(lane < share, found[k, 0:16, :LANES][6:14], 0.0)
        small = small + (pltpu.roll(part, k * share, 1) if k else part)
    skip, step, rate = small[0:1], small[1:2], small[2:3]
    lane = lane[0:1]
    rate = pltpu.roll(small, HEADS, 1)[2:3]
    skip = pltpu.roll(small, 2 * HEADS, 1)[0:1]
    first = jnp.where(lane < HEADS, step, jnp.where(lane < 2 * HEADS, rate, skip))
    out[SMALL : SMALL + 1, :] = first
    out[SMALL + 1 : SMALL + 2, :] = jnp.where(lane < 3 * HEADS - LANES, skip, 0.0)


def block_kernel(
    depth,
    lengths,
    hidden,
    out_grad,
    in_low,
    out_proj,
    vec,
    mixed_out,
    upstream_out,
    main_out,
    lines_out,
    vector_out,
    x_kept,
    x,
    g,
    w,
    wo,
    p,
    y,
    h,
    pre_kept,
    decay_kept,
    par,
    state,
    later,
    sums,
    shared_low,
    moments,
    moments_sum,
    slots,
    beside_in,
    halves_in,
    last_in,
    grad_last,
    lines,
    lines_in,
    main,
    gate_in,
    main_in,
    slabs_recv,
    common,
    common_beside,
    common_recv,
    common_line,
    common_last,
    common_sum,
    gain_sums,
    vector_line,
    vector_all,
    vector_full,
    send,
    recv,
    moves,
    credit,
):
    streams, length = x.shape[0], x.shape[1]
    block = hidden.shape[0] // streams
    chunks = length // Q
    rows = in_low.shape[0]
    out_rows = out_proj.shape[0]
    channels = wo.shape[0]
    share = channels // HEAD_DIM
    mixed = channels + 2 * STATE
    tiles = channels // LANES
    slab = depth * rows
    here = Place(depth)
    s, f = here.s, here.f
    links = Links(send, recv)
    dp = x
    part_of = [slice(i * channels, (i + 1) * channels) for i in range(4)]
    projected = slice(0, 3 * channels)
    ends = []
    for k in range(streams):
        total = lengths[k, 0]
        ends.append([total])
        for i in range(1, lengths.shape[1]):
            total = total + lengths[k, i]
            ends[k].append(total)

    def slab_rows(source, plane):
        return ahead((source * depth + plane) * rows, rows)

    def block_rows(source):
        return ahead(source * block, block)

    finish = []

    def started(copy):
        copy.start()
        finish.append(copy)
        return copy

    narrow = 2 * STATE + HEADS
    shared_low[:, narrow:] = jnp.zeros((rows, shared_low.shape[1] - narrow), BF16)
    shared_low[:, :narrow] = in_low[:, 2 * CHANNELS :]
    here.greet()
    order = (0, 1, 2, 4, 3, 5, 6, 7)
    own = slab_rows(s, f)
    turned = {}
    for part in (1, 0):
        for k in order[1:]:
            lanes = ahead(part * CHANNELS + here.peer(k) * channels, channels)
            turned[part, k] = started(
                links.copy(in_low.at[:, lanes], w.at[own, part_of[part]], here.at(k))
            )
    shared = [
        started(links.copy(shared_low, w.at[own, 2 * channels :], here.beyond(d)))
        for d in range(1, depth)
    ]
    w[own, 2 * channels :] = shared_low[...]
    for part in range(2):
        w[own, part_of[part]] = in_low[:, ahead(part * CHANNELS + s * channels, channels)]
    gain = jnp.concatenate([vec[i : i + 1, :] for i in range(FIRST_INNER)], axis=1)

    def scaled_rows(at):
        upstream = hidden[at, :].astype(F32)
        mean = jnp.mean(upstream * upstream, axis=-1, keepdims=True)
        return upstream, lax.rsqrt(mean + EPS_NORM)

    for stream in range(streams):

        def normalize(i, carry, stream=stream):
            upstream, inverse = scaled_rows(ahead(stream * block + i * FEW, FEW))
            x[stream, ahead(s * block + i * FEW, FEW), :] = (upstream * inverse * gain).astype(BF16)
            return carry

        lax.fori_loop(0, block // FEW, normalize, 0)

    def token_block(ref, stream, k):
        return ref.at[stream, block_rows(here.peer(k))]

    def token_half(ref, stream, way, k):
        rows = block // 2
        return ref.at[stream, ahead(here.peer(k) * block + way * rows, rows)]

    class Tokens:
        def __init__(self, ref, stream):
            self.ref, self.stream = ref, stream
            mine = token_block(ref, stream, 0)
            self.near = [links.copy(mine, mine, here.at(2 << way)) for way in range(2)]
            halves_out = [token_half(ref, stream, way, 2 << way) for way in range(2)]
            self.across = [
                links.copy(halves_out[way], halves_out[way], here.at(4 >> way)) for way in range(2)
            ]
            blocks = [token_block(ref, stream, k) for k in (0, 2, 4)]
            blocks += [token_half(ref, stream, way, 6) for way in range(2)]
            self.beside = [links.copy(part, part, here.at(1)) for part in blocks]

        def begin(self):
            for copy in self.near:
                copy.start()
            self.beside[0].start()

        def go_on(self):
            for way in range(2):
                self.near[way].wait_recv()
                self.across[way].start()
                self.beside[1 + way].start()

        def end(self):
            for way in range(2):
                self.across[way].wait_recv()
                self.beside[3 + way].start()
            for copy in self.beside:
                copy.wait_recv()

        def settle(self):
            for copy in self.near + self.across + self.beside:
                copy.wait_send()

    x_tokens = [Tokens(x, k) for k in range(streams)]
    g_tokens = [Tokens(g, k) for k in range(streams)]
    x_tokens[0].begin()
    g_in = [
        pltpu.make_async_copy(
            out_grad.at[pl.ds(k * block, block)], g.at[k, block_rows(s)], moves.at[2 + k]
        )
        for k in range(streams)
    ]
    for copy in g_in:
        copy.start()
    wo[ahead(f * out_rows, out_rows)] = out_proj[...].astype(BF16)
    own_parameters(vec, par, s, share)

    def hop(part, k, d, up):
        plane = f - d if up else f + d
        target = w.at[slab_rows(here.peer(k), plane), part_of[part]]
        return links.copy(target, target, (s, f + 1 if up else f - 1))

    hops = {}
    for part in range(2):
        for k in range(8):
            for d in range(depth - 1):
                hops[part, k, d] = (hop(part, k, d, True), hop(part, k, d, False))

    def sends(d):
        return ((f >= d) & (f < depth - 1), (f <= depth - 1 - d) & (f > 0))

    def gets(d):
        return (f >= d + 1, f <= depth - 2 - d)

    def launch(part, k, d):
        for way in range(2):
            pl.when(sends(d)[way])(hops[part, k, d][way].start)

    def arrive(part, k, d):
        for way in range(2):
            pl.when(gets(d)[way])(hops[part, k, d][way].wait_recv)

    def first_hops(part):
        for k in order:
            if k:
                turned[part, k].wait_recv()
            launch(part, k, 0)

    def next_hops(part, d):
        for k in order:
            arrive(part, k, d - 1)
            launch(part, k, d)

    def project(stream, parts):
        def tile(i, carry):
            at = ahead(i * TILE, TILE)
            left = x[stream, at, :]
            for lanes in parts:
                p[stream, at, lanes] = mul(left, w[:, lanes])
            return carry

        lax.fori_loop(0, length // TILE, tile, 0)

    first_hops(1)
    for copy in shared:
        copy.wait_recv()
    group = w.at[ahead(s * slab, slab), 2 * channels :]
    spread_common = [links.copy(group, group, here.at(k)) for k in (2, 4, 6, 1)]
    for copy in spread_common:
        copy.start()
    last = depth - 1
    for d in range(1, last):
        if d == last - 1:
            x_tokens[0].go_on()
            for k in range(1, streams):
                x_tokens[k].begin()
            for copy in g_in:
                copy.wait()
            g_tokens[0].begin()
        next_hops(1, d)
    first_hops(0)
    for copy in spread_common[:3]:
        copy.wait_recv()
    for k in (2, 4, 6):
        group = w.at[ahead(here.peer(k) * slab, slab), 2 * channels :]
        spread_common.append(links.copy(group, group, here.at(1)))
        spread_common[-1].start()
    for copy in spread_common[3:]:
        copy.wait_recv()
    for copy in spread_common:
        copy.wait_send()
    column_at = lax.broadcasted_iota(jnp.int32, (LANES, LANES), 0)
    wanted_at = lax.broadcasted_iota(jnp.int32, (LANES, LANES), 1)
    pick = ((column_at == wanted_at + s * share) & (wanted_at < share)).astype(BF16)
    for part in range(0, D, TILE):
        steps = w[part : part + TILE, mixed + channels :]
        w[part : part + TILE, mixed + channels :] = mul(steps, pick).astype(BF16)
    x_out = [
        pltpu.make_async_copy(x.at[k], x_kept.at[k], moves.at[k]) for k in range(streams)
    ]
    x_tokens[0].end()
    x_out[0].start()
    for k in order:
        arrive(1, k, last - 1)
    project(0, part_of[1:3])
    for k in range(1, streams):
        x_tokens[k].go_on()
        g_tokens[k].begin()

    skip = par[6:7, :channels]
    g_inner = par[5:6, :channels]
    state[...] = jnp.zeros_like(state)

    def tell_moments(which, stream):
        mine_m = moments.at[s, which, stream]
        return [started(links.copy(mine_m, mine_m, here.at(k))) for k in range(1, 8)]

    def hear_moments(which, stream):
        for copy in told_moments[which, stream]:
            copy.wait_recv()
        moments_sum[which, stream] = jnp.sum(moments[:, which, stream], axis=0)

    told_moments = {}
    ones = jnp.ones((8, 2 * channels), BF16)

    def forward_step(stream, chunk, carry):
        base = pl.multiple_of(chunk * Q, Q)
        at = pl.ds(base, Q)
        seg, seg_row = chunk_places(ends, stream, base)
        pre = chunk_convolve(p, par, stream, base, seg)
        delta, cumulative = chunk_decay(chunk_raw(p, par, stream, base), par)
        pre_kept[stream, at] = pre.astype(BF16)
        decay_kept[stream, at] = cumulative
        front = chunk_front(pre, delta, cumulative, seg, seg_row)
        before = state[stream]
        h[stream, chunk] = before.astype(BF16)
        result, after = chunk_forward(front, before, skip)
        y[stream, at] = result
        state[stream] = after
        if stream == 0:

            @pl.when(chunk == 2 * chunks // 8)
            def _():
                for d in range(1, last - 1):
                    next_hops(0, d)

        @pl.when(chunk == (5 if stream == 0 else 3) * chunks // 8)
        def _():
            g_tokens[stream].go_on()

        return carry

    def flat_step(stream, chunk, carry):
        at = ahead(chunk * Q, Q)
        gate_in = p[stream, at, :channels]
        flat = y[stream, at] * (gate_in * jax.nn.sigmoid(gate_in))
        dp[stream, at, part_of[2]] = (flat * g_inner).astype(BF16)
        squares = jnp.concatenate(halves(flat * flat), axis=1)
        moments[s, 0, stream, pl.ds(chunk, 1), :] = mul(ones, squares, ((1,), (1,)))[0:1]
        return carry

    lax.fori_loop(0, chunks, functools.partial(forward_step, 0), 0)
    next_hops(0, last - 1)
    lent = wo.at[ahead(f * out_rows, out_rows)]
    outs = [started(links.copy(lent, lent, here.beyond(d))) for d in range(1, depth)]
    for k in range(1, streams):
        x_tokens[k].end()
        x_out[k].start()
        project(k, part_of[1:3])
        lax.fori_loop(0, chunks, functools.partial(forward_step, k), 0)
    for k in order:
        arrive(0, k, last - 1)
    for k in range(streams):
        project(k, part_of[:1])
        x_out[k].wait()
        x_tokens[k].settle()
        lax.fori_loop(0, chunks, functools.partial(flat_step, k), 0)
        told_moments[0, k] = tell_moments(0, k)

    long_tiles = length // TILE
    pieces = TILE // Q

    def weigh(stream, i, carry):
        at = ahead(i * TILE, TILE)
        dp[stream, at, part_of[3]] = mul(g[stream, at], wo[...], ((1,), (1,))).astype(BF16)
        for j in range(pieces):
            at = ahead(i * TILE + j * Q, Q)
            product = dp[stream, at, part_of[3]].astype(F32) * dp[stream, at, part_of[2]].astype(F32)
            found = mul(ones, jnp.concatenate(halves(product), axis=1), ((1,), (1,)))
            moments[s, 1, stream, pl.ds(i * pieces + j, 1), :] = found[0:1]
        return carry

    mixed_sum = Summing(
        here,
        links,
        [slots.at[r] for r in range(4)],
        [beside_in.at[r] for r in range(4)],
        [halves_in.at[i] for i in range(2)],
        [last_in.at[i] for i in range(2)],
        mixed_out,
    )

    def grad_of(stream):
        rows = pl.ds(stream * block, block)
        few = pl.ds(stream * block // 2, block // 2)
        return Summing(
            here,
            links,
            [slots.at[r, rows] for r in range(4)],
            [beside_in.at[r, rows] for r in range(4)],
            [halves_in.at[i, few] for i in range(2)],
            [grad_last.at[i, rows] for i in range(2)],
            upstream_out.at[rows],
        )

    grad_sums = [grad_of(k) for k in range(streams)]

    def branch(other, lanes):
        rows_at = [block_rows(mixed_sum.owner(r, other)) for r in range(4)]
        low = [dp[k, at, part_of[2]] for at in rows_at for k in range(streams)]
        return mul(jnp.concatenate(low, axis=0), wo[:, lanes])

    for copy in outs:
        copy.wait_recv()
    mixed_sum.give_beside(branch)
    mixed_sum.join(branch)

    def column(row):
        return jnp.broadcast_to(row, (Q, Q)).T

    def norm_row(stream, chunk):
        first = moments_sum[0, stream, pl.ds(chunk, 1), :]
        return lax.rsqrt(first / CHANNELS + EPS_NORM)

    def scale_step(stream, chunk, carry):
        at = ahead(chunk * Q, Q)
        scale = wide(column(norm_row(stream, chunk)), tiles)
        dp[stream, at, part_of[1]] = (dp[stream, at, part_of[2]].astype(F32) * scale).astype(BF16)
        return carry

    for stream in range(streams):
        hear_moments(0, stream)
        lax.fori_loop(0, chunks, functools.partial(scale_step, stream), 0)
    for stream in range(streams):
        g_tokens[stream].end()
        lax.fori_loop(0, long_tiles, functools.partial(weigh, stream), 0)
        told_moments[1, stream] = tell_moments(1, stream)
    sums[...] = jnp.zeros_like(sums)
    state[...] = jnp.zeros_like(state)
    later[...] = jnp.zeros_like(later)

    def gate_step(stream, chunk, carry):
        at = ahead(chunk * Q, Q)
        scale = norm_row(stream, chunk)
        second = moments_sum[1, stream, pl.ds(chunk, 1), :]
        pull = column(scale * scale * scale * second / CHANNELS)
        scale = column(scale)
        scale, pull = wide(scale, tiles), wide(pull, tiles)
        gate_in = p[stream, at, :channels]
        result = y[stream, at]
        sig = jax.nn.sigmoid(gate_in)
        silu = gate_in * sig
        flat = result * silu
        scaled = flat * scale
        grad = dp[stream, at, part_of[3]].astype(F32)
        grad_flat = scale * g_inner * grad - flat * pull
        p[stream, at, :channels] = grad_flat * silu
        grad_gate = grad_flat * result * (sig * (1.0 + gate_in * (1.0 - sig)))
        dp[stream, at, part_of[0]] = grad_gate.astype(BF16)
        sums[5:6, :channels] += jnp.sum(grad * scaled, axis=0, keepdims=True)
        return carry

    def line_step(j, carry):
        lanes = ahead(j * LINE, LINE)
        total = jnp.zeros((channels, LINE), F32)
        for k in range(streams):
            total = total + mul(dp[k, :, part_of[1]], g[k, :, lanes], ((0,), (0,)))
        lines[:, lanes] = total.astype(BF16)
        return carry

    lax.fori_loop(0, D // LINE, line_step, 0)
    for copy in finish:
        copy.wait_send()
    for each in g_tokens:
        each.settle()
    x_in = pltpu.make_async_copy(x_kept, g, moves.at[4])
    x_in.start()
    tokens = g
    line_sends = []
    for d in range(1, depth):
        theirs = lines.at[ahead(here.plane(d) * out_rows, out_rows)]
        line_sends.append(links.copy(theirs, lines_in.at[d - 1], here.beyond(d)))
        line_sends[-1].start()
    for i in range(2):
        mixed_sum.pass_on(i)
    for i, k in enumerate((1, 2, 4)):
        pl.semaphore_signal(credit.at[i], inc=1, device_id=here.at(k), device_id_type=MESH)
    for stream in range(streams):
        hear_moments(1, stream)
        lax.fori_loop(0, chunks, functools.partial(gate_step, stream), 0)

    def gradient_rows(j, lanes):
        wanted = ahead(j * GROUP, GROUP)
        total = jnp.zeros((GROUP, channels), F32)
        for k in range(streams):
            total = total + mul(tokens[k, :, wanted], dp[k, :, lanes], ((0,), (0,)))
        product = total * w[wanted, lanes].astype(F32)
        folded = product[:, :LANES]
        for i in range(1, tiles):
            folded = folded + product[:, i * LANES : (i + 1) * LANES]
        line = jnp.ones((8, 2 * LANES), BF16)
        gain_sums[:, wanted] += mul(line, jnp.concatenate(halves(folded), axis=1), ((1,), (1,)))
        return total

    gain_sums[...] = jnp.zeros_like(gain_sums)
    def main_group(part, chip):
        total = gradient_rows(chip, part_of[part]).astype(BF16)
        for i in range(GROUP // rows):
            main[part, i % depth, 2 * chip + i // depth] = total[i * rows : (i + 1) * rows]

    def backward_step(stream, k, carry):
        chunk = chunks - 1 - k
        base = pl.multiple_of(chunk * Q, Q)
        at = pl.ds(base, Q)
        seg, seg_row = chunk_places(ends, stream, base)
        raw = chunk_raw(p, par, stream, base)
        rate = jnp.exp(par[8:9, :LANES])
        pre = pre_kept[stream, at].astype(F32)
        front = chunk_front(pre, soft_plus(raw), decay_kept[stream, at], seg, seg_row)
        grad_after = state[stream]
        before = h[stream, chunk].astype(F32)
        after = h[stream, jnp.minimum(chunk + 1, chunks - 1)].astype(F32)
        gv, gb, gc, graw, grate, gskip, gbefore = chunk_backward(
            front,
            raw,
            rate,
            before,
            after,
            grad_after,
            y[stream, at],
            p[stream, at, :channels],
            skip,
        )
        state[stream] = gbefore
        grad_active = jnp.concatenate([gv, gb, gc], axis=1)
        grad_x, head, rows_w = conv_backward(
            front, p[stream, at, channels : channels + mixed], grad_active, later[stream], par
        )
        later[stream] = head
        dp[stream, at, channels : channels + mixed] = grad_x.astype(BF16)
        dp[stream, at, channels + mixed : 3 * channels] = graw.astype(BF16)
        for i, row in enumerate(rows_w):
            sums[i : i + 1, :] += row
        sums[6:7, :channels] += gskip
        sums[7:8, :LANES] += jnp.sum(graw, axis=0, keepdims=True)
        sums[8:9, :LANES] += grate
        if stream:

            @pl.when(k == 5 * chunks // 8)
            def _():
                for i in range(2):
                    grad_sums[0].pass_on(i)

        return carry

    def back_of(stream):
        def back(other, lanes):
            rows_at = [block_rows(grad_sums[stream].owner(r, other)) for r in range(4)]
            low = jnp.concatenate([dp[stream, at, projected] for at in rows_at], axis=0)
            return mul(low, w[lanes, :], ((1,), (1,)))

        return back

    x_in.wait()

    def gate_group(j, carry):
        main_group(0, j)
        return carry

    lax.fori_loop(0, D // GROUP, gate_group, 0)
    gate_sends = []
    for d in range(1, depth):
        copy = links.copy(main.at[0, here.plane(d)], gate_in.at[d - 1], here.beyond(d))
        copy.start()
        gate_sends.append(copy)

    lax.fori_loop(0, chunks, functools.partial(backward_step, 0), 0)
    mixed_sum.settle()
    for i in range(3):
        pl.semaphore_wait(credit.at[i], 1)
    for stream in range(streams):
        if stream:
            lax.fori_loop(0, chunks, functools.partial(backward_step, stream), 0)
            break
        grad_sums[stream].give_beside(back_of(stream))
        grad_sums[stream].join(back_of(stream))

    slab_sends = []

    def hand_over(part, k):
        if k == 0:
            slabs_recv[part, s] = main[part, f, s]
            return
        copy = links.copy(main.at[part, f, here.peer(k)], slabs_recv.at[part, s], here.at(k))
        copy.start()
        slab_sends.append(copy)

    place = ((wanted_at == column_at + s * share) & (column_at < share)).astype(BF16)

    def common_group(j, carry):
        total = gradient_rows(j, part_of[2]).astype(BF16)
        at = ahead(j * GROUP, GROUP)
        common[at, : 2 * STATE] = total[:, : 2 * STATE]
        common[at, 2 * STATE :] = mul(total[:, 2 * STATE :], place).astype(BF16)
        return carry

    lax.fori_loop(0, D // GROUP, common_group, 0)

    def owned(k):
        return common.at[ahead(here.peer(k) * slab, slab)]

    common_sends = [
        links.copy(owned(2 * r + 1), common_beside.at[r], here.at(1)) for r in range(4)
    ]
    for copy in common_sends:
        copy.start()
    chips = (3, 1, 2, 0)
    common_across = []
    for r in chips:
        if r == 2:
            for copy in common_sends:
                copy.wait_recv()
            for i in chips:
                at = ahead(here.peer(2 * i) * slab, slab)
                joined = common[at, :].astype(F32) + common_beside[i].astype(F32)
                common[at, :] = joined.astype(BF16)
                if i:
                    copy = links.copy(owned(2 * i), common_recv.at[i - 1], here.at(2 * i))
                    copy.start()
                    common_across.append(copy)
        main_group(1, here.peer(2 * r) // 2)

    for i in range(3):
        third = D // 3
        sums[9 + i : 10 + i, :third] = gain_sums[0:1, i * third : (i + 1) * third]
    by_channel = jnp.broadcast_to(sums[6:7, :channels], (8, channels))
    sums[6:7, :LANES] = gather_heads([by_channel], channels)[0][0:1]
    vector_line[f] = sums[...]
    told = [links.copy(sums, vector_line.at[f], here.beyond(d)) for d in range(1, depth)]
    for copy in told:
        copy.start()
    value_sends = {}
    for r in chips:
        pair = pl.ds(2 * (here.peer(2 * r) // 2), 2)
        value_sends[r] = []
        for d in range(1, depth):
            copy = links.copy(
                main.at[1, here.plane(d), pair], main_in.at[d - 1, pair], here.beyond(d)
            )
            copy.start()
            value_sends[r].append(copy)
    grad_own = g.at[0, pl.ds(0, streams * block)]
    grad_again = pltpu.make_async_copy(out_grad, grad_own, moves.at[5])
    grad_again.start()

    def hand_values(r):
        chip = here.peer(2 * r) // 2
        pair = pl.ds(2 * chip, 2)
        total = main[1, f, pair].astype(F32)
        for d in range(1, depth):
            value_sends[r][d - 1].wait_recv()
            total = total + main_in[d - 1, pair].astype(F32)
        main[1, f, pair] = total.astype(BF16)
        for k in (2 * r + 1, 2 * r):
            hand_over(1, k)

    last_stream = streams - 1
    tail = grad_sums[last_stream]
    tail.give_beside(back_of(last_stream))
    tail.join(back_of(last_stream))
    total = main[0, f].astype(F32)
    for d in range(1, depth):
        gate_sends[d - 1].wait_recv()
        total = total + gate_in[d - 1].astype(F32)
    main[0, f] = total.astype(BF16)
    for k in range(1, 8):
        hand_over(0, k)
    hand_over(0, 0)
    for copy in told:
        copy.wait_recv()
    vector_all[s] = jnp.sum(vector_line[...], axis=0).astype(BF16)
    mine_v = vector_all.at[s]
    heard = [links.copy(mine_v, mine_v, here.at(k)) for k in range(1, 8)]
    for copy in heard:
        copy.start()
    mixed_sum.arrived()
    for stream in range(streams):
        row_scale = column(norm_row(stream, s))

        for i in range(block // FEW):
            span = slice(stream * block + i * FEW, stream * block + (i + 1) * FEW)
            branch_sum = mixed_sum.total(span) * wide(row_scale[i * FEW : (i + 1) * FEW], D // LANES)
            mixed_out[span] = (hidden[span].astype(F32) + branch_sum).astype(BF16)
    for i in range(2):
        tail.pass_on(i)
    hand_values(3)
    grad_again.wait()

    def finish_tokens(stream):
        grad_sums[stream].arrived()
        for i in range(block // FEW):
            span = slice(i * FEW, (i + 1) * FEW)
            at = slice(stream * block + i * FEW, stream * block + (i + 1) * FEW)
            upstream, inverse = scaled_rows(at)
            unit = upstream * inverse
            grad_normed = grad_sums[stream].total(span) * gain
            along = jnp.mean(grad_normed * unit, axis=-1, keepdims=True)
            moved = inverse * (grad_normed - unit * along)
            upstream_out[at] = grad_own[at].astype(F32) + moved

    for k in range(last_stream):
        finish_tokens(k)
    for copy in heard:
        copy.wait_recv()
    vector_full[...] = vector_all[...].astype(F32)
    all_parameters(vec, vector_full, vector_out, share)
    hand_values(1)
    total = lines[ahead(f * out_rows, out_rows), :].astype(F32)
    for d in range(1, depth):
        line_sends[d - 1].wait_recv()
        total = total + lines_in[d - 1].astype(F32)
    lines_out[...] = total.astype(BF16)
    for copy in common_across:
        copy.wait_recv()
    at = ahead(s * slab, slab)
    joined = common[at, :].astype(F32)
    for r in range(3):
        joined = joined + common_recv[r].astype(F32)
    common_line[...] = joined.astype(BF16).reshape(depth, rows, common.shape[1])
    common_sends_z = []
    for d in range(1, depth):
        copy = links.copy(common_line.at[here.plane(d)], common_last.at[d - 1], here.beyond(d))
        copy.start()
        common_sends_z.append(copy)

    hand_values(2)
    finish_tokens(last_stream)
    hand_values(0)
    for copy in slab_sends:
        copy.wait_recv()
    main_moves = []
    for part in range(2):
        for k in range(CHANNELS // channels):
            lanes = slice(part * CHANNELS + k * channels, part * CHANNELS + (k + 1) * channels)
            main_moves.append(
                pltpu.make_async_copy(
                    slabs_recv.at[part, k], main_out.at[:, lanes], moves.at[6 + len(main_moves)]
                )
            )
            main_moves[-1].start()
    for copy in common_sends_z:
        copy.wait_recv()
    total = common_line[f].astype(F32)
    for d in range(1, depth):
        total = total + common_last[d - 1].astype(F32)
    common_sum[...] = total.astype(BF16)
    common_move = pltpu.make_async_copy(
        common_sum, main_out.at[:, 2 * CHANNELS :], moves.at[31]
    )
    common_move.start()
    for each in grad_sums:
        each.settle()
    for r in chips:
        for copy in value_sends[r]:
            copy.wait_send()
    for k in range(8):
        for d in range(depth - 1):
            for way in range(2):
                for part in range(2):
                    pl.when(sends(d)[way])(hops[part, k, d][way].wait_send)
    pending = line_sends + gate_sends + common_sends + told + heard
    for copy in pending + common_across + slab_sends + common_sends_z:
        copy.wait_send()
    for copy in main_moves + [common_move]:
        copy.wait()


def vmem_call(kernel, name, out_shape, out_specs, inputs, in_specs, scratch, vmem_mib):
    return pl.pallas_call(
        kernel,
        out_shape=out_shape,
        in_specs=[pl.BlockSpec(memory_space=space) for space in in_specs],
        out_specs=[pl.BlockSpec(memory_space=space) for space in out_specs],
        scratch_shapes=scratch,
        name=name,
        compiler_params=pltpu.CompilerParams(
            vmem_limit_bytes=vmem_mib << 20, collective_id=0, has_side_effects=True
        ),
    )(*inputs)


def heads_plan(
    hidden_in,
    out_grad,
    lengths,
    in_proj,
    in_first,
    in_second,
    out_proj,
    out_first,
    out_second,
    vector,
    vector_first,
    vector_second,
):
    count = lax.axis_size("seq")
    depth = lax.axis_size("fsdp")
    share = HEADS // count
    channels = share * HEAD_DIM
    mixed = channels + 2 * STATE
    streams, block = hidden_in.shape[0], hidden_in.shape[1]
    length = block * count
    chunks = length // Q
    rows = in_proj.shape[0]
    columns = 3 * channels
    out_rows = out_proj.shape[0]
    across = 2 * STATE + LANES
    slab = depth * rows
    size = vector.shape[0]
    padded = jnp.pad(vector, (0, VECTOR_ROWS * LANES - size)).reshape(VECTOR_ROWS, LANES)
    shape = jax.ShapeDtypeStruct
    dma = pltpu.SemaphoreType.DMA
    low = lambda *dims: pltpu.VMEM(dims, BF16)
    full = lambda *dims: pltpu.VMEM(dims, F32)
    mixed_out, input_grad, main, out_summed, small, _ = vmem_call(
        functools.partial(block_kernel, depth),
        "block",
        [
            shape((streams * block, D), BF16),
            shape((streams * block, D), F32),
            shape((rows, 2 * CHANNELS + across), BF16),
            shape((out_rows, D), BF16),
            shape((VECTOR_ROWS, LANES), F32),
            shape((streams, length, D), BF16),
        ],
        [pltpu.VMEM] * 2 + [pl.ANY] + [pltpu.VMEM] * 2 + [pl.ANY],
        (lengths, hidden_in.reshape(-1, D), out_grad.reshape(-1, D))
        + (in_proj.astype(BF16), out_proj, padded),
        [pltpu.SMEM, pltpu.VMEM, pl.ANY] + [pltpu.VMEM] * 3,
        [
            low(streams, length, D),
            low(streams, length, D),
            low(D, columns),
            low(channels, D),
            full(streams, length, columns),
            full(streams, length, channels),
            low(streams, chunks, STATE, channels),
            low(streams, length, mixed),
            full(streams, length, LANES),
            full(16, mixed),
            full(streams, STATE, channels),
            full(streams, 8, mixed),
            full(16, mixed),
            low(rows, across),
            full(count, 2, streams, chunks, Q),
            full(2, streams, chunks, Q),
            low(4, streams * block, D),
            low(4, streams * block, D),
            low(2, streams * block // 2, D),
            low(2, streams * block, D),
            low(2, streams * block, D),
            low(channels, D),
            low(depth - 1, out_rows, D),
            low(2, depth, count, rows, channels),
            low(depth - 1, count, rows, channels),
            low(depth - 1, count, rows, channels),
            low(2, count, rows, channels),
            low(D, across),
            low(4, slab, across),
            low(3, slab, across),
            low(depth, rows, across),
            low(depth - 1, rows, across),
            low(rows, across),
            full(8, D),
            full(depth, 16, mixed),
            low(count, 16, mixed),
            full(count, 16, mixed),
            dma((288,)),
            dma((288,)),
            dma((32,)),
            pltpu.SemaphoreType.REGULAR((3,)),
        ],
        63,
    )
    in_summed = main[:, : in_proj.shape[1]].astype(F32)
    out_summed = out_summed.astype(F32)
    vector_summed = small.reshape(-1)[:size]
    in_new = adam_update(in_proj, in_first, in_second, in_summed, RATE_MATRIX, DECAY_MATRIX)
    out_new = adam_update(out_proj, out_first, out_second, out_summed, RATE_MATRIX, DECAY_MATRIX)
    vec_new = adam_update(vector, vector_first, vector_second, vector_summed, RATE_VECTOR, 0.0)
    mixed_out = mixed_out.reshape(hidden_in.shape)
    input_grad = input_grad.reshape(hidden_in.shape)
    return (mixed_out, input_grad, *in_new, *out_new, *vec_new)


def solution(mesh):
    return jax.shard_map(
        heads_plan if mesh.shape["seq"] == 8 else positions_plan,
        mesh=mesh,
        in_specs=(
            P("fsdp", "seq", None),
            P("fsdp", "seq", None),
            P("fsdp", None),
            P(("seq", "fsdp"), None),
            P(("seq", "fsdp"), None),
            P(("seq", "fsdp"), None),
            P(("seq", "fsdp"), None),
            P(("seq", "fsdp"), None),
            P(("seq", "fsdp"), None),
            P(),
            P(),
            P(),
        ),
        out_specs=(
            P("fsdp", "seq", None),
            P("fsdp", "seq", None),
            P(("seq", "fsdp"), None),
            P(("seq", "fsdp"), None),
            P(("seq", "fsdp"), None),
            P(("seq", "fsdp"), None),
            P(("seq", "fsdp"), None),
            P(("seq", "fsdp"), None),
            P(),
            P(),
            P(),
        ),
        check_vma=False,
    )
```

```python
import functools

import jax
import jax.numpy as jnp
from jax import lax
from jax.experimental import pallas as pl
from jax.experimental.pallas import tpu as pltpu
from jax.sharding import PartitionSpec as P

D = 1536
HEADS = 48
HEAD_DIM = 64
STATE = 128
CONV = 4
STEP = 5


HIGH = lax.Precision.HIGHEST
EPS_NORM = 1e-05
BETA_ONE = 0.9
BETA_TWO = 0.95
ADAM_EPS = 1e-08
RATE_MATRIX = 0.03
RATE_VECTOR = 0.1
DECAY_MATRIX = 0.1


def passed_along(block, axis, distance):
    devices = range(lax.axis_size(axis))
    route = [(i - distance, i) for i in devices if i - distance in devices]
    return lax.ppermute(block, axis, route)


def entering(shard, axis, combine, identity, reverse):
    length, here = (lax.axis_size(axis), lax.axis_index(axis))
    everything = jax.tree.map(
        lambda part, kind: lax.all_gather(part.astype(kind), axis),
        shard,
        jax.tree.map(lambda a: jnp.bfloat16 if a.dtype == jnp.float32 else a.dtype, shard),
    )
    start = jax.tree.map(
        lambda part, zero: jnp.broadcast_to(jnp.asarray(zero, part.dtype), part.shape),
        shard,
        identity,
    )

    def step(k, before):
        at = length - 1 - k if reverse else k
        reached = at > here if reverse else at < here
        new = combine(
            before, jax.tree.map(lambda part, own: part[at].astype(own.dtype), everything, shard)
        )
        return jax.tree.map(lambda a, b: jnp.where(reached, a, b), new, before)

    return lax.fori_loop(0, length, step, start)


def as_sent(shard):
    return jax.tree.map(lambda a: a.astype(jnp.bfloat16) if a.dtype == jnp.float32 else a, shard)


def split_vector(vector):
    inner = HEADS * HEAD_DIM
    width = inner + 2 * STATE
    counts = [D, inner, CONV * width, width, HEADS, HEADS, HEADS]
    pieces = []
    offset = 0
    for amount in counts:
        pieces.append(vector[offset : offset + amount])
        offset += amount
    return (
        pieces[0],
        pieces[1],
        pieces[2].reshape(CONV, width),
        pieces[3],
        pieces[4],
        pieces[5],
        pieces[6],
    )


def rms_norm(value, gain):
    return value * lax.rsqrt(jnp.mean(value * value, axis=-1, keepdims=True) + EPS_NORM) * gain


def segment_ids(lengths, positions):
    ends = jnp.cumsum(lengths, axis=-1, dtype=jnp.int32)
    return jnp.sum(
        (ends[:, None, :] <= positions[None, :, None]).astype(jnp.int32), axis=-1, dtype=jnp.int32
    )


def convolve(padded, seg_ext, conv_w, conv_b):
    count = padded.shape[-2] - (CONV - 1)
    seg_here = seg_ext[..., CONV - 1 :]
    summed = conv_b + jnp.zeros(padded.shape[:-2] + (count, padded.shape[-1]), jnp.float32)
    for tap in range(CONV):
        agree = (seg_ext[..., tap : tap + count] == seg_here).astype(jnp.float32)
        summed = summed + conv_w[tap] * padded[..., tap : tap + count, :] * agree[..., None]
    return jax.nn.silu(summed)


def block_masks(seg, starts):
    order = jnp.arange(seg.shape[-1], dtype=jnp.int32)
    lower = order[:, None] >= order[None, :]
    agree = (lower & (seg[..., :, None] == seg[..., None, :])).astype(jnp.float32)
    keeping = (jnp.cumsum(starts, axis=-1, dtype=jnp.int32) == 0).astype(jnp.float32)
    same_last = (seg == seg[..., -1:]).astype(jnp.float32)
    return (agree, keeping, same_last)


def front_part(seg_ext):

    def front_apply(previous, xbc, dt_raw, conv_w, conv_b, dt_bias, a_log):
        inner = HEADS * HEAD_DIM
        padded = jnp.concatenate([previous, xbc], axis=1)
        active = convolve(padded, seg_ext, conv_w, conv_b)
        values = active[..., :inner].reshape(xbc.shape[0], xbc.shape[1], HEADS, HEAD_DIM)
        b_proj = active[..., inner : inner + STATE]
        c_proj = active[..., inner + STATE :]
        delta = jax.nn.softplus(dt_raw + dt_bias)
        log_decay = -delta * jnp.exp(a_log)
        return (values, b_proj, c_proj, delta, log_decay)

    return front_apply


def summary_part(keeping, same_last):

    def summary_apply(values, b_proj, delta, log_decay):
        cumulative = jnp.cumsum(log_decay, axis=1)
        final = cumulative[:, -1]
        tails = jnp.exp(final[:, None, :] - cumulative) * same_last[:, :, None] * delta
        summed = jnp.einsum("suh,suhp,sun->shpn", tails, values, b_proj, precision=HIGH)
        return (jnp.exp(final) * keeping[:, -1:], summed)

    return summary_apply


def output_part(agree, keeping):

    def output_apply(values, b_proj, c_proj, delta, log_decay, d_skip, carried):
        cumulative = jnp.cumsum(log_decay, axis=1)
        spacing = cumulative[:, :, None, :] - cumulative[:, None, :, :]
        masked = agree[..., None]
        decays = jnp.exp(jnp.where(masked > 0, spacing, 0.0)) * masked
        scores = jnp.einsum("stn,sun->stu", c_proj, b_proj, precision=HIGH)
        weights = decays * scores[..., None] * delta[:, None, :, :]
        result = jnp.einsum("stuh,suhp->sthp", weights, values, precision=HIGH)
        inflow = jnp.exp(cumulative) * keeping[..., None]
        result = (
            result
            + jnp.einsum("stn,shpn->sthp", c_proj, carried, precision=HIGH) * inflow[..., None]
        )
        return result + d_skip[:, None] * values

    return output_apply


def gate_part(mixer_out, gate_in, g_inner):
    flat = mixer_out.reshape(gate_in.shape) * jax.nn.silu(gate_in)
    return rms_norm(flat, g_inner)


def chain_combine(earlier, later):
    return (earlier[0] * later[0], earlier[1] * later[0][..., None, None] + later[1])


def adam_update(weight, moment_one, moment_two, gradient, rate, decay_rate):
    new_first = BETA_ONE * moment_one + (1 - BETA_ONE) * gradient
    new_second = BETA_TWO * moment_two + (1 - BETA_TWO) * gradient * gradient
    corrected = (
        new_first / (1 - BETA_ONE**STEP) / (jnp.sqrt(new_second / (1 - BETA_TWO**STEP)) + ADAM_EPS)
    )
    new_weight = weight - rate * (corrected + decay_rate * weight)
    return (new_first, new_second, new_weight)


def positions_plan(
    hidden_in,
    out_grad,
    lengths,
    in_proj,
    in_first,
    in_second,
    out_proj,
    out_first,
    out_second,
    vector,
    vector_first,
    vector_second,
):
    g_norm, g_inner, conv_w, conv_b, dt_bias, a_log, d_skip = split_vector(vector)
    inner = HEADS * HEAD_DIM
    width = inner + 2 * STATE
    count = hidden_in.shape[1]
    upstream = hidden_in.astype(jnp.float32)
    normed, norm_back = jax.vjp(rms_norm, upstream, g_norm)
    normed_low = normed.astype(jnp.bfloat16)
    in_full, out_full = (
        lax.all_gather(in_proj.astype(jnp.bfloat16), ("seq", "fsdp"), axis=0, tiled=True),
        lax.all_gather(out_proj.astype(jnp.bfloat16), ("seq", "fsdp"), axis=0, tiled=True),
    )
    projected = jnp.einsum("std,dk->stk", normed_low, in_full, preferred_element_type=jnp.float32)
    gate_in = projected[..., :inner]
    xbc = projected[..., inner : inner + width]
    dt_raw = projected[..., inner + width :]
    previous = passed_along(xbc[:, count - (CONV - 1) :].astype(jnp.bfloat16), "seq", 1).astype(
        jnp.float32
    )
    offset_base = lax.axis_index("seq") * count
    positions = offset_base - (CONV - 1) + jnp.arange(count + CONV - 1, dtype=jnp.int32)
    seg_ext = segment_ids(lengths, positions)
    seg_here = seg_ext[:, CONV - 1 :]
    starts = ((seg_here != seg_ext[:, CONV - 2 : -1]) | (positions[None, CONV - 1 :] == 0)).astype(
        jnp.int32
    )
    agree, keeping, same_last = block_masks(seg_here, starts)
    front_pieces, front_back = jax.vjp(
        front_part(seg_ext), previous, xbc, dt_raw, conv_w, conv_b, dt_bias, a_log
    )
    values, b_proj, c_proj, delta, log_decay = front_pieces
    block_pair, summary_back = jax.vjp(
        summary_part(keeping, same_last), values, b_proj, delta, log_decay
    )
    ones_init = jnp.ones_like(block_pair[0])
    zeros_init = jnp.zeros_like(block_pair[1])
    carried = entering(block_pair, "seq", chain_combine, (ones_init, zeros_init), False)[1]
    mixer_out, output_back = jax.vjp(
        output_part(agree, keeping), values, b_proj, c_proj, delta, log_decay, d_skip, carried
    )
    gated, gate_back = jax.vjp(gate_part, mixer_out, gate_in, g_inner)
    gated_low = gated.astype(jnp.bfloat16)
    branch = jnp.einsum("stc,cd->std", gated_low, out_full, preferred_element_type=jnp.float32)
    mixed = (upstream + branch).astype(jnp.bfloat16)
    in_again, out_again = (
        lax.all_gather(in_proj.astype(jnp.bfloat16), ("seq", "fsdp"), axis=0, tiled=True),
        lax.all_gather(out_proj.astype(jnp.bfloat16), ("seq", "fsdp"), axis=0, tiled=True),
    )
    grad_out_proj = jnp.einsum(
        "stc,std->cd", gated_low, out_grad, preferred_element_type=jnp.float32
    )
    grad_gated = jnp.einsum("std,cd->stc", out_grad, out_again, preferred_element_type=jnp.float32)
    grad_mixer, grad_gate_in, grad_g_inner = gate_back(grad_gated)
    grad_values, grad_b, grad_c, grad_delta, grad_log, grad_skip, grad_carried = output_back(
        grad_mixer
    )
    grad_final = entering(
        (block_pair[0], grad_carried), "seq", chain_combine, (ones_init, zeros_init), True
    )[1]
    grad_decay_total = jnp.sum(grad_final * carried, axis=(2, 3))
    more_values, more_b, more_delta, more_log = summary_back((grad_decay_total, grad_final))
    grad_front = (
        grad_values + more_values,
        grad_b + more_b,
        grad_c,
        grad_delta + more_delta,
        grad_log + more_log,
    )
    grad_previous, grad_xbc, grad_dt_raw, grad_conv_w, grad_conv_b, grad_dt_bias, grad_a_log = (
        front_back(grad_front)
    )
    returned = passed_along(as_sent(grad_previous), "seq", -1).astype(grad_previous.dtype)
    grad_xbc = jnp.concatenate(
        [grad_xbc[:, : count - (CONV - 1)], grad_xbc[:, count - (CONV - 1) :] + returned], axis=1
    )
    grad_projected = jnp.concatenate([grad_gate_in, grad_xbc, grad_dt_raw], axis=-1).astype(
        jnp.bfloat16
    )
    grad_in_proj = jnp.einsum(
        "std,stk->dk", normed_low, grad_projected, preferred_element_type=jnp.float32
    )
    grad_normed = jnp.einsum(
        "stk,dk->std", grad_projected, in_again, preferred_element_type=jnp.float32
    )
    grad_upstream, grad_g_norm = norm_back(grad_normed)
    input_grad = out_grad.astype(jnp.float32) + grad_upstream
    in_summed, out_summed = (
        lax.psum_scatter(grad_in_proj, ("seq", "fsdp"), scatter_dimension=0, tiled=True),
        lax.psum_scatter(grad_out_proj, ("seq", "fsdp"), scatter_dimension=0, tiled=True),
    )
    local_vector = jnp.concatenate(
        [
            grad_g_norm,
            grad_g_inner,
            grad_conv_w.reshape(-1),
            grad_conv_b,
            grad_dt_bias,
            grad_a_log,
            grad_skip,
        ]
    )
    vector_summed = lax.psum(local_vector, ("seq", "fsdp"))
    in_new = adam_update(in_proj, in_first, in_second, in_summed, RATE_MATRIX, DECAY_MATRIX)
    out_new = adam_update(out_proj, out_first, out_second, out_summed, RATE_MATRIX, DECAY_MATRIX)
    vec_new = adam_update(vector, vector_first, vector_second, vector_summed, RATE_VECTOR, 0.0)
    return (
        mixed,
        input_grad,
        in_new[0],
        in_new[1],
        in_new[2],
        out_new[0],
        out_new[1],
        out_new[2],
        vec_new[0],
        vec_new[1],
        vec_new[2],
    )


Q = 128
LANES = 128
CHANNELS = HEADS * HEAD_DIM
WIDTH = CHANNELS + 2 * STATE
BF16 = jnp.bfloat16
F32 = jnp.float32


def mul(a, b, dims=((1,), (0,))):
    return lax.dot_general(a, b, (dims, ((), ())), preferred_element_type=F32)


def halves(x):
    high = x.astype(BF16)
    return high, (x - high.astype(F32)).astype(BF16)


def wide(mask, copies):
    return jnp.concatenate([mask] * copies, axis=1)


def head_map(channels):
    head = lax.broadcasted_iota(jnp.int32, (LANES, channels), 0)
    owner = lax.broadcasted_iota(jnp.int32, (LANES, channels), 1) // HEAD_DIM
    return (head == owner).astype(BF16)


def spread(parts, channels):
    stacked = jnp.concatenate([jnp.concatenate(halves(x), axis=1) for x in parts], axis=0)
    one = head_map(channels)
    out = mul(stacked, jnp.concatenate([one, one], axis=0))
    rows = parts[0].shape[0]
    return [out[i * rows : (i + 1) * rows] for i in range(len(parts))]


def gather_heads(parts, channels):
    stacked = jnp.concatenate([jnp.concatenate(halves(x), axis=1) for x in parts], axis=0)
    one = head_map(channels)
    out = mul(stacked, jnp.concatenate([one, one], axis=1), ((1,), (1,)))
    rows = parts[0].shape[0]
    return [out[i * rows : (i + 1) * rows] for i in range(len(parts))]


def running_sum(x, backward):
    t = lax.broadcasted_iota(jnp.int32, (Q, Q), 0)
    u = lax.broadcasted_iota(jnp.int32, (Q, Q), 1)
    tri = ((t <= u) if backward else (t >= u)).astype(BF16)
    return mul(jnp.concatenate([tri, tri], axis=1), jnp.concatenate(halves(x), axis=0))


def segments(ends, stream, positions):
    seg = jnp.zeros(positions.shape, jnp.int32)
    for end in ends[stream]:
        seg = seg + (end <= positions).astype(jnp.int32)
    return jnp.where(positions < 0, -1, seg)


def chunk_places(ends, stream, base):
    column = lax.broadcasted_iota(jnp.int32, (Q + 16, LANES), 0) + (base - 8)
    row = lax.broadcasted_iota(jnp.int32, (8, LANES), 1) + base
    return segments(ends, stream, column), segments(ends, stream, row)[0:1]


def chunk_convolve(p_ref, par_ref, stream, base, seg):
    mixed = par_ref.shape[1]
    channels = mixed - 2 * STATE
    before = pl.multiple_of(jnp.maximum(base - 8, 0), 8)
    xbc = p_ref[stream, pl.ds(base, Q), channels : channels + mixed]
    halo = p_ref[stream, pl.ds(before, 8), channels : channels + mixed]
    both = jnp.concatenate([halo, xbc], axis=0)
    here = seg[8 : Q + 8]
    pre = par_ref[4:5, :] + par_ref[3:4, :] * xbc
    for k in range(CONV - 1):
        agree = (seg[5 + k : Q + 5 + k] == here).astype(F32)
        tap = both[5 + k : Q + 5 + k] * wide(agree, mixed // LANES)
        pre = pre + par_ref[k : k + 1, :] * tap
    return pre


def chunk_raw(p_ref, par_ref, stream, base):
    mixed = par_ref.shape[1]
    at = 2 * mixed - 2 * STATE
    return p_ref[stream, pl.ds(base, Q), at:] + par_ref[7:8, :LANES]


def soft_plus(raw):
    return jnp.maximum(raw, 0.0) + jnp.log1p(jnp.exp(-jnp.abs(raw)))


def chunk_decay(raw, par_ref):
    delta = soft_plus(raw)
    rate = jnp.exp(par_ref[8:9, :LANES])
    return delta, running_sum(-delta * rate, False)


def chunk_front(pre, delta, cumulative, seg, seg_row):
    channels = pre.shape[1] - 2 * STATE
    here = seg[8 : Q + 8]
    gate = jax.nn.sigmoid(pre)
    active = pre * gate
    values = active[:, :channels]
    last = cumulative[Q - 1 : Q]
    keep = (here == seg[7:8]).astype(F32)
    same_last = (here == seg[Q + 7 : Q + 8]).astype(F32)
    inflow = jnp.exp(cumulative) * keep
    tail = jnp.exp(last - cumulative) * same_last
    delta_wide, inflow_wide, tail_wide = spread([delta, inflow, tail], channels)
    t = lax.broadcasted_iota(jnp.int32, (Q, Q), 0)
    u = lax.broadcasted_iota(jnp.int32, (Q, Q), 1)
    mask = (t >= u) & (here == seg_row)
    turned = cumulative.T

    def decays(head):
        spacing = cumulative[:, head : head + 1] - turned[head : head + 1, :]
        return jnp.exp(jnp.where(mask, spacing, -1e30))

    return dict(
        seg=seg,
        pre=pre,
        gate=gate,
        values=values,
        b_low=active[:, channels : channels + STATE].astype(BF16),
        c_low=active[:, channels + STATE :].astype(BF16),
        delta=delta,
        delta_wide=delta_wide,
        inflow_wide=inflow_wide,
        tail_wide=tail_wide,
        scaled=values * delta_wide,
        decays=decays,
        channels=channels,
    )


def two_heads(pair):
    left = lax.broadcasted_iota(jnp.int32, pair.shape, 1) < HEAD_DIM
    low = pair.astype(BF16)
    zero = jnp.zeros_like(low)
    return jnp.concatenate([jnp.where(left, low, zero), jnp.where(left, zero, low)], axis=0)


def chunk_forward(front, state, skip):
    channels = front["channels"]
    scores = mul(front["c_low"], front["b_low"], ((1,), (1,)))
    pieces = []
    for pair in range(channels // LANES):
        weights = jnp.concatenate(
            [(front["decays"](2 * pair + i) * scores).astype(BF16) for i in range(2)], axis=1
        )
        scaled = front["scaled"][:, pair * LANES : (pair + 1) * LANES]
        pieces.append(mul(weights, two_heads(scaled)))
    result = jnp.concatenate(pieces, axis=1)
    result = result + mul(front["c_low"], state.astype(BF16)) * front["inflow_wide"]
    result = result + skip * front["values"]
    fed = (front["scaled"] * front["tail_wide"]).astype(BF16)
    after = front["inflow_wide"][Q - 1 : Q] * state + mul(front["b_low"], fed, ((0,), (0,)))
    return result, after


def chunk_backward(front, raw, rate, before, after, grad_after, result, grad, skip):
    channels = front["channels"]
    b_low, c_low = front["b_low"], front["c_low"]
    scaled, values = front["scaled"], front["values"]
    scores = mul(c_low, b_low, ((1,), (1,)))
    grad_scores = jnp.zeros((Q, Q), F32)
    pieces = []
    for pair in range(channels // LANES):
        lanes = slice(pair * LANES, (pair + 1) * LANES)
        decays = [front["decays"](2 * pair + i) for i in range(2)]
        weights = jnp.concatenate([(d * scores).astype(BF16) for d in decays], axis=0)
        split = two_heads(grad[:, lanes])
        pieces.append(mul(weights, split, ((0,), (0,))))
        cross = mul(split, scaled[:, lanes].astype(BF16), ((1,), (1,)))
        grad_scores = grad_scores + decays[0] * cross[:Q] + decays[1] * cross[Q:]
    grad_after_low = grad_after.astype(BF16)
    inner = jnp.concatenate(pieces, axis=1) + mul(b_low, grad_after_low) * front["tail_wide"]
    fed = (scaled * front["tail_wide"]).astype(BF16)
    flowing = (grad * front["inflow_wide"]).astype(BF16)
    low_scores = grad_scores.astype(BF16)
    grad_c = mul(low_scores, b_low) + mul(flowing, before.astype(BF16), ((1,), (1,)))
    grad_b = mul(low_scores, c_low, ((0,), (0,))) + mul(fed, grad_after_low, ((1,), (1,)))
    grad_values = skip * grad + front["delta_wide"] * inner
    grad_skip = jnp.sum(grad * values, axis=0, keepdims=True)
    held = jnp.sum(after * grad_after, axis=0, keepdims=True)
    grad_delta, grad_cumulative = gather_heads(
        [values * inner, grad * (result - skip * values) - scaled * inner], channels
    )
    held_heads = gather_heads([jnp.broadcast_to(held, (8, channels))], channels)[0][0:1]
    grad_log = running_sum(grad_cumulative, True) + held_heads
    grad_delta = grad_delta - rate * grad_log
    grad_raw = grad_delta * jax.nn.sigmoid(raw)
    grad_rate = -rate * jnp.sum(grad_log * front["delta"], axis=0, keepdims=True)
    grad_before = front["inflow_wide"][Q - 1 : Q] * grad_after + mul(c_low, flowing, ((0,), (0,)))
    return grad_values, grad_b, grad_c, grad_raw, grad_rate, grad_skip, grad_before


def conv_backward(front, xbc, grad_active, next_grad, par_ref):
    gate, pre, seg = front["gate"], front["pre"], front["seg"]
    mixed = pre.shape[1]
    grad_pre = grad_active * (gate * (1.0 + pre * (1.0 - gate)))
    both = jnp.concatenate([grad_pre, next_grad], axis=0)
    grad_x = par_ref[CONV - 1 : CONV, :] * grad_pre
    rows = []
    for k in range(CONV - 1):
        ahead = CONV - 1 - k
        agree = (seg[8 + ahead : Q + 8 + ahead] == seg[8 : Q + 8]).astype(F32)
        moved = both[ahead : Q + ahead] * wide(agree, mixed // LANES)
        grad_x = grad_x + par_ref[k : k + 1, :] * moved
        rows.append(jnp.sum(xbc * moved, axis=0, keepdims=True))
    rows.append(jnp.sum(xbc * grad_pre, axis=0, keepdims=True))
    rows.append(jnp.sum(grad_pre, axis=0, keepdims=True))
    return grad_x, grad_pre[:8], rows


MESH = pl.DeviceIdType.MESH
TILE = 512


class Links:
    def __init__(self, send, recv):
        self.send, self.recv, self.used = send, recv, 0

    def copy(self, source, target, device):
        slot = self.used
        self.used += 1
        assert slot < self.send.shape[0]
        return pltpu.make_async_remote_copy(
            src_ref=source,
            dst_ref=target,
            send_sem=self.send.at[slot],
            recv_sem=self.recv.at[slot],
            device_id=device,
            device_id_type=MESH,
        )


class Place:
    def __init__(self, depth):
        self.s = lax.axis_index("seq")
        self.f = lax.axis_index("fsdp")
        self.depth = depth
        self.core = lax.rem(self.s, 2)
        x = lax.rem(self.s // 2, 2)
        y = self.s // 4
        self.steps = (1 - 2 * self.core, 2 - 4 * x, 4 - 8 * y)

    def peer(self, k):
        index = self.s
        for bit in range(3):
            if k >> bit & 1:
                index = index + self.steps[bit]
        return index

    def at(self, k):
        return (self.peer(k), self.f)

    def plane(self, d):
        return lax.rem(self.f + d, self.depth)

    def beyond(self, d):
        return (self.s, self.plane(d))

    def greet(self):
        barrier = pltpu.get_barrier_semaphore()
        others = [self.at(k) for k in range(1, 8)] + [self.beyond(d) for d in range(1, self.depth)]
        for other in others:
            pl.semaphore_signal(barrier, inc=1, device_id=other, device_id_type=MESH)

        def met():
            pl.semaphore_wait(barrier, len(others))

        return met


def ahead(start, size):
    return pl.ds(pl.multiple_of(start, size), size)


PIECES = [slice(i, i + 512) for i in range(0, D, 512)]
FEW = 64


class Summing:
    def __init__(self, here, links, slots, beside, halves_in, final_in, own):
        self.here, self.slots, self.beside = here, slots, beside
        self.halves_in, self.final_in, self.own = halves_in, final_in, own
        self.count = slots[0].shape[0]
        self.half = self.count // 2
        make = links.copy
        self.to_beside = [make(slots[r], beside[r], here.at(1)) for r in range(4)]
        self.by = [
            make(slots[3].at[self.rows(i)], halves_in[i], here.at(2 << i)) for i in range(2)
        ]
        self.last = [make(slots[1 + i], final_in[i], here.at(2 << i)) for i in range(2)]

    def rows(self, i):
        return pl.ds(i * self.half, self.half)

    def owner(self, r, other):
        return self.here.peer(2 * r + (1 if other else 0))

    def give_beside(self, value):
        for lanes in PIECES:
            found = value(True, lanes).astype(BF16)
            for r in range(4):
                self.slots[r][:, lanes] = found[r * self.count : (r + 1) * self.count]
        for r in (3, 1, 2, 0):
            self.to_beside[r].start()

    def join(self, value):
        for copy in self.to_beside:
            copy.wait()
        targets = [self.own] + self.slots[1:]
        for lanes in PIECES:
            found = value(False, lanes)
            for r in range(4):
                mine = found[r * self.count : (r + 1) * self.count]
                joined = mine + self.beside[r][:, lanes].astype(F32)
                targets[r][:, lanes] = joined.astype(targets[r].dtype)
        for copy in self.by:
            copy.start()

    def pass_on(self, i):
        other = 1 - i
        self.by[other].wait_recv()
        part = self.slots[1 + i].at[self.rows(other)]
        part[...] = (part[...].astype(F32) + self.halves_in[other][...].astype(F32)).astype(BF16)
        self.last[i].start()

    def arrived(self):
        for copy in self.last:
            copy.wait_recv()

    def total(self, rows):
        total = self.own[rows].astype(F32) + self.final_in[0][rows].astype(F32)
        return total + self.final_in[1][rows].astype(F32)

    def settle(self):
        for copy in self.by + self.last:
            copy.wait_send()


class Passing:
    def __init__(self, here, links, blocks, from_below, from_above, depth):
        f, s = here.f, here.s
        self.f, self.depth, self.blocks = f, depth, blocks
        self.came = (from_below, from_above)
        self.copies = []
        for j in range(depth - 1):
            far = depth - 1 - j
            self.copies.append(
                (
                    links.copy(blocks(f + far), from_below.at[far - 1], (s, f + 1)),
                    links.copy(blocks(f - far), from_above.at[far - 1], (s, f - 1)),
                )
            )

    def sends(self, j):
        return (self.f <= j, self.depth - 1 - self.f <= j)

    def gets(self, j):
        return (
            (self.f >= 1) & (self.f <= j + 1),
            (self.f <= self.depth - 2) & (self.depth - 1 - self.f <= j + 1),
        )

    def begin(self):
        for j in range(self.depth - 1):
            pl.when(self.f == 0)(self.copies[j][0].start)
            pl.when(self.f == self.depth - 1)(self.copies[j][1].start)

    def step(self, j):
        far = self.depth - 1 - j
        for way, sign in ((0, 1), (1, -1)):

            @pl.when(self.gets(j - 1)[way])
            def _(way=way, sign=sign):
                self.copies[j - 1][way].wait_recv()
                block = self.blocks(self.f + sign * far)
                block[...] = (
                    block[...].astype(F32) + self.came[way][far].astype(F32)
                ).astype(BF16)
                self.copies[j][way].start()

    def finish(self):
        last = self.depth - 2
        block = self.blocks(self.f)
        for way in range(2):

            @pl.when(self.gets(last)[way])
            def _(way=way):
                self.copies[last][way].wait_recv()
                block[...] = (
                    block[...].astype(F32) + self.came[way][0].astype(F32)
                ).astype(BF16)

    def settle(self):
        for j in range(self.depth - 1):
            for way in range(2):
                pl.when(self.sends(j)[way])(self.copies[j][way].wait_send)


LINE = 512
LONG = 256
GROUP = 384
FIRST_GAIN = 0
FIRST_INNER = D // LANES
FIRST_CONV = FIRST_INNER + CHANNELS // LANES
CONV_ROWS = WIDTH // LANES
SMALL = FIRST_CONV + (CONV + 1) * CONV_ROWS
VECTOR_ROWS = SMALL + 2


def thirds(x):
    high, low = halves(x)
    rest = x - high.astype(F32) - low.astype(F32)
    return high, low, rest.astype(BF16)


def chosen(x, picks):
    return sum(mul(part, picks) for part in thirds(x))


def own_parameters(vec, par, s, share):
    channels = share * HEAD_DIM
    tiles = channels // LANES
    par[...] = jnp.zeros_like(par)
    for k in range(CONV + 1):
        base = FIRST_CONV + k * CONV_ROWS
        for i in range(tiles):
            par[k : k + 1, i * LANES : (i + 1) * LANES] = vec[pl.ds(base + s * tiles + i, 1), :]
        for i in range(2 * STATE // LANES):
            at = channels + i * LANES
            row = base + CHANNELS // LANES + i
            par[k : k + 1, at : at + LANES] = vec[row : row + 1, :]
    for i in range(tiles):
        row = vec[pl.ds(FIRST_INNER + s * tiles + i, 1), :]
        par[5:6, i * LANES : (i + 1) * LANES] = row
    small = jnp.concatenate([vec[SMALL : SMALL + 1, :], vec[SMALL + 1 : SMALL + 2, :]], axis=1)
    small = jnp.broadcast_to(small, (8, 2 * LANES))
    source = lax.broadcasted_iota(jnp.int32, (2 * LANES, LANES), 0)
    lane = lax.broadcasted_iota(jnp.int32, (2 * LANES, LANES), 1)
    found = []
    for which in range(3):
        picks = (source == which * HEADS + s * share + lane) & (lane < share)
        found.append(chosen(small, picks.astype(BF16)))
    par[6:7, :channels] = chosen(found[2], head_map(channels))[0:1]
    par[7:8, :LANES] = found[0][0:1]
    par[8:9, :LANES] = found[1][0:1]


def all_parameters(vec, found, out, share):
    count = found.shape[0]
    channels = share * HEAD_DIM
    tiles = channels // LANES
    out[...] = jnp.zeros_like(out)
    wide_rows = D // 3 // LANES
    for i in range(FIRST_INNER):
        at = (i % wide_rows) * LANES
        row = found[0, 9 + i // wide_rows : 10 + i // wide_rows, at : at + LANES]
        for k in range(1, count):
            row = row + found[k, 9 + i // wide_rows : 10 + i // wide_rows, at : at + LANES]
        out[i : i + 1, :] = row / vec[i : i + 1, :]
    for k in range(count):
        for i in range(tiles):
            lanes = slice(i * LANES, (i + 1) * LANES)
            row = FIRST_INNER + k * tiles + i
            out[row : row + 1, :] = found[k, 5:6, lanes]
            for j in range(CONV + 1):
                row = FIRST_CONV + j * CONV_ROWS + k * tiles + i
                out[row : row + 1, :] = found[k, j : j + 1, lanes]
    for j in range(CONV + 1):
        for i in range(2 * STATE // LANES):
            lanes = slice(channels + i * LANES, channels + (i + 1) * LANES)
            total = found[0, j : j + 1, lanes]
            for k in range(1, count):
                total = total + found[k, j : j + 1, lanes]
            row = FIRST_CONV + j * CONV_ROWS + CHANNELS // LANES + i
            out[row : row + 1, :] = total
    lane = lax.broadcasted_iota(jnp.int32, (8, LANES), 1)
    small = jnp.zeros((8, LANES), F32)
    for k in range(count):
        part = jnp.where(lane < share, found[k, 0:16, :LANES][6:14], 0.0)
        small = small + (pltpu.roll(part, k * share, 1) if k else part)
    skip, step, rate = small[0:1], small[1:2], small[2:3]
    lane = lane[0:1]
    rate = pltpu.roll(small, HEADS, 1)[2:3]
    skip = pltpu.roll(small, 2 * HEADS, 1)[0:1]
    first = jnp.where(lane < HEADS, step, jnp.where(lane < 2 * HEADS, rate, skip))
    out[SMALL : SMALL + 1, :] = first
    out[SMALL + 1 : SMALL + 2, :] = jnp.where(lane < 3 * HEADS - LANES, skip, 0.0)


def block_kernel(
    depth,
    lengths,
    hidden,
    out_grad,
    in_low,
    out_proj,
    vec,
    mixed_out,
    upstream_out,
    main_out,
    lines_out,
    vector_out,
    x_kept,
    x,
    g,
    w,
    wo,
    p,
    y,
    h,
    pre_kept,
    decay_kept,
    par,
    state,
    later,
    sums,
    shared_low,
    moments,
    moments_sum,
    slots,
    beside_in,
    halves_in,
    last_in,
    grad_last,
    lines,
    lines_in,
    main,
    gate_in,
    main_in,
    slabs_recv,
    common,
    common_beside,
    common_recv,
    common_line,
    common_last,
    common_sum,
    gain_sums,
    vector_line,
    vector_all,
    vector_full,
    send,
    recv,
    moves,
    credit,
):
    streams, length = x.shape[0], x.shape[1]
    block = hidden.shape[0] // streams
    chunks = length // Q
    rows = in_low.shape[0]
    out_rows = out_proj.shape[0]
    channels = wo.shape[0]
    share = channels // HEAD_DIM
    mixed = channels + 2 * STATE
    tiles = channels // LANES
    slab = depth * rows
    here = Place(depth)
    s, f = here.s, here.f
    links = Links(send, recv)
    dp = x
    part_of = [slice(i * channels, (i + 1) * channels) for i in range(4)]
    projected = slice(0, 3 * channels)
    ends = []
    for k in range(streams):
        total = lengths[k, 0]
        ends.append([total])
        for i in range(1, lengths.shape[1]):
            total = total + lengths[k, i]
            ends[k].append(total)

    def slab_rows(source, plane):
        return ahead((source * depth + plane) * rows, rows)

    def block_rows(source):
        return ahead(source * block, block)

    finish = []

    def started(copy):
        copy.start()
        finish.append(copy)
        return copy

    met = here.greet()
    narrow = 2 * STATE + HEADS
    shared_low[:, narrow:] = jnp.zeros((rows, shared_low.shape[1] - narrow), BF16)
    shared_low[:, :narrow] = in_low[:, 2 * CHANNELS :]
    own = slab_rows(s, f)
    w[own, 2 * channels :] = shared_low[...]
    for part in range(2):
        w[own, part_of[part]] = in_low[:, ahead(part * CHANNELS + s * channels, channels)]
    gain = jnp.concatenate([vec[i : i + 1, :] for i in range(FIRST_INNER)], axis=1)

    def scaled_rows(at):
        upstream = hidden[at, :].astype(F32)
        mean = jnp.mean(upstream * upstream, axis=-1, keepdims=True)
        return upstream, lax.rsqrt(mean + EPS_NORM)

    for stream in range(streams):

        def normalize(i, carry, stream=stream):
            upstream, inverse = scaled_rows(ahead(stream * block + i * FEW, FEW))
            x[stream, ahead(s * block + i * FEW, FEW), :] = (upstream * inverse * gain).astype(BF16)
            return carry

        lax.fori_loop(0, block // FEW, normalize, 0)
    wo[ahead(f * out_rows, out_rows)] = out_proj[...].astype(BF16)
    met()
    order = (0, 1, 2, 4, 3, 5, 6, 7)
    own = slab_rows(s, f)
    turned = {}
    for part in (1, 0):
        for k in order[1:]:
            lanes = ahead(part * CHANNELS + here.peer(k) * channels, channels)
            turned[part, k] = started(
                links.copy(in_low.at[:, lanes], w.at[own, part_of[part]], here.at(k))
            )
    shared = [
        started(links.copy(shared_low, w.at[own, 2 * channels :], here.beyond(d)))
        for d in range(1, depth)
    ]
    def token_block(ref, stream, k):
        return ref.at[stream, block_rows(here.peer(k))]

    def token_half(ref, stream, way, k):
        rows = block // 2
        return ref.at[stream, ahead(here.peer(k) * block + way * rows, rows)]

    class Tokens:
        def __init__(self, ref, stream):
            self.ref, self.stream = ref, stream
            mine = token_block(ref, stream, 0)
            self.near = [links.copy(mine, mine, here.at(2 << way)) for way in range(2)]
            halves_out = [token_half(ref, stream, way, 2 << way) for way in range(2)]
            self.across = [
                links.copy(halves_out[way], halves_out[way], here.at(4 >> way)) for way in range(2)
            ]
            blocks = [token_block(ref, stream, k) for k in (0, 2, 4)]
            blocks += [token_half(ref, stream, way, 6) for way in range(2)]
            self.beside = [links.copy(part, part, here.at(1)) for part in blocks]

        def begin(self):
            for copy in self.near:
                copy.start()
            self.beside[0].start()

        def go_on(self):
            for way in range(2):
                self.near[way].wait_recv()
                self.across[way].start()
                self.beside[1 + way].start()

        def end(self):
            for way in range(2):
                self.across[way].wait_recv()
                self.beside[3 + way].start()
            for copy in self.beside:
                copy.wait_recv()

        def settle(self):
            for copy in self.near + self.across + self.beside:
                copy.wait_send()

    x_tokens = [Tokens(x, k) for k in range(streams)]
    g_tokens = [Tokens(g, k) for k in range(streams)]
    x_tokens[0].begin()
    g_in = [
        pltpu.make_async_copy(
            out_grad.at[pl.ds(k * block, block)], g.at[k, block_rows(s)], moves.at[2 + k]
        )
        for k in range(streams)
    ]
    for copy in g_in:
        copy.start()
    own_parameters(vec, par, s, share)

    def hop(part, k, d, up):
        plane = f - d if up else f + d
        target = w.at[slab_rows(here.peer(k), plane), part_of[part]]
        return links.copy(target, target, (s, f + 1 if up else f - 1))

    hops = {}
    for part in range(2):
        for k in range(8):
            for d in range(depth - 1):
                hops[part, k, d] = (hop(part, k, d, True), hop(part, k, d, False))

    def sends(d):
        return ((f >= d) & (f < depth - 1), (f <= depth - 1 - d) & (f > 0))

    def gets(d):
        return (f >= d + 1, f <= depth - 2 - d)

    def launch(part, k, d):
        for way in range(2):
            pl.when(sends(d)[way])(hops[part, k, d][way].start)

    def arrive(part, k, d):
        for way in range(2):
            pl.when(gets(d)[way])(hops[part, k, d][way].wait_recv)

    def first_hops(part):
        for k in order:
            if k:
                turned[part, k].wait_recv()
            launch(part, k, 0)

    def next_hops(part, d):
        for k in order:
            arrive(part, k, d - 1)
            launch(part, k, d)

    def project(stream, parts):
        def tile(i, carry):
            at = ahead(i * TILE, TILE)
            left = x[stream, at, :]
            for lanes in parts:
                p[stream, at, lanes] = mul(left, w[:, lanes])
            return carry

        lax.fori_loop(0, length // TILE, tile, 0)

    first_hops(1)
    for copy in shared:
        copy.wait_recv()
    group = w.at[ahead(s * slab, slab), 2 * channels :]
    spread_common = [links.copy(group, group, here.at(k)) for k in (2, 4, 6, 1)]
    for copy in spread_common:
        copy.start()
    last = depth - 1
    for d in range(1, last):
        if d == last - 1:
            x_tokens[0].go_on()
            for k in range(1, streams):
                x_tokens[k].begin()
            for copy in g_in:
                copy.wait()
            g_tokens[0].begin()
        next_hops(1, d)
    first_hops(0)
    for copy in spread_common[:3]:
        copy.wait_recv()
    for k in (2, 4, 6):
        group = w.at[ahead(here.peer(k) * slab, slab), 2 * channels :]
        spread_common.append(links.copy(group, group, here.at(1)))
        spread_common[-1].start()
    for copy in spread_common[3:]:
        copy.wait_recv()
    for copy in spread_common:
        copy.wait_send()
    column_at = lax.broadcasted_iota(jnp.int32, (LANES, LANES), 0)
    wanted_at = lax.broadcasted_iota(jnp.int32, (LANES, LANES), 1)
    pick = ((column_at == wanted_at + s * share) & (wanted_at < share)).astype(BF16)
    for part in range(0, D, TILE):
        steps = w[part : part + TILE, mixed + channels :]
        w[part : part + TILE, mixed + channels :] = mul(steps, pick).astype(BF16)
    x_out = [
        pltpu.make_async_copy(x.at[k], x_kept.at[k], moves.at[k]) for k in range(streams)
    ]
    x_tokens[0].end()
    x_out[0].start()
    for k in order:
        arrive(1, k, last - 1)
    project(0, part_of[1:3])
    for k in range(1, streams):
        x_tokens[k].go_on()
        g_tokens[k].begin()

    skip = par[6:7, :channels]
    g_inner = par[5:6, :channels]
    state[...] = jnp.zeros_like(state)

    def tell_moments(which, stream):
        mine_m = moments.at[s, which, stream]
        return [started(links.copy(mine_m, mine_m, here.at(k))) for k in range(1, 8)]

    def hear_moments(which, stream):
        for copy in told_moments[which, stream]:
            copy.wait_recv()
        moments_sum[which, stream] = jnp.sum(moments[:, which, stream], axis=0)

    told_moments = {}
    ones = jnp.ones((8, 2 * channels), BF16)

    def forward_step(stream, chunk, carry):
        base = pl.multiple_of(chunk * Q, Q)
        at = pl.ds(base, Q)
        seg, seg_row = chunk_places(ends, stream, base)
        pre = chunk_convolve(p, par, stream, base, seg)
        delta, cumulative = chunk_decay(chunk_raw(p, par, stream, base), par)
        pre_kept[stream, at] = pre.astype(BF16)
        decay_kept[stream, at] = cumulative
        front = chunk_front(pre, delta, cumulative, seg, seg_row)
        before = state[stream]
        h[stream, chunk] = before.astype(BF16)
        result, after = chunk_forward(front, before, skip)
        y[stream, at] = result
        state[stream] = after
        if stream == 0:

            @pl.when(chunk == 2 * chunks // 8)
            def _():
                for d in range(1, last - 1):
                    next_hops(0, d)

        @pl.when(chunk == (5 if stream == 0 else 3) * chunks // 8)
        def _():
            g_tokens[stream].go_on()

        return carry

    def flat_step(stream, chunk, carry):
        at = ahead(chunk * Q, Q)
        gate_in = p[stream, at, :channels]
        flat = y[stream, at] * (gate_in * jax.nn.sigmoid(gate_in))
        dp[stream, at, part_of[2]] = (flat * g_inner).astype(BF16)
        squares = jnp.concatenate(halves(flat * flat), axis=1)
        moments[s, 0, stream, pl.ds(chunk, 1), :] = mul(ones, squares, ((1,), (1,)))[0:1]
        return carry

    lax.fori_loop(0, chunks, functools.partial(forward_step, 0), 0)
    next_hops(0, last - 1)
    lent = wo.at[ahead(f * out_rows, out_rows)]
    outs = [started(links.copy(lent, lent, here.beyond(d))) for d in range(1, depth)]
    for k in range(1, streams):
        x_tokens[k].end()
        x_out[k].start()
        project(k, part_of[1:3])
        lax.fori_loop(0, chunks, functools.partial(forward_step, k), 0)
    for k in order:
        arrive(0, k, last - 1)
    for k in range(streams):
        project(k, part_of[:1])
        x_out[k].wait()
        x_tokens[k].settle()
        lax.fori_loop(0, chunks, functools.partial(flat_step, k), 0)
        told_moments[0, k] = tell_moments(0, k)

    long_tiles = length // TILE
    pieces = TILE // Q

    def weigh(stream, i, carry):
        at = ahead(i * TILE, TILE)
        dp[stream, at, part_of[3]] = mul(g[stream, at], wo[...], ((1,), (1,))).astype(BF16)
        for j in range(pieces):
            at = ahead(i * TILE + j * Q, Q)
            product = dp[stream, at, part_of[3]].astype(F32) * dp[stream, at, part_of[2]].astype(F32)
            found = mul(ones, jnp.concatenate(halves(product), axis=1), ((1,), (1,)))
            moments[s, 1, stream, pl.ds(i * pieces + j, 1), :] = found[0:1]
        return carry

    mixed_sum = Summing(
        here,
        links,
        [slots.at[r] for r in range(4)],
        [beside_in.at[r] for r in range(4)],
        [halves_in.at[i] for i in range(2)],
        [last_in.at[i] for i in range(2)],
        mixed_out,
    )

    def grad_of(stream):
        rows = pl.ds(stream * block, block)
        few = pl.ds(stream * block // 2, block // 2)
        return Summing(
            here,
            links,
            [slots.at[r, rows] for r in range(4)],
            [beside_in.at[r, rows] for r in range(4)],
            [halves_in.at[i, few] for i in range(2)],
            [grad_last.at[i, rows] for i in range(2)],
            upstream_out.at[rows],
        )

    grad_sums = [grad_of(k) for k in range(streams)]

    def branch(other, lanes):
        rows_at = [block_rows(mixed_sum.owner(r, other)) for r in range(4)]
        low = [dp[k, at, part_of[2]] for at in rows_at for k in range(streams)]
        return mul(jnp.concatenate(low, axis=0), wo[:, lanes])

    for copy in outs:
        copy.wait_recv()
    mixed_sum.give_beside(branch)
    mixed_sum.join(branch)

    def column(row):
        return jnp.broadcast_to(row, (Q, Q)).T

    def norm_row(stream, chunk):
        first = moments_sum[0, stream, pl.ds(chunk, 1), :]
        return lax.rsqrt(first / CHANNELS + EPS_NORM)

    def scale_step(stream, chunk, carry):
        at = ahead(chunk * Q, Q)
        scale = wide(column(norm_row(stream, chunk)), tiles)
        dp[stream, at, part_of[1]] = (dp[stream, at, part_of[2]].astype(F32) * scale).astype(BF16)
        return carry

    for stream in range(streams):
        hear_moments(0, stream)
        lax.fori_loop(0, chunks, functools.partial(scale_step, stream), 0)
    for stream in range(streams):
        g_tokens[stream].end()
        lax.fori_loop(0, long_tiles, functools.partial(weigh, stream), 0)
        told_moments[1, stream] = tell_moments(1, stream)
    sums[...] = jnp.zeros_like(sums)
    state[...] = jnp.zeros_like(state)
    later[...] = jnp.zeros_like(later)

    def gate_step(stream, chunk, carry):
        at = ahead(chunk * Q, Q)
        scale = norm_row(stream, chunk)
        second = moments_sum[1, stream, pl.ds(chunk, 1), :]
        pull = column(scale * scale * scale * second / CHANNELS)
        scale = column(scale)
        scale, pull = wide(scale, tiles), wide(pull, tiles)
        gate_in = p[stream, at, :channels]
        result = y[stream, at]
        sig = jax.nn.sigmoid(gate_in)
        silu = gate_in * sig
        flat = result * silu
        scaled = flat * scale
        grad = dp[stream, at, part_of[3]].astype(F32)
        grad_flat = scale * g_inner * grad - flat * pull
        p[stream, at, :channels] = grad_flat * silu
        grad_gate = grad_flat * result * (sig * (1.0 + gate_in * (1.0 - sig)))
        dp[stream, at, part_of[0]] = grad_gate.astype(BF16)
        sums[5:6, :channels] += jnp.sum(grad * scaled, axis=0, keepdims=True)
        return carry

    def line_step(j, carry):
        lanes = ahead(j * LINE, LINE)
        total = jnp.zeros((channels, LINE), F32)
        for k in range(streams):
            total = total + mul(dp[k, :, part_of[1]], g[k, :, lanes], ((0,), (0,)))
        lines[:, lanes] = total.astype(BF16)
        return carry

    lax.fori_loop(0, D // LINE, line_step, 0)
    for copy in finish:
        copy.wait_send()
    for each in g_tokens:
        each.settle()
    x_in = pltpu.make_async_copy(x_kept, g, moves.at[4])
    x_in.start()
    tokens = g
    line_sends = []
    for d in range(1, depth):
        theirs = lines.at[ahead(here.plane(d) * out_rows, out_rows)]
        line_sends.append(links.copy(theirs, lines_in.at[d - 1], here.beyond(d)))
        line_sends[-1].start()
    for i in range(2):
        mixed_sum.pass_on(i)
    for i, k in enumerate((1, 2, 4)):
        pl.semaphore_signal(credit.at[i], inc=1, device_id=here.at(k), device_id_type=MESH)
    for stream in range(streams):
        hear_moments(1, stream)
        lax.fori_loop(0, chunks, functools.partial(gate_step, stream), 0)

    def gradient_rows(j, lanes):
        wanted = ahead(j * GROUP, GROUP)
        total = jnp.zeros((GROUP, channels), F32)
        for k in range(streams):
            total = total + mul(tokens[k, :, wanted], dp[k, :, lanes], ((0,), (0,)))
        product = total * w[wanted, lanes].astype(F32)
        folded = product[:, :LANES]
        for i in range(1, tiles):
            folded = folded + product[:, i * LANES : (i + 1) * LANES]
        line = jnp.ones((8, 2 * LANES), BF16)
        gain_sums[:, wanted] += mul(line, jnp.concatenate(halves(folded), axis=1), ((1,), (1,)))
        return total

    gain_sums[...] = jnp.zeros_like(gain_sums)
    def main_group(part, chip):
        total = gradient_rows(chip, part_of[part]).astype(BF16)
        for i in range(GROUP // rows):
            main[part, i % depth, 2 * chip + i // depth] = total[i * rows : (i + 1) * rows]

    def backward_step(stream, k, carry):
        chunk = chunks - 1 - k
        base = pl.multiple_of(chunk * Q, Q)
        at = pl.ds(base, Q)
        seg, seg_row = chunk_places(ends, stream, base)
        raw = chunk_raw(p, par, stream, base)
        rate = jnp.exp(par[8:9, :LANES])
        pre = pre_kept[stream, at].astype(F32)
        front = chunk_front(pre, soft_plus(raw), decay_kept[stream, at], seg, seg_row)
        grad_after = state[stream]
        before = h[stream, chunk].astype(F32)
        after = h[stream, jnp.minimum(chunk + 1, chunks - 1)].astype(F32)
        gv, gb, gc, graw, grate, gskip, gbefore = chunk_backward(
            front,
            raw,
            rate,
            before,
            after,
            grad_after,
            y[stream, at],
            p[stream, at, :channels],
            skip,
        )
        state[stream] = gbefore
        grad_active = jnp.concatenate([gv, gb, gc], axis=1)
        grad_x, head, rows_w = conv_backward(
            front, p[stream, at, channels : channels + mixed], grad_active, later[stream], par
        )
        later[stream] = head
        dp[stream, at, channels : channels + mixed] = grad_x.astype(BF16)
        dp[stream, at, channels + mixed : 3 * channels] = graw.astype(BF16)
        for i, row in enumerate(rows_w):
            sums[i : i + 1, :] += row
        sums[6:7, :channels] += gskip
        sums[7:8, :LANES] += jnp.sum(graw, axis=0, keepdims=True)
        sums[8:9, :LANES] += grate
        if stream:

            @pl.when(k == 5 * chunks // 8)
            def _():
                for i in range(2):
                    grad_sums[0].pass_on(i)

        return carry

    def back_of(stream):
        def back(other, lanes):
            rows_at = [block_rows(grad_sums[stream].owner(r, other)) for r in range(4)]
            low = jnp.concatenate([dp[stream, at, projected] for at in rows_at], axis=0)
            return mul(low, w[lanes, :], ((1,), (1,)))

        return back

    x_in.wait()

    def gate_group(j, carry):
        main_group(0, j)
        return carry

    lax.fori_loop(0, D // GROUP, gate_group, 0)
    gate_sends = []
    for d in range(1, depth):
        copy = links.copy(main.at[0, here.plane(d)], gate_in.at[d - 1], here.beyond(d))
        copy.start()
        gate_sends.append(copy)

    lax.fori_loop(0, chunks, functools.partial(backward_step, 0), 0)
    mixed_sum.settle()
    for i in range(3):
        pl.semaphore_wait(credit.at[i], 1)
    for stream in range(streams):
        if stream:
            lax.fori_loop(0, chunks, functools.partial(backward_step, stream), 0)
            break
        grad_sums[stream].give_beside(back_of(stream))
        grad_sums[stream].join(back_of(stream))

    slab_sends = []

    def hand_over(part, k):
        if k == 0:
            slabs_recv[part, s] = main[part, f, s]
            return
        copy = links.copy(main.at[part, f, here.peer(k)], slabs_recv.at[part, s], here.at(k))
        copy.start()
        slab_sends.append(copy)

    place = ((wanted_at == column_at + s * share) & (column_at < share)).astype(BF16)

    def common_group(j, carry):
        total = gradient_rows(j, part_of[2]).astype(BF16)
        at = ahead(j * GROUP, GROUP)
        common[at, : 2 * STATE] = total[:, : 2 * STATE]
        common[at, 2 * STATE :] = mul(total[:, 2 * STATE :], place).astype(BF16)
        return carry

    lax.fori_loop(0, D // GROUP, common_group, 0)

    def owned(k):
        return common.at[ahead(here.peer(k) * slab, slab)]

    common_sends = [
        links.copy(owned(2 * r + 1), common_beside.at[r], here.at(1)) for r in range(4)
    ]
    for copy in common_sends:
        copy.start()
    chips = (3, 1, 2, 0)
    common_across = []
    for r in chips:
        if r == 2:
            for copy in common_sends:
                copy.wait_recv()
            for i in chips:
                at = ahead(here.peer(2 * i) * slab, slab)
                joined = common[at, :].astype(F32) + common_beside[i].astype(F32)
                common[at, :] = joined.astype(BF16)
                if i:
                    copy = links.copy(owned(2 * i), common_recv.at[i - 1], here.at(2 * i))
                    copy.start()
                    common_across.append(copy)
        main_group(1, here.peer(2 * r) // 2)

    total = main[0, f].astype(F32)
    for d in range(1, depth):
        gate_sends[d - 1].wait_recv()
        total = total + gate_in[d - 1].astype(F32)
    main[0, f] = total.astype(BF16)
    for k in range(1, 8):
        hand_over(0, k)
    hand_over(0, 0)

    for i in range(3):
        third = D // 3
        sums[9 + i : 10 + i, :third] = gain_sums[0:1, i * third : (i + 1) * third]
    by_channel = jnp.broadcast_to(sums[6:7, :channels], (8, channels))
    sums[6:7, :LANES] = gather_heads([by_channel], channels)[0][0:1]
    vector_line[f] = sums[...]
    told = [links.copy(sums, vector_line.at[f], here.beyond(d)) for d in range(1, depth)]
    for copy in told:
        copy.start()
    value_sends = {}
    for r in chips:
        pair = pl.ds(2 * (here.peer(2 * r) // 2), 2)
        value_sends[r] = []
        for d in range(1, depth):
            copy = links.copy(
                main.at[1, here.plane(d), pair], main_in.at[d - 1, pair], here.beyond(d)
            )
            copy.start()
            value_sends[r].append(copy)
    grad_own = g.at[0, pl.ds(0, streams * block)]
    grad_again = pltpu.make_async_copy(out_grad, grad_own, moves.at[5])
    grad_again.start()

    def hand_values(r):
        chip = here.peer(2 * r) // 2
        pair = pl.ds(2 * chip, 2)
        total = main[1, f, pair].astype(F32)
        for d in range(1, depth):
            value_sends[r][d - 1].wait_recv()
            total = total + main_in[d - 1, pair].astype(F32)
        main[1, f, pair] = total.astype(BF16)
        for k in (2 * r + 1, 2 * r):
            hand_over(1, k)

    last_stream = streams - 1
    tail = grad_sums[last_stream]
    tail.give_beside(back_of(last_stream))
    tail.join(back_of(last_stream))
    for copy in told:
        copy.wait_recv()
    vector_all[s] = jnp.sum(vector_line[...], axis=0).astype(BF16)
    mine_v = vector_all.at[s]
    heard = [links.copy(mine_v, mine_v, here.at(k)) for k in range(1, 8)]
    for copy in heard:
        copy.start()
    mixed_sum.arrived()
    for stream in range(streams):
        row_scale = column(norm_row(stream, s))

        for i in range(block // FEW):
            span = slice(stream * block + i * FEW, stream * block + (i + 1) * FEW)
            branch_sum = mixed_sum.total(span) * wide(row_scale[i * FEW : (i + 1) * FEW], D // LANES)
            mixed_out[span] = (hidden[span].astype(F32) + branch_sum).astype(BF16)
    for copy in common_across:
        copy.wait_recv()
    at = ahead(s * slab, slab)
    joined = common[at, :].astype(F32)
    for r in range(3):
        joined = joined + common_recv[r].astype(F32)
    common_line[...] = joined.astype(BF16).reshape(depth, rows, common.shape[1])
    common_sends_z = []
    for d in range(1, depth):
        copy = links.copy(common_line.at[here.plane(d)], common_last.at[d - 1], here.beyond(d))
        copy.start()
        common_sends_z.append(copy)

    for i in range(2):
        tail.pass_on(i)
    hand_values(3)
    grad_again.wait()

    def finish_tokens(stream):
        grad_sums[stream].arrived()
        for i in range(block // FEW):
            span = slice(i * FEW, (i + 1) * FEW)
            at = slice(stream * block + i * FEW, stream * block + (i + 1) * FEW)
            upstream, inverse = scaled_rows(at)
            unit = upstream * inverse
            grad_normed = grad_sums[stream].total(span) * gain
            along = jnp.mean(grad_normed * unit, axis=-1, keepdims=True)
            moved = inverse * (grad_normed - unit * along)
            upstream_out[at] = grad_own[at].astype(F32) + moved

    for k in range(last_stream):
        finish_tokens(k)
    for copy in heard:
        copy.wait_recv()
    vector_full[...] = vector_all[...].astype(F32)
    all_parameters(vec, vector_full, vector_out, share)
    hand_values(1)
    total = lines[ahead(f * out_rows, out_rows), :].astype(F32)
    for d in range(1, depth):
        line_sends[d - 1].wait_recv()
        total = total + lines_in[d - 1].astype(F32)
    lines_out[...] = total.astype(BF16)
    hand_values(2)
    finish_tokens(last_stream)
    hand_values(0)
    for copy in slab_sends:
        copy.wait_recv()
    main_moves = []
    for part in range(2):
        for k in range(CHANNELS // channels):
            lanes = slice(part * CHANNELS + k * channels, part * CHANNELS + (k + 1) * channels)
            main_moves.append(
                pltpu.make_async_copy(
                    slabs_recv.at[part, k], main_out.at[:, lanes], moves.at[6 + len(main_moves)]
                )
            )
            main_moves[-1].start()
    for copy in common_sends_z:
        copy.wait_recv()
    total = common_line[f].astype(F32)
    for d in range(1, depth):
        total = total + common_last[d - 1].astype(F32)
    common_sum[...] = total.astype(BF16)
    common_move = pltpu.make_async_copy(
        common_sum, main_out.at[:, 2 * CHANNELS :], moves.at[31]
    )
    common_move.start()
    for each in grad_sums:
        each.settle()
    for r in chips:
        for copy in value_sends[r]:
            copy.wait_send()
    for k in range(8):
        for d in range(depth - 1):
            for way in range(2):
                for part in range(2):
                    pl.when(sends(d)[way])(hops[part, k, d][way].wait_send)
    pending = line_sends + gate_sends + common_sends + told + heard
    for copy in pending + common_across + slab_sends + common_sends_z:
        copy.wait_send()
    for copy in main_moves + [common_move]:
        copy.wait()


def vmem_call(kernel, name, out_shape, out_specs, inputs, in_specs, scratch, vmem_mib):
    return pl.pallas_call(
        kernel,
        out_shape=out_shape,
        in_specs=[pl.BlockSpec(memory_space=space) for space in in_specs],
        out_specs=[pl.BlockSpec(memory_space=space) for space in out_specs],
        scratch_shapes=scratch,
        name=name,
        compiler_params=pltpu.CompilerParams(
            vmem_limit_bytes=vmem_mib << 20, collective_id=0, has_side_effects=True
        ),
    )(*inputs)


def heads_plan(
    hidden_in,
    out_grad,
    lengths,
    in_proj,
    in_first,
    in_second,
    out_proj,
    out_first,
    out_second,
    vector,
    vector_first,
    vector_second,
):
    count = lax.axis_size("seq")
    depth = lax.axis_size("fsdp")
    share = HEADS // count
    channels = share * HEAD_DIM
    mixed = channels + 2 * STATE
    streams, block = hidden_in.shape[0], hidden_in.shape[1]
    length = block * count
    chunks = length // Q
    rows = in_proj.shape[0]
    columns = 3 * channels
    out_rows = out_proj.shape[0]
    across = 2 * STATE + LANES
    slab = depth * rows
    size = vector.shape[0]
    padded = jnp.pad(vector, (0, VECTOR_ROWS * LANES - size)).reshape(VECTOR_ROWS, LANES)
    shape = jax.ShapeDtypeStruct
    dma = pltpu.SemaphoreType.DMA
    low = lambda *dims: pltpu.VMEM(dims, BF16)
    full = lambda *dims: pltpu.VMEM(dims, F32)
    mixed_out, input_grad, main, out_summed, small, _ = vmem_call(
        functools.partial(block_kernel, depth),
        "block",
        [
            shape((streams * block, D), BF16),
            shape((streams * block, D), F32),
            shape((rows, 2 * CHANNELS + across), BF16),
            shape((out_rows, D), BF16),
            shape((VECTOR_ROWS, LANES), F32),
            shape((streams, length, D), BF16),
        ],
        [pltpu.VMEM] * 2 + [pl.ANY] + [pltpu.VMEM] * 2 + [pl.ANY],
        (lengths, hidden_in.reshape(-1, D), out_grad.reshape(-1, D))
        + (in_proj.astype(BF16), out_proj, padded),
        [pltpu.SMEM, pltpu.VMEM, pl.ANY] + [pltpu.VMEM] * 3,
        [
            low(streams, length, D),
            low(streams, length, D),
            low(D, columns),
            low(channels, D),
            full(streams, length, columns),
            full(streams, length, channels),
            low(streams, chunks, STATE, channels),
            low(streams, length, mixed),
            full(streams, length, LANES),
            full(16, mixed),
            full(streams, STATE, channels),
            full(streams, 8, mixed),
            full(16, mixed),
            low(rows, across),
            full(count, 2, streams, chunks, Q),
            full(2, streams, chunks, Q),
            low(4, streams * block, D),
            low(4, streams * block, D),
            low(2, streams * block // 2, D),
            low(2, streams * block, D),
            low(2, streams * block, D),
            low(channels, D),
            low(depth - 1, out_rows, D),
            low(2, depth, count, rows, channels),
            low(depth - 1, count, rows, channels),
            low(depth - 1, count, rows, channels),
            low(2, count, rows, channels),
            low(D, across),
            low(4, slab, across),
            low(3, slab, across),
            low(depth, rows, across),
            low(depth - 1, rows, across),
            low(rows, across),
            full(8, D),
            full(depth, 16, mixed),
            low(count, 16, mixed),
            full(count, 16, mixed),
            dma((288,)),
            dma((288,)),
            dma((32,)),
            pltpu.SemaphoreType.REGULAR((3,)),
        ],
        63,
    )
    in_summed = main[:, : in_proj.shape[1]].astype(F32)
    out_summed = out_summed.astype(F32)
    vector_summed = small.reshape(-1)[:size]
    in_new = adam_update(in_proj, in_first, in_second, in_summed, RATE_MATRIX, DECAY_MATRIX)
    out_new = adam_update(out_proj, out_first, out_second, out_summed, RATE_MATRIX, DECAY_MATRIX)
    vec_new = adam_update(vector, vector_first, vector_second, vector_summed, RATE_VECTOR, 0.0)
    mixed_out = mixed_out.reshape(hidden_in.shape)
    input_grad = input_grad.reshape(hidden_in.shape)
    return (mixed_out, input_grad, *in_new, *out_new, *vec_new)


def solution(mesh):
    return jax.shard_map(
        heads_plan if mesh.shape["seq"] == 8 else positions_plan,
        mesh=mesh,
        in_specs=(
            P("fsdp", "seq", None),
            P("fsdp", "seq", None),
            P("fsdp", None),
            P(("seq", "fsdp"), None),
            P(("seq", "fsdp"), None),
            P(("seq", "fsdp"), None),
            P(("seq", "fsdp"), None),
            P(("seq", "fsdp"), None),
            P(("seq", "fsdp"), None),
            P(),
            P(),
            P(),
        ),
        out_specs=(
            P("fsdp", "seq", None),
            P("fsdp", "seq", None),
            P(("seq", "fsdp"), None),
            P(("seq", "fsdp"), None),
            P(("seq", "fsdp"), None),
            P(("seq", "fsdp"), None),
            P(("seq", "fsdp"), None),
            P(("seq", "fsdp"), None),
            P(),
            P(),
            P(),
        ),
        check_vma=False,
    )
```
